32 devices in a mesh: fsdp: 8 (over y, x, core), ctx: 4 (over z).
Axes of the slice: x: 2, y: 2, z: 4, core: 2. Of those that a mesh axis runs over, the one named last changes fastest.
Arguments:
- tokens: bfloat16 [8, 1024, 1536], P('fsdp', 'ctx'), may hold values from -6 to 6
- positions: int32 [8, 1024], P('fsdp', 'ctx'), may hold values from 0 to 1023, as said below
- cotangent: bfloat16 [8, 1024, 1536], P('fsdp', 'ctx'), may hold values from -6 to 6
- attn_norm: float32 [1536], P('fsdp'), may hold values from 0.25 to 1.75
- ffn_norm: float32 [1536], P('fsdp'), may hold values from 0.25 to 1.75
- in_proj: bfloat16 [1536, 2048], P('fsdp'), may hold values from -0.15625 to 0.15625
- in_bias: float32 [2048], P('fsdp'), may hold values from -1.8 to 1.8
- out_proj: bfloat16 [1536, 1536], P('fsdp'), may hold values from -0.875 to 0.875
- gate_up: bfloat16 [1536, 17920], P('fsdp'), may hold values from -0.15625 to 0.15625
- down_proj: bfloat16 [8960, 1536], P('fsdp'), may hold values from -0.0625 to 0.0625
Outputs:
- block_out: bfloat16 [8, 1024, 1536], P('fsdp', 'ctx')
- tokens_grad: float32 [8, 1024, 1536], P('fsdp', 'ctx')
- attn_norm_grad: float32 [1536], P('fsdp')
- ffn_norm_grad: float32 [1536], P('fsdp')
- in_proj_grad: float32 [1536, 2048], P('fsdp')
- in_bias_grad: float32 [2048], P('fsdp')
- out_proj_grad: float32 [1536, 1536], P('fsdp')
- gate_up_grad: float32 [1536, 17920], P('fsdp')
- down_proj_grad: float32 [8960, 1536], P('fsdp')
The draws below stay inside these ranges and needn't reach their ends.
Inputs may be any that keep to these rules, and one draw needn't show every extreme that they name: `positions`: each sequence is a pack of documents: a position is 0 at a document's first token and one more than the token before it elsewhere; in every sequence one document starts within the first 256 tokens and ends within the last 256, and in one sequence a single document fills all 1024 tokens.
All inputs are finite; a program needn't handle non-finite values.
Results may differ from the reference program's by a relative error of at most 0.018.
Values may be sent and summed in bfloat16 or wider, within the bound.
No kernel may reach another device: no remote copies, remote signals or barrier semaphores. Data moves between devices by JAX's collectives and lax.ppermute only.
A program may use at most 384 MiB of HBM per device.

```python
import jax
import jax.numpy as jnp
from jax import lax

D = 1536
QUERY_HEADS = 12
KEY_VALUE_HEADS = 2
HEAD_SIZE = 128
FF = 8960
BLOCK_TOKENS = 256
QD = 1536
QKV = 2048
SEQ = 1024
SEQS = 8


def draw_positions(key, part):
    key = jax.random.fold_in(key, 7)
    pick_key, seqs_key = jax.random.split(key)
    chosen = jax.random.randint(pick_key, (), 0, SEQS)

    def one_sequence(seq_key, whole_doc):
        first_key, last_key, cut_key = jax.random.split(seq_key, 3)
        doc_begin = jax.random.randint(first_key, (), 0, BLOCK_TOKENS)
        doc_finish = jax.random.randint(last_key, (), SEQ - BLOCK_TOKENS + 1, SEQ + 1)
        doc_begin = jnp.where(whole_doc, 0, doc_begin)
        doc_finish = jnp.where(whole_doc, SEQ, doc_finish)
        token_position_index = jnp.arange(SEQ, dtype=jnp.int32)
        restarts = jax.random.randint(cut_key, (SEQ,), 0, 24) == 0
        inside = (token_position_index > doc_begin) & (token_position_index < doc_finish)
        restarts = restarts & jnp.logical_not(inside) | (token_position_index == doc_begin) | (token_position_index == doc_finish) | (token_position_index == 0)
        last_start = lax.cummax(jnp.where(restarts, token_position_index, 0), axis=0)
        return (token_position_index - last_start).astype(jnp.int32)
    seq_keys = jax.random.split(seqs_key, SEQS)
    whole_flags = jnp.arange(SEQS, dtype=jnp.int32) == chosen
    return jax.vmap(one_sequence)(seq_keys, whole_flags)


def steps_of(key, dims, pieces, least, largest):
    gain = 1.0
    for position, shards_of in pieces:
        draws = jax.random.uniform(jax.random.fold_in(jax.random.fold_in(key, 6), position), (shards_of,), jnp.float32, least / len(pieces), largest / len(pieces))
        gain = gain * jnp.repeat(jnp.exp(draws), dims[position] // shards_of).reshape((-1,) + (1,) * (len(dims) - 1 - position))
    return gain


def scatter_about(key, shape, deviation, bound, cuts=(), kind=jnp.bfloat16):
    drawn = jax.random.normal(key, shape, jnp.float32) * deviation
    if len(cuts) > 0:
        drawn = steps_of(key, shape, cuts, -0.22, 0.18) * drawn
    return jnp.clip(drawn, min=-bound, max=bound).astype(kind)


def setup_inputs(seed: int = 0) -> dict:
    key_of = jax.random.split(jax.random.key(seed), 11)
    tokens = scatter_about(key_of[0], (SEQS, SEQ, D), 1.0, 6.0, ((0, 8), (1, 4)))
    positions = draw_positions(jax.random.fold_in(key_of[10], 71), 0)
    cotangent = scatter_about(key_of[2], (SEQS, SEQ, D), 1.0, 6.0, ((0, 8), (1, 4)))
    attn_norm = jnp.clip(1.0 + 0.15 * jax.random.normal(key_of[3], (D,), jnp.float32), 0.25, 1.75)
    ffn_norm = jnp.clip(1.0 + 0.15 * jax.random.normal(key_of[4], (D,), jnp.float32), 0.25, 1.75)
    in_proj = scatter_about(key_of[5], (D, QKV), D ** -0.5, 0.15625, ((0, 8),))
    in_bias = scatter_about(key_of[6], (QKV,), 0.3, 1.8, ((0, 8),), jnp.float32)
    out_proj = scatter_about(key_of[7], (QD, D), (QD // 32) ** -0.5, 0.875, ((0, 8),))
    gate_up = scatter_about(key_of[8], (D, 2 * FF), D ** -0.5, 0.15625, ((0, 8),))
    down_proj = scatter_about(key_of[9], (FF, D), FF ** -0.5, 0.0625, ((0, 8),))
    return dict(tokens=tokens, positions=positions, cotangent=cotangent, attn_norm=attn_norm, ffn_norm=ffn_norm, in_proj=in_proj, in_bias=in_bias, out_proj=out_proj, gate_up=gate_up, down_proj=down_proj)


@jax.custom_vjp
def lower_bound(v):
    return lax.optimization_barrier(v.astype(jnp.bfloat16)).astype(jnp.float32)

@jax.custom_vjp
def low_back(v):
    return v

def low_keep(v):
    return (lower_bound(v), None)

def low_pass(kept, grad):
    return (grad,)

def back_keep(v):
    return (v, None)

def back_low(kept, grad):
    return (lower_bound(grad),)
lower_bound.defvjp(low_keep, low_pass)
low_back.defvjp(back_keep, back_low)
norm_eps = 1e-06
rope_base = 1000000.0
masked_score = -1e+30
highest = lax.Precision.HIGHEST

def rms_scale(value_rows, scale_vec):
    return value_rows * lax.rsqrt(lax.optimization_barrier(jnp.mean(value_rows * value_rows, axis=-1, keepdims=True)) + norm_eps) * scale_vec

def frequencies():
    return rope_base ** (-(jnp.arange(HEAD_SIZE // 2, dtype=jnp.float32) * (2.0 / HEAD_SIZE)))

def apply_rotary(value_rows, rotary_angles):
    half_width = HEAD_SIZE // 2
    cosine = jnp.cos(rotary_angles)[:, None, :]
    sine_part = jnp.sin(rotary_angles)[:, None, :]
    first_half = value_rows[..., :half_width]
    second_half = value_rows[..., half_width:]
    return jnp.concatenate([first_half * cosine - second_half * sine_part, second_half * cosine + first_half * sine_part], axis=-1)

def attention(query_rows, key_rows, value_rows, positions):
    sequence_length = query_rows.shape[0]
    head_groups = QUERY_HEADS // KEY_VALUE_HEADS
    block_list = sequence_length // BLOCK_TOKENS
    token_position_index = jnp.arange(sequence_length, dtype=jnp.int32)
    document_begin = token_position_index - positions

    def single_block(block_args):
        query_block, query_index, start_index = block_args
        scores = jnp.einsum('qcgd,kcd->cgqk', query_block, key_rows, precision=highest) * HEAD_SIZE ** (-0.5)
        scores = low_back(scores)
        allowed = (token_position_index[None, :] <= query_index[:, None]) & (token_position_index[None, :] >= start_index[:, None])
        scores = jnp.where(allowed[None, None], scores, masked_score)
        weights = lower_bound(jax.nn.softmax(scores, axis=-1))
        return jnp.einsum('cgqk,kcd->qcgd', weights, value_rows, precision=highest)
    block_outputs = lax.map(jax.checkpoint(single_block), (query_rows.reshape(block_list, BLOCK_TOKENS, KEY_VALUE_HEADS, head_groups, HEAD_SIZE), token_position_index.reshape(block_list, BLOCK_TOKENS), document_begin.reshape(block_list, BLOCK_TOKENS)))
    return block_outputs.reshape(sequence_length, QUERY_HEADS * HEAD_SIZE)

def one_sequence(tokens, positions, attn_norm, ffn_norm, in_proj, in_bias, out_proj, gate_up, down_proj):
    sequence_length = tokens.shape[0]
    query_span_width = QUERY_HEADS * HEAD_SIZE
    key_span_width = KEY_VALUE_HEADS * HEAD_SIZE
    normed = lower_bound(rms_scale(tokens, attn_norm))
    projected_rows = low_back(jnp.dot(normed, in_proj, precision=highest) + in_bias)
    rotary_angles = positions.astype(jnp.float32)[:, None] * frequencies()[None, :]
    query_rows = lower_bound(apply_rotary(projected_rows[:, :query_span_width].reshape(sequence_length, QUERY_HEADS, HEAD_SIZE), rotary_angles))
    key_rows = lower_bound(apply_rotary(projected_rows[:, query_span_width:query_span_width + key_span_width].reshape(sequence_length, KEY_VALUE_HEADS, HEAD_SIZE), rotary_angles))
    value_rows = lower_bound(projected_rows[:, query_span_width + key_span_width:].reshape(sequence_length, KEY_VALUE_HEADS, HEAD_SIZE))
    attended = low_back(lower_bound(attention(query_rows, key_rows, value_rows, positions)))
    middle = tokens + low_back(jnp.dot(attended, out_proj, precision=highest))
    normed_ffn = lower_bound(rms_scale(middle, ffn_norm))
    gate_values = low_back(jnp.dot(normed_ffn, gate_up, precision=highest))
    hidden = lower_bound(jax.nn.silu(gate_values[:, :FF]) * gate_values[:, FF:])
    return middle + low_back(jnp.dot(hidden, down_proj, precision=highest))

def reference(tokens, positions, cotangent, attn_norm, ffn_norm, in_proj, in_bias, out_proj, gate_up, down_proj):
    params = (attn_norm.astype(jnp.float32), ffn_norm.astype(jnp.float32), in_proj.astype(jnp.float32), in_bias.astype(jnp.float32), out_proj.astype(jnp.float32), gate_up.astype(jnp.float32), down_proj.astype(jnp.float32))

    def forward(inputs, *weights):

        def per_sequence(seq_args):
            return one_sequence(seq_args[0], seq_args[1], *weights)
        return lax.map(jax.checkpoint(per_sequence), (inputs, positions))
    block_out, pullback = jax.vjp(forward, tokens.astype(jnp.float32), *params)
    gradients = pullback(cotangent.astype(jnp.float32))
    return (block_out.astype(jnp.bfloat16), gradients[0], gradients[1], gradients[2], gradients[3], gradients[4], gradients[5], gradients[6], gradients[7])
```

```python
import jax
import jax.numpy as jnp
from jax import lax
from jax.sharding import PartitionSpec as P

D = 1536
QUERY_HEADS = 12
KEY_VALUE_HEADS = 2
HEAD_SIZE = 128
FF = 8960


norm_eps = 1e-06
rope_base = 1000000.0
masked_score = -1e30


def rms_scale(value_rows, scale_vec):
    return (
        value_rows
        * lax.rsqrt(jnp.mean(value_rows * value_rows, axis=-1, keepdims=True) + norm_eps)
        * scale_vec
    )


def norm_backward(value_rows, scale_vec, incoming):
    unused_out, pullback = jax.vjp(rms_scale, value_rows, scale_vec)
    return pullback(incoming)


def frequencies():
    return rope_base ** (-(jnp.arange(HEAD_SIZE // 2, dtype=jnp.float32) * (2.0 / HEAD_SIZE)))


def apply_rotary(value_rows, rotary_angles):
    half_width = HEAD_SIZE // 2
    cosine = jnp.cos(rotary_angles)[:, None, :]
    sine_part = jnp.sin(rotary_angles)[:, None, :]
    first_half = value_rows[..., :half_width]
    second_half = value_rows[..., half_width:]
    return jnp.concatenate(
        [
            first_half * cosine - second_half * sine_part,
            second_half * cosine + first_half * sine_part,
        ],
        axis=-1,
    )


def dot_f32(left, right):
    return jnp.dot(left, right, preferred_element_type=jnp.float32)


def dot_right_t(left, right):
    return jnp.einsum("tn,dn->td", left, right, preferred_element_type=jnp.float32)


def dot_left_t(left, right):
    return jnp.einsum("tr,tn->rn", left, right, preferred_element_type=jnp.float32)


def add_low(left, right):
    total = left.astype(jnp.float32) + right.astype(jnp.float32)
    return lax.reduce_precision(total, 8, 7).astype(jnp.bfloat16)


def ctx_total(part):
    count = lax.axis_size("ctx")
    middle = count // 2
    me = lax.axis_index("ctx")
    for hop in range(middle - 1):
        got = lax.ppermute(part, "ctx", [(hop, hop + 1), (count - 1 - hop, count - 2 - hop)])
        part = add_low(part, got)
    part = add_low(
        part, lax.ppermute(part, "ctx", [(middle - 1, middle), (middle, middle - 1)])
    )
    for hop in reversed(range(middle - 1)):
        got = lax.ppermute(part, "ctx", [(hop + 1, hop), (count - 2 - hop, count - 1 - hop)])
        part = jnp.where((me == hop) | (me == count - 1 - hop), got, part)
    return part


def ctx_total_rows(part, pieces):
    rows = part.shape[0] // pieces
    return jnp.concatenate(
        [
            ctx_total(part[piece * rows : (piece + 1) * rows]).astype(jnp.float32)
            for piece in range(pieces)
        ],
        axis=0,
    )


def fsdp_shard_sum(part):
    return lax.psum_scatter(
        part.astype(jnp.bfloat16), "fsdp", scatter_dimension=0, tiled=True
    )


def score_block(query_b, keys_all, allowed):
    scores = jnp.einsum(
        "qcgd,kcd->cgqk", query_b, keys_all, preferred_element_type=jnp.float32
    ) * HEAD_SIZE ** (-0.5)
    return jnp.where(allowed[None, None], scores, masked_score)


def shards(
    tokens,
    positions,
    cotangent,
    attn_norm,
    ffn_norm,
    in_proj,
    in_bias,
    out_proj,
    gate_up,
    down_proj,
):
    token_rows = tokens.shape[1]
    fsdp_count = lax.axis_size("fsdp")
    units = FF // fsdp_count
    shard_d = D // fsdp_count
    query_span_width = QUERY_HEADS * HEAD_SIZE
    key_span_width = KEY_VALUE_HEADS * HEAD_SIZE
    head_groups = QUERY_HEADS // KEY_VALUE_HEADS
    score_scale = HEAD_SIZE ** (-0.5)
    residual_in = tokens[0].astype(jnp.float32)
    position = positions[0]
    vectors = lax.all_gather(
        jnp.concatenate([attn_norm, ffn_norm, in_bias])[None], "fsdp", axis=0, tiled=True
    )
    attn_scale = vectors[:, :shard_d].reshape(D)
    ffn_scale = vectors[:, shard_d : 2 * shard_d].reshape(D)
    bias_full = vectors[:, 2 * shard_d :].reshape(-1)
    in_full = lax.all_gather(in_proj, "fsdp", axis=0, tiled=True)
    out_full = lax.all_gather(out_proj, "fsdp", axis=0, tiled=True)
    gate_up_mine = lax.all_to_all(
        gate_up.reshape(shard_d, 2, fsdp_count, units), "fsdp", 2, 0, tiled=True
    ).reshape(D, 2 * units)
    grad_out_b = cotangent[0]
    grad_out = grad_out_b.astype(jnp.float32)
    grad_out_all = lax.all_gather(grad_out_b, "fsdp", axis=0, tiled=True)

    normed_b = rms_scale(residual_in, attn_scale).astype(jnp.bfloat16)
    projected_rows = dot_f32(normed_b, in_full) + bias_full
    rotary_angles = position.astype(jnp.float32)[:, None] * frequencies()[None, :]
    query_b = (
        apply_rotary(
            projected_rows[:, :query_span_width].reshape(token_rows, QUERY_HEADS, HEAD_SIZE),
            rotary_angles,
        )
        .astype(jnp.bfloat16)
        .reshape(token_rows, KEY_VALUE_HEADS, head_groups, HEAD_SIZE)
    )
    keys_b = apply_rotary(
        projected_rows[:, query_span_width : query_span_width + key_span_width].reshape(
            token_rows, KEY_VALUE_HEADS, HEAD_SIZE
        ),
        rotary_angles,
    ).astype(jnp.bfloat16)
    values_b = (
        projected_rows[:, query_span_width + key_span_width :]
        .reshape(token_rows, KEY_VALUE_HEADS, HEAD_SIZE)
        .astype(jnp.bfloat16)
    )
    both_all = lax.all_gather(
        jnp.concatenate([keys_b, values_b], axis=1), "ctx", axis=0, tiled=True
    )
    keys_all = both_all[:, :KEY_VALUE_HEADS]
    values_all = both_all[:, KEY_VALUE_HEADS:]
    query_index = lax.axis_index("ctx") * token_rows + jnp.arange(token_rows, dtype=jnp.int32)
    document_begin = query_index - position
    key_index = jnp.arange(keys_all.shape[0], dtype=jnp.int32)
    allowed = (key_index[None, :] <= query_index[:, None]) & (
        key_index[None, :] >= document_begin[:, None]
    )
    scores = score_block(query_b, keys_all, allowed)
    top_score = jnp.max(scores, axis=-1, keepdims=True)
    raised = jnp.exp(scores - top_score)
    row_total = jnp.sum(raised, axis=-1, keepdims=True)
    probs_b = (raised / row_total).astype(jnp.bfloat16)
    log_total = top_score + jnp.log(row_total)
    attended_b = (
        jnp.einsum("cgqk,kcd->qcgd", probs_b, values_all, preferred_element_type=jnp.float32)
        .reshape(token_rows, query_span_width)
        .astype(jnp.bfloat16)
    )
    middle = residual_in + dot_f32(attended_b, out_full)
    normed_ffn_b = rms_scale(middle, ffn_scale).astype(jnp.bfloat16)
    normed_ffn_all = lax.all_gather(normed_ffn_b, "fsdp", axis=0, tiled=True)

    gate_values = dot_f32(normed_ffn_all, gate_up_mine)
    gate_part = gate_values[:, :units]
    up_part = gate_values[:, units:]
    hidden_b = (jax.nn.silu(gate_part) * up_part).astype(jnp.bfloat16)
    grad_hidden = dot_right_t(grad_out_all, down_proj)
    unused_out, gate_pullback = jax.vjp(
        lambda gate_arg, up_arg: jax.nn.silu(gate_arg) * up_arg, gate_part, up_part
    )
    grad_gate, grad_up = gate_pullback(grad_hidden)
    grad_gate_values_b = jnp.concatenate([grad_gate, grad_up], axis=1).astype(jnp.bfloat16)

    down_grad = ctx_total_rows(dot_left_t(hidden_b, grad_out_all).astype(jnp.bfloat16), 4)
    grad_normed_ffn = fsdp_shard_sum(dot_right_t(grad_gate_values_b, gate_up_mine)).astype(
        jnp.float32
    )
    gate_grad_mine = dot_left_t(normed_ffn_all, grad_gate_values_b).astype(jnp.bfloat16)
    gate_grad_part = lax.all_to_all(
        gate_grad_mine.reshape(D, 2, 1, units), "fsdp", 0, 2, tiled=True
    ).reshape(shard_d, 2 * FF)
    gate_grad = ctx_total_rows(gate_grad_part, 6)
    block_out = middle + fsdp_shard_sum(dot_f32(hidden_b, down_proj)).astype(jnp.float32)

    grad_mid_norm, ffn_grad = norm_backward(middle, ffn_scale, grad_normed_ffn)
    grad_middle = grad_out + grad_mid_norm
    grad_middle_b = grad_middle.astype(jnp.bfloat16)
    out_grad = ctx_total_rows(fsdp_shard_sum(dot_left_t(attended_b, grad_middle_b)), 1)
    grad_attended_b = (
        dot_right_t(grad_middle_b, out_full)
        .astype(jnp.bfloat16)
        .reshape(token_rows, KEY_VALUE_HEADS, head_groups, HEAD_SIZE)
    )
    scores = score_block(query_b, keys_all, allowed)
    probs_full = jnp.exp(scores - log_total)
    probs_again_b = probs_full.astype(jnp.bfloat16)
    grad_probs = jnp.einsum(
        "qcgd,kcd->cgqk", grad_attended_b, values_all, preferred_element_type=jnp.float32
    )
    inner_sum = jnp.sum(grad_probs * probs_full, axis=-1, keepdims=True)
    grad_scores_b = (probs_full * (grad_probs - inner_sum)).astype(jnp.bfloat16)
    grad_query = (
        jnp.einsum("cgqk,kcd->qcgd", grad_scores_b, keys_all, preferred_element_type=jnp.float32)
        * score_scale
    )
    grad_keys_all = (
        jnp.einsum("cgqk,qcgd->kcd", grad_scores_b, query_b, preferred_element_type=jnp.float32)
        * score_scale
    )
    grad_values_all = jnp.einsum(
        "cgqk,qcgd->kcd", probs_again_b, grad_attended_b, preferred_element_type=jnp.float32
    )
    grad_both = lax.psum_scatter(
        jnp.concatenate([grad_keys_all, grad_values_all], axis=1).astype(jnp.bfloat16),
        "ctx",
        scatter_dimension=0,
        tiled=True,
    ).astype(jnp.float32)
    grad_keys = grad_both[:, :KEY_VALUE_HEADS]
    grad_values = grad_both[:, KEY_VALUE_HEADS:]
    grad_projected_b = jnp.concatenate(
        [
            apply_rotary(
                grad_query.reshape(token_rows, QUERY_HEADS, HEAD_SIZE), -rotary_angles
            ).reshape(token_rows, query_span_width),
            apply_rotary(grad_keys, -rotary_angles).reshape(token_rows, key_span_width),
            grad_values.reshape(token_rows, key_span_width),
        ],
        axis=1,
    ).astype(jnp.bfloat16)
    bias_grad = jnp.sum(grad_projected_b.astype(jnp.float32), axis=0)
    in_grad = ctx_total_rows(fsdp_shard_sum(dot_left_t(normed_b, grad_projected_b)), 1)
    grad_normed = dot_right_t(grad_projected_b, in_full)
    grad_in_norm, attn_grad = norm_backward(residual_in, attn_scale, grad_normed)
    tokens_grad = grad_middle + grad_in_norm
    vector_total = lax.psum(
        jnp.concatenate(
            [
                attn_grad.reshape(fsdp_count, -1),
                ffn_grad.reshape(fsdp_count, -1),
                bias_grad.reshape(fsdp_count, -1),
            ],
            axis=1,
        ),
        ("fsdp", "ctx"),
    )
    vector_mine = lax.dynamic_index_in_dim(
        vector_total, lax.axis_index("fsdp"), axis=0, keepdims=False
    )
    return (
        block_out.astype(jnp.bfloat16).reshape(1, token_rows, D),
        tokens_grad.reshape(1, token_rows, D),
        vector_mine[:shard_d],
        vector_mine[shard_d : 2 * shard_d],
        in_grad,
        vector_mine[2 * shard_d :],
        out_grad,
        gate_grad,
        down_grad,
    )


def solution(mesh):
    in_specs = (
        P("fsdp", "ctx", None),
        P("fsdp", "ctx"),
        P("fsdp", "ctx", None),
        P("fsdp"),
        P("fsdp"),
        P("fsdp", None),
        P("fsdp"),
        P("fsdp", None),
        P("fsdp", None),
        P("fsdp", None),
    )
    out_specs = (
        P("fsdp", "ctx", None),
        P("fsdp", "ctx", None),
        P("fsdp"),
        P("fsdp"),
        P("fsdp", None),
        P("fsdp"),
        P("fsdp", None),
        P("fsdp", None),
        P("fsdp", None),
    )
    return jax.shard_map(shards, mesh=mesh, in_specs=in_specs, out_specs=out_specs, check_vma=False)
```

```python
import jax
import jax.numpy as jnp
from jax import lax
from jax.experimental import pallas as pl
from jax.experimental.pallas import tpu as pltpu
from jax.sharding import PartitionSpec as P

D = 1536
QUERY_HEADS = 12
KEY_VALUE_HEADS = 2
HEAD_SIZE = 128
FF = 8960


norm_eps = 1e-06
rope_base = 1000000.0
masked_score = -1e30


def rms_scale(value_rows, scale_vec):
    return (
        value_rows
        * lax.rsqrt(jnp.mean(value_rows * value_rows, axis=-1, keepdims=True) + norm_eps)
        * scale_vec
    )


def norm_backward(value_rows, scale_vec, incoming):
    unused_out, pullback = jax.vjp(lambda rows: rms_scale(rows, scale_vec), value_rows)
    return pullback(incoming)[0]


def frequencies():
    return rope_base ** (-(jnp.arange(HEAD_SIZE // 2, dtype=jnp.float32) * (2.0 / HEAD_SIZE)))


def apply_rotary(value_rows, rotary_angles):
    half_width = HEAD_SIZE // 2
    cosine = jnp.cos(rotary_angles)[:, None, :]
    sine_part = jnp.sin(rotary_angles)[:, None, :]
    first_half = value_rows[..., :half_width]
    second_half = value_rows[..., half_width:]
    return jnp.concatenate(
        [
            first_half * cosine - second_half * sine_part,
            second_half * cosine + first_half * sine_part,
        ],
        axis=-1,
    )


def dot_f32(left, right):
    return jnp.dot(left, right, preferred_element_type=jnp.float32)


def dot_right_t(left, right):
    return jnp.einsum("tn,dn->td", left, right, preferred_element_type=jnp.float32)


def dot_left_t(left, right):
    return jnp.einsum("tr,tn->rn", left, right, preferred_element_type=jnp.float32)


def add_low(left, right):
    total = left.astype(jnp.float32) + right.astype(jnp.float32)
    return lax.reduce_precision(total, 8, 7).astype(jnp.bfloat16)


def after(value, earlier):
    return lax.optimization_barrier((value, earlier))[0]


def exchange(value, mask):
    count = lax.axis_size("fsdp")
    return lax.ppermute(value, "fsdp", [(place, place ^ mask) for place in range(count)])


def fsdp_pieces(block):
    count = lax.axis_size("fsdp")
    pieces = [(0, 0, block)]
    if count == 8:
        half = block.shape[0] // 2
        by_x = exchange(block, 2)
        by_y = exchange(block, 4)
        pieces += [
            (2, 0, by_x),
            (4, 0, by_y),
            (6, 0, exchange(by_x[:half], 4)),
            (6, half, exchange(by_y[half:], 2)),
        ]
    else:
        pieces += [(mask, 0, exchange(block, mask)) for mask in range(2, count, 2)]
    return pieces + [(mask + 1, first, exchange(rows, 1)) for mask, first, rows in pieces]


def fsdp_gather_rows(block):
    me = lax.axis_index("fsdp")
    rows = block.shape[0]
    whole = jnp.zeros((lax.axis_size("fsdp") * rows, block.shape[1]), block.dtype)
    for mask, first, piece in fsdp_pieces(block):
        whole = lax.dynamic_update_slice(whole, piece, ((me ^ mask) * rows + first, 0))
    return whole


def mask_order():
    count = lax.axis_size("fsdp")
    return list(range(1, count, 2)) + list(range(0, count, 2))


def fsdp_gather_masks(block):
    order = mask_order()
    pieces = sorted(fsdp_pieces(block), key=lambda piece: (order.index(piece[0]), piece[1]))
    return jnp.concatenate([rows for unused_mask, unused_first, rows in pieces], axis=0)


def fsdp_sum_masks(odd, even):
    count = lax.axis_size("fsdp")
    kept = add_low(even, exchange(odd, 1))
    if count == 8:
        half = kept.shape[1] // 2
        by_x = exchange(kept[1::2, :half], 2)
        by_y = exchange(kept[2:, half:], 4)
        top = add_low(kept[0::2, :half], by_x)
        bottom = add_low(kept[:2, half:], by_y)
        last_y = exchange(top[1], 4)
        last_x = exchange(bottom[1], 2)
        return jnp.concatenate(
            [
                top[0].astype(jnp.float32) + last_y.astype(jnp.float32),
                bottom[0].astype(jnp.float32) + last_x.astype(jnp.float32),
            ],
            axis=0,
        )
    span = count
    while kept.shape[0] > 1:
        span //= 2
        half = kept.shape[0] // 2
        kept = add_low(kept[:half], exchange(kept[half:], span))
    return kept[0].astype(jnp.float32)


def fsdp_shard_sum(part):
    return lax.psum_scatter(
        part.astype(jnp.bfloat16), "fsdp", scatter_dimension=0, tiled=True
    )


def ctx_totals(chunks):
    count = lax.axis_size("ctx")
    middle = count // 2
    me = lax.axis_index("ctx")
    raw = jnp.stack(chunks)
    last = len(chunks) - 1

    def value_of(tick, place, crossing, got):
        base = lax.dynamic_index_in_dim(
            raw, jnp.clip(tick - place, 0, last), axis=0, keepdims=False
        )
        if crossing is not None:
            base = jnp.where(place < middle, base, crossing)
            if middle < count - 1:
                base = jnp.where(place > middle, jnp.zeros_like(base), base)
        return base if got is None else add_low(base, got)

    right, left = [], []
    got_right = got_left = None
    for tick in range(len(chunks) + count - 1):
        right_now = value_of(tick, me, left[-1] if left else None, got_right)
        left_now = value_of(tick, count - 1 - me, right[-1] if right else None, got_left)
        right.append(right_now)
        left.append(left_now)
        senders = [place for place in range(count - 1) if 0 <= tick - place <= last]
        if senders:
            got_right = lax.ppermute(right_now, "ctx", [(s, s + 1) for s in senders])
            got_left = lax.ppermute(
                left_now, "ctx", [(count - 1 - s, count - 2 - s) for s in senders]
            )
    totals = []
    for index in range(len(chunks)):
        total = right[index + middle]
        for place in range(middle + 1, count):
            total = jnp.where(me == place, right[index + place], total)
        for place in range(middle):
            total = jnp.where(me == place, left[index + count - 1 - place], total)
        totals.append(total)
    return totals


def row_chunks(part, pieces):
    rows = part.shape[0] // pieces
    return [part[piece * rows : (piece + 1) * rows] for piece in range(pieces)]


def unit_widths(units):
    first = units // 256 * 128
    second = units - first
    return first, second, -(-second // 128) * 128


def split_units(gate_up, count):
    rows, columns = gate_up.shape
    span = columns // 2
    units = span // count
    first, second, padded = unit_widths(units)
    block = 48

    def kernel(weight_ref, first_ref, second_ref):
        for owner in range(count):
            for side in range(2):
                begin = side * span + owner * units
                first_ref[owner, :, side * first : (side + 1) * first] = weight_ref[
                    :, begin : begin + first
                ]
                second_ref[owner, :, side * padded : side * padded + second] = weight_ref[
                    :, begin + first : begin + units
                ]
                if padded > second:
                    second_ref[
                        owner, :, side * padded + second : (side + 1) * padded
                    ] = jnp.zeros((block, padded - second), gate_up.dtype)

    return pl.pallas_call(
        kernel,
        grid=(rows // block,),
        in_specs=[pl.BlockSpec((block, columns), lambda step: (step, 0))],
        out_specs=[
            pl.BlockSpec((count, block, 2 * first), lambda step: (0, step, 0)),
            pl.BlockSpec((count, block, 2 * padded), lambda step: (0, step, 0)),
        ],
        out_shape=[
            jax.ShapeDtypeStruct((count, rows, 2 * first), gate_up.dtype),
            jax.ShapeDtypeStruct((count, rows, 2 * padded), gate_up.dtype),
        ],
        compiler_params=pltpu.CompilerParams(vmem_limit_bytes=32 * 1024 * 1024),
    )(gate_up)


def join_units(first_part, second_part, units):
    count, rows = first_part.shape[:2]
    span = count * units
    first, second, padded = unit_widths(units)
    block = 48

    def kernel(first_ref, second_ref, whole_ref):
        for owner in range(count):
            for side in range(2):
                begin = side * span + owner * units
                whole_ref[:, begin : begin + first] = first_ref[
                    owner, :, side * first : (side + 1) * first
                ].astype(jnp.float32)
                whole_ref[:, begin + first : begin + units] = second_ref[
                    owner, :, side * padded : side * padded + second
                ].astype(jnp.float32)

    return pl.pallas_call(
        kernel,
        grid=(rows // block,),
        in_specs=[
            pl.BlockSpec((count, block, 2 * first), lambda step: (0, step, 0)),
            pl.BlockSpec((count, block, 2 * padded), lambda step: (0, step, 0)),
        ],
        out_specs=pl.BlockSpec((block, 2 * span), lambda step: (step, 0)),
        out_shape=jax.ShapeDtypeStruct((rows, 2 * span), jnp.float32),
        compiler_params=pltpu.CompilerParams(vmem_limit_bytes=32 * 1024 * 1024),
    )(first_part, second_part)


def swap_blocks(blocks):
    return lax.all_to_all(blocks, "fsdp", 0, 0, tiled=True)


def score_block(query_b, keys_all, allowed):
    scores = jnp.einsum(
        "qcgd,kcd->cgqk", query_b, keys_all, preferred_element_type=jnp.float32
    ) * HEAD_SIZE ** (-0.5)
    return jnp.where(allowed[None, None], scores, masked_score)


def shards(
    tokens,
    positions,
    cotangent,
    attn_norm,
    ffn_norm,
    in_proj,
    in_bias,
    out_proj,
    gate_up,
    down_proj,
):
    token_rows = tokens.shape[1]
    fsdp_count = lax.axis_size("fsdp")
    units = FF // fsdp_count
    shard_d = D // fsdp_count
    query_span_width = QUERY_HEADS * HEAD_SIZE
    key_span_width = KEY_VALUE_HEADS * HEAD_SIZE
    head_groups = QUERY_HEADS // KEY_VALUE_HEADS
    score_scale = HEAD_SIZE ** (-0.5)
    residual_in = tokens[0].astype(jnp.float32)
    position = positions[0]
    vectors = lax.all_gather(
        jnp.concatenate([attn_norm, ffn_norm, in_bias])[None], "fsdp", axis=0, tiled=True
    )
    attn_scale = vectors[:, :shard_d].reshape(D)
    ffn_scale = vectors[:, shard_d : 2 * shard_d].reshape(D)
    bias_full = vectors[:, 2 * shard_d :].reshape(-1)
    in_full = fsdp_gather_rows(in_proj)
    first_units, second_units, padded_units = unit_widths(units)
    first_blocks, second_blocks = split_units(gate_up, fsdp_count)
    down_first = down_proj[:first_units]
    down_second = jnp.pad(down_proj[first_units:], ((0, padded_units - second_units), (0, 0)))
    out_full = lax.all_gather(after(out_proj, in_full), "fsdp", axis=0, tiled=True)
    gate_up_first = swap_blocks(after(first_blocks, in_full)).reshape(D, 2 * first_units)
    grad_out_b = cotangent[0]
    grad_out = grad_out_b.astype(jnp.float32)
    grad_out_gathered = lax.all_gather(after(grad_out_b, out_full), "fsdp", axis=0, tiled=True)
    grad_out_all = jnp.concatenate(
        [
            lax.dynamic_slice_in_dim(
                grad_out_gathered,
                (lax.axis_index("fsdp") ^ mask) * token_rows,
                token_rows,
                axis=0,
            )
            for mask in mask_order()
        ],
        axis=0,
    )

    normed_b = rms_scale(residual_in, attn_scale).astype(jnp.bfloat16)
    projected_rows = dot_f32(normed_b, in_full) + bias_full
    rotary_angles = position.astype(jnp.float32)[:, None] * frequencies()[None, :]
    query_b = (
        apply_rotary(
            projected_rows[:, :query_span_width].reshape(token_rows, QUERY_HEADS, HEAD_SIZE),
            rotary_angles,
        )
        .astype(jnp.bfloat16)
        .reshape(token_rows, KEY_VALUE_HEADS, head_groups, HEAD_SIZE)
    )
    keys_b = apply_rotary(
        projected_rows[:, query_span_width : query_span_width + key_span_width].reshape(
            token_rows, KEY_VALUE_HEADS, HEAD_SIZE
        ),
        rotary_angles,
    ).astype(jnp.bfloat16)
    values_b = (
        projected_rows[:, query_span_width + key_span_width :]
        .reshape(token_rows, KEY_VALUE_HEADS, HEAD_SIZE)
        .astype(jnp.bfloat16)
    )
    both_b = jnp.concatenate([keys_b, values_b], axis=1)
    ctx_count = lax.axis_size("ctx")
    both_all = jnp.concatenate(
        [both_b]
        + [
            lax.ppermute(both_b, "ctx", [(s, s + back) for s in range(ctx_count - back)])
            for back in range(1, ctx_count)
        ],
        axis=0,
    )
    keys_all = both_all[:, :KEY_VALUE_HEADS]
    values_all = both_all[:, KEY_VALUE_HEADS:]
    query_index = lax.axis_index("ctx") * token_rows + jnp.arange(token_rows, dtype=jnp.int32)
    document_begin = query_index - position
    key_index = (
        (lax.axis_index("ctx") - jnp.arange(ctx_count, dtype=jnp.int32))[:, None] * token_rows
        + jnp.arange(token_rows, dtype=jnp.int32)[None, :]
    ).reshape(-1)
    allowed = (key_index[None, :] <= query_index[:, None]) & (
        key_index[None, :] >= document_begin[:, None]
    )
    scores = score_block(query_b, keys_all, allowed)
    top_score = jnp.max(scores, axis=-1, keepdims=True)
    raised = jnp.exp(scores - top_score)
    row_total = jnp.sum(raised, axis=-1, keepdims=True)
    probs_b = (raised / row_total).astype(jnp.bfloat16)
    log_total = top_score + jnp.log(row_total)
    attended_b = (
        jnp.einsum("cgqk,kcd->qcgd", probs_b, values_all, preferred_element_type=jnp.float32)
        .reshape(token_rows, query_span_width)
        .astype(jnp.bfloat16)
    )
    middle = residual_in + dot_f32(attended_b, out_full)
    normed_ffn_b = rms_scale(middle, ffn_scale).astype(jnp.bfloat16)
    normed_ffn_all = fsdp_gather_masks(normed_ffn_b)
    gate_up_second = swap_blocks(after(second_blocks, normed_ffn_all)).reshape(
        D, 2 * padded_units
    )

    def unit_part(gate_up_part, down_part, tokens_in):
        gate_values = dot_f32(tokens_in, gate_up_part)
        width = down_part.shape[0]
        gate_part = gate_values[:, :width]
        up_part = gate_values[:, width:]
        hidden_b = (jax.nn.silu(gate_part) * up_part).astype(jnp.bfloat16)
        grad_hidden = dot_right_t(grad_out_all, down_part)
        unused_out, gate_pullback = jax.vjp(
            lambda gate_arg, up_arg: jax.nn.silu(gate_arg) * up_arg, gate_part, up_part
        )
        grad_gate, grad_up = gate_pullback(grad_hidden)
        return hidden_b, jnp.concatenate([grad_gate, grad_up], axis=1).astype(jnp.bfloat16)

    hidden_first, grad_first = unit_part(gate_up_first, down_first, normed_ffn_all)
    down_grad_first = dot_left_t(hidden_first, grad_out_all).astype(jnp.bfloat16)
    gate_grad_first = dot_left_t(normed_ffn_all, after(grad_first, down_grad_first)).astype(
        jnp.bfloat16
    )
    hidden_second, grad_second = unit_part(
        gate_up_second, down_second, after(normed_ffn_all, gate_grad_first)
    )
    odd_rows = normed_ffn_all.shape[0] // 2

    def input_grads(first_rows):
        rows = slice(first_rows, first_rows + odd_rows)
        return (
            (
                dot_right_t(grad_first[rows], gate_up_first)
                + dot_right_t(grad_second[rows], gate_up_second)
            )
            .astype(jnp.bfloat16)
            .reshape(fsdp_count // 2, token_rows, D)
        )

    grad_normed_odd = input_grads(0)
    grad_normed_even = input_grads(odd_rows)
    grad_normed_ffn = fsdp_sum_masks(grad_normed_odd, grad_normed_even)
    down_grad_second = dot_left_t(
        after(hidden_second, grad_normed_even), grad_out_all
    ).astype(jnp.bfloat16)[:second_units]
    gate_grad_second = dot_left_t(
        normed_ffn_all, after(grad_second, down_grad_second)
    ).astype(jnp.bfloat16)
    down_out = (
        dot_f32(hidden_first, down_first)
        + dot_f32(after(hidden_second, gate_grad_second), down_second)
    ).astype(jnp.bfloat16)
    down_out = jnp.concatenate(
        [
            lax.dynamic_slice_in_dim(
                down_out,
                lax.dynamic_index_in_dim(
                    jnp.asarray([mask_order().index(m) for m in range(fsdp_count)], jnp.int32),
                    lax.axis_index("fsdp") ^ place,
                    keepdims=False,
                )
                * token_rows,
                token_rows,
                axis=0,
            )
            for place in range(fsdp_count)
        ],
        axis=0,
    )
    block_out = middle + fsdp_shard_sum(after(down_out, grad_normed_ffn)).astype(jnp.float32)

    down_grad = jnp.concatenate(
        ctx_totals(row_chunks(down_grad_first, 2))
        + ctx_totals(row_chunks(down_grad_second, 2)),
        axis=0,
    ).astype(jnp.float32)
    gate_grad = join_units(
        jnp.concatenate(
            ctx_totals(
                row_chunks(
                    swap_blocks(gate_grad_first.reshape(fsdp_count, shard_d, -1)), 4
                )
            )
        ),
        jnp.concatenate(
            ctx_totals(
                row_chunks(
                    swap_blocks(gate_grad_second.reshape(fsdp_count, shard_d, -1)), 4
                )
            )
        ),
        units,
    )

    grad_mid_norm = norm_backward(middle, ffn_scale, grad_normed_ffn)
    ffn_grad = jnp.sum(gate_grad * gate_up.astype(jnp.float32), axis=1) / ffn_norm
    grad_middle = grad_out + grad_mid_norm
    grad_middle_b = grad_middle.astype(jnp.bfloat16)
    out_grad = ctx_totals([fsdp_shard_sum(dot_left_t(attended_b, grad_middle_b))])[0].astype(
        jnp.float32
    )
    grad_attended_b = (
        dot_right_t(grad_middle_b, out_full)
        .astype(jnp.bfloat16)
        .reshape(token_rows, KEY_VALUE_HEADS, head_groups, HEAD_SIZE)
    )
    scores = score_block(query_b, keys_all, allowed)
    probs_full = jnp.exp(scores - log_total)
    probs_again_b = probs_full.astype(jnp.bfloat16)
    grad_probs = jnp.einsum(
        "qcgd,kcd->cgqk", grad_attended_b, values_all, preferred_element_type=jnp.float32
    )
    inner_sum = jnp.sum(grad_probs * probs_full, axis=-1, keepdims=True)
    grad_scores_b = (probs_full * (grad_probs - inner_sum)).astype(jnp.bfloat16)
    grad_query = (
        jnp.einsum("cgqk,kcd->qcgd", grad_scores_b, keys_all, preferred_element_type=jnp.float32)
        * score_scale
    )
    grad_keys_all = (
        jnp.einsum("cgqk,qcgd->kcd", grad_scores_b, query_b, preferred_element_type=jnp.float32)
        * score_scale
    )
    grad_values_all = jnp.einsum(
        "cgqk,qcgd->kcd", probs_again_b, grad_attended_b, preferred_element_type=jnp.float32
    )
    grad_both_all = jnp.concatenate([grad_keys_all, grad_values_all], axis=1)
    grad_both = grad_both_all[:token_rows]
    for back in range(1, ctx_count):
        grad_both = grad_both + lax.ppermute(
            grad_both_all[back * token_rows : (back + 1) * token_rows].astype(jnp.bfloat16),
            "ctx",
            [(s + back, s) for s in range(ctx_count - back)],
        ).astype(jnp.float32)
    grad_keys = grad_both[:, :KEY_VALUE_HEADS]
    grad_values = grad_both[:, KEY_VALUE_HEADS:]
    grad_projected_b = jnp.concatenate(
        [
            apply_rotary(
                grad_query.reshape(token_rows, QUERY_HEADS, HEAD_SIZE), -rotary_angles
            ).reshape(token_rows, query_span_width),
            apply_rotary(grad_keys, -rotary_angles).reshape(token_rows, key_span_width),
            grad_values.reshape(token_rows, key_span_width),
        ],
        axis=1,
    ).astype(jnp.bfloat16)
    normed_ones = jnp.concatenate(
        [
            normed_b.reshape(token_rows, fsdp_count, shard_d),
            jnp.ones((token_rows, fsdp_count, 1), jnp.bfloat16),
            jnp.zeros((token_rows, fsdp_count, 15), jnp.bfloat16),
        ],
        axis=2,
    ).reshape(token_rows, -1)
    in_total = ctx_totals([fsdp_shard_sum(dot_left_t(normed_ones, grad_projected_b))])[0].astype(
        jnp.float32
    )
    in_grad = in_total[:shard_d]
    bias_span = in_bias.shape[0]
    bias_grad = lax.dynamic_slice_in_dim(
        in_total[shard_d], lax.axis_index("fsdp") * bias_span, bias_span
    )
    attn_grad = jnp.sum(in_grad * in_proj.astype(jnp.float32), axis=1) / attn_norm
    grad_normed = dot_right_t(grad_projected_b, in_full)
    grad_in_norm = norm_backward(residual_in, attn_scale, grad_normed)
    tokens_grad = grad_middle + grad_in_norm
    return (
        block_out.astype(jnp.bfloat16).reshape(1, token_rows, D),
        tokens_grad.reshape(1, token_rows, D),
        attn_grad,
        ffn_grad,
        in_grad,
        bias_grad,
        out_grad,
        gate_grad,
        down_grad,
    )


def solution(mesh):
    in_specs = (
        P("fsdp", "ctx", None),
        P("fsdp", "ctx"),
        P("fsdp", "ctx", None),
        P("fsdp"),
        P("fsdp"),
        P("fsdp", None),
        P("fsdp"),
        P("fsdp", None),
        P("fsdp", None),
        P("fsdp", None),
    )
    out_specs = (
        P("fsdp", "ctx", None),
        P("fsdp", "ctx", None),
        P("fsdp"),
        P("fsdp"),
        P("fsdp", None),
        P("fsdp"),
        P("fsdp", None),
        P("fsdp", None),
        P("fsdp", None),
    )
    return jax.shard_map(shards, mesh=mesh, in_specs=in_specs, out_specs=out_specs, check_vma=False)
```

```python
import jax
import jax.numpy as jnp
from jax import lax
from jax.experimental import pallas as pl
from jax.experimental.pallas import tpu as pltpu
from jax.sharding import PartitionSpec as P

D = 1536
QUERY_HEADS = 12
KEY_VALUE_HEADS = 2
HEAD_SIZE = 128
FF = 8960
QD = QUERY_HEADS * HEAD_SIZE
KD = KEY_VALUE_HEADS * HEAD_SIZE
GROUP = QUERY_HEADS // KEY_VALUE_HEADS


norm_eps = 1e-06
rope_base = 1000000.0
masked_score = -1e30
score_scale = HEAD_SIZE ** (-0.5)
vmem_params = pltpu.CompilerParams(vmem_limit_bytes=48 * 1024 * 1024)


def rms_scale(value_rows, scale_vec):
    return (
        value_rows
        * lax.rsqrt(jnp.mean(value_rows * value_rows, axis=-1, keepdims=True) + norm_eps)
        * scale_vec
    )


def norm_backward(value_rows, scale_vec, incoming):
    unused_out, pullback = jax.vjp(lambda rows: rms_scale(rows, scale_vec), value_rows)
    return pullback(incoming)[0]


def rotary_tables(position):
    frequencies = rope_base ** (
        -(jnp.arange(HEAD_SIZE // 2, dtype=jnp.float32) * (2.0 / HEAD_SIZE))
    )
    angles = position.astype(jnp.float32)[:, None] * frequencies[None, :]
    cosine = jnp.cos(angles)
    sine = jnp.sin(angles)
    return (
        jnp.concatenate([cosine, cosine], axis=1),
        jnp.concatenate([-sine, sine], axis=1),
    )


def dot_f32(left, right):
    return jnp.dot(left, right, preferred_element_type=jnp.float32)


def dot_right_t(left, right):
    return lax.dot_general(
        left, right, (((1,), (1,)), ((), ())), preferred_element_type=jnp.float32
    )


def dot_left_t(left, right):
    return lax.dot_general(
        left, right, (((0,), (0,)), ((), ())), preferred_element_type=jnp.float32
    )


def add_low(left, right):
    total = left.astype(jnp.float32) + right.astype(jnp.float32)
    return lax.reduce_precision(total, 8, 7).astype(jnp.bfloat16)


def after(value, *earlier):
    return lax.optimization_barrier((value, earlier))[0]


def exchange(value, mask):
    count = lax.axis_size("fsdp")
    return lax.ppermute(value, "fsdp", [(place, place ^ mask) for place in range(count)])


def gather_into(whole, block, row_of, *gates):
    count = lax.axis_size("fsdp")

    def put(whole, mask, first, piece):
        return lax.dynamic_update_slice(whole, piece, (row_of(mask) + first, 0))

    if count != 8:
        for mask in range(0, count, 2):
            piece = exchange(block, mask) if mask else block
            whole = put(whole, mask, 0, piece)
            whole = put(whole, mask + 1, 0, exchange(piece, 1))
        return whole
    half = block.shape[0] // 2
    by_x = exchange(block, 2)
    by_y = exchange(block, 4)
    other = exchange(block, 1)
    whole = put(whole, 0, 0, block)
    by_x, by_y, whole = after((by_x, by_y, whole), *gates)
    top = exchange(by_x[:half], 4)
    bottom = exchange(by_y[half:], 2)
    other_x = exchange(by_x, 1)
    other_y = exchange(by_y, 1)
    whole = put(whole, 2, 0, by_x)
    whole = put(whole, 4, 0, by_y)
    whole = put(whole, 1, 0, other)
    top, bottom, whole = after((top, bottom, whole))
    other_top = exchange(top, 1)
    other_bottom = exchange(bottom, 1)
    whole = put(whole, 3, 0, other_x)
    whole = put(whole, 5, 0, other_y)
    whole = put(whole, 6, 0, top)
    whole = put(whole, 6, half, bottom)
    whole = put(whole, 7, 0, other_top)
    return put(whole, 7, half, other_bottom)


def place_of(mask, count):
    return mask // 2 if mask % 2 else count // 2 + mask // 2


def mask_at(place, count):
    return jnp.where(place < count // 2, 2 * place + 1, 2 * place - count)


class MaskSum:
    def __init__(self, odd):
        self.got = exchange(odd, 1)

    def second(self, even, *gates):
        count = lax.axis_size("fsdp")
        self.kept = add_low(even, after(self.got, *gates))
        if count == 8:
            half = self.kept.shape[1] // 2
            self.by_x = exchange(self.kept[1::2, :half], 2)
            self.by_y = exchange(self.kept[2:, half:], 4)
        else:
            span = count
            while self.kept.shape[0] > 1:
                span //= 2
                half = self.kept.shape[0] // 2
                self.kept = add_low(self.kept[:half], exchange(self.kept[half:], span))
        return self.kept

    def third(self, *gates):
        if lax.axis_size("fsdp") != 8:
            return self.kept
        half = self.kept.shape[1] // 2
        by_x, by_y = after((self.by_x, self.by_y), *gates)
        self.top = add_low(self.kept[0::2, :half], by_x)
        self.bottom = add_low(self.kept[:2, half:], by_y)
        self.last_y = exchange(self.top[1], 4)
        self.last_x = exchange(self.bottom[1], 2)
        return self.top, self.bottom

    def result(self, *gates):
        if lax.axis_size("fsdp") != 8:
            return self.kept[0]
        last_y, last_x = after((self.last_y, self.last_x), *gates)
        return jnp.concatenate(
            [add_low(self.top[0], last_y), add_low(self.bottom[0], last_x)], axis=0
        )


def swap_blocks(blocks):
    return lax.all_to_all(blocks, "fsdp", 0, 0, tiled=True)


class Wave:
    def __init__(self, raw):
        self.raw = raw
        self.right, self.left = [], []
        self.got_right = self.got_left = None

    def value_of(self, place, crossing, got):
        count = lax.axis_size("ctx")
        middle = count // 2
        tick = len(self.right)
        base = lax.dynamic_index_in_dim(
            self.raw, jnp.clip(tick - place, 0, self.raw.shape[0] - 1), axis=0, keepdims=False
        )
        if crossing is not None:
            base = jnp.where(place < middle, base, crossing)
            base = jnp.where(place > middle, jnp.zeros_like(base), base)
        return base if got is None else add_low(base, got)

    def tick(self, *gates):
        count = lax.axis_size("ctx")
        me = lax.axis_index("ctx")
        if self.got_right is None:
            self.raw = after(self.raw, *gates)
        else:
            self.got_right, self.got_left = after((self.got_right, self.got_left), *gates)
        right_now = self.value_of(me, self.left[-1] if self.left else None, self.got_right)
        left_now = self.value_of(
            count - 1 - me, self.right[-1] if self.right else None, self.got_left
        )
        senders = [
            place
            for place in range(count - 1)
            if 0 <= len(self.right) - place < self.raw.shape[0]
        ]
        if senders:
            self.got_right = lax.ppermute(right_now, "ctx", [(s, s + 1) for s in senders])
            self.got_left = lax.ppermute(
                left_now, "ctx", [(count - 1 - s, count - 2 - s) for s in senders]
            )
        self.right.append(right_now)
        self.left.append(left_now)
        return right_now, left_now

    def totals(self):
        count = lax.axis_size("ctx")
        me = lax.axis_index("ctx")
        chunks = self.raw.shape[0]
        while len(self.right) < chunks + count - 1:
            self.tick()
        totals = []
        for index in range(chunks):
            total = self.right[index + count // 2]
            for place in range(count // 2 + 1, count):
                total = jnp.where(me == place, self.right[index + place], total)
            for place in range(count // 2):
                total = jnp.where(me == place, self.left[index + count - 1 - place], total)
            totals.append(total.astype(jnp.float32))
        return jnp.concatenate(totals, axis=0)


def unit_widths(units):
    first = units // 256 * 128
    second = units - first
    return first, second, -(-second // 128) * 128


def split_units(gate_up, count):
    rows, columns = gate_up.shape
    span = columns // 2
    units = span // count
    first, second, padded = unit_widths(units)
    block = 48

    def kernel(weight_ref, first_ref, second_ref):
        for owner in range(count):
            for side in range(2):
                begin = side * span + owner * units
                first_ref[owner, :, side * first : (side + 1) * first] = weight_ref[
                    :, begin : begin + first
                ]
                second_ref[owner, :, side * padded : side * padded + second] = weight_ref[
                    :, begin + first : begin + units
                ]
                if padded > second:
                    second_ref[
                        owner, :, side * padded + second : (side + 1) * padded
                    ] = jnp.zeros((block, padded - second), gate_up.dtype)

    return pl.pallas_call(
        kernel,
        grid=(rows // block,),
        in_specs=[pl.BlockSpec((block, columns), lambda step: (step, 0))],
        out_specs=[
            pl.BlockSpec((count, block, 2 * first), lambda step: (0, step, 0)),
            pl.BlockSpec((count, block, 2 * padded), lambda step: (0, step, 0)),
        ],
        out_shape=[
            jax.ShapeDtypeStruct((count, rows, 2 * first), gate_up.dtype),
            jax.ShapeDtypeStruct((count, rows, 2 * padded), gate_up.dtype),
        ],
        compiler_params=vmem_params,
        cost_estimate=pl.CostEstimate(
            flops=0, bytes_accessed=4 * rows * columns, transcendentals=0
        ),
    )(gate_up)


def join_units(first_part, second_part, gate_up):
    count, rows = first_part.shape[:2]
    span = gate_up.shape[1] // 2
    units = span // count
    first, second, padded = unit_widths(units)
    block = 48

    def kernel(first_ref, second_ref, weight_ref, whole_ref, sums_ref):
        for owner in range(count):
            for side in range(2):
                begin = side * span + owner * units
                whole_ref[:, begin : begin + first] = first_ref[
                    owner, :, side * first : (side + 1) * first
                ].astype(jnp.float32)
                whole_ref[:, begin + first : begin + units] = second_ref[
                    owner, :, side * padded : side * padded + second
                ].astype(jnp.float32)
        total = jnp.sum(
            whole_ref[...] * weight_ref[...].astype(jnp.float32), axis=1, keepdims=True
        )
        sums_ref[...] = jnp.broadcast_to(total, (block, 128))

    whole, sums = pl.pallas_call(
        kernel,
        grid=(rows // block,),
        in_specs=[
            pl.BlockSpec((count, block, 2 * first), lambda step: (0, step, 0)),
            pl.BlockSpec((count, block, 2 * padded), lambda step: (0, step, 0)),
            pl.BlockSpec((block, 2 * span), lambda step: (step, 0)),
        ],
        out_specs=[
            pl.BlockSpec((block, 2 * span), lambda step: (step, 0)),
            pl.BlockSpec((block, 128), lambda step: (step, 0)),
        ],
        out_shape=[
            jax.ShapeDtypeStruct((rows, 2 * span), jnp.float32),
            jax.ShapeDtypeStruct((rows, 128), jnp.float32),
        ],
        compiler_params=vmem_params,
        cost_estimate=pl.CostEstimate(
            flops=4 * rows * span, bytes_accessed=16 * rows * span, transcendentals=0
        ),
    )(first_part, second_part, gate_up)
    return whole, sums[:, 0]


def project(normed, weight, bias, cosine, sine):
    tokens = normed.shape[0]
    width = weight.shape[1]
    block = 512

    def kernel(normed_ref, weight_ref, bias_ref, cosine_ref, sine_ref, out_ref):
        product = dot_f32(normed_ref[...], weight_ref[...]) + bias_ref[...]
        for head in range(block // HEAD_SIZE):
            lanes = slice(head * HEAD_SIZE, (head + 1) * HEAD_SIZE)
            plain = product[:, lanes]
            turned = plain * cosine_ref[...] + pltpu.roll(plain, HEAD_SIZE // 2, 1) * sine_ref[...]
            column = pl.program_id(0) * block + head * HEAD_SIZE
            out_ref[:, lanes] = jnp.where(column < QD + KD, turned, plain).astype(jnp.bfloat16)

    return pl.pallas_call(
        kernel,
        grid=(width // block,),
        in_specs=[
            pl.BlockSpec((tokens, D), lambda step: (0, 0)),
            pl.BlockSpec((D, block), lambda step: (0, step)),
            pl.BlockSpec((1, block), lambda step: (0, step)),
            pl.BlockSpec((tokens, HEAD_SIZE), lambda step: (0, 0)),
            pl.BlockSpec((tokens, HEAD_SIZE), lambda step: (0, 0)),
        ],
        out_specs=pl.BlockSpec((tokens, block), lambda step: (0, step)),
        out_shape=jax.ShapeDtypeStruct((tokens, width), jnp.bfloat16),
        compiler_params=vmem_params,
        cost_estimate=pl.CostEstimate(
            flops=2 * tokens * D * width, bytes_accessed=2 * D * width, transcendentals=0
        ),
    )(normed, weight, bias[None], cosine, sine)


def fill_bias(at_ref, position_ref, bias_ref):
    tokens, keys = bias_ref.shape
    row = lax.broadcasted_iota(jnp.int32, (tokens, keys), 0)
    column = lax.broadcasted_iota(jnp.int32, (tokens, keys), 1)
    back = column // tokens
    query_index = at_ref[0] * tokens + row
    key_index = (at_ref[0] - back) * tokens + (column - back * tokens)
    allowed = (key_index <= query_index) & (key_index >= query_index - position_ref[...])
    bias_ref[...] = jnp.where(allowed, 0.0, masked_score)


def attend(at, position, projected, both_all):
    tokens = projected.shape[0]
    keys = both_all.shape[0]

    def kernel(at_ref, position_ref, query_ref, key_ref, value_ref, out_ref, turn_ref, log_ref, bias_ref):
        @pl.when(pl.program_id(0) == 0)
        def _():
            fill_bias(at_ref, position_ref, bias_ref)

        scores = dot_right_t(query_ref[...], key_ref[...]) * score_scale + bias_ref[...]
        top = jnp.max(scores, axis=1, keepdims=True)
        raised = jnp.exp(scores - top)
        total = jnp.sum(raised, axis=1, keepdims=True)
        probs = (raised * (1.0 / total)).astype(jnp.bfloat16)
        result = dot_f32(probs, value_ref[...])
        out_ref[...] = result.astype(jnp.bfloat16)
        turn_ref[...] = result.T.astype(jnp.bfloat16)
        log_ref[0] = top + jnp.log(total)

    return pl.pallas_call(
        kernel,
        grid_spec=pltpu.PrefetchScalarGridSpec(
            num_scalar_prefetch=1,
            grid=(QUERY_HEADS,),
            in_specs=[
                pl.BlockSpec((tokens, 1), lambda head, at: (0, 0)),
                pl.BlockSpec((tokens, HEAD_SIZE), lambda head, at: (0, head)),
                pl.BlockSpec((keys, HEAD_SIZE), lambda head, at: (0, head // GROUP)),
                pl.BlockSpec(
                    (keys, HEAD_SIZE), lambda head, at: (0, KEY_VALUE_HEADS + head // GROUP)
                ),
            ],
            out_specs=[
                pl.BlockSpec((tokens, HEAD_SIZE), lambda head, at: (0, head)),
                pl.BlockSpec((HEAD_SIZE, tokens), lambda head, at: (head, 0)),
                pl.BlockSpec((1, tokens, 1), lambda head, at: (head, 0, 0)),
            ],
            scratch_shapes=[pltpu.VMEM((tokens, keys), jnp.float32)],
        ),
        out_shape=[
            jax.ShapeDtypeStruct((tokens, QD), jnp.bfloat16),
            jax.ShapeDtypeStruct((QD, tokens), jnp.bfloat16),
            jax.ShapeDtypeStruct((QUERY_HEADS, tokens, 1), jnp.float32),
        ],
        compiler_params=vmem_params,
        cost_estimate=pl.CostEstimate(
            flops=8 * tokens * keys * QD,
            bytes_accessed=8 * tokens * QD,
            transcendentals=QUERY_HEADS * tokens * keys,
        ),
    )(at, position, projected, both_all, both_all)


def attend_backward(at, position, projected, both_all, incoming, log_total, cosine, sine):
    tokens = projected.shape[0]
    keys = both_all.shape[0]

    def kernel(
        at_ref,
        position_ref,
        query_ref,
        key_ref,
        value_ref,
        incoming_ref,
        log_ref,
        cosine_ref,
        sine_ref,
        query_grad_ref,
        key_grad_ref,
        value_grad_ref,
        bias_ref,
        key_total,
        value_total,
    ):
        head = pl.program_id(0)

        @pl.when(head == 0)
        def _():
            fill_bias(at_ref, position_ref, bias_ref)

        @pl.when(head % GROUP == 0)
        def _():
            key_total[...] = jnp.zeros_like(key_total)
            value_total[...] = jnp.zeros_like(value_total)

        scores = dot_right_t(query_ref[...], key_ref[...]) * score_scale + bias_ref[...]
        probs = jnp.exp(scores - log_ref[0])
        grad_probs = dot_right_t(incoming_ref[...], value_ref[...])
        inner = jnp.sum(grad_probs * probs, axis=1, keepdims=True)
        grad_scores = (probs * (grad_probs - inner)).astype(jnp.bfloat16)
        value_total[...] += dot_left_t(incoming_ref[...], probs.astype(jnp.bfloat16))
        key_total[...] += dot_left_t(query_ref[...], grad_scores)
        plain = dot_f32(grad_scores, key_ref[...]) * score_scale
        query_grad_ref[...] = (
            plain * cosine_ref[...] - pltpu.roll(plain, HEAD_SIZE // 2, 1) * sine_ref[...]
        ).astype(jnp.bfloat16)

        @pl.when(head % GROUP == GROUP - 1)
        def _():
            key_grad_ref[...] = (key_total[...] * score_scale).T
            value_grad_ref[...] = value_total[...].T

    return pl.pallas_call(
        kernel,
        grid_spec=pltpu.PrefetchScalarGridSpec(
            num_scalar_prefetch=1,
            grid=(QUERY_HEADS,),
            in_specs=[
                pl.BlockSpec((tokens, 1), lambda head, at: (0, 0)),
                pl.BlockSpec((tokens, HEAD_SIZE), lambda head, at: (0, head)),
                pl.BlockSpec((keys, HEAD_SIZE), lambda head, at: (0, head // GROUP)),
                pl.BlockSpec(
                    (keys, HEAD_SIZE), lambda head, at: (0, KEY_VALUE_HEADS + head // GROUP)
                ),
                pl.BlockSpec((tokens, HEAD_SIZE), lambda head, at: (0, head)),
                pl.BlockSpec((1, tokens, 1), lambda head, at: (head, 0, 0)),
                pl.BlockSpec((tokens, HEAD_SIZE), lambda head, at: (0, 0)),
                pl.BlockSpec((tokens, HEAD_SIZE), lambda head, at: (0, 0)),
            ],
            out_specs=[
                pl.BlockSpec((tokens, HEAD_SIZE), lambda head, at: (0, head)),
                pl.BlockSpec((keys, HEAD_SIZE), lambda head, at: (0, head // GROUP)),
                pl.BlockSpec((keys, HEAD_SIZE), lambda head, at: (0, head // GROUP)),
            ],
            scratch_shapes=[
                pltpu.VMEM((tokens, keys), jnp.float32),
                pltpu.VMEM((HEAD_SIZE, keys), jnp.float32),
                pltpu.VMEM((HEAD_SIZE, keys), jnp.float32),
            ],
        ),
        out_shape=[
            jax.ShapeDtypeStruct((tokens, QD), jnp.bfloat16),
            jax.ShapeDtypeStruct((keys, KD), jnp.float32),
            jax.ShapeDtypeStruct((keys, KD), jnp.float32),
        ],
        compiler_params=vmem_params,
        cost_estimate=pl.CostEstimate(
            flops=20 * tokens * keys * QD,
            bytes_accessed=8 * tokens * QD,
            transcendentals=QUERY_HEADS * tokens * keys,
        ),
    )(at, position, projected, both_all, both_all, incoming, log_total, cosine, sine)


def unit_part(me, normed_all, grad_out_all, gate_up, down, count, reorder):
    tokens = normed_all.shape[0]
    block = tokens // count
    width = down.shape[0]

    def kernel(me_ref, normed_ref, out_grad_ref, gate_up_ref, down_ref, hidden_ref, grad_ref, *rest):
        values = dot_f32(normed_ref[...], gate_up_ref[...])
        gate = values[:, :width]
        up = values[:, width:]
        grad_hidden = dot_right_t(out_grad_ref[...], down_ref[...])
        share = 1.0 / (1.0 + jnp.exp(-gate))
        passed = gate * share
        hidden_ref[...] = (passed * up).astype(jnp.bfloat16)
        grad_ref[:, :width] = (
            grad_hidden * up * share * (1.0 + gate * (1.0 - share))
        ).astype(jnp.bfloat16)
        grad_ref[:, width:] = (grad_hidden * passed).astype(jnp.bfloat16)
        if rest:
            rest[0][...] = out_grad_ref[...]

    def out_grad_index(step, me_ref):
        return (me_ref[0] ^ mask_at(step, count), 0) if reorder else (step, 0)

    row = lambda step, me_ref: (step, 0)
    fixed = lambda step, me_ref: (0, 0)
    out_specs = [pl.BlockSpec((block, width), row), pl.BlockSpec((block, 2 * width), row)]
    out_shape = [
        jax.ShapeDtypeStruct((tokens, width), jnp.bfloat16),
        jax.ShapeDtypeStruct((tokens, 2 * width), jnp.bfloat16),
    ]
    if reorder:
        out_specs.append(pl.BlockSpec((block, D), row))
        out_shape.append(jax.ShapeDtypeStruct((tokens, D), jnp.bfloat16))
    return pl.pallas_call(
        kernel,
        grid_spec=pltpu.PrefetchScalarGridSpec(
            num_scalar_prefetch=1,
            grid=(count,),
            in_specs=[
                pl.BlockSpec((block, D), row),
                pl.BlockSpec((block, D), out_grad_index),
                pl.BlockSpec((D, 2 * width), fixed),
                pl.BlockSpec((width, D), fixed),
            ],
            out_specs=out_specs,
        ),
        out_shape=out_shape,
        compiler_params=vmem_params,
        cost_estimate=pl.CostEstimate(
            flops=6 * tokens * D * width,
            bytes_accessed=4 * tokens * D + 6 * tokens * width + 6 * D * width,
            transcendentals=tokens * width,
        ),
    )(me, normed_all, grad_out_all, gate_up, down)


def row_block_terms(me, turned, right):
    count, rows, tokens = turned.shape
    width = right.shape[1]

    def kernel(me_ref, turned_ref, right_ref, out_ref):
        out_ref[0] = dot_f32(turned_ref[0], right_ref[...]).astype(jnp.bfloat16)

    return pl.pallas_call(
        kernel,
        grid_spec=pltpu.PrefetchScalarGridSpec(
            num_scalar_prefetch=1,
            grid=(count,),
            in_specs=[
                pl.BlockSpec(
                    (1, rows, tokens),
                    lambda step, me_ref: (me_ref[0] ^ mask_at(step, count), 0, 0),
                ),
                pl.BlockSpec((tokens, width), lambda step, me_ref: (0, 0)),
            ],
            out_specs=pl.BlockSpec((1, rows, width), lambda step, me_ref: (step, 0, 0)),
        ),
        out_shape=jax.ShapeDtypeStruct((count, rows, width), jnp.bfloat16),
        compiler_params=vmem_params,
        cost_estimate=pl.CostEstimate(
            flops=2 * count * rows * tokens * width,
            bytes_accessed=2 * count * rows * width,
            transcendentals=0,
        ),
    )(me, turned, right)


def shards(
    tokens,
    positions,
    cotangent,
    attn_norm,
    ffn_norm,
    in_proj,
    in_bias,
    out_proj,
    gate_up,
    down_proj,
):
    token_rows = tokens.shape[1]
    fsdp_count = lax.axis_size("fsdp")
    ctx_count = lax.axis_size("ctx")
    fsdp_me = lax.axis_index("fsdp")
    me = fsdp_me.astype(jnp.int32)[None]
    at = lax.axis_index("ctx").astype(jnp.int32)[None]
    units = FF // fsdp_count
    shard_d = D // fsdp_count
    residual_in = tokens[0].astype(jnp.float32)
    position = positions[0]
    grad_out_b = cotangent[0]

    first_units, second_units, padded_units = unit_widths(units)
    first_blocks, second_blocks = split_units(gate_up, fsdp_count)
    vectors = lax.all_gather(
        jnp.concatenate([attn_norm, ffn_norm, in_bias])[None], "fsdp", axis=0, tiled=True
    )
    attn_scale = vectors[:, :shard_d].reshape(D)
    ffn_scale = vectors[:, shard_d : 2 * shard_d].reshape(D)
    bias_full = vectors[:, 2 * shard_d :].reshape(-1)
    normed_b = rms_scale(residual_in, attn_scale).astype(jnp.bfloat16)
    cosine, sine = rotary_tables(position)
    in_full = gather_into(
        jnp.zeros((D, in_proj.shape[1]), jnp.bfloat16),
        in_proj,
        lambda mask: (fsdp_me ^ mask) * shard_d,
        normed_b,
        cosine,
        first_blocks,
    )
    gate_up_first = swap_blocks(after(first_blocks, in_full)).reshape(D, 2 * first_units)
    out_full = lax.all_gather(after(out_proj, in_full), "fsdp", axis=0, tiled=True)
    grad_out_all = lax.all_gather(after(grad_out_b, out_full), "fsdp", axis=0, tiled=True)
    down_first = down_proj[:first_units]
    down_second = jnp.pad(down_proj[first_units:], ((0, padded_units - second_units), (0, 0)))

    projected = project(normed_b, in_full, bias_full, cosine, sine)
    both_b = projected[:, QD:]
    both_pieces = [both_b] + [
        lax.ppermute(both_b, "ctx", [(s, s + back) for s in range(ctx_count - back)])
        for back in range(1, ctx_count)
    ]
    normed_turned = jnp.concatenate(
        [
            normed_b.T.reshape(fsdp_count, shard_d, token_rows),
            jnp.ones((fsdp_count, 1, token_rows), jnp.bfloat16),
            jnp.zeros((fsdp_count, 15, token_rows), jnp.bfloat16),
        ],
        axis=1,
    )
    both_all = jnp.concatenate(after(both_pieces, normed_turned, down_second), axis=0)
    attended_b, attended_turned, log_total = attend(at, position[:, None], projected, both_all)
    middle = residual_in + dot_f32(attended_b, out_full)
    normed_ffn_b = rms_scale(middle, ffn_scale).astype(jnp.bfloat16)

    normed_ffn_all = gather_into(
        jnp.zeros((fsdp_count * token_rows, D), jnp.bfloat16),
        normed_ffn_b,
        lambda mask: place_of(mask, fsdp_count) * token_rows,
    )
    gate_up_second = swap_blocks(after(second_blocks, normed_ffn_all)).reshape(
        D, 2 * padded_units
    )
    hidden_first, grad_first, grad_out_all = unit_part(
        me, normed_ffn_all, grad_out_all, gate_up_first, down_first, fsdp_count, True
    )
    down_grad_first = dot_left_t(hidden_first, grad_out_all).astype(jnp.bfloat16)
    down_wave_first = Wave(down_grad_first.reshape(2, first_units // 2, D))
    sent = down_wave_first.tick()
    gate_grad_first = dot_left_t(normed_ffn_all, after(grad_first, sent)).astype(jnp.bfloat16)
    gate_swapped_first = swap_blocks(gate_grad_first.reshape(fsdp_count, shard_d, -1))
    hidden_second, grad_second = unit_part(
        me,
        after(normed_ffn_all, gate_grad_first),
        grad_out_all,
        gate_up_second,
        down_second,
        fsdp_count,
        False,
    )
    sent = down_wave_first.tick(hidden_second)
    odd_rows = normed_ffn_all.shape[0] // 2

    def input_grads(rows, *gates):
        return (
            (
                dot_right_t(after(grad_first, *gates)[rows], gate_up_first)
                + dot_right_t(grad_second[rows], gate_up_second)
            )
            .astype(jnp.bfloat16)
            .reshape(fsdp_count // 2, token_rows, D)
        )

    grad_normed_odd = input_grads(slice(0, odd_rows), sent)
    normed_sum = MaskSum(grad_normed_odd)
    grad_normed_even = input_grads(slice(odd_rows, None), grad_normed_odd)
    gate_summed_first = lax.psum(gate_swapped_first, "ctx")
    sent = normed_sum.second(grad_normed_even)
    down_grad_second = dot_left_t(after(hidden_second, sent), grad_out_all).astype(
        jnp.bfloat16
    )[:second_units]
    down_wave_second = Wave(down_grad_second.reshape(2, second_units // 2, D))
    sent = down_wave_first.tick(down_grad_second)
    sent = down_wave_second.tick(sent)
    gate_grad_second = dot_left_t(normed_ffn_all, after(grad_second, sent)).astype(jnp.bfloat16)
    gate_swapped_second = swap_blocks(gate_grad_second.reshape(fsdp_count, shard_d, -1))
    gate_summed_second = lax.psum(after(gate_swapped_second, gate_summed_first), "ctx")
    sent = normed_sum.third(gate_grad_second)

    def down_outs(rows, *gates):
        return (
            (
                dot_f32(after(hidden_first, *gates)[rows], down_first)
                + dot_f32(hidden_second[rows], down_second)
            )
            .astype(jnp.bfloat16)
            .reshape(fsdp_count // 2, token_rows, D)
        )

    down_odd = down_outs(slice(0, odd_rows), sent)
    down_sum = MaskSum(down_odd)
    grad_normed_ffn = normed_sum.result(down_odd).astype(jnp.float32)

    grad_out = grad_out_b.astype(jnp.float32)
    grad_middle = grad_out + norm_backward(middle, ffn_scale, grad_normed_ffn)
    grad_middle_b = grad_middle.astype(jnp.bfloat16)
    grad_attended_b = dot_right_t(grad_middle_b, out_full).astype(jnp.bfloat16)
    query_grad, key_grads, value_grads = attend_backward(
        at,
        position[:, None],
        projected,
        both_all,
        grad_attended_b,
        log_total,
        cosine,
        sine,
    )
    both_grads = jnp.concatenate([key_grads, value_grads], axis=1)
    both_sent = [
        lax.ppermute(
            both_grads[back * token_rows : (back + 1) * token_rows].astype(jnp.bfloat16),
            "ctx",
            [(s + back, s) for s in range(ctx_count - back)],
        )
        for back in range(1, ctx_count)
    ]
    out_terms = row_block_terms(
        me,
        attended_turned.reshape(fsdp_count, shard_d, token_rows),
        after(grad_middle_b, both_grads),
    )
    half = fsdp_count // 2
    out_sum = MaskSum(out_terms[:half])
    down_even = down_outs(slice(odd_rows, None), out_terms)
    both_grad = both_grads[:token_rows]
    for piece in after(both_sent, down_even):
        both_grad = both_grad + piece.astype(jnp.float32)
    turned_back = []
    for head in range(KEY_VALUE_HEADS):
        plain = both_grad[:, head * HEAD_SIZE : (head + 1) * HEAD_SIZE]
        turned_back.append(plain * cosine - jnp.roll(plain, HEAD_SIZE // 2, axis=1) * sine)
    grad_projected_b = jnp.concatenate(
        [query_grad]
        + [part.astype(jnp.bfloat16) for part in turned_back]
        + [both_grad[:, KD:].astype(jnp.bfloat16)],
        axis=1,
    )
    in_terms = row_block_terms(me, normed_turned, grad_projected_b)
    in_sum = MaskSum(in_terms[:half])
    sent = out_sum.second(out_terms[half:], in_terms)
    sent = in_sum.second(in_terms[half:], sent)
    sent = down_sum.second(down_even, sent)
    grad_normed = dot_right_t(after(grad_projected_b, sent), in_full)
    tokens_grad = grad_middle + norm_backward(residual_in, attn_scale, grad_normed)
    sent = out_sum.third(tokens_grad)
    sent = in_sum.third(sent)
    out_wave = Wave(out_sum.result(sent)[None])
    sent = out_wave.tick()
    in_wave = Wave(in_sum.result(sent)[None])
    sent = in_wave.tick()
    sent = down_sum.third(sent)
    sent = out_wave.tick(sent)
    sent = in_wave.tick(sent)
    block_out = middle + down_sum.result(sent).astype(jnp.float32)
    sent = out_wave.tick(sent)
    sent = in_wave.tick(sent)
    down_grad = jnp.concatenate([down_wave_first.totals(), down_wave_second.totals()], axis=0)
    gate_grad, gate_sums = join_units(gate_summed_first, gate_summed_second, gate_up)
    ffn_grad = gate_sums / ffn_norm
    out_grad = out_wave.totals()
    in_total = in_wave.totals()
    in_grad = in_total[:shard_d]
    bias_span = in_bias.shape[0]
    bias_grad = lax.dynamic_slice_in_dim(in_total[shard_d], fsdp_me * bias_span, bias_span)
    attn_grad = jnp.sum(in_grad * in_proj.astype(jnp.float32), axis=1) / attn_norm
    return (
        block_out.astype(jnp.bfloat16).reshape(1, token_rows, D),
        tokens_grad.reshape(1, token_rows, D),
        attn_grad,
        ffn_grad,
        in_grad,
        bias_grad,
        out_grad,
        gate_grad,
        down_grad,
    )


def solution(mesh):
    in_specs = (
        P("fsdp", "ctx", None),
        P("fsdp", "ctx"),
        P("fsdp", "ctx", None),
        P("fsdp"),
        P("fsdp"),
        P("fsdp", None),
        P("fsdp"),
        P("fsdp", None),
        P("fsdp", None),
        P("fsdp", None),
    )
    out_specs = (
        P("fsdp", "ctx", None),
        P("fsdp", "ctx", None),
        P("fsdp"),
        P("fsdp"),
        P("fsdp", None),
        P("fsdp"),
        P("fsdp", None),
        P("fsdp", None),
        P("fsdp", None),
    )
    return jax.shard_map(shards, mesh=mesh, in_specs=in_specs, out_specs=out_specs, check_vma=False)
```

```python
import jax
import jax.numpy as jnp
from jax import lax
from jax.experimental import pallas as pl
from jax.experimental.pallas import tpu as pltpu
from jax.sharding import PartitionSpec as P

D = 1536
QUERY_HEADS = 12
KEY_VALUE_HEADS = 2
HEAD_SIZE = 128
FF = 8960
QD = QUERY_HEADS * HEAD_SIZE
KD = KEY_VALUE_HEADS * HEAD_SIZE
GROUP = QUERY_HEADS // KEY_VALUE_HEADS


norm_eps = 1e-06
rope_base = 1000000.0
masked_score = -1e30
score_scale = HEAD_SIZE ** (-0.5)
vmem_params = pltpu.CompilerParams(vmem_limit_bytes=48 * 1024 * 1024)


def rms_scale(value_rows, scale_vec):
    return (
        value_rows
        * lax.rsqrt(jnp.mean(value_rows * value_rows, axis=-1, keepdims=True) + norm_eps)
        * scale_vec
    )


def norm_backward(value_rows, scale_vec, incoming):
    unused_out, pullback = jax.vjp(lambda rows: rms_scale(rows, scale_vec), value_rows)
    return pullback(incoming)[0]


def rotary_tables(position):
    frequencies = rope_base ** (
        -(jnp.arange(HEAD_SIZE // 2, dtype=jnp.float32) * (2.0 / HEAD_SIZE))
    )
    angles = position.astype(jnp.float32)[:, None] * frequencies[None, :]
    cosine = jnp.cos(angles)
    sine = jnp.sin(angles)
    return (
        jnp.concatenate([cosine, cosine], axis=1),
        jnp.concatenate([-sine, sine], axis=1),
    )


def dot_f32(left, right):
    return jnp.dot(left, right, preferred_element_type=jnp.float32)


def dot_right_t(left, right):
    return lax.dot_general(
        left, right, (((1,), (1,)), ((), ())), preferred_element_type=jnp.float32
    )


def dot_left_t(left, right):
    return lax.dot_general(
        left, right, (((0,), (0,)), ((), ())), preferred_element_type=jnp.float32
    )


def add_low(left, right):
    return left + right


def after(value, *earlier):
    return lax.optimization_barrier((value, earlier))[0]


def exchange(value, mask):
    count = lax.axis_size("fsdp")
    return lax.ppermute(value, "fsdp", [(place, place ^ mask) for place in range(count)])


def gather_pieces(block, *gates):
    count = lax.axis_size("fsdp")
    if count != 8:
        found = [[block]] + [[exchange(block, mask)] for mask in range(2, count, 2)]
    else:
        half = block.shape[0] // 2
        by_x = exchange(block, 2)
        by_y = exchange(block, 4)
        other = exchange(block, 1)
        by_x, by_y = after((by_x, by_y), *gates)
        top = exchange(by_x[:half], 4)
        bottom = exchange(by_y[half:], 2)
        found = [[block], [by_x], [by_y], [top, bottom]]
        others = [[other], [exchange(by_x, 1)], [exchange(by_y, 1)]]
        others.append([exchange(top, 1), exchange(bottom, 1)])
        return [(2 * place, rows) for place, rows in enumerate(found)] + [
            (2 * place + 1, rows) for place, rows in enumerate(others)
        ]
    pieces = []
    for place, rows in enumerate(found):
        pieces.append((2 * place, rows))
        pieces.append((2 * place + 1, [exchange(part, 1) for part in rows]))
    return pieces


def gather_masks(block, *gates):
    count = lax.axis_size("fsdp")
    rows = block.shape[0]
    whole = jnp.zeros((count * rows, block.shape[1]), block.dtype)
    for mask, parts in gather_pieces(block, *gates):
        first = place_of(mask, count) * rows
        for part in parts:
            whole = lax.dynamic_update_slice(whole, part, (first, 0))
            first += part.shape[0]
    return whole


def gather_small(value):
    count = lax.axis_size("fsdp")
    me = lax.axis_index("fsdp")
    found = value[None]
    masks = [1 << bit for bit in range(count.bit_length() - 1)]
    for mask in masks[1:] + masks[:1]:
        found = jnp.concatenate([found, exchange(found, mask)], axis=0)
    order = []
    for place in range(count):
        spot = 0
        for mask in reversed(masks[1:] + masks[:1]):
            spot = 2 * spot + (1 if place & mask else 0)
        order.append(spot)
    return jnp.concatenate(
        [
            lax.dynamic_index_in_dim(
                found,
                lax.dynamic_index_in_dim(jnp.asarray(order, jnp.int32), me ^ device, 0, False),
                0,
            )
            for device in range(count)
        ],
        axis=0,
    )


def place_of(mask, count):
    return mask // 2 if mask % 2 else count // 2 + mask // 2


def mask_at(place, count):
    return jnp.where(place < count // 2, 2 * place + 1, 2 * place - count)


class MaskSum:
    def __init__(self, odd):
        self.got = exchange(odd, 1)

    def second(self, even, *gates):
        count = lax.axis_size("fsdp")
        self.kept = add_low(even, after(self.got, *gates))
        if count == 8:
            half = self.kept.shape[1] // 2
            self.by_x = exchange(self.kept[1::2, :half], 2)
            self.by_y = exchange(self.kept[2:, half:], 4)
        else:
            span = count
            while self.kept.shape[0] > 1:
                span //= 2
                half = self.kept.shape[0] // 2
                self.kept = add_low(self.kept[:half], exchange(self.kept[half:], span))
        return self.kept

    def third(self, *gates):
        if lax.axis_size("fsdp") != 8:
            return self.kept
        half = self.kept.shape[1] // 2
        by_x, by_y = after((self.by_x, self.by_y), *gates)
        self.top = add_low(self.kept[0::2, :half], by_x)
        self.bottom = add_low(self.kept[:2, half:], by_y)
        self.last_y = exchange(self.top[1], 4)
        self.last_x = exchange(self.bottom[1], 2)
        return self.top, self.bottom

    def result(self, *gates):
        if lax.axis_size("fsdp") != 8:
            return self.kept[0]
        last_y, last_x = after((self.last_y, self.last_x), *gates)
        return jnp.concatenate(
            [add_low(self.top[0], last_y), add_low(self.bottom[0], last_x)], axis=0
        )


def swap_blocks(blocks):
    return lax.all_to_all(blocks, "fsdp", 0, 0, tiled=True)


class Wave:
    def __init__(self, raw):
        self.raw = raw
        self.right, self.left = [], []
        self.got_right = self.got_left = None

    def value_of(self, place, crossing, got):
        count = lax.axis_size("ctx")
        middle = count // 2
        tick = len(self.right)
        base = lax.dynamic_index_in_dim(
            self.raw, jnp.clip(tick - place, 0, self.raw.shape[0] - 1), axis=0, keepdims=False
        )
        if crossing is not None:
            base = jnp.where(place < middle, base, crossing)
            base = jnp.where(place > middle, jnp.zeros_like(base), base)
        return base if got is None else add_low(base, got)

    def tick(self, *gates):
        count = lax.axis_size("ctx")
        me = lax.axis_index("ctx")
        if self.got_right is None:
            self.raw = after(self.raw, *gates)
        else:
            self.got_right, self.got_left = after((self.got_right, self.got_left), *gates)
        right_now = self.value_of(me, self.left[-1] if self.left else None, self.got_right)
        left_now = self.value_of(
            count - 1 - me, self.right[-1] if self.right else None, self.got_left
        )
        senders = [
            place
            for place in range(count - 1)
            if 0 <= len(self.right) - place < self.raw.shape[0]
        ]
        if senders:
            self.got_right = lax.ppermute(right_now, "ctx", [(s, s + 1) for s in senders])
            self.got_left = lax.ppermute(
                left_now, "ctx", [(count - 1 - s, count - 2 - s) for s in senders]
            )
        self.right.append(right_now)
        self.left.append(left_now)
        return right_now, left_now

    def totals(self):
        count = lax.axis_size("ctx")
        me = lax.axis_index("ctx")
        chunks = self.raw.shape[0]
        while len(self.right) < chunks + count - 1:
            self.tick()
        totals = []
        for index in range(chunks):
            total = self.right[index + count // 2]
            for place in range(count // 2 + 1, count):
                total = jnp.where(me == place, self.right[index + place], total)
            for place in range(count // 2):
                total = jnp.where(me == place, self.left[index + count - 1 - place], total)
            totals.append(total)
        return lax.optimization_barrier(totals)


def unit_widths(units):
    first = units // 256 * 128
    second = units - first
    return first, second, -(-second // 128) * 128


def split_units(gate_up, count):
    rows, columns = gate_up.shape
    span = columns // 2
    units = span // count
    first, second, padded = unit_widths(units)
    block = 48

    def kernel(weight_ref, first_ref, second_ref):
        for owner in range(count):
            for side in range(2):
                begin = side * span + owner * units
                first_ref[owner, :, side * first : (side + 1) * first] = weight_ref[
                    :, begin : begin + first
                ]
                second_ref[owner, :, side * padded : side * padded + second] = weight_ref[
                    :, begin + first : begin + units
                ]
                if padded > second:
                    second_ref[
                        owner, :, side * padded + second : (side + 1) * padded
                    ] = jnp.zeros((block, padded - second), gate_up.dtype)

    return pl.pallas_call(
        kernel,
        grid=(rows // block,),
        in_specs=[pl.BlockSpec((block, columns), lambda step: (step, 0))],
        out_specs=[
            pl.BlockSpec((count, block, 2 * first), lambda step: (0, step, 0)),
            pl.BlockSpec((count, block, 2 * padded), lambda step: (0, step, 0)),
        ],
        out_shape=[
            jax.ShapeDtypeStruct((count, rows, 2 * first), gate_up.dtype),
            jax.ShapeDtypeStruct((count, rows, 2 * padded), gate_up.dtype),
        ],
        compiler_params=vmem_params,
        cost_estimate=pl.CostEstimate(
            flops=0, bytes_accessed=4 * rows * columns, transcendentals=0
        ),
    )(gate_up)


def join_units(first_part, second_part, gate_up):
    count, rows = first_part.shape[:2]
    span = gate_up.shape[1] // 2
    units = span // count
    first, second, padded = unit_widths(units)
    block = 48

    def kernel(first_ref, second_ref, weight_ref, whole_ref, sums_ref):
        for owner in range(count):
            for side in range(2):
                begin = side * span + owner * units
                whole_ref[:, begin : begin + first] = first_ref[
                    owner, :, side * first : (side + 1) * first
                ].astype(jnp.float32)
                whole_ref[:, begin + first : begin + units] = second_ref[
                    owner, :, side * padded : side * padded + second
                ].astype(jnp.float32)
        total = jnp.sum(
            whole_ref[...] * weight_ref[...].astype(jnp.float32), axis=1, keepdims=True
        )
        sums_ref[...] = jnp.broadcast_to(total, (block, 128))

    whole, sums = pl.pallas_call(
        kernel,
        grid=(rows // block,),
        in_specs=[
            pl.BlockSpec((count, block, 2 * first), lambda step: (0, step, 0)),
            pl.BlockSpec((count, block, 2 * padded), lambda step: (0, step, 0)),
            pl.BlockSpec((block, 2 * span), lambda step: (step, 0)),
        ],
        out_specs=[
            pl.BlockSpec((block, 2 * span), lambda step: (step, 0)),
            pl.BlockSpec((block, 128), lambda step: (step, 0)),
        ],
        out_shape=[
            jax.ShapeDtypeStruct((rows, 2 * span), jnp.float32),
            jax.ShapeDtypeStruct((rows, 128), jnp.float32),
        ],
        compiler_params=vmem_params,
        cost_estimate=pl.CostEstimate(
            flops=4 * rows * span, bytes_accessed=16 * rows * span, transcendentals=0
        ),
    )(first_part, second_part, gate_up)
    return whole, sums[:, 0]


def project(me, normed, pieces, bias, cosine, sine):
    tokens, features = normed.shape[1:]
    width = bias.shape[0]
    block = 512
    flat = [part for unused_mask, parts in pieces for part in parts]

    def kernel(me_ref, normed_ref, bias_ref, cosine_ref, sine_ref, *refs):
        out_ref = refs[-1]
        product = bias_ref[...]
        place = 0
        for mask, parts in pieces:
            weight = jnp.concatenate([ref[...] for ref in refs[place : place + len(parts)]], axis=0)
            place += len(parts)
            product = product + dot_f32(normed_ref[me_ref[0] ^ mask], weight)
        for head in range(block // HEAD_SIZE):
            lanes = slice(head * HEAD_SIZE, (head + 1) * HEAD_SIZE)
            plain = product[:, lanes]
            turned = plain * cosine_ref[...] + pltpu.roll(plain, HEAD_SIZE // 2, 1) * sine_ref[...]
            column = pl.program_id(0) * block + head * HEAD_SIZE
            out_ref[:, lanes] = jnp.where(column < QD + KD, turned, plain).astype(jnp.bfloat16)

    return pl.pallas_call(
        kernel,
        grid_spec=pltpu.PrefetchScalarGridSpec(
            num_scalar_prefetch=1,
            grid=(width // block,),
            in_specs=[
                pl.BlockSpec(normed.shape, lambda step, me_ref: (0, 0, 0)),
                pl.BlockSpec((1, block), lambda step, me_ref: (0, step)),
                pl.BlockSpec((tokens, HEAD_SIZE), lambda step, me_ref: (0, 0)),
                pl.BlockSpec((tokens, HEAD_SIZE), lambda step, me_ref: (0, 0)),
            ]
            + [
                pl.BlockSpec((part.shape[0], block), lambda step, me_ref: (0, step))
                for part in flat
            ],
            out_specs=pl.BlockSpec((tokens, block), lambda step, me_ref: (0, step)),
        ),
        out_shape=jax.ShapeDtypeStruct((tokens, width), jnp.bfloat16),
        compiler_params=vmem_params,
        cost_estimate=pl.CostEstimate(
            flops=2 * tokens * D * width, bytes_accessed=2 * D * width, transcendentals=0
        ),
    )(me, normed, bias[None], cosine, sine, *flat)


def project_back(me, grad_projected, pieces, shard_d):
    tokens = grad_projected.shape[0]
    count = len(pieces)
    flat = [part for unused_mask, parts in pieces for part in parts]

    def kernel(me_ref, grad_ref, *refs):
        out_ref = refs[-1]
        place = 0
        for mask, parts in pieces:
            weight = jnp.concatenate([ref[...] for ref in refs[place : place + len(parts)]], axis=0)
            place += len(parts)
            out_ref[me_ref[0] ^ mask] = dot_right_t(grad_ref[...], weight)

    whole = lambda part: pl.BlockSpec(part.shape, lambda step, me_ref: (0, 0))
    return pl.pallas_call(
        kernel,
        grid_spec=pltpu.PrefetchScalarGridSpec(
            num_scalar_prefetch=1,
            grid=(1,),
            in_specs=[whole(grad_projected)] + [whole(part) for part in flat],
            out_specs=pl.BlockSpec(
                (count, tokens, shard_d), lambda step, me_ref: (0, 0, 0)
            ),
        ),
        out_shape=jax.ShapeDtypeStruct((count, tokens, shard_d), jnp.float32),
        compiler_params=vmem_params,
        cost_estimate=pl.CostEstimate(
            flops=2 * grad_projected.size * D,
            bytes_accessed=2 * D * grad_projected.shape[1],
            transcendentals=0,
        ),
    )(me, grad_projected, *flat)


def fill_bias(at_ref, position_ref, bias_ref):
    tokens, keys = bias_ref.shape
    row = lax.broadcasted_iota(jnp.int32, (tokens, keys), 0)
    column = lax.broadcasted_iota(jnp.int32, (tokens, keys), 1)
    back = column // tokens
    query_index = at_ref[0] * tokens + row
    key_index = (at_ref[0] - back) * tokens + (column - back * tokens)
    allowed = (key_index <= query_index) & (key_index >= query_index - position_ref[...])
    bias_ref[...] = jnp.where(allowed, 0.0, masked_score)


def join_keys(refs, key_ref, value_ref):
    @pl.when(pl.program_id(0) % GROUP == 0)
    def _():
        for place in range(len(refs)):
            tokens = refs[0].shape[0]
            if (place + 1) * tokens > key_ref.shape[0]:
                break
            rows = slice(place * tokens, (place + 1) * tokens)
            key_ref[rows] = refs[2 * place][...]
            value_ref[rows] = refs[2 * place + 1][...]


def key_specs(both_pieces):
    specs = []
    for piece in both_pieces:
        shape = (piece.shape[0], HEAD_SIZE)
        specs.append(pl.BlockSpec(shape, lambda head, at: (0, head // GROUP)))
        specs.append(pl.BlockSpec(shape, lambda head, at: (0, KEY_VALUE_HEADS + head // GROUP)))
    return specs


def attend(at, position, projected, both_pieces):
    tokens = projected.shape[0]
    count = len(both_pieces)
    keys = count * tokens

    def kernel(at_ref, position_ref, query_ref, *refs):
        out_ref, turn_ref, log_ref, bias_ref, key_ref, value_ref = refs[2 * count :]

        @pl.when(pl.program_id(0) == 0)
        def _():
            fill_bias(at_ref, position_ref, bias_ref)

        join_keys(refs, key_ref, value_ref)

        scores = dot_right_t(query_ref[...], key_ref[...]) * score_scale + bias_ref[...]
        top = jnp.max(scores, axis=1, keepdims=True)
        raised = jnp.exp(scores - top)
        total = jnp.sum(raised, axis=1, keepdims=True)
        probs = (raised * (1.0 / total)).astype(jnp.bfloat16)
        result = dot_f32(probs, value_ref[...])
        out_ref[...] = result.astype(jnp.bfloat16)
        turn_ref[...] = result.T.astype(jnp.bfloat16)
        log_ref[0] = top + jnp.log(total)

    return pl.pallas_call(
        kernel,
        grid_spec=pltpu.PrefetchScalarGridSpec(
            num_scalar_prefetch=1,
            grid=(QUERY_HEADS,),
            in_specs=[
                pl.BlockSpec((tokens, 1), lambda head, at: (0, 0)),
                pl.BlockSpec((tokens, HEAD_SIZE), lambda head, at: (0, head)),
            ]
            + key_specs(both_pieces),
            out_specs=[
                pl.BlockSpec((tokens, HEAD_SIZE), lambda head, at: (0, head)),
                pl.BlockSpec((HEAD_SIZE, tokens), lambda head, at: (head, 0)),
                pl.BlockSpec((1, tokens, 1), lambda head, at: (head, 0, 0)),
            ],
            scratch_shapes=[
                pltpu.VMEM((tokens, keys), jnp.float32),
                pltpu.VMEM((keys, HEAD_SIZE), jnp.bfloat16),
                pltpu.VMEM((keys, HEAD_SIZE), jnp.bfloat16),
            ],
        ),
        out_shape=[
            jax.ShapeDtypeStruct((tokens, QD), jnp.bfloat16),
            jax.ShapeDtypeStruct((QD, tokens), jnp.bfloat16),
            jax.ShapeDtypeStruct((QUERY_HEADS, tokens, 1), jnp.float32),
        ],
        compiler_params=vmem_params,
        cost_estimate=pl.CostEstimate(
            flops=8 * tokens * keys * QD,
            bytes_accessed=8 * tokens * QD,
            transcendentals=QUERY_HEADS * tokens * keys,
        ),
    )(at, position, projected, *[piece for piece in both_pieces for unused in range(2)])


def attend_backward(at, position, projected, both_pieces, incoming, log_total, cosine, sine):
    tokens = projected.shape[0]
    count = len(both_pieces)
    keys = count * tokens

    def kernel(
        at_ref,
        position_ref,
        query_ref,
        incoming_ref,
        log_ref,
        cosine_ref,
        sine_ref,
        *refs,
    ):
        query_grad_ref, key_grad_ref, value_grad_ref = refs[2 * count : 2 * count + 3]
        bias_ref, key_total, value_total, key_ref, value_ref = refs[2 * count + 3 :]
        head = pl.program_id(0)
        join_keys(refs, key_ref, value_ref)

        @pl.when(head == 0)
        def _():
            fill_bias(at_ref, position_ref, bias_ref)

        @pl.when(head % GROUP == 0)
        def _():
            key_total[...] = jnp.zeros_like(key_total)
            value_total[...] = jnp.zeros_like(value_total)

        scores = dot_right_t(query_ref[...], key_ref[...]) * score_scale + bias_ref[...]
        probs = jnp.exp(scores - log_ref[0])
        grad_probs = dot_right_t(incoming_ref[...], value_ref[...])
        inner = jnp.sum(grad_probs * probs, axis=1, keepdims=True)
        grad_scores = (probs * (grad_probs - inner)).astype(jnp.bfloat16)
        value_total[...] += dot_left_t(incoming_ref[...], probs.astype(jnp.bfloat16))
        key_total[...] += dot_left_t(query_ref[...], grad_scores)
        plain = dot_f32(grad_scores, key_ref[...]) * score_scale
        query_grad_ref[...] = (
            plain * cosine_ref[...] - pltpu.roll(plain, HEAD_SIZE // 2, 1) * sine_ref[...]
        ).astype(jnp.bfloat16)

        @pl.when(head % GROUP == GROUP - 1)
        def _():
            key_grad_ref[...] = (key_total[...] * score_scale).T
            value_grad_ref[...] = value_total[...].T

    return pl.pallas_call(
        kernel,
        grid_spec=pltpu.PrefetchScalarGridSpec(
            num_scalar_prefetch=1,
            grid=(QUERY_HEADS,),
            in_specs=[
                pl.BlockSpec((tokens, 1), lambda head, at: (0, 0)),
                pl.BlockSpec((tokens, HEAD_SIZE), lambda head, at: (0, head)),
                pl.BlockSpec((tokens, HEAD_SIZE), lambda head, at: (0, head)),
                pl.BlockSpec((1, tokens, 1), lambda head, at: (head, 0, 0)),
                pl.BlockSpec((tokens, HEAD_SIZE), lambda head, at: (0, 0)),
                pl.BlockSpec((tokens, HEAD_SIZE), lambda head, at: (0, 0)),
            ]
            + key_specs(both_pieces),
            out_specs=[
                pl.BlockSpec((tokens, HEAD_SIZE), lambda head, at: (0, head)),
                pl.BlockSpec((keys, HEAD_SIZE), lambda head, at: (0, head // GROUP)),
                pl.BlockSpec((keys, HEAD_SIZE), lambda head, at: (0, head // GROUP)),
            ],
            scratch_shapes=[
                pltpu.VMEM((tokens, keys), jnp.float32),
                pltpu.VMEM((HEAD_SIZE, keys), jnp.float32),
                pltpu.VMEM((HEAD_SIZE, keys), jnp.float32),
                pltpu.VMEM((keys, HEAD_SIZE), jnp.bfloat16),
                pltpu.VMEM((keys, HEAD_SIZE), jnp.bfloat16),
            ],
        ),
        out_shape=[
            jax.ShapeDtypeStruct((tokens, QD), jnp.bfloat16),
            jax.ShapeDtypeStruct((keys, KD), jnp.float32),
            jax.ShapeDtypeStruct((keys, KD), jnp.float32),
        ],
        compiler_params=vmem_params,
        cost_estimate=pl.CostEstimate(
            flops=20 * tokens * keys * QD,
            bytes_accessed=8 * tokens * QD,
            transcendentals=QUERY_HEADS * tokens * keys,
        ),
    )(
        at,
        position,
        projected,
        incoming,
        log_total,
        cosine,
        sine,
        *[piece for piece in both_pieces for unused in range(2)],
    )


def unit_part(me, normed_all, grad_out_all, gate_up, down, count, reorder):
    tokens = normed_all.shape[0]
    block = tokens // count
    width = down.shape[0]

    def kernel(me_ref, normed_ref, out_grad_ref, gate_up_ref, down_ref, hidden_ref, grad_ref, *rest):
        values = dot_f32(normed_ref[...], gate_up_ref[...])
        gate = values[:, :width]
        up = values[:, width:]
        grad_hidden = dot_right_t(out_grad_ref[...], down_ref[...])
        share = 1.0 / (1.0 + jnp.exp(-gate))
        passed = gate * share
        hidden_ref[...] = (passed * up).astype(jnp.bfloat16)
        grad_ref[:, :width] = (
            grad_hidden * up * share * (1.0 + gate * (1.0 - share))
        ).astype(jnp.bfloat16)
        grad_ref[:, width:] = (grad_hidden * passed).astype(jnp.bfloat16)
        if rest:
            rest[0][...] = out_grad_ref[...]

    def out_grad_index(step, me_ref):
        return (me_ref[0] ^ mask_at(step, count), 0) if reorder else (step, 0)

    row = lambda step, me_ref: (step, 0)
    fixed = lambda step, me_ref: (0, 0)
    out_specs = [pl.BlockSpec((block, width), row), pl.BlockSpec((block, 2 * width), row)]
    out_shape = [
        jax.ShapeDtypeStruct((tokens, width), jnp.bfloat16),
        jax.ShapeDtypeStruct((tokens, 2 * width), jnp.bfloat16),
    ]
    if reorder:
        out_specs.append(pl.BlockSpec((block, D), row))
        out_shape.append(jax.ShapeDtypeStruct((tokens, D), jnp.bfloat16))
    return pl.pallas_call(
        kernel,
        grid_spec=pltpu.PrefetchScalarGridSpec(
            num_scalar_prefetch=1,
            grid=(count,),
            in_specs=[
                pl.BlockSpec((block, D), row),
                pl.BlockSpec((block, D), out_grad_index),
                pl.BlockSpec((D, 2 * width), fixed),
                pl.BlockSpec((width, D), fixed),
            ],
            out_specs=out_specs,
        ),
        out_shape=out_shape,
        compiler_params=vmem_params,
        cost_estimate=pl.CostEstimate(
            flops=6 * tokens * D * width,
            bytes_accessed=4 * tokens * D + 6 * tokens * width + 6 * D * width,
            transcendentals=tokens * width,
        ),
    )(me, normed_all, grad_out_all, gate_up, down)


def row_block_terms(me, turned, right):
    count, rows, tokens = turned.shape
    width = right.shape[1]

    def kernel(me_ref, turned_ref, right_ref, out_ref):
        out_ref[0] = dot_f32(turned_ref[0], right_ref[...]).astype(jnp.bfloat16)

    return pl.pallas_call(
        kernel,
        grid_spec=pltpu.PrefetchScalarGridSpec(
            num_scalar_prefetch=1,
            grid=(count,),
            in_specs=[
                pl.BlockSpec(
                    (1, rows, tokens),
                    lambda step, me_ref: (me_ref[0] ^ mask_at(step, count), 0, 0),
                ),
                pl.BlockSpec((tokens, width), lambda step, me_ref: (0, 0)),
            ],
            out_specs=pl.BlockSpec((1, rows, width), lambda step, me_ref: (step, 0, 0)),
        ),
        out_shape=jax.ShapeDtypeStruct((count, rows, width), jnp.bfloat16),
        compiler_params=vmem_params,
        cost_estimate=pl.CostEstimate(
            flops=2 * count * rows * tokens * width,
            bytes_accessed=2 * count * rows * width,
            transcendentals=0,
        ),
    )(me, turned, right)


def shards(
    tokens,
    positions,
    cotangent,
    attn_norm,
    ffn_norm,
    in_proj,
    in_bias,
    out_proj,
    gate_up,
    down_proj,
):
    token_rows = tokens.shape[1]
    fsdp_count = lax.axis_size("fsdp")
    ctx_count = lax.axis_size("ctx")
    fsdp_me = lax.axis_index("fsdp")
    me = fsdp_me.astype(jnp.int32)[None]
    at = lax.axis_index("ctx").astype(jnp.int32)[None]
    units = FF // fsdp_count
    shard_d = D // fsdp_count
    residual_in = tokens[0].astype(jnp.float32)
    position = positions[0]
    grad_out_b = cotangent[0]

    first_units, second_units, padded_units = unit_widths(units)
    vectors = gather_small(jnp.concatenate([attn_norm, ffn_norm, in_bias]))
    first_blocks, second_blocks = split_units(gate_up, fsdp_count)
    attn_scale = vectors[:, :shard_d].reshape(D)
    ffn_scale = vectors[:, shard_d : 2 * shard_d].reshape(D)
    bias_full = vectors[:, 2 * shard_d :].reshape(-1)
    cosine, sine = rotary_tables(position)
    in_pieces = gather_pieces(in_proj, first_blocks, cosine)
    normed_b = rms_scale(residual_in, attn_scale).astype(jnp.bfloat16)
    normed_blocks = normed_b.reshape(token_rows, fsdp_count, shard_d).transpose(1, 0, 2)
    gate_up_first = swap_blocks(after(first_blocks, in_pieces)).reshape(D, 2 * first_units)
    out_full = lax.all_gather(after(out_proj, in_pieces), "fsdp", axis=0, tiled=True)
    down_first = down_proj[:first_units]
    down_second = jnp.pad(down_proj[first_units:], ((0, padded_units - second_units), (0, 0)))

    projected = project(me, normed_blocks, in_pieces, bias_full, cosine, sine)
    both_b = projected[:, QD:]
    both_pieces = [both_b] + [
        lax.ppermute(both_b, "ctx", [(s, s + back) for s in range(ctx_count - back)])
        for back in range(1, ctx_count)
    ]
    normed_turned = jnp.concatenate(
        [
            normed_b.T.reshape(fsdp_count, shard_d, token_rows),
            jnp.ones((fsdp_count, 1, token_rows), jnp.bfloat16),
            jnp.zeros((fsdp_count, 15, token_rows), jnp.bfloat16),
        ],
        axis=1,
    )
    both_pieces = after(both_pieces, normed_turned, down_first, down_second)
    grad_out_all = lax.all_gather(
        after(grad_out_b, out_full, both_pieces), "fsdp", axis=0, tiled=True
    )
    attended_b, attended_turned, log_total = attend(at, position[:, None], projected, both_pieces)
    middle = residual_in + dot_f32(after(attended_b, gate_up_first), out_full)
    normed_ffn_b = rms_scale(middle, ffn_scale).astype(jnp.bfloat16)

    normed_ffn_all = gather_masks(normed_ffn_b)
    gate_up_second = swap_blocks(after(second_blocks, normed_ffn_all)).reshape(
        D, 2 * padded_units
    )
    hidden_first, grad_first, grad_out_all = unit_part(
        me, normed_ffn_all, grad_out_all, gate_up_first, down_first, fsdp_count, True
    )
    odd_rows = normed_ffn_all.shape[0] // 2

    def down_term(hidden, *gates):
        return dot_left_t(after(hidden, *gates), grad_out_all).astype(jnp.bfloat16)

    def gate_term(grad, *gates):
        term = dot_left_t(normed_ffn_all, after(grad, *gates)).astype(jnp.bfloat16)
        swapped = swap_blocks(term.reshape(fsdp_count, shard_d, -1))
        return term, Wave(swapped.reshape(4, -1, shard_d, term.shape[1]))

    def input_grads(rows, *gates):
        return (
            (
                dot_right_t(after(grad_first, *gates)[rows], gate_up_first)
                + dot_right_t(grad_second[rows], gate_up_second)
            )
            .astype(jnp.bfloat16)
            .reshape(fsdp_count // 2, token_rows, D)
        )

    def down_outs(rows, *gates):
        return (
            (
                dot_f32(after(hidden_first, *gates)[rows], down_first)
                + dot_f32(hidden_second[rows], down_second)
            )
            .astype(jnp.bfloat16)
            .reshape(fsdp_count // 2, token_rows, D)
        )

    down_a = Wave(down_term(hidden_first).reshape(2, first_units // 2, D))
    sent = down_a.tick()
    gate_term_a, gate_a = gate_term(grad_first, sent)
    hidden_second, grad_second = unit_part(
        me,
        after(normed_ffn_all, gate_term_a),
        grad_out_all,
        gate_up_second,
        down_second,
        fsdp_count,
        False,
    )
    sent = down_a.tick(hidden_second)
    grad_normed_odd = input_grads(slice(0, odd_rows), sent)
    normed_sum = MaskSum(grad_normed_odd)
    sent = down_a.tick(grad_normed_odd)
    sent = gate_a.tick(sent)
    grad_normed_even = input_grads(slice(odd_rows, None), sent)
    sent = normed_sum.second(grad_normed_even)
    sent = down_a.tick(sent)
    sent = gate_a.tick(sent)
    down_b = Wave(down_term(hidden_second, sent)[:second_units].reshape(2, second_units // 2, D))
    sent = gate_a.tick(down_b.raw)
    gate_term_b, gate_b = gate_term(grad_second, sent)
    sent = normed_sum.third(gate_term_b)
    sent = gate_a.tick(sent)
    down_odd = down_outs(slice(0, odd_rows), sent)
    down_sum = MaskSum(down_odd)
    grad_normed_ffn = normed_sum.result(down_odd).astype(jnp.float32)

    grad_out = grad_out_b.astype(jnp.float32)
    grad_middle = grad_out + norm_backward(middle, ffn_scale, grad_normed_ffn)
    grad_middle_b = grad_middle.astype(jnp.bfloat16)
    sent = gate_a.tick(grad_middle_b)
    sent = down_b.tick(sent)
    grad_attended_b = dot_right_t(after(grad_middle_b, sent), out_full).astype(jnp.bfloat16)
    query_grad, key_grads, value_grads = attend_backward(
        at,
        position[:, None],
        projected,
        both_pieces,
        grad_attended_b,
        log_total,
        cosine,
        sine,
    )
    both_sent = [
        lax.ppermute(
            jnp.concatenate(
                [
                    grads[back * token_rows : (back + 1) * token_rows].astype(jnp.bfloat16)
                    for grads in (key_grads, value_grads)
                ],
                axis=1,
            ),
            "ctx",
            [(s + back, s) for s in range(ctx_count - back)],
        )
        for back in range(1, ctx_count)
    ]
    sent = gate_a.tick(query_grad)
    sent = down_b.tick(sent)
    out_terms = row_block_terms(
        me,
        attended_turned.reshape(fsdp_count, shard_d, token_rows),
        after(grad_middle_b, sent),
    )
    half = fsdp_count // 2
    out_sum = MaskSum(out_terms[:half])
    down_even = down_outs(slice(odd_rows, None), out_terms)
    sent = down_b.tick(down_even)
    sent = gate_b.tick(sent)
    both_grad = jnp.concatenate([key_grads[:token_rows], value_grads[:token_rows]], axis=1)
    for piece in after(both_sent, sent):
        both_grad = both_grad + piece.astype(jnp.float32)
    turned_back = []
    for head in range(KEY_VALUE_HEADS):
        plain = both_grad[:, head * HEAD_SIZE : (head + 1) * HEAD_SIZE]
        turned_back.append(plain * cosine - jnp.roll(plain, HEAD_SIZE // 2, axis=1) * sine)
    grad_projected_b = jnp.concatenate(
        [query_grad]
        + [part.astype(jnp.bfloat16) for part in turned_back]
        + [both_grad[:, KD:].astype(jnp.bfloat16)],
        axis=1,
    )
    in_terms = row_block_terms(me, normed_turned, grad_projected_b)
    in_sum = MaskSum(in_terms[:half])
    sent = down_b.tick(in_terms)
    sent = gate_b.tick(sent)
    sent = out_sum.second(out_terms[half:], sent)
    sent = in_sum.second(in_terms[half:], sent)
    sent = down_sum.second(down_even, sent)
    sent = gate_b.tick(sent)
    grad_normed = project_back(me, after(grad_projected_b, sent), in_pieces, shard_d)
    grad_normed = grad_normed.transpose(1, 0, 2).reshape(token_rows, D)
    tokens_grad = grad_middle + norm_backward(residual_in, attn_scale, grad_normed)
    sent = out_sum.third(tokens_grad)
    sent = in_sum.third(sent)
    sent = gate_b.tick(sent)
    out_wave = Wave(out_sum.result(sent)[None])
    sent = out_wave.tick()
    sent = gate_b.tick(sent)
    sent = down_sum.third(sent)
    in_wave = Wave(in_sum.result(sent)[None])
    sent = in_wave.tick()
    sent = out_wave.tick(sent)
    sent = gate_b.tick(sent)
    block_out = middle + down_sum.result(sent).astype(jnp.float32)
    down_grad = jnp.concatenate(
        down_a.totals() + after(down_b.totals(), block_out), axis=0
    ).astype(jnp.float32)
    sent = in_wave.tick(down_grad)
    sent = out_wave.tick(sent)
    gate_grad, gate_sums = join_units(
        jnp.concatenate(gate_a.totals(), axis=0),
        jnp.concatenate(after(gate_b.totals(), sent), axis=0),
        gate_up,
    )
    ffn_grad = gate_sums / ffn_norm
    sent = in_wave.tick(gate_grad)
    out_grad = out_wave.totals()[0].astype(jnp.float32)
    in_total = in_wave.totals()[0].astype(jnp.float32)
    in_grad = in_total[:shard_d]
    bias_span = in_bias.shape[0]
    bias_grad = lax.dynamic_slice_in_dim(in_total[shard_d], fsdp_me * bias_span, bias_span)
    attn_grad = jnp.sum(in_grad * in_proj.astype(jnp.float32), axis=1) / attn_norm
    return (
        block_out.astype(jnp.bfloat16).reshape(1, token_rows, D),
        tokens_grad.reshape(1, token_rows, D),
        attn_grad,
        ffn_grad,
        in_grad,
        bias_grad,
        out_grad,
        gate_grad,
        down_grad,
    )


def solution(mesh):
    in_specs = (
        P("fsdp", "ctx", None),
        P("fsdp", "ctx"),
        P("fsdp", "ctx", None),
        P("fsdp"),
        P("fsdp"),
        P("fsdp", None),
        P("fsdp"),
        P("fsdp", None),
        P("fsdp", None),
        P("fsdp", None),
    )
    out_specs = (
        P("fsdp", "ctx", None),
        P("fsdp", "ctx", None),
        P("fsdp"),
        P("fsdp"),
        P("fsdp", None),
        P("fsdp"),
        P("fsdp", None),
        P("fsdp", None),
        P("fsdp", None),
    )
    return jax.shard_map(shards, mesh=mesh, in_specs=in_specs, out_specs=out_specs, check_vma=False)
```

```python
import jax
import jax.numpy as jnp
from jax import lax
from jax.experimental import pallas as pl
from jax.experimental.pallas import tpu as pltpu
from jax.sharding import PartitionSpec as P

D = 1536
QUERY_HEADS = 12
KEY_VALUE_HEADS = 2
HEAD_SIZE = 128
FF = 8960
QD = QUERY_HEADS * HEAD_SIZE
KD = KEY_VALUE_HEADS * HEAD_SIZE
GROUP = QUERY_HEADS // KEY_VALUE_HEADS


norm_eps = 1e-06
rope_base = 1000000.0
masked_score = -1e30
score_scale = HEAD_SIZE ** (-0.5)
vmem_params = pltpu.CompilerParams(vmem_limit_bytes=48 * 1024 * 1024)


def rms_scale(value_rows, scale_vec):
    return (
        value_rows
        * lax.rsqrt(jnp.mean(value_rows * value_rows, axis=-1, keepdims=True) + norm_eps)
        * scale_vec
    )


def norm_backward(value_rows, scale_vec, incoming):
    unused_out, pullback = jax.vjp(lambda rows: rms_scale(rows, scale_vec), value_rows)
    return pullback(incoming)[0]


def rotary_tables(position):
    frequencies = rope_base ** (
        -(jnp.arange(HEAD_SIZE // 2, dtype=jnp.float32) * (2.0 / HEAD_SIZE))
    )
    angles = position.astype(jnp.float32)[:, None] * frequencies[None, :]
    cosine = jnp.cos(angles)
    sine = jnp.sin(angles)
    return (
        jnp.concatenate([cosine, cosine], axis=1),
        jnp.concatenate([-sine, sine], axis=1),
    )


def dot_f32(left, right):
    return jnp.dot(left, right, preferred_element_type=jnp.float32)


def dot_right_t(left, right):
    return lax.dot_general(
        left, right, (((1,), (1,)), ((), ())), preferred_element_type=jnp.float32
    )


def dot_left_t(left, right):
    return lax.dot_general(
        left, right, (((0,), (0,)), ((), ())), preferred_element_type=jnp.float32
    )


def add_low(left, right):
    return left + right


def after(value, *earlier):
    return lax.optimization_barrier((value, earlier))[0]


def exchange(value, mask):
    count = lax.axis_size("fsdp")
    return lax.ppermute(value, "fsdp", [(place, place ^ mask) for place in range(count)])


def gather_pieces(block, *gates):
    count = lax.axis_size("fsdp")
    if count != 8:
        found = [[block]] + [[exchange(block, mask)] for mask in range(2, count, 2)]
    else:
        half = block.shape[0] // 2
        by_x = exchange(block, 2)
        by_y = exchange(block, 4)
        other = exchange(block, 1)
        by_x, by_y = after((by_x, by_y), *gates)
        top = exchange(by_x[:half], 4)
        bottom = exchange(by_y[half:], 2)
        found = [[block], [by_x], [by_y], [top, bottom]]
        others = [[other], [exchange(by_x, 1)], [exchange(by_y, 1)]]
        others.append([exchange(top, 1), exchange(bottom, 1)])
        return [(2 * place, rows) for place, rows in enumerate(found)] + [
            (2 * place + 1, rows) for place, rows in enumerate(others)
        ]
    pieces = []
    for place, rows in enumerate(found):
        pieces.append((2 * place, rows))
        pieces.append((2 * place + 1, [exchange(part, 1) for part in rows]))
    return pieces


def gather_masks(block, *gates):
    count = lax.axis_size("fsdp")
    rows = block.shape[0]
    whole = jnp.zeros((count * rows, block.shape[1]), block.dtype)
    for mask, parts in gather_pieces(block, *gates):
        first = place_of(mask, count) * rows
        for part in parts:
            whole = lax.dynamic_update_slice(whole, part, (first, 0))
            first += part.shape[0]
    return whole


def gather_small(value):
    count = lax.axis_size("fsdp")
    me = lax.axis_index("fsdp")
    bits = count.bit_length() - 1
    found = value
    for bit in list(range(1, bits)) + [0]:
        got = exchange(found, 1 << bit)
        low = (me >> bit) % 2 == 0
        found = jnp.stack([jnp.where(low, found, got), jnp.where(low, got, found)])
    return jnp.moveaxis(found, 0, bits - 1).reshape(count, -1)


def place_of(mask, count):
    return mask // 2 + (1 - mask % 2) * (count // 2)


def mask_at(place, count):
    return jnp.where(place < count // 2, 2 * place + 1, 2 * place - count)


class MaskSum:
    def __init__(self, odd):
        self.got = exchange(odd, 1)

    def second(self, even, *gates):
        count = lax.axis_size("fsdp")
        self.kept = add_low(even, after(self.got, *gates))
        if count == 8:
            half = self.kept.shape[1] // 2
            self.by_x = exchange(self.kept[1::2, :half], 2)
            self.by_y = exchange(self.kept[2:, half:], 4)
        else:
            span = count
            while self.kept.shape[0] > 1:
                span //= 2
                half = self.kept.shape[0] // 2
                self.kept = add_low(self.kept[:half], exchange(self.kept[half:], span))
        return self.kept

    def third(self, *gates):
        if lax.axis_size("fsdp") != 8:
            return self.kept
        half = self.kept.shape[1] // 2
        by_x, by_y = after((self.by_x, self.by_y), *gates)
        self.top = add_low(self.kept[0::2, :half], by_x)
        self.bottom = add_low(self.kept[:2, half:], by_y)
        self.last_y = exchange(self.top[1], 4)
        self.last_x = exchange(self.bottom[1], 2)
        return self.top, self.bottom

    def result(self, *gates):
        if lax.axis_size("fsdp") != 8:
            return self.kept[0]
        last_y, last_x = after((self.last_y, self.last_x), *gates)
        return jnp.concatenate(
            [add_low(self.top[0], last_y), add_low(self.bottom[0], last_x)], axis=0
        )


def swap_blocks(blocks):
    return lax.all_to_all(blocks, "fsdp", 0, 0, tiled=True)


class Stream:
    steps = 4

    def __init__(self, at, rows, chunks):
        self.at = at
        self.rows, self.chunks = rows, chunks
        self.time = 0
        self.inward = None
        self.got_right = self.got_left = None
        self.totals = None

    def tick(self, sources, *gates):
        count = lax.axis_size("ctx")
        middle = count // 2
        time = self.time
        chunks, rows = self.chunks, self.rows // self.steps
        sources = [
            source
            for source in sources
            if source[1] <= time and time - (middle - 1) < source[1] + source[2]
        ]
        gots = [] if self.got_right is None else [self.got_right, self.got_left]
        arrays = [source[0] for source in sources]
        before = [] if self.inward is None else [self.inward]
        kept = [] if self.totals is None else [self.totals]
        gots, arrays = after((gots, arrays), *gates)

        def depth_of(at_ref):
            return jnp.minimum(at_ref[0], count - 1 - at_ref[0])

        def kernel(at_ref, *refs):
            refs = list(refs)
            got_refs = [refs.pop(0) for unused in gots]
            source_refs = [refs.pop(0) for unused in arrays]
            before_refs = [refs.pop(0) for unused in before]
            del refs[: len(kept)]
            right_ref, left_ref, inward_ref, totals_ref = refs
            on_left = at_ref[0] < middle
            chunk = time - depth_of(at_ref)
            for source, ref in zip(sources, source_refs):

                @pl.when((chunk >= source[1]) & (chunk < source[1] + source[2]))
                def _():
                    source[5](ref, inward_ref)

            if gots:
                right, left = got_refs[0][...], got_refs[1][...]
                inward = inward_ref[...] + jnp.where(on_left, right, left)
                outward = jnp.where(on_left, left, right)
                if before:
                    crossing = before_refs[0][...] + outward
                    outward = jnp.where(depth_of(at_ref) == middle - 1, crossing, outward)
                inward_ref[...] = inward
            else:
                inward = outward = inward_ref[...]
            right_ref[...] = jnp.where(on_left, inward, outward)
            left_ref[...] = jnp.where(on_left, outward, inward)
            totals_ref[0] = outward

        def source_spec(source):
            def index(step, at_ref):
                chunk = jnp.clip(time - depth_of(at_ref) - source[1], 0, source[2] - 1)
                return source[4](chunk, step)

            return pl.BlockSpec(source[3], index)

        def totals_index(step, at_ref):
            chunk = time - (count - 1) + depth_of(at_ref)
            return (jnp.where((chunk >= 0) & (chunk < chunks), chunk, chunks), step, 0)

        flat = pl.BlockSpec((rows, 128), lambda step, at_ref: (step, 0))
        buffer = jax.ShapeDtypeStruct((self.rows, 128), jnp.bfloat16)
        operands = gots + arrays + before + kept
        right, left, self.inward, self.totals = pl.pallas_call(
            kernel,
            grid_spec=pltpu.PrefetchScalarGridSpec(
                num_scalar_prefetch=1,
                grid=(self.steps,),
                in_specs=[flat] * len(gots)
                + [source_spec(source) for source in sources]
                + [flat] * len(before)
                + [pl.BlockSpec(memory_space=pl.ANY)] * len(kept),
                out_specs=[flat, flat, flat, pl.BlockSpec((1, rows, 128), totals_index)],
            ),
            out_shape=[buffer, buffer, buffer]
            + [jax.ShapeDtypeStruct((chunks + 1, self.rows, 128), jnp.bfloat16)],
            input_output_aliases={len(operands): 3} if kept else {},
            compiler_params=vmem_params,
            cost_estimate=pl.CostEstimate(
                flops=4 * 128 * self.rows, bytes_accessed=14 * 128 * self.rows, transcendentals=0
            ),
        )(self.at, *operands)
        senders = [place for place in range(count - 1) if 0 <= time - place < chunks]
        if senders:
            self.got_right = lax.ppermute(right, "ctx", [(s, s + 1) for s in senders])
            self.got_left = lax.ppermute(
                left, "ctx", [(count - 1 - s, count - 2 - s) for s in senders]
            )
        self.time += 1
        return self.totals

    def finish(self, sources, *gates):
        while self.time < self.chunks + lax.axis_size("ctx") - 1:
            self.tick(sources, *gates)
        return self.totals


def load_lanes(ref, rows_ref):
    value = ref[...]
    value = value.reshape(-1, *value.shape[-2:])
    place = 0
    for part in range(value.shape[0]):
        for first in range(0, value.shape[2], 128):
            rows_ref[place : place + value.shape[1]] = value[part, :, first : first + 128]
            place += value.shape[1]


halves = 2


def unit_sources(down_term, gate_term, halves):
    width = down_term.shape[0]
    sources = [
        (
            down_term,
            0,
            halves,
            (width // halves, D // Stream.steps),
            lambda chunk, step: (chunk, step),
            load_lanes,
        )
    ]
    if gate_term is not None:
        owners, rows, lanes = gate_term.shape
        per_chunk = owners // (2 * halves)
        spread = max(Stream.steps // per_chunk, 1)
        per_block = max(per_chunk // Stream.steps, 1)
        sources.append(
            (
                gate_term,
                halves,
                2 * halves,
                (per_block, rows, lanes // spread),
                lambda chunk, step: (
                    (chunk * Stream.steps + step) // spread,
                    0,
                    step % spread,
                ),
                load_lanes,
            )
        )
    return sources


def unit_widths(units):
    first = units // 256 * 128
    second = units - first
    return first, second, -(-second // 128) * 128


def split_units(me, gate_up, count):
    rows, columns = gate_up.shape
    span = columns // 2
    units = span // count
    first, second, padded = unit_widths(units)
    block = 48

    def kernel(me_ref, weight_ref, first_ref, second_ref):
        for owner in range(count):
            for side in range(2):
                begin = side * span + owner * units
                first_ref[me_ref[0] ^ owner, :, side * first : (side + 1) * first] = weight_ref[
                    :, begin : begin + first
                ]
                second_ref[owner, :, side * padded : side * padded + second] = weight_ref[
                    :, begin + first : begin + units
                ]
                if padded > second:
                    second_ref[
                        owner, :, side * padded + second : (side + 1) * padded
                    ] = jnp.zeros((block, padded - second), gate_up.dtype)

    return pl.pallas_call(
        kernel,
        grid_spec=pltpu.PrefetchScalarGridSpec(
            num_scalar_prefetch=1,
            grid=(rows // block,),
            in_specs=[pl.BlockSpec((block, columns), lambda step, me_ref: (step, 0))],
            out_specs=[
                pl.BlockSpec((count, block, 2 * first), lambda step, me_ref: (0, step, 0)),
                pl.BlockSpec((count, block, 2 * padded), lambda step, me_ref: (0, step, 0)),
            ],
        ),
        out_shape=[
            jax.ShapeDtypeStruct((count, rows, 2 * first), gate_up.dtype),
            jax.ShapeDtypeStruct((count, rows, 2 * padded), gate_up.dtype),
        ],
        compiler_params=vmem_params,
        cost_estimate=pl.CostEstimate(
            flops=0, bytes_accessed=4 * rows * columns, transcendentals=0
        ),
    )(me, gate_up)


def join_units(first_totals, second_totals, gate_up, halves, count):
    rows, columns = gate_up.shape
    span = columns // 2
    units = span // count
    first, second, padded = unit_widths(units)
    per_chunk = count // (2 * halves)
    block = 48

    def lanes_of(totals_ref, owner, width):
        groups = 2 * width // 128
        return [
            totals_ref[(owner % per_chunk) * groups + group] for group in range(groups)
        ]

    def kernel(*refs):
        first_refs = refs[: 2 * halves]
        second_refs = refs[2 * halves : 4 * halves]
        weight_ref, whole_ref, sums_ref = refs[4 * halves :]
        for owner in range(count):
            for part_refs, width, used, start in (
                (first_refs, first, first, 0),
                (second_refs, padded, second, first),
            ):
                groups = width // 128
                ref = part_refs[owner // per_chunk]
                for side in range(2):
                    for group in range(groups):
                        lanes = min(128, used - group * 128)
                        if lanes <= 0:
                            continue
                        begin = side * span + owner * units + start + group * 128
                        place = (owner % per_chunk) * 2 * groups + side * groups + group
                        whole_ref[:, begin : begin + lanes] = ref[0, place, :, :lanes].astype(
                            jnp.float32
                        )
        total = jnp.sum(
            whole_ref[...] * weight_ref[...].astype(jnp.float32), axis=1, keepdims=True
        )
        sums_ref[...] = jnp.broadcast_to(total, (block, 128))

    def totals_specs(width):
        places = per_chunk * 2 * width // 128
        return [
            pl.BlockSpec(
                (1, places, block, 128), lambda step, chunk=halves + chunk: (chunk, 0, step, 0)
            )
            for chunk in range(2 * halves)
        ]

    def by_rows(totals):
        return totals.reshape(totals.shape[0], -1, rows, 128)

    whole, sums = pl.pallas_call(
        kernel,
        grid=(rows // block,),
        in_specs=totals_specs(first)
        + totals_specs(padded)
        + [pl.BlockSpec((block, columns), lambda step: (step, 0))],
        out_specs=[
            pl.BlockSpec((block, columns), lambda step: (step, 0)),
            pl.BlockSpec((block, 128), lambda step: (step, 0)),
        ],
        out_shape=[
            jax.ShapeDtypeStruct((rows, columns), jnp.float32),
            jax.ShapeDtypeStruct((rows, 128), jnp.float32),
        ],
        compiler_params=vmem_params,
        cost_estimate=pl.CostEstimate(
            flops=2 * rows * columns, bytes_accessed=8 * rows * columns, transcendentals=0
        ),
    )(
        *[by_rows(first_totals)] * (2 * halves),
        *[by_rows(second_totals)] * (2 * halves),
        gate_up,
    )
    return whole, sums[:, 0]


def join_down(first_totals, second_totals, first, second, padded, halves):
    lanes = D // 128

    def kernel(first_ref, second_ref, whole_ref):
        for ref, width, start in ((first_ref, first, 0), (second_ref, padded, first)):
            rows = width // halves
            for half in range(halves):
                used = min(rows, first + second - start - half * rows)
                begin = start + half * rows
                whole_ref[begin : begin + used] = ref[half, 0, :used].astype(jnp.float32)

    def by_lanes(totals, width):
        return totals.reshape(totals.shape[0], lanes, width // halves, 128)

    def spec(width):
        return pl.BlockSpec((halves, 1, width // halves, 128), lambda step: (0, step, 0, 0))

    return pl.pallas_call(
        kernel,
        grid=(lanes,),
        in_specs=[spec(first), spec(padded)],
        out_specs=pl.BlockSpec((first + second, 128), lambda step: (0, step)),
        out_shape=jax.ShapeDtypeStruct((first + second, D), jnp.float32),
        compiler_params=vmem_params,
        cost_estimate=pl.CostEstimate(
            flops=0, bytes_accessed=6 * (first + second) * D, transcendentals=0
        ),
    )(by_lanes(first_totals, first), by_lanes(second_totals, padded))


def project(me, normed, pieces, bias, cosine, sine):
    tokens, features = normed.shape[1:]
    width = bias.shape[0]
    block = 512
    flat = [part for unused_mask, parts in pieces for part in parts]

    def kernel(me_ref, normed_ref, bias_ref, cosine_ref, sine_ref, *refs):
        out_ref = refs[-1]
        product = bias_ref[...]
        place = 0
        for mask, parts in pieces:
            weight = jnp.concatenate([ref[...] for ref in refs[place : place + len(parts)]], axis=0)
            place += len(parts)
            product = product + dot_f32(normed_ref[me_ref[0] ^ mask], weight)
        for head in range(block // HEAD_SIZE):
            lanes = slice(head * HEAD_SIZE, (head + 1) * HEAD_SIZE)
            plain = product[:, lanes]
            turned = plain * cosine_ref[...] + pltpu.roll(plain, HEAD_SIZE // 2, 1) * sine_ref[...]
            column = pl.program_id(0) * block + head * HEAD_SIZE
            out_ref[:, lanes] = jnp.where(column < QD + KD, turned, plain).astype(jnp.bfloat16)

    return pl.pallas_call(
        kernel,
        grid_spec=pltpu.PrefetchScalarGridSpec(
            num_scalar_prefetch=1,
            grid=(width // block,),
            in_specs=[
                pl.BlockSpec(normed.shape, lambda step, me_ref: (0, 0, 0)),
                pl.BlockSpec((1, block), lambda step, me_ref: (0, step)),
                pl.BlockSpec((tokens, HEAD_SIZE), lambda step, me_ref: (0, 0)),
                pl.BlockSpec((tokens, HEAD_SIZE), lambda step, me_ref: (0, 0)),
            ]
            + [
                pl.BlockSpec((part.shape[0], block), lambda step, me_ref: (0, step))
                for part in flat
            ],
            out_specs=pl.BlockSpec((tokens, block), lambda step, me_ref: (0, step)),
        ),
        out_shape=jax.ShapeDtypeStruct((tokens, width), jnp.bfloat16),
        compiler_params=vmem_params,
        cost_estimate=pl.CostEstimate(
            flops=2 * tokens * D * width, bytes_accessed=2 * D * width, transcendentals=0
        ),
    )(me, normed, bias[None], cosine, sine, *flat)


def project_back(me, grad_projected, pieces, shard_d):
    tokens = grad_projected.shape[0]
    count = len(pieces)
    flat = [part for unused_mask, parts in pieces for part in parts]

    def kernel(me_ref, grad_ref, *refs):
        out_ref = refs[-1]
        place = 0
        for mask, parts in pieces:
            weight = jnp.concatenate([ref[...] for ref in refs[place : place + len(parts)]], axis=0)
            place += len(parts)
            out_ref[me_ref[0] ^ mask] = dot_right_t(grad_ref[...], weight)

    whole = lambda part: pl.BlockSpec(part.shape, lambda step, me_ref: (0, 0))
    return pl.pallas_call(
        kernel,
        grid_spec=pltpu.PrefetchScalarGridSpec(
            num_scalar_prefetch=1,
            grid=(1,),
            in_specs=[whole(grad_projected)] + [whole(part) for part in flat],
            out_specs=pl.BlockSpec(
                (count, tokens, shard_d), lambda step, me_ref: (0, 0, 0)
            ),
        ),
        out_shape=jax.ShapeDtypeStruct((count, tokens, shard_d), jnp.float32),
        compiler_params=vmem_params,
        cost_estimate=pl.CostEstimate(
            flops=2 * grad_projected.size * D,
            bytes_accessed=2 * D * grad_projected.shape[1],
            transcendentals=0,
        ),
    )(me, grad_projected, *flat)


def fill_bias(at_ref, position_ref, bias_ref):
    tokens, keys = bias_ref.shape
    row = lax.broadcasted_iota(jnp.int32, (tokens, keys), 0)
    column = lax.broadcasted_iota(jnp.int32, (tokens, keys), 1)
    back = column // tokens
    query_index = at_ref[0] * tokens + row
    key_index = (at_ref[0] - back) * tokens + (column - back * tokens)
    allowed = (key_index <= query_index) & (key_index >= query_index - position_ref[...])
    bias_ref[...] = jnp.where(allowed, 0.0, masked_score)


def join_keys(refs, key_ref, value_ref):
    @pl.when(pl.program_id(0) % GROUP == 0)
    def _():
        for place in range(len(refs)):
            tokens = refs[0].shape[0]
            if (place + 1) * tokens > key_ref.shape[0]:
                break
            rows = slice(place * tokens, (place + 1) * tokens)
            key_ref[rows] = refs[2 * place][...]
            value_ref[rows] = refs[2 * place + 1][...]


def key_specs(both_pieces):
    specs = []
    for piece in both_pieces:
        shape = (piece.shape[0], HEAD_SIZE)
        specs.append(pl.BlockSpec(shape, lambda head, at: (0, head // GROUP)))
        specs.append(pl.BlockSpec(shape, lambda head, at: (0, KEY_VALUE_HEADS + head // GROUP)))
    return specs


def attend(at, position, projected, both_pieces):
    tokens = projected.shape[0]
    count = len(both_pieces)
    keys = count * tokens

    def kernel(at_ref, position_ref, query_ref, *refs):
        out_ref, turn_ref, log_ref, bias_ref, key_ref, value_ref = refs[2 * count :]

        @pl.when(pl.program_id(0) == 0)
        def _():
            fill_bias(at_ref, position_ref, bias_ref)

        join_keys(refs, key_ref, value_ref)

        scores = dot_right_t(query_ref[...], key_ref[...]) * score_scale + bias_ref[...]
        top = jnp.max(scores, axis=1, keepdims=True)
        raised = jnp.exp(scores - top)
        total = jnp.sum(raised, axis=1, keepdims=True)
        probs = (raised * (1.0 / total)).astype(jnp.bfloat16)
        result = dot_f32(probs, value_ref[...])
        out_ref[...] = result.astype(jnp.bfloat16)
        turn_ref[...] = result.T.astype(jnp.bfloat16)
        log_ref[0] = top + jnp.log(total)

    return pl.pallas_call(
        kernel,
        grid_spec=pltpu.PrefetchScalarGridSpec(
            num_scalar_prefetch=1,
            grid=(QUERY_HEADS,),
            in_specs=[
                pl.BlockSpec((tokens, 1), lambda head, at: (0, 0)),
                pl.BlockSpec((tokens, HEAD_SIZE), lambda head, at: (0, head)),
            ]
            + key_specs(both_pieces),
            out_specs=[
                pl.BlockSpec((tokens, HEAD_SIZE), lambda head, at: (0, head)),
                pl.BlockSpec((HEAD_SIZE, tokens), lambda head, at: (head, 0)),
                pl.BlockSpec((1, tokens, 1), lambda head, at: (head, 0, 0)),
            ],
            scratch_shapes=[
                pltpu.VMEM((tokens, keys), jnp.float32),
                pltpu.VMEM((keys, HEAD_SIZE), jnp.bfloat16),
                pltpu.VMEM((keys, HEAD_SIZE), jnp.bfloat16),
            ],
        ),
        out_shape=[
            jax.ShapeDtypeStruct((tokens, QD), jnp.bfloat16),
            jax.ShapeDtypeStruct((QD, tokens), jnp.bfloat16),
            jax.ShapeDtypeStruct((QUERY_HEADS, tokens, 1), jnp.float32),
        ],
        compiler_params=vmem_params,
        cost_estimate=pl.CostEstimate(
            flops=8 * tokens * keys * QD,
            bytes_accessed=8 * tokens * QD,
            transcendentals=QUERY_HEADS * tokens * keys,
        ),
    )(at, position, projected, *[piece for piece in both_pieces for unused in range(2)])


def attend_backward(at, position, projected, both_pieces, incoming, log_total, cosine, sine):
    tokens = projected.shape[0]
    count = len(both_pieces)
    keys = count * tokens

    def kernel(
        at_ref,
        position_ref,
        query_ref,
        incoming_ref,
        log_ref,
        cosine_ref,
        sine_ref,
        *refs,
    ):
        query_grad_ref, key_grad_ref, value_grad_ref = refs[2 * count : 2 * count + 3]
        bias_ref, key_total, value_total, key_ref, value_ref = refs[2 * count + 3 :]
        head = pl.program_id(0)
        join_keys(refs, key_ref, value_ref)

        @pl.when(head == 0)
        def _():
            fill_bias(at_ref, position_ref, bias_ref)

        @pl.when(head % GROUP == 0)
        def _():
            key_total[...] = jnp.zeros_like(key_total)
            value_total[...] = jnp.zeros_like(value_total)

        scores = dot_right_t(query_ref[...], key_ref[...]) * score_scale + bias_ref[...]
        probs = jnp.exp(scores - log_ref[0])
        grad_probs = dot_right_t(incoming_ref[...], value_ref[...])
        inner = jnp.sum(grad_probs * probs, axis=1, keepdims=True)
        grad_scores = (probs * (grad_probs - inner)).astype(jnp.bfloat16)
        value_total[...] += dot_left_t(incoming_ref[...], probs.astype(jnp.bfloat16))
        key_total[...] += dot_left_t(query_ref[...], grad_scores)
        plain = dot_f32(grad_scores, key_ref[...]) * score_scale
        query_grad_ref[...] = (
            plain * cosine_ref[...] - pltpu.roll(plain, HEAD_SIZE // 2, 1) * sine_ref[...]
        ).astype(jnp.bfloat16)

        @pl.when(head % GROUP == GROUP - 1)
        def _():
            key_grad_ref[...] = (key_total[...] * score_scale).T
            value_grad_ref[...] = value_total[...].T

    return pl.pallas_call(
        kernel,
        grid_spec=pltpu.PrefetchScalarGridSpec(
            num_scalar_prefetch=1,
            grid=(QUERY_HEADS,),
            in_specs=[
                pl.BlockSpec((tokens, 1), lambda head, at: (0, 0)),
                pl.BlockSpec((tokens, HEAD_SIZE), lambda head, at: (0, head)),
                pl.BlockSpec((tokens, HEAD_SIZE), lambda head, at: (0, head)),
                pl.BlockSpec((1, tokens, 1), lambda head, at: (head, 0, 0)),
                pl.BlockSpec((tokens, HEAD_SIZE), lambda head, at: (0, 0)),
                pl.BlockSpec((tokens, HEAD_SIZE), lambda head, at: (0, 0)),
            ]
            + key_specs(both_pieces),
            out_specs=[
                pl.BlockSpec((tokens, HEAD_SIZE), lambda head, at: (0, head)),
                pl.BlockSpec((keys, HEAD_SIZE), lambda head, at: (0, head // GROUP)),
                pl.BlockSpec((keys, HEAD_SIZE), lambda head, at: (0, head // GROUP)),
            ],
            scratch_shapes=[
                pltpu.VMEM((tokens, keys), jnp.float32),
                pltpu.VMEM((HEAD_SIZE, keys), jnp.float32),
                pltpu.VMEM((HEAD_SIZE, keys), jnp.float32),
                pltpu.VMEM((keys, HEAD_SIZE), jnp.bfloat16),
                pltpu.VMEM((keys, HEAD_SIZE), jnp.bfloat16),
            ],
        ),
        out_shape=[
            jax.ShapeDtypeStruct((tokens, QD), jnp.bfloat16),
            jax.ShapeDtypeStruct((keys, KD), jnp.float32),
            jax.ShapeDtypeStruct((keys, KD), jnp.float32),
        ],
        compiler_params=vmem_params,
        cost_estimate=pl.CostEstimate(
            flops=20 * tokens * keys * QD,
            bytes_accessed=8 * tokens * QD,
            transcendentals=QUERY_HEADS * tokens * keys,
        ),
    )(
        at,
        position,
        projected,
        incoming,
        log_total,
        cosine,
        sine,
        *[piece for piece in both_pieces for unused in range(2)],
    )


def unit_part(me, normed_all, grad_out_all, gate_up, down, count, first):
    tokens = normed_all.shape[0]
    block = tokens // count
    width = down.shape[0]
    shard = D // count
    weights = list(gate_up) if first else [gate_up]

    def kernel(me_ref, normed_ref, out_grad_ref, down_ref, *refs):
        weight_refs = refs[: len(weights)]
        hidden_ref, grad_ref = refs[len(weights) : len(weights) + 2]
        weight_ref = weight_refs[0]
        if first:
            ordered_ref, weight_ref = refs[len(weights) + 2 :]
            ordered_ref[...] = out_grad_ref[...]

            @pl.when(pl.program_id(0) == 0)
            def _():
                for mask, ref in enumerate(weight_refs):
                    begin = pl.multiple_of((me_ref[0] ^ mask) * shard, shard)
                    weight_ref[pl.ds(begin, shard)] = ref[...]

        values = dot_f32(normed_ref[...], weight_ref[...])
        gate = values[:, :width]
        up = values[:, width:]
        grad_hidden = dot_right_t(out_grad_ref[...], down_ref[...])
        share = 1.0 / (1.0 + jnp.exp(-gate))
        passed = gate * share
        hidden_ref[...] = (passed * up).astype(jnp.bfloat16)
        grad_ref[:, :width] = (
            grad_hidden * up * share * (1.0 + gate * (1.0 - share))
        ).astype(jnp.bfloat16)
        grad_ref[:, width:] = (grad_hidden * passed).astype(jnp.bfloat16)

    def out_grad_index(step, me_ref):
        return (me_ref[0] ^ mask_at(step, count), 0) if first else (step, 0)

    row = lambda step, me_ref: (step, 0)
    fixed = lambda step, me_ref: (0, 0)
    out_specs = [pl.BlockSpec((block, width), row), pl.BlockSpec((block, 2 * width), row)]
    out_shape = [
        jax.ShapeDtypeStruct((tokens, width), jnp.bfloat16),
        jax.ShapeDtypeStruct((tokens, 2 * width), jnp.bfloat16),
    ]
    if first:
        out_specs += [pl.BlockSpec((block, D), row), pl.BlockSpec((D, 2 * width), fixed)]
        out_shape += [
            jax.ShapeDtypeStruct((tokens, D), jnp.bfloat16),
            jax.ShapeDtypeStruct((D, 2 * width), jnp.bfloat16),
        ]
    return pl.pallas_call(
        kernel,
        grid_spec=pltpu.PrefetchScalarGridSpec(
            num_scalar_prefetch=1,
            grid=(count,),
            in_specs=[
                pl.BlockSpec((block, D), row),
                pl.BlockSpec((block, D), out_grad_index),
                pl.BlockSpec((width, D), fixed),
            ]
            + [pl.BlockSpec(weight.shape, fixed) for weight in weights],
            out_specs=out_specs,
        ),
        out_shape=out_shape,
        compiler_params=vmem_params,
        cost_estimate=pl.CostEstimate(
            flops=6 * tokens * D * width,
            bytes_accessed=4 * tokens * D + 6 * tokens * width + 6 * D * width,
            transcendentals=tokens * width,
        ),
    )(me, normed_all, grad_out_all, down, *weights)


def down_products(me, hidden_first, hidden_second, down_first, down_second, count):
    block = hidden_first.shape[0] // count

    def kernel(me_ref, first_ref, second_ref, down_first_ref, down_second_ref, out_ref):
        out_ref[...] = (
            dot_f32(first_ref[...], down_first_ref[...])
            + dot_f32(second_ref[...], down_second_ref[...])
        ).astype(jnp.bfloat16)

    row = lambda step, me_ref: (place_of(me_ref[0] ^ step, count), 0)
    fixed = lambda step, me_ref: (0, 0)
    return pl.pallas_call(
        kernel,
        grid_spec=pltpu.PrefetchScalarGridSpec(
            num_scalar_prefetch=1,
            grid=(count,),
            in_specs=[
                pl.BlockSpec((block, hidden_first.shape[1]), row),
                pl.BlockSpec((block, hidden_second.shape[1]), row),
                pl.BlockSpec(down_first.shape, fixed),
                pl.BlockSpec(down_second.shape, fixed),
            ],
            out_specs=pl.BlockSpec((block, D), lambda step, me_ref: (step, 0)),
        ),
        out_shape=jax.ShapeDtypeStruct((block * count, D), jnp.bfloat16),
        compiler_params=vmem_params,
        cost_estimate=pl.CostEstimate(
            flops=2 * block * count * D * (down_first.shape[0] + down_second.shape[0]),
            bytes_accessed=4 * block * count * D,
            transcendentals=0,
        ),
    )(me, hidden_first, hidden_second, down_first, down_second)


def projection_terms(me, normed_turned, attended_turned, grad_projected, grad_middle, rows_out):
    count, shard, tokens = normed_turned.shape
    in_width = grad_projected.shape[1]
    out_width = grad_middle.shape[1]
    in_lanes, out_lanes = in_width // 128, out_width // 128

    def kernel(me_ref, normed_ref, attended_ref, projected_ref, middle_ref, out_ref, bias_ref):
        @pl.when(pl.program_id(0) == 0)
        def _():
            bias = jnp.sum(projected_ref[...].astype(jnp.float32), axis=0, keepdims=True)
            bias_ref[...] = jnp.zeros_like(bias_ref)
            for group in range(in_lanes):
                bias_ref[group : group + 1] = bias[:, group * 128 : (group + 1) * 128]

        place = 0
        for turned_ref, right_ref, lanes in (
            (normed_ref, projected_ref, in_lanes),
            (attended_ref, middle_ref, out_lanes),
        ):
            term = dot_f32(turned_ref[0], right_ref[...]).astype(jnp.bfloat16)
            for group in range(lanes):
                out_ref[0, place : place + shard] = term[:, group * 128 : (group + 1) * 128]
                place += shard
        out_ref[0, place:] = bias_ref[...].astype(jnp.bfloat16)

    def turned_index(step, me_ref):
        return (me_ref[0] ^ mask_at(step, count), 0, 0)

    fixed = lambda step, me_ref: (0, 0)
    return pl.pallas_call(
        kernel,
        grid_spec=pltpu.PrefetchScalarGridSpec(
            num_scalar_prefetch=1,
            grid=(count,),
            in_specs=[
                pl.BlockSpec((1, shard, tokens), turned_index),
                pl.BlockSpec((1, shard, tokens), turned_index),
                pl.BlockSpec((tokens, in_width), fixed),
                pl.BlockSpec((tokens, out_width), fixed),
            ],
            out_specs=pl.BlockSpec((1, rows_out, 128), lambda step, me_ref: (step, 0, 0)),
            scratch_shapes=[
                pltpu.VMEM((rows_out - shard * (in_lanes + out_lanes), 128), jnp.float32)
            ],
        ),
        out_shape=jax.ShapeDtypeStruct((count, rows_out, 128), jnp.bfloat16),
        compiler_params=vmem_params,
        cost_estimate=pl.CostEstimate(
            flops=2 * D * tokens * (in_width + out_width),
            bytes_accessed=256 * count * rows_out,
            transcendentals=0,
        ),
    )(me, normed_turned, attended_turned, grad_projected, grad_middle)


def shards(
    tokens,
    positions,
    cotangent,
    attn_norm,
    ffn_norm,
    in_proj,
    in_bias,
    out_proj,
    gate_up,
    down_proj,
):
    token_rows = tokens.shape[1]
    fsdp_count = lax.axis_size("fsdp")
    ctx_count = lax.axis_size("ctx")
    fsdp_me = lax.axis_index("fsdp")
    me = fsdp_me.astype(jnp.int32)[None]
    at = lax.axis_index("ctx").astype(jnp.int32)[None]
    units = FF // fsdp_count
    shard_d = D // fsdp_count
    residual_in = tokens[0].astype(jnp.float32)
    position = positions[0]
    grad_out_b = cotangent[0]

    first_units, second_units, padded_units = unit_widths(units)
    vectors = gather_small(jnp.concatenate([attn_norm, ffn_norm, in_bias]))
    first_blocks, second_blocks = split_units(me, gate_up, fsdp_count)
    attn_scale = vectors[:, :shard_d].reshape(D)
    ffn_scale = vectors[:, shard_d : 2 * shard_d].reshape(D)
    bias_full = vectors[:, 2 * shard_d :].reshape(-1)
    cosine, sine = rotary_tables(position)
    in_pieces = gather_pieces(in_proj, first_blocks, cosine)
    normed_b = rms_scale(residual_in, attn_scale).astype(jnp.bfloat16)
    normed_blocks = normed_b.reshape(token_rows, fsdp_count, shard_d).transpose(1, 0, 2)
    gated_blocks = after(first_blocks, in_pieces[0], in_pieces[2], in_pieces[4])
    gate_up_first = [gated_blocks[0]] + [
        exchange(gated_blocks[mask], mask) for mask in range(1, fsdp_count)
    ]
    out_full = lax.all_gather(after(out_proj, in_pieces), "fsdp", axis=0, tiled=True)

    projected = project(me, normed_blocks, in_pieces, bias_full, cosine, sine)
    both_b = projected[:, QD:]
    both_pieces = [both_b] + [
        lax.ppermute(both_b, "ctx", [(s, s + back) for s in range(ctx_count - back)])
        for back in range(1, ctx_count)
    ]
    normed_again, down_again = after((normed_b, down_proj), projected)
    normed_turned = normed_again.T.reshape(fsdp_count, shard_d, token_rows)
    down_first = down_again[:first_units]
    down_second = jnp.pad(down_again[first_units:], ((0, padded_units - second_units), (0, 0)))
    both_pieces = after(both_pieces, normed_turned, down_first, down_second)
    grad_out_all = lax.all_gather(
        after(grad_out_b, out_full, both_pieces), "fsdp", axis=0, tiled=True
    )
    attended_b, attended_turned, log_total = attend(at, position[:, None], projected, both_pieces)
    middle = residual_in + dot_f32(after(attended_b, gate_up_first), out_full)
    normed_ffn_b = rms_scale(middle, ffn_scale).astype(jnp.bfloat16)

    normed_ffn_all = gather_masks(normed_ffn_b)
    gate_up_second = swap_blocks(after(second_blocks, normed_ffn_all)).reshape(
        D, 2 * padded_units
    )
    hidden_first, grad_first, grad_out_all, gate_up_first = unit_part(
        me, normed_ffn_all, grad_out_all, gate_up_first, down_first, fsdp_count, True
    )
    odd_rows = normed_ffn_all.shape[0] // 2

    def down_term(hidden, *gates):
        return dot_left_t(after(hidden, *gates), grad_out_all).astype(jnp.bfloat16)

    def gate_term(grad, *gates):
        term = dot_left_t(normed_ffn_all, after(grad, *gates)).astype(jnp.bfloat16)
        return term, swap_blocks(term.reshape(fsdp_count, shard_d, -1))

    def input_grads(rows, *gates):
        return (
            (
                dot_right_t(after(grad_first, *gates)[rows], gate_up_first)
                + dot_right_t(grad_second[rows], gate_up_second)
            )
            .astype(jnp.bfloat16)
            .reshape(fsdp_count // 2, token_rows, D)
        )

    gate_term_a, gate_swapped_a = gate_term(grad_first, hidden_first)
    down_term_a = down_term(hidden_first, gate_term_a)
    stream_a = Stream(at, down_term_a.size // 128 // halves, 3 * halves)
    sources_a = unit_sources(down_term_a, gate_swapped_a, halves)
    sent = stream_a.tick(sources_a)
    hidden_second, grad_second = unit_part(
        me,
        after(normed_ffn_all, sent),
        grad_out_all,
        gate_up_second,
        down_second,
        fsdp_count,
        False,
    )
    sent = stream_a.tick(sources_a, hidden_second)
    grad_normed_odd = input_grads(slice(0, odd_rows), sent)
    normed_sum = MaskSum(grad_normed_odd)
    sent = stream_a.tick(sources_a, grad_normed_odd)
    grad_normed_even = input_grads(slice(odd_rows, None), sent)
    sent = stream_a.tick(sources_a, grad_normed_even)
    sent = normed_sum.second(grad_normed_even, sent)
    gate_term_b, gate_swapped_b = gate_term(grad_second, sent)
    sent = stream_a.tick(sources_a, gate_term_b)
    down_term_b = down_term(hidden_second, sent)
    stream_b = Stream(at, down_term_b.size // 128 // halves, 3 * halves)
    sources_b = unit_sources(down_term_b, gate_swapped_b, halves)
    sent = normed_sum.third(down_term_b)
    sent = stream_a.tick(sources_a, sent)
    sent = stream_b.tick(sources_b, sent) if halves == 1 else sent
    down_out = down_products(
        me, after(hidden_first, sent), hidden_second, down_first, down_second, fsdp_count
    )
    grad_normed_ffn = normed_sum.result(down_out).astype(jnp.float32)
    down_sum = lax.psum_scatter(
        after(down_out, grad_normed_ffn), "fsdp", scatter_dimension=0, tiled=True
    )

    grad_out = grad_out_b.astype(jnp.float32)
    grad_middle = grad_out + norm_backward(middle, ffn_scale, grad_normed_ffn)
    grad_middle_b = grad_middle.astype(jnp.bfloat16)
    grad_attended_b = dot_right_t(grad_middle_b, out_full).astype(jnp.bfloat16)
    sent = stream_a.tick(sources_a, grad_attended_b)
    sent = stream_b.tick(sources_b, sent)
    query_grad, key_grads, value_grads = attend_backward(
        at,
        position[:, None],
        projected,
        both_pieces,
        after(grad_attended_b, sent),
        log_total,
        cosine,
        sine,
    )
    both_sent = [
        lax.ppermute(
            jnp.concatenate(
                [
                    grads[back * token_rows : (back + 1) * token_rows].astype(jnp.bfloat16)
                    for grads in (key_grads, value_grads)
                ],
                axis=1,
            ),
            "ctx",
            [(s + back, s) for s in range(ctx_count - back)],
        )
        for back in range(1, ctx_count)
    ]
    sent = stream_a.tick(sources_a, query_grad)
    sent = stream_b.tick(sources_b, sent)
    both_grad = jnp.concatenate([key_grads[:token_rows], value_grads[:token_rows]], axis=1)
    for piece in after(both_sent, sent):
        both_grad = both_grad + piece.astype(jnp.float32)
    turned_back = []
    for head in range(KEY_VALUE_HEADS):
        plain = both_grad[:, head * HEAD_SIZE : (head + 1) * HEAD_SIZE]
        turned_back.append(plain * cosine - jnp.roll(plain, HEAD_SIZE // 2, axis=1) * sine)
    grad_projected_b = jnp.concatenate(
        [query_grad]
        + [part.astype(jnp.bfloat16) for part in turned_back]
        + [both_grad[:, KD:].astype(jnp.bfloat16)],
        axis=1,
    )
    in_rows = shard_d * in_proj.shape[1] // 128
    out_rows = shard_d * D // 128
    terms = projection_terms(
        me,
        normed_turned,
        attended_turned.reshape(fsdp_count, shard_d, token_rows),
        grad_projected_b,
        grad_middle_b,
        in_rows + out_rows + 32,
    )
    half = fsdp_count // 2
    terms_sum = MaskSum(terms[:half])
    sent = stream_a.tick(sources_a, terms)
    sent = stream_b.tick(sources_b, sent)
    sent = terms_sum.second(terms[half:], sent)
    grad_normed = project_back(me, after(grad_projected_b, sent), in_pieces, shard_d)
    grad_normed = grad_normed.transpose(1, 0, 2).reshape(token_rows, D)
    tokens_grad = grad_middle + norm_backward(residual_in, attn_scale, grad_normed)
    sent = stream_b.tick(sources_b, tokens_grad)
    sent = terms_sum.third(sent)
    down_grad_parts = stream_a.finish(sources_a, sent)
    sent = stream_b.tick(sources_b, down_grad_parts)
    terms_total = jnp.concatenate(
        [terms_sum.result(sent), jnp.zeros((in_rows - out_rows - 32, 128), jnp.bfloat16)], axis=0
    )
    stream_c = Stream(at, in_rows, 2)
    sources_c = [
        (
            terms_total,
            0,
            2,
            (in_rows // Stream.steps, 128),
            lambda chunk, step: (Stream.steps * chunk + step, 0),
            load_lanes,
        )
    ]
    sent = stream_c.tick(sources_c)
    sent = stream_b.tick(sources_b, sent)
    sent = stream_c.tick(sources_c, sent)
    sent = stream_b.tick(sources_b, sent)
    block_out = middle + after(down_sum, sent).astype(jnp.float32)
    sent = stream_c.tick(sources_c, block_out)
    totals_b = stream_b.finish(sources_b, sent)
    totals_a = stream_a.totals
    down_grad = join_down(
        totals_a, totals_b, first_units, second_units, padded_units, halves
    )
    sent = stream_c.tick(sources_c, down_grad)
    gate_grad, gate_sums = join_units(
        totals_a, after(totals_b, sent), gate_up, halves, fsdp_count
    )
    ffn_grad = gate_sums / ffn_norm
    totals_c = stream_c.finish(sources_c, gate_grad).astype(jnp.float32)

    def lanes_back(rows):
        return rows.reshape(-1, shard_d, 128).transpose(1, 0, 2).reshape(shard_d, -1)

    in_grad = lanes_back(totals_c[0])
    out_grad = lanes_back(totals_c[1, :out_rows])
    bias_span = in_bias.shape[0]
    bias_grad = lax.dynamic_slice_in_dim(
        totals_c[1, out_rows : out_rows + in_proj.shape[1] // 128].reshape(-1),
        fsdp_me * bias_span,
        bias_span,
    )
    attn_grad = jnp.sum(in_grad * in_proj.astype(jnp.float32), axis=1) / attn_norm
    return (
        block_out.astype(jnp.bfloat16).reshape(1, token_rows, D),
        tokens_grad.reshape(1, token_rows, D),
        attn_grad,
        ffn_grad,
        in_grad,
        bias_grad,
        out_grad,
        gate_grad,
        down_grad,
    )


def solution(mesh):
    in_specs = (
        P("fsdp", "ctx", None),
        P("fsdp", "ctx"),
        P("fsdp", "ctx", None),
        P("fsdp"),
        P("fsdp"),
        P("fsdp", None),
        P("fsdp"),
        P("fsdp", None),
        P("fsdp", None),
        P("fsdp", None),
    )
    out_specs = (
        P("fsdp", "ctx", None),
        P("fsdp", "ctx", None),
        P("fsdp"),
        P("fsdp"),
        P("fsdp", None),
        P("fsdp"),
        P("fsdp", None),
        P("fsdp", None),
        P("fsdp", None),
    )
    return jax.shard_map(shards, mesh=mesh, in_specs=in_specs, out_specs=out_specs, check_vma=False)
```

```python
import jax
import jax.numpy as jnp
from jax import lax
from jax.experimental import pallas as pl
from jax.experimental.pallas import tpu as pltpu
from jax.sharding import PartitionSpec as P

D = 1536
QUERY_HEADS = 12
KEY_VALUE_HEADS = 2
HEAD_SIZE = 128
FF = 8960
QD = QUERY_HEADS * HEAD_SIZE
KD = KEY_VALUE_HEADS * HEAD_SIZE
GROUP = QUERY_HEADS // KEY_VALUE_HEADS


norm_eps = 1e-06
rope_base = 1000000.0
masked_score = -1e30
score_scale = HEAD_SIZE ** (-0.5)
vmem_params = pltpu.CompilerParams(vmem_limit_bytes=48 * 1024 * 1024)


def rms_scale(value_rows):
    return value_rows * lax.rsqrt(
        jnp.mean(value_rows * value_rows, axis=-1, keepdims=True) + norm_eps
    )


def norm_backward(value_rows, incoming):
    unused_out, pullback = jax.vjp(rms_scale, value_rows)
    return pullback(incoming)[0]


def rotary_tables(position):
    lane = jnp.arange(HEAD_SIZE, dtype=jnp.int32)
    half = HEAD_SIZE // 2
    frequencies = rope_base ** (-((lane % half).astype(jnp.float32) * (2.0 / HEAD_SIZE)))
    angles = position.astype(jnp.float32)[:, None] * frequencies[None, :]
    sign = jnp.where(lane < half, -1.0, 1.0)
    return jnp.cos(angles), jnp.sin(angles) * sign[None, :]


def dot_f32(left, right):
    return jnp.dot(left, right, preferred_element_type=jnp.float32)


def dot_right_t(left, right):
    return lax.dot_general(
        left, right, (((1,), (1,)), ((), ())), preferred_element_type=jnp.float32
    )


def dot_left_t(left, right):
    return lax.dot_general(
        left, right, (((0,), (0,)), ((), ())), preferred_element_type=jnp.float32
    )


def add_low(left, right):
    return left + right


def after(value, *earlier):
    return lax.optimization_barrier((value, earlier))[0]


def exchange(value, mask):
    count = lax.axis_size("fsdp")
    return lax.ppermute(value, "fsdp", [(place, place ^ mask) for place in range(count)])


def gather_pieces(block, *gates):
    count = lax.axis_size("fsdp")
    if count != 8:
        found = [[block]] + [[exchange(block, mask)] for mask in range(2, count, 2)]
    else:
        half = block.shape[0] // 2
        by_x = exchange(block, 2)
        by_y = exchange(block, 4)
        other = exchange(block, 1)
        by_x, by_y = after((by_x, by_y), *gates)
        top = exchange(by_x[:half], 4)
        bottom = exchange(by_y[half:], 2)
        found = [[block], [by_x], [by_y], [top, bottom]]
        others = [[other], [exchange(by_x, 1)], [exchange(by_y, 1)]]
        others.append([exchange(top, 1), exchange(bottom, 1)])
        return [(2 * place, rows) for place, rows in enumerate(found)] + [
            (2 * place + 1, rows) for place, rows in enumerate(others)
        ]
    pieces = []
    for place, rows in enumerate(found):
        pieces.append((2 * place, rows))
        pieces.append((2 * place + 1, [exchange(part, 1) for part in rows]))
    return pieces


def gather_masks(block, *gates):
    count = lax.axis_size("fsdp")
    rows = block.shape[0]
    whole = jnp.zeros((count * rows, block.shape[1]), block.dtype)
    for mask, parts in gather_pieces(block, *gates):
        first = place_of(mask, count) * rows
        for part in parts:
            whole = lax.dynamic_update_slice(whole, part, (first, 0))
            first += part.shape[0]
    return whole


def gather_small(value):
    count = lax.axis_size("fsdp")
    me = lax.axis_index("fsdp")
    bits = count.bit_length() - 1
    found = value
    for bit in list(range(1, bits)) + [0]:
        got = exchange(found, 1 << bit)
        low = (me >> bit) % 2 == 0
        found = jnp.stack([jnp.where(low, found, got), jnp.where(low, got, found)])
    return jnp.moveaxis(found, 0, bits - 1).reshape(count, -1)


def place_of(mask, count):
    return mask // 2 + (1 - mask % 2) * (count // 2)


def mask_at(place, count):
    return jnp.where(place < count // 2, 2 * place + 1, 2 * place - count)


class MaskSum:
    def __init__(self, odd):
        self.got = exchange(odd, 1)

    def second(self, even, *gates):
        count = lax.axis_size("fsdp")
        self.kept = add_low(even, after(self.got, *gates))
        if count == 8:
            half = self.kept.shape[1] // 2
            self.by_x = exchange(self.kept[1::2, :half], 2)
            self.by_y = exchange(self.kept[2:, half:], 4)
        else:
            span = count
            while self.kept.shape[0] > 1:
                span //= 2
                half = self.kept.shape[0] // 2
                self.kept = add_low(self.kept[:half], exchange(self.kept[half:], span))
        return self.kept

    def third(self, *gates):
        if lax.axis_size("fsdp") != 8:
            return self.kept
        half = self.kept.shape[1] // 2
        by_x, by_y = after((self.by_x, self.by_y), *gates)
        self.top = add_low(self.kept[0::2, :half], by_x)
        self.bottom = add_low(self.kept[:2, half:], by_y)
        self.last_y = exchange(self.top[1], 4)
        self.last_x = exchange(self.bottom[1], 2)
        return self.top, self.bottom

    def result(self, *gates):
        if lax.axis_size("fsdp") != 8:
            return self.kept[0]
        last_y, last_x = after((self.last_y, self.last_x), *gates)
        return jnp.concatenate(
            [add_low(self.top[0], last_y), add_low(self.bottom[0], last_x)], axis=0
        )


def swap_blocks(blocks):
    return lax.all_to_all(blocks, "fsdp", 0, 0, tiled=True)


def ctx_scatter(terms):
    return lax.psum_scatter(terms, "ctx", scatter_dimension=0, tiled=True)


class CtxGather:
    def __init__(self, block, *gates):
        self.block = block
        self.from_left, self.from_right = [], []
        self.hop(*gates)

    def hop(self, *gates):
        count = lax.axis_size("ctx")
        if len(self.from_left) < count - 1:
            left = self.from_left[-1] if self.from_left else self.block
            right = self.from_right[-1] if self.from_right else self.block
            left, right = after((left, right), *gates)
            self.from_left.append(lax.ppermute(left, "ctx", [(s, s + 1) for s in range(count - 1)]))
            self.from_right.append(
                lax.ppermute(right, "ctx", [(s + 1, s) for s in range(count - 1)])
            )

    def result(self, *gates):
        count = lax.axis_size("ctx")
        me = lax.axis_index("ctx")
        while len(self.from_left) < count - 1:
            self.hop(*gates)
        shape = self.block.shape
        whole = jnp.zeros((count,) + shape, self.block.dtype)
        rest = (0,) * len(shape)
        whole = lax.dynamic_update_slice(whole, self.block[None], (me,) + rest)
        for back in range(1, count):
            piece = jnp.where(
                me >= back, self.from_left[back - 1], self.from_right[count - back - 1]
            )
            whole = lax.dynamic_update_slice(whole, piece[None], ((me - back) % count,) + rest)
        return whole


def unit_widths(units):
    first = units // 256 * 128
    second = units - first
    return first, second, -(-second // 128) * 128


def split_units(me, gate_up, gain, count):
    rows, columns = gate_up.shape
    span = columns // 2
    units = span // count
    first, second, padded = unit_widths(units)
    block = 48

    def kernel(me_ref, weight_ref, gain_ref, first_ref, second_ref):
        def scaled(begin, end):
            value = weight_ref[:, begin:end].astype(jnp.float32) * gain_ref[...]
            return value.astype(gate_up.dtype)

        for owner in range(count):
            for side in range(2):
                begin = side * span + owner * units
                first_ref[me_ref[0] ^ owner, :, side * first : (side + 1) * first] = scaled(
                    begin, begin + first
                )
                second_ref[owner, :, side * padded : side * padded + second] = scaled(
                    begin + first, begin + units
                )
                if padded > second:
                    second_ref[
                        owner, :, side * padded + second : (side + 1) * padded
                    ] = jnp.zeros((block, padded - second), gate_up.dtype)

    return pl.pallas_call(
        kernel,
        grid_spec=pltpu.PrefetchScalarGridSpec(
            num_scalar_prefetch=1,
            grid=(rows // block,),
            in_specs=[
                pl.BlockSpec((block, columns), lambda step, me_ref: (step, 0)),
                pl.BlockSpec((block, 1), lambda step, me_ref: (step, 0)),
            ],
            out_specs=[
                pl.BlockSpec((count, block, 2 * first), lambda step, me_ref: (0, step, 0)),
                pl.BlockSpec((count, block, 2 * padded), lambda step, me_ref: (0, step, 0)),
            ],
        ),
        out_shape=[
            jax.ShapeDtypeStruct((count, rows, 2 * first), gate_up.dtype),
            jax.ShapeDtypeStruct((count, rows, 2 * padded), gate_up.dtype),
        ],
        compiler_params=vmem_params,
        cost_estimate=pl.CostEstimate(
            flops=0, bytes_accessed=4 * rows * columns, transcendentals=0
        ),
    )(me, gate_up, gain[:, None])


def join_units(first_part, second_part, gate_up, gain):
    rows, columns = gate_up.shape
    if first_part.shape[2] % 16:
        first_part, second_part = (
            part.transpose(1, 0, 2, 3)
            .reshape(part.shape[1], rows // 48, 48, -1)
            .transpose(1, 0, 2, 3)
            for part in (first_part, second_part)
        )
    pieces, count, block = first_part.shape[:3]
    span = columns // 2
    units = span // count
    first, second, padded = unit_widths(units)

    def kernel(first_ref, second_ref, weight_ref, gain_ref, whole_ref, sums_ref):
        for owner in range(count):
            for side in range(2):
                begin = side * span + owner * units
                whole_ref[:, begin : begin + first] = first_ref[
                    0, owner, :, side * first : (side + 1) * first
                ].astype(jnp.float32)
                whole_ref[:, begin + first : begin + units] = second_ref[
                    0, owner, :, side * padded : side * padded + second
                ].astype(jnp.float32)
        whole = whole_ref[...]
        total = jnp.sum(whole * weight_ref[...].astype(jnp.float32), axis=1, keepdims=True)
        sums_ref[...] = jnp.broadcast_to(total, (block, 128))
        whole_ref[...] = whole * gain_ref[...]

    whole, sums = pl.pallas_call(
        kernel,
        grid=(pieces,),
        in_specs=[
            pl.BlockSpec((1, count, block, 2 * first), lambda step: (step, 0, 0, 0)),
            pl.BlockSpec((1, count, block, 2 * padded), lambda step: (step, 0, 0, 0)),
            pl.BlockSpec((block, columns), lambda step: (step, 0)),
            pl.BlockSpec((block, 1), lambda step: (step, 0)),
        ],
        out_specs=[
            pl.BlockSpec((block, columns), lambda step: (step, 0)),
            pl.BlockSpec((block, 128), lambda step: (step, 0)),
        ],
        out_shape=[
            jax.ShapeDtypeStruct((rows, columns), jnp.float32),
            jax.ShapeDtypeStruct((rows, 128), jnp.float32),
        ],
        compiler_params=vmem_params,
        cost_estimate=pl.CostEstimate(
            flops=2 * rows * columns, bytes_accessed=8 * rows * columns, transcendentals=0
        ),
    )(first_part, second_part, gate_up, gain[:, None])
    return whole, sums[:, 0]


def place_rows(me_ref, pieces, refs, weight_ref):
    place = 0
    for mask, parts in pieces:
        shard = sum(part.shape[0] for part in parts)
        begin = (me_ref[0] ^ mask) * shard
        for part in parts:
            rows = part.shape[0]
            weight_ref[pl.ds(pl.multiple_of(begin, rows), rows)] = refs[place][...]
            begin = begin + rows
            place += 1


def project(me, normed, pieces, bias, cosine, sine):
    tokens = normed.shape[0]
    width = bias.shape[0]
    block = 512
    flat = [part for unused_mask, parts in pieces for part in parts]

    def kernel(me_ref, normed_ref, bias_ref, cosine_ref, sine_ref, *refs):
        out_ref, weight_ref = refs[len(flat) :]
        place_rows(me_ref, pieces, refs, weight_ref)
        product = dot_f32(normed_ref[...], weight_ref[...]) + bias_ref[...]
        for head in range(block // HEAD_SIZE):
            lanes = slice(head * HEAD_SIZE, (head + 1) * HEAD_SIZE)
            plain = product[:, lanes]
            turned = plain * cosine_ref[...] + pltpu.roll(plain, HEAD_SIZE // 2, 1) * sine_ref[...]
            column = pl.program_id(0) * block + head * HEAD_SIZE
            out_ref[:, lanes] = jnp.where(column < QD + KD, turned, plain).astype(jnp.bfloat16)

    return pl.pallas_call(
        kernel,
        grid_spec=pltpu.PrefetchScalarGridSpec(
            num_scalar_prefetch=1,
            grid=(width // block,),
            in_specs=[
                pl.BlockSpec((tokens, D), lambda step, me_ref: (0, 0)),
                pl.BlockSpec((1, block), lambda step, me_ref: (0, step)),
                pl.BlockSpec((tokens, HEAD_SIZE), lambda step, me_ref: (0, 0)),
                pl.BlockSpec((tokens, HEAD_SIZE), lambda step, me_ref: (0, 0)),
            ]
            + [
                pl.BlockSpec((part.shape[0], block), lambda step, me_ref: (0, step))
                for part in flat
            ],
            out_specs=pl.BlockSpec((tokens, block), lambda step, me_ref: (0, step)),
            scratch_shapes=[pltpu.VMEM((D, block), jnp.bfloat16)],
        ),
        out_shape=jax.ShapeDtypeStruct((tokens, width), jnp.bfloat16),
        compiler_params=vmem_params,
        cost_estimate=pl.CostEstimate(
            flops=2 * tokens * D * width, bytes_accessed=2 * D * width, transcendentals=0
        ),
    )(me, normed, bias[None], cosine, sine, *flat)


def project_back(me, grad_projected, pieces):
    tokens, width = grad_projected.shape
    flat = [part for unused_mask, parts in pieces for part in parts]

    def kernel(me_ref, grad_ref, *refs):
        out_ref, weight_ref = refs[len(flat) :]
        place_rows(me_ref, pieces, refs, weight_ref)
        out_ref[...] = dot_right_t(grad_ref[...], weight_ref[...])

    whole = lambda part: pl.BlockSpec(part.shape, lambda step, me_ref: (0, 0))
    return pl.pallas_call(
        kernel,
        grid_spec=pltpu.PrefetchScalarGridSpec(
            num_scalar_prefetch=1,
            grid=(1,),
            in_specs=[whole(grad_projected)] + [whole(part) for part in flat],
            out_specs=pl.BlockSpec((tokens, D), lambda step, me_ref: (0, 0)),
            scratch_shapes=[pltpu.VMEM((D, width), jnp.bfloat16)],
        ),
        out_shape=jax.ShapeDtypeStruct((tokens, D), jnp.float32),
        compiler_params=vmem_params,
        cost_estimate=pl.CostEstimate(
            flops=2 * tokens * D * width, bytes_accessed=2 * D * width, transcendentals=0
        ),
    )(me, grad_projected, *flat)


def fill_bias(at_ref, position_ref, bias_ref):
    tokens, keys = bias_ref.shape
    row = lax.broadcasted_iota(jnp.int32, (tokens, keys), 0)
    column = lax.broadcasted_iota(jnp.int32, (tokens, keys), 1)
    back = column // tokens
    query_index = at_ref[0] * tokens + row
    key_index = (at_ref[0] - back) * tokens + (column - back * tokens)
    allowed = (key_index <= query_index) & (key_index >= query_index - position_ref[...])
    bias_ref[...] = jnp.where(allowed, 0.0, masked_score)


def join_keys(refs, key_ref, value_ref):
    @pl.when(pl.program_id(0) % GROUP == 0)
    def _():
        for place in range(len(refs)):
            tokens = refs[0].shape[0]
            if (place + 1) * tokens > key_ref.shape[0]:
                break
            rows = slice(place * tokens, (place + 1) * tokens)
            key_ref[rows] = refs[2 * place][...]
            value_ref[rows] = refs[2 * place + 1][...]


def key_specs(both_pieces):
    specs = []
    for piece in both_pieces:
        shape = (piece.shape[0], HEAD_SIZE)
        specs.append(pl.BlockSpec(shape, lambda head, at: (0, head // GROUP)))
        specs.append(pl.BlockSpec(shape, lambda head, at: (0, KEY_VALUE_HEADS + head // GROUP)))
    return specs


def attend(at, position, projected, both_pieces):
    tokens = projected.shape[0]
    count = len(both_pieces)
    keys = count * tokens

    def kernel(at_ref, position_ref, query_ref, *refs):
        out_ref, turn_ref, log_ref, bias_ref, key_ref, value_ref = refs[2 * count :]

        @pl.when(pl.program_id(0) == 0)
        def _():
            fill_bias(at_ref, position_ref, bias_ref)

        join_keys(refs, key_ref, value_ref)

        scores = dot_right_t(query_ref[...], key_ref[...]) * score_scale + bias_ref[...]
        top = jnp.max(scores, axis=1, keepdims=True)
        raised = jnp.exp(scores - top)
        total = jnp.sum(raised, axis=1, keepdims=True)
        probs = (raised * (1.0 / total)).astype(jnp.bfloat16)
        result = dot_f32(probs, value_ref[...])
        out_ref[...] = result.astype(jnp.bfloat16)
        turn_ref[...] = result.T.astype(jnp.bfloat16)
        log_ref[0] = top + jnp.log(total)

    return pl.pallas_call(
        kernel,
        grid_spec=pltpu.PrefetchScalarGridSpec(
            num_scalar_prefetch=1,
            grid=(QUERY_HEADS,),
            in_specs=[
                pl.BlockSpec((tokens, 1), lambda head, at: (0, 0)),
                pl.BlockSpec((tokens, HEAD_SIZE), lambda head, at: (0, head)),
            ]
            + key_specs(both_pieces),
            out_specs=[
                pl.BlockSpec((tokens, HEAD_SIZE), lambda head, at: (0, head)),
                pl.BlockSpec((HEAD_SIZE, tokens), lambda head, at: (head, 0)),
                pl.BlockSpec((1, tokens, 1), lambda head, at: (head, 0, 0)),
            ],
            scratch_shapes=[
                pltpu.VMEM((tokens, keys), jnp.float32),
                pltpu.VMEM((keys, HEAD_SIZE), jnp.bfloat16),
                pltpu.VMEM((keys, HEAD_SIZE), jnp.bfloat16),
            ],
        ),
        out_shape=[
            jax.ShapeDtypeStruct((tokens, QD), jnp.bfloat16),
            jax.ShapeDtypeStruct((QD, tokens), jnp.bfloat16),
            jax.ShapeDtypeStruct((QUERY_HEADS, tokens, 1), jnp.float32),
        ],
        compiler_params=vmem_params,
        cost_estimate=pl.CostEstimate(
            flops=8 * tokens * keys * QD,
            bytes_accessed=8 * tokens * QD,
            transcendentals=QUERY_HEADS * tokens * keys,
        ),
    )(at, position, projected, *[piece for piece in both_pieces for unused in range(2)])


def attend_backward(at, position, projected, both_pieces, incoming, log_total, cosine, sine):
    tokens = projected.shape[0]
    count = len(both_pieces)
    keys = count * tokens

    def kernel(
        at_ref,
        position_ref,
        query_ref,
        incoming_ref,
        log_ref,
        cosine_ref,
        sine_ref,
        *refs,
    ):
        query_grad_ref, key_grad_ref, value_grad_ref = refs[2 * count : 2 * count + 3]
        bias_ref, key_total, value_total, key_ref, value_ref = refs[2 * count + 3 :]
        head = pl.program_id(0)
        join_keys(refs, key_ref, value_ref)

        @pl.when(head == 0)
        def _():
            fill_bias(at_ref, position_ref, bias_ref)

        @pl.when(head % GROUP == 0)
        def _():
            key_total[...] = jnp.zeros_like(key_total)
            value_total[...] = jnp.zeros_like(value_total)

        scores = dot_right_t(query_ref[...], key_ref[...]) * score_scale + bias_ref[...]
        probs = jnp.exp(scores - log_ref[0])
        grad_probs = dot_right_t(incoming_ref[...], value_ref[...])
        inner = jnp.sum(grad_probs * probs, axis=1, keepdims=True)
        grad_scores = (probs * (grad_probs - inner)).astype(jnp.bfloat16)
        value_total[...] += dot_left_t(incoming_ref[...], probs.astype(jnp.bfloat16))
        key_total[...] += dot_left_t(query_ref[...], grad_scores)
        plain = dot_f32(grad_scores, key_ref[...]) * score_scale
        query_grad_ref[...] = (
            plain * cosine_ref[...] - pltpu.roll(plain, HEAD_SIZE // 2, 1) * sine_ref[...]
        ).astype(jnp.bfloat16)

        @pl.when(head % GROUP == GROUP - 1)
        def _():
            key_grad_ref[...] = (key_total[...] * score_scale).T
            value_grad_ref[...] = value_total[...].T

    return pl.pallas_call(
        kernel,
        grid_spec=pltpu.PrefetchScalarGridSpec(
            num_scalar_prefetch=1,
            grid=(QUERY_HEADS,),
            in_specs=[
                pl.BlockSpec((tokens, 1), lambda head, at: (0, 0)),
                pl.BlockSpec((tokens, HEAD_SIZE), lambda head, at: (0, head)),
                pl.BlockSpec((tokens, HEAD_SIZE), lambda head, at: (0, head)),
                pl.BlockSpec((1, tokens, 1), lambda head, at: (head, 0, 0)),
                pl.BlockSpec((tokens, HEAD_SIZE), lambda head, at: (0, 0)),
                pl.BlockSpec((tokens, HEAD_SIZE), lambda head, at: (0, 0)),
            ]
            + key_specs(both_pieces),
            out_specs=[
                pl.BlockSpec((tokens, HEAD_SIZE), lambda head, at: (0, head)),
                pl.BlockSpec((keys, HEAD_SIZE), lambda head, at: (0, head // GROUP)),
                pl.BlockSpec((keys, HEAD_SIZE), lambda head, at: (0, head // GROUP)),
            ],
            scratch_shapes=[
                pltpu.VMEM((tokens, keys), jnp.float32),
                pltpu.VMEM((HEAD_SIZE, keys), jnp.float32),
                pltpu.VMEM((HEAD_SIZE, keys), jnp.float32),
                pltpu.VMEM((keys, HEAD_SIZE), jnp.bfloat16),
                pltpu.VMEM((keys, HEAD_SIZE), jnp.bfloat16),
            ],
        ),
        out_shape=[
            jax.ShapeDtypeStruct((tokens, QD), jnp.bfloat16),
            jax.ShapeDtypeStruct((keys, KD), jnp.float32),
            jax.ShapeDtypeStruct((keys, KD), jnp.float32),
        ],
        compiler_params=vmem_params,
        cost_estimate=pl.CostEstimate(
            flops=20 * tokens * keys * QD,
            bytes_accessed=8 * tokens * QD,
            transcendentals=QUERY_HEADS * tokens * keys,
        ),
    )(
        at,
        position,
        projected,
        incoming,
        log_total,
        cosine,
        sine,
        *[piece for piece in both_pieces for unused in range(2)],
    )


def unit_part(me, normed_all, grad_out_all, gate_up, down, count, first):
    tokens = normed_all.shape[0]
    block = tokens // count
    width = down.shape[0]
    shard = D // count
    weights = list(gate_up) if first else [gate_up]

    def kernel(me_ref, normed_ref, out_grad_ref, down_ref, *refs):
        weight_refs = refs[: len(weights)]
        hidden_ref, grad_ref = refs[len(weights) : len(weights) + 2]
        weight_ref = weight_refs[0]
        if first:
            ordered_ref, weight_ref = refs[len(weights) + 2 :]
            ordered_ref[...] = out_grad_ref[...]

            @pl.when(pl.program_id(0) == 0)
            def _():
                for mask, ref in enumerate(weight_refs):
                    begin = pl.multiple_of((me_ref[0] ^ mask) * shard, shard)
                    weight_ref[pl.ds(begin, shard)] = ref[...]

        values = dot_f32(normed_ref[...], weight_ref[...])
        gate = values[:, :width]
        up = values[:, width:]
        grad_hidden = dot_right_t(out_grad_ref[...], down_ref[...])
        share = 1.0 / (1.0 + jnp.exp(-gate))
        passed = gate * share
        hidden_ref[...] = (passed * up).astype(jnp.bfloat16)
        grad_ref[:, :width] = (
            grad_hidden * up * share * (1.0 + gate * (1.0 - share))
        ).astype(jnp.bfloat16)
        grad_ref[:, width:] = (grad_hidden * passed).astype(jnp.bfloat16)

    def out_grad_index(step, me_ref):
        return (me_ref[0] ^ mask_at(step, count), 0) if first else (step, 0)

    row = lambda step, me_ref: (step, 0)
    fixed = lambda step, me_ref: (0, 0)
    out_specs = [pl.BlockSpec((block, width), row), pl.BlockSpec((block, 2 * width), row)]
    out_shape = [
        jax.ShapeDtypeStruct((tokens, width), jnp.bfloat16),
        jax.ShapeDtypeStruct((tokens, 2 * width), jnp.bfloat16),
    ]
    if first:
        out_specs += [pl.BlockSpec((block, D), row), pl.BlockSpec((D, 2 * width), fixed)]
        out_shape += [
            jax.ShapeDtypeStruct((tokens, D), jnp.bfloat16),
            jax.ShapeDtypeStruct((D, 2 * width), jnp.bfloat16),
        ]
    return pl.pallas_call(
        kernel,
        grid_spec=pltpu.PrefetchScalarGridSpec(
            num_scalar_prefetch=1,
            grid=(count,),
            in_specs=[
                pl.BlockSpec((block, D), row),
                pl.BlockSpec((block, D), out_grad_index),
                pl.BlockSpec((width, D), fixed),
            ]
            + [pl.BlockSpec(weight.shape, fixed) for weight in weights],
            out_specs=out_specs,
        ),
        out_shape=out_shape,
        compiler_params=vmem_params,
        cost_estimate=pl.CostEstimate(
            flops=6 * tokens * D * width,
            bytes_accessed=4 * tokens * D + 6 * tokens * width + 6 * D * width,
            transcendentals=tokens * width,
        ),
    )(me, normed_all, grad_out_all, down, *weights)


def projection_terms(me, normed_turned, attended_turned, grad_projected, grad_middle, rows_out):
    count, shard, tokens = normed_turned.shape
    in_width = grad_projected.shape[1]
    out_width = grad_middle.shape[1]
    in_lanes, out_lanes = in_width // 128, out_width // 128

    def kernel(me_ref, normed_ref, attended_ref, projected_ref, middle_ref, out_ref, bias_ref):
        @pl.when(pl.program_id(0) == 0)
        def _():
            bias = jnp.sum(projected_ref[...].astype(jnp.float32), axis=0, keepdims=True)
            bias_ref[...] = jnp.zeros_like(bias_ref)
            for group in range(in_lanes):
                bias_ref[group : group + 1] = bias[:, group * 128 : (group + 1) * 128]

        place = 0
        for turned_ref, right_ref, lanes in (
            (normed_ref, projected_ref, in_lanes),
            (attended_ref, middle_ref, out_lanes),
        ):
            term = dot_f32(turned_ref[0], right_ref[...]).astype(jnp.bfloat16)
            for group in range(lanes):
                out_ref[0, place : place + shard] = term[:, group * 128 : (group + 1) * 128]
                place += shard
        out_ref[0, place:] = bias_ref[...].astype(jnp.bfloat16)

    def turned_index(step, me_ref):
        return (me_ref[0] ^ mask_at(step, count), 0, 0)

    fixed = lambda step, me_ref: (0, 0)
    return pl.pallas_call(
        kernel,
        grid_spec=pltpu.PrefetchScalarGridSpec(
            num_scalar_prefetch=1,
            grid=(count,),
            in_specs=[
                pl.BlockSpec((1, shard, tokens), turned_index),
                pl.BlockSpec((1, shard, tokens), turned_index),
                pl.BlockSpec((tokens, in_width), fixed),
                pl.BlockSpec((tokens, out_width), fixed),
            ],
            out_specs=pl.BlockSpec((1, rows_out, 128), lambda step, me_ref: (step, 0, 0)),
            scratch_shapes=[
                pltpu.VMEM((rows_out - shard * (in_lanes + out_lanes), 128), jnp.float32)
            ],
        ),
        out_shape=jax.ShapeDtypeStruct((count, rows_out, 128), jnp.bfloat16),
        compiler_params=vmem_params,
        cost_estimate=pl.CostEstimate(
            flops=2 * D * tokens * (in_width + out_width),
            bytes_accessed=256 * count * rows_out,
            transcendentals=0,
        ),
    )(me, normed_turned, attended_turned, grad_projected, grad_middle)


def shards(
    tokens,
    positions,
    cotangent,
    attn_norm,
    ffn_norm,
    in_proj,
    in_bias,
    out_proj,
    gate_up,
    down_proj,
):
    token_rows = tokens.shape[1]
    fsdp_count = lax.axis_size("fsdp")
    ctx_count = lax.axis_size("ctx")
    fsdp_me = lax.axis_index("fsdp")
    me = fsdp_me.astype(jnp.int32)[None]
    at = lax.axis_index("ctx").astype(jnp.int32)[None]
    units = FF // fsdp_count
    shard_d = D // fsdp_count
    residual_in = tokens[0].astype(jnp.float32)
    position = positions[0]
    grad_out_b = cotangent[0]

    first_units, second_units, padded_units = unit_widths(units)
    bias_full = gather_small(in_bias).reshape(-1)
    in_scaled = (in_proj.astype(jnp.float32) * attn_norm[:, None]).astype(jnp.bfloat16)
    first_blocks, second_blocks = split_units(me, gate_up, ffn_norm, fsdp_count)
    cosine, sine = rotary_tables(position)
    normed_b = rms_scale(residual_in).astype(jnp.bfloat16)
    in_pieces = gather_pieces(in_scaled, first_blocks, cosine, normed_b)
    gated_blocks = after(first_blocks, in_pieces[0], in_pieces[2], in_pieces[4])
    gate_up_first = [gated_blocks[0]] + [
        exchange(gated_blocks[mask], mask) for mask in range(1, fsdp_count)
    ]
    out_full = lax.all_gather(after(out_proj, in_pieces), "fsdp", axis=0, tiled=True)

    projected = project(me, after(normed_b, gate_up_first), in_pieces, bias_full, cosine, sine)
    both_b = projected[:, QD:]
    both_pieces = [both_b] + [
        lax.ppermute(both_b, "ctx", [(s, s + back) for s in range(ctx_count - back)])
        for back in range(1, ctx_count)
    ]
    normed_again, down_again = after((normed_b, down_proj), projected)
    normed_turned = normed_again.T.reshape(fsdp_count, shard_d, token_rows)
    down_first = down_again[:first_units]
    down_second = jnp.pad(down_again[first_units:], ((0, padded_units - second_units), (0, 0)))
    both_pieces = after(both_pieces, normed_turned, down_first, down_second)
    attended_b, attended_turned, log_total = attend(at, position[:, None], projected, both_pieces)
    grad_out_all = lax.all_gather(
        after(grad_out_b, out_full, both_pieces), "fsdp", axis=0, tiled=True
    )
    middle = residual_in + dot_f32(attended_b, out_full)
    normed_ffn_b = rms_scale(middle).astype(jnp.bfloat16)

    normed_ffn_all = gather_masks(normed_ffn_b)
    gate_up_second = swap_blocks(after(second_blocks, normed_ffn_all)).reshape(
        D, 2 * padded_units
    )
    hidden_first, grad_first, grad_out_all, gate_up_first = unit_part(
        me, normed_ffn_all, grad_out_all, gate_up_first, down_first, fsdp_count, True
    )
    odd_rows = normed_ffn_all.shape[0] // 2

    def down_term(hidden, *gates):
        return dot_left_t(after(hidden, *gates), grad_out_all).astype(jnp.bfloat16)

    def gate_term(grad, *gates):
        term = dot_left_t(normed_ffn_all, after(grad, *gates)).astype(jnp.bfloat16)
        return (
            term.reshape(fsdp_count, ctx_count, shard_d // ctx_count, -1)
            .transpose(1, 0, 2, 3)
            .reshape(D, -1)
        )

    def gate_swap(summed):
        return swap_blocks(summed.reshape(fsdp_count, shard_d // ctx_count, -1))

    def input_grads(rows, *gates):
        return (
            (
                dot_right_t(after(grad_first, *gates)[rows], gate_up_first)
                + dot_right_t(grad_second[rows], gate_up_second)
            )
            .astype(jnp.bfloat16)
            .reshape(fsdp_count // 2, token_rows, D)
        )

    def down_outs(rows, *gates):
        return (
            (
                dot_f32(after(hidden_first, *gates)[rows], down_first)
                + dot_f32(hidden_second[rows], down_second)
            )
            .astype(jnp.bfloat16)
            .reshape(fsdp_count // 2, token_rows, D)
        )

    down_term_a = down_term(hidden_first)
    down_sum_a = ctx_scatter(down_term_a)
    gate_term_a = gate_term(grad_first, down_term_a)
    gate_sum_a = ctx_scatter(gate_term_a)
    hidden_second, grad_second = unit_part(
        me,
        after(normed_ffn_all, gate_term_a),
        grad_out_all,
        gate_up_second,
        down_second,
        fsdp_count,
        False,
    )
    grad_normed_odd = input_grads(slice(0, odd_rows), hidden_second)
    normed_sum = MaskSum(grad_normed_odd)
    grad_normed_even = input_grads(slice(odd_rows, None), grad_normed_odd)
    down_a = CtxGather(down_sum_a, grad_normed_even)
    sent = normed_sum.second(grad_normed_even)
    down_term_b = down_term(hidden_second, sent)[:second_units]
    down_sum_b = ctx_scatter(after(down_term_b, gate_term_a))
    gate_term_b = gate_term(grad_second, down_term_b)
    gate_sum_b = ctx_scatter(after(gate_term_b, down_term_b))
    down_a.hop(gate_term_b)
    sent = normed_sum.third(gate_term_b)
    down_odd = down_outs(slice(0, odd_rows), sent)
    down_a.hop(down_odd)
    grad_normed_ffn = normed_sum.result(down_odd).astype(jnp.float32)

    grad_out = grad_out_b.astype(jnp.float32)
    grad_middle = grad_out + norm_backward(middle, grad_normed_ffn)
    grad_middle_b = grad_middle.astype(jnp.bfloat16)
    grad_attended_b = dot_right_t(grad_middle_b, out_full).astype(jnp.bfloat16)
    gate_swapped_a = gate_swap(after(gate_sum_a, grad_attended_b))
    query_grad, key_grads, value_grads = attend_backward(
        at,
        position[:, None],
        projected,
        both_pieces,
        grad_attended_b,
        log_total,
        cosine,
        sine,
    )
    both_sent = [
        lax.ppermute(
            jnp.concatenate(
                [
                    grads[back * token_rows : (back + 1) * token_rows].astype(jnp.bfloat16)
                    for grads in (key_grads, value_grads)
                ],
                axis=1,
            ),
            "ctx",
            [(s + back, s) for s in range(ctx_count - back)],
        )
        for back in range(1, ctx_count)
    ]
    block_sum = MaskSum(after(down_odd, query_grad))
    down_even = down_outs(slice(odd_rows, None), query_grad)
    both_grad = jnp.concatenate([key_grads[:token_rows], value_grads[:token_rows]], axis=1)
    for piece in after(both_sent, down_even):
        both_grad = both_grad + piece.astype(jnp.float32)
    turned_back = []
    for head in range(KEY_VALUE_HEADS):
        plain = both_grad[:, head * HEAD_SIZE : (head + 1) * HEAD_SIZE]
        turned_back.append(plain * cosine - jnp.roll(plain, HEAD_SIZE // 2, axis=1) * sine)
    grad_projected_b = jnp.concatenate(
        [query_grad]
        + [part.astype(jnp.bfloat16) for part in turned_back]
        + [both_grad[:, KD:].astype(jnp.bfloat16)],
        axis=1,
    )
    in_rows = shard_d * in_proj.shape[1] // 128
    out_rows = shard_d * D // 128
    terms = projection_terms(
        me,
        normed_turned,
        attended_turned.reshape(fsdp_count, shard_d, token_rows),
        grad_projected_b,
        grad_middle_b,
        in_rows + out_rows + 64,
    )
    half = fsdp_count // 2
    terms_sum = MaskSum(terms[:half])
    grad_normed = project_back(me, after(grad_projected_b, terms), in_pieces)
    sent = terms_sum.second(terms[half:], grad_normed)
    tokens_grad = grad_middle + norm_backward(residual_in, after(grad_normed, sent))
    gate_a = CtxGather(gate_swapped_a, tokens_grad)
    sent = terms_sum.third(tokens_grad)
    sent = block_sum.second(down_even, sent)
    gate_a.hop(sent)
    terms_part = terms_sum.result(sent)
    terms_ctx = ctx_scatter(after(terms_part, gate_term_b))
    sent = block_sum.third(terms_part)
    down_b = CtxGather(down_sum_b, sent)
    gate_a.hop(sent)
    down_b.hop(sent)
    block_out = middle + block_sum.result(sent).astype(jnp.float32)
    down_b.hop(block_out)
    gate_b = CtxGather(gate_swap(gate_sum_b), block_out)
    down_grad = jnp.concatenate(
        [
            part.result(block_out).reshape(-1, D).astype(jnp.float32)
            for part in (down_a, down_b)
        ],
        axis=0,
    )
    gate_b.hop(down_grad)
    gate_first = gate_a.result(down_grad)
    gate_b.hop(gate_first)
    terms_all = CtxGather(terms_ctx, gate_first)
    terms_all.hop()
    gate_grad, ffn_grad = join_units(gate_first, gate_b.result(), gate_up, ffn_norm)
    terms_all.hop(gate_grad)
    terms_total = terms_all.result().reshape(-1, 128).astype(jnp.float32)

    def lanes_back(rows):
        return rows.reshape(-1, shard_d, 128).transpose(1, 0, 2).reshape(shard_d, -1)

    in_total = lanes_back(terms_total[:in_rows])
    out_grad = lanes_back(terms_total[in_rows : in_rows + out_rows])
    bias_span = in_bias.shape[0]
    bias_grad = lax.dynamic_slice_in_dim(
        terms_total[in_rows + out_rows : in_rows + out_rows + in_proj.shape[1] // 128].reshape(-1),
        fsdp_me * bias_span,
        bias_span,
    )
    in_grad = in_total * attn_norm[:, None]
    attn_grad = jnp.sum(in_total * in_proj.astype(jnp.float32), axis=1)
    return (
        block_out.astype(jnp.bfloat16).reshape(1, token_rows, D),
        tokens_grad.reshape(1, token_rows, D),
        attn_grad,
        ffn_grad,
        in_grad,
        bias_grad,
        out_grad,
        gate_grad,
        down_grad,
    )


def solution(mesh):
    in_specs = (
        P("fsdp", "ctx", None),
        P("fsdp", "ctx"),
        P("fsdp", "ctx", None),
        P("fsdp"),
        P("fsdp"),
        P("fsdp", None),
        P("fsdp"),
        P("fsdp", None),
        P("fsdp", None),
        P("fsdp", None),
    )
    out_specs = (
        P("fsdp", "ctx", None),
        P("fsdp", "ctx", None),
        P("fsdp"),
        P("fsdp"),
        P("fsdp", None),
        P("fsdp"),
        P("fsdp", None),
        P("fsdp", None),
        P("fsdp", None),
    )
    return jax.shard_map(shards, mesh=mesh, in_specs=in_specs, out_specs=out_specs, check_vma=False)
```

```python
import jax
import jax.numpy as jnp
from jax import lax
from jax.experimental import pallas as pl
from jax.experimental.pallas import tpu as pltpu
from jax.sharding import PartitionSpec as P

D = 1536
QUERY_HEADS = 12
KEY_VALUE_HEADS = 2
HEAD_SIZE = 128
FF = 8960
QD = QUERY_HEADS * HEAD_SIZE
KD = KEY_VALUE_HEADS * HEAD_SIZE
GROUP = QUERY_HEADS // KEY_VALUE_HEADS


norm_eps = 1e-06
rope_base = 1000000.0
masked_score = -1e30
score_scale = HEAD_SIZE ** (-0.5)
vmem_params = pltpu.CompilerParams(vmem_limit_bytes=48 * 1024 * 1024)


def rms_scale(value_rows):
    return value_rows * lax.rsqrt(
        jnp.mean(value_rows * value_rows, axis=-1, keepdims=True) + norm_eps
    )


def norm_backward(value_rows, incoming):
    unused_out, pullback = jax.vjp(rms_scale, value_rows)
    return pullback(incoming)[0]


def rotary_tables(position):
    lane = jnp.arange(HEAD_SIZE, dtype=jnp.int32)
    half = HEAD_SIZE // 2
    frequencies = rope_base ** (-((lane % half).astype(jnp.float32) * (2.0 / HEAD_SIZE)))
    angles = position.astype(jnp.float32)[:, None] * frequencies[None, :]
    sign = jnp.where(lane < half, -1.0, 1.0)
    return jnp.cos(angles), jnp.sin(angles) * sign[None, :]


def dot_f32(left, right):
    return jnp.dot(left, right, preferred_element_type=jnp.float32)


def dot_right_t(left, right):
    return lax.dot_general(
        left, right, (((1,), (1,)), ((), ())), preferred_element_type=jnp.float32
    )


def dot_left_t(left, right):
    return lax.dot_general(
        left, right, (((0,), (0,)), ((), ())), preferred_element_type=jnp.float32
    )


def add_low(left, right):
    return left + right


def after(value, *earlier):
    return lax.optimization_barrier((value, earlier))[0]


def exchange(value, mask):
    count = lax.axis_size("fsdp")
    return lax.ppermute(value, "fsdp", [(place, place ^ mask) for place in range(count)])


def gather_pieces(block, *gates):
    count = lax.axis_size("fsdp")
    if count != 8:
        found = [[block]] + [[exchange(block, mask)] for mask in range(2, count, 2)]
    else:
        half = block.shape[0] // 2
        by_x = exchange(block, 2)
        by_y = exchange(block, 4)
        other = exchange(block, 1)
        by_x, by_y = after((by_x, by_y), *gates)
        top = exchange(by_x[:half], 4)
        bottom = exchange(by_y[half:], 2)
        found = [[block], [by_x], [by_y], [top, bottom]]
        others = [[other], [exchange(by_x, 1)], [exchange(by_y, 1)]]
        others.append([exchange(top, 1), exchange(bottom, 1)])
        return [(2 * place, rows) for place, rows in enumerate(found)] + [
            (2 * place + 1, rows) for place, rows in enumerate(others)
        ]
    pieces = []
    for place, rows in enumerate(found):
        pieces.append((2 * place, rows))
        pieces.append((2 * place + 1, [exchange(part, 1) for part in rows]))
    return pieces


def gather_masks(block, *gates):
    count = lax.axis_size("fsdp")
    rows = block.shape[0]
    whole = jnp.zeros((count * rows, block.shape[1]), block.dtype)
    for mask, parts in gather_pieces(block, *gates):
        first = place_of(mask, count) * rows
        for part in parts:
            whole = lax.dynamic_update_slice(whole, part, (first, 0))
            first += part.shape[0]
    return whole


def gather_small(value):
    count = lax.axis_size("fsdp")
    me = lax.axis_index("fsdp")
    bits = count.bit_length() - 1
    found = value
    for bit in list(range(1, bits)) + [0]:
        got = exchange(found, 1 << bit)
        low = (me >> bit) % 2 == 0
        found = jnp.stack([jnp.where(low, found, got), jnp.where(low, got, found)])
    return jnp.moveaxis(found, 0, bits - 1).reshape(count, -1)


def place_of(mask, count):
    return mask // 2 + (1 - mask % 2) * (count // 2)


def mask_at(place, count):
    return jnp.where(place < count // 2, 2 * place + 1, 2 * place - count)


class MaskSum:
    def __init__(self, odd):
        self.got = exchange(odd, 1)

    def second(self, even, *gates):
        count = lax.axis_size("fsdp")
        self.kept = add_low(even, after(self.got, *gates))
        if count == 8:
            half = self.kept.shape[1] // 2
            self.by_x = exchange(self.kept[1::2, :half], 2)
            self.by_y = exchange(self.kept[2:, half:], 4)
        else:
            span = count
            while self.kept.shape[0] > 1:
                span //= 2
                half = self.kept.shape[0] // 2
                self.kept = add_low(self.kept[:half], exchange(self.kept[half:], span))
        return self.kept

    def third(self, *gates):
        if lax.axis_size("fsdp") != 8:
            return self.kept
        half = self.kept.shape[1] // 2
        by_x, by_y = after((self.by_x, self.by_y), *gates)
        self.top = add_low(self.kept[0::2, :half], by_x)
        self.bottom = add_low(self.kept[:2, half:], by_y)
        self.last_y = exchange(self.top[1], 4)
        self.last_x = exchange(self.bottom[1], 2)
        return self.top, self.bottom

    def result(self, *gates):
        if lax.axis_size("fsdp") != 8:
            return self.kept[0]
        last_y, last_x = after((self.last_y, self.last_x), *gates)
        return jnp.concatenate(
            [add_low(self.top[0], last_y), add_low(self.bottom[0], last_x)], axis=0
        )


def swap_blocks(blocks):
    return lax.all_to_all(blocks, "fsdp", 0, 0, tiled=True)


def ctx_scatter(terms):
    return lax.psum_scatter(terms, "ctx", scatter_dimension=0, tiled=True)


class CtxGather:
    def __init__(self, block):
        self.block = block
        self.four = lax.axis_size("ctx") == 4

    def pairs(self, *gates):
        if not self.four:
            return self.block
        self.block = after(self.block, *gates)
        self.got = lax.ppermute(self.block, "ctx", [(0, 1), (1, 0), (2, 3), (3, 2)])
        return self.block

    def middle(self, *gates):
        if not self.four:
            return self.block
        even = lax.axis_index("ctx") % 2 == 0
        got = after(self.got, *gates)
        self.pair = jnp.stack(
            [jnp.where(even, self.block, got), jnp.where(even, got, self.block)]
        )
        self.crossed = lax.ppermute(self.pair, "ctx", [(1, 2), (2, 1)])
        return self.pair

    def outward(self, *gates):
        if not self.four:
            return self.block
        self.crossed = after(self.crossed, *gates)
        self.passed = lax.ppermute(self.crossed, "ctx", [(1, 0), (2, 3)])
        return self.crossed

    def result(self, *gates):
        me = lax.axis_index("ctx")
        if self.four:
            other = jnp.where((me == 0) | (me == 3), after(self.passed, *gates), self.crossed)
            return jnp.concatenate(
                [jnp.where(me < 2, self.pair, other), jnp.where(me < 2, other, self.pair)]
            )
        return lax.all_gather(after(self.block, *gates), "ctx", axis=0)


def unit_widths(units):
    first = units // 256 * 128
    second = units - first
    return first, second, -(-second // 128) * 128


def split_units(me, gate_up, gain, count):
    rows, columns = gate_up.shape
    span = columns // 2
    units = span // count
    first, second, padded = unit_widths(units)
    block = 48

    def kernel(me_ref, weight_ref, gain_ref, first_ref, second_ref):
        def scaled(begin, end):
            value = weight_ref[:, begin:end].astype(jnp.float32) * gain_ref[...]
            return value.astype(gate_up.dtype)

        for owner in range(count):
            for side in range(2):
                begin = side * span + owner * units
                first_ref[me_ref[0] ^ owner, :, side * first : (side + 1) * first] = scaled(
                    begin, begin + first
                )
                second_ref[owner, :, side * padded : side * padded + second] = scaled(
                    begin + first, begin + units
                )
                if padded > second:
                    second_ref[
                        owner, :, side * padded + second : (side + 1) * padded
                    ] = jnp.zeros((block, padded - second), gate_up.dtype)

    return pl.pallas_call(
        kernel,
        grid_spec=pltpu.PrefetchScalarGridSpec(
            num_scalar_prefetch=1,
            grid=(rows // block,),
            in_specs=[
                pl.BlockSpec((block, columns), lambda step, me_ref: (step, 0)),
                pl.BlockSpec((block, 1), lambda step, me_ref: (step, 0)),
            ],
            out_specs=[
                pl.BlockSpec((count, block, 2 * first), lambda step, me_ref: (0, step, 0)),
                pl.BlockSpec((count, block, 2 * padded), lambda step, me_ref: (0, step, 0)),
            ],
        ),
        out_shape=[
            jax.ShapeDtypeStruct((count, rows, 2 * first), gate_up.dtype),
            jax.ShapeDtypeStruct((count, rows, 2 * padded), gate_up.dtype),
        ],
        compiler_params=vmem_params,
        cost_estimate=pl.CostEstimate(
            flops=0, bytes_accessed=4 * rows * columns, transcendentals=0
        ),
    )(me, gate_up, gain[:, None])


def join_units(first_part, second_part, gate_up, gain):
    rows, columns = gate_up.shape
    if first_part.shape[2] % 16:
        first_part, second_part = (
            part.transpose(1, 0, 2, 3)
            .reshape(part.shape[1], rows // 48, 48, -1)
            .transpose(1, 0, 2, 3)
            for part in (first_part, second_part)
        )
    pieces, count, block = first_part.shape[:3]
    span = columns // 2
    units = span // count
    first, second, padded = unit_widths(units)

    def kernel(first_ref, second_ref, weight_ref, gain_ref, whole_ref, sums_ref):
        for owner in range(count):
            for side in range(2):
                begin = side * span + owner * units
                whole_ref[:, begin : begin + first] = first_ref[
                    0, owner, :, side * first : (side + 1) * first
                ].astype(jnp.float32)
                whole_ref[:, begin + first : begin + units] = second_ref[
                    0, owner, :, side * padded : side * padded + second
                ].astype(jnp.float32)
        whole = whole_ref[...]
        total = jnp.sum(whole * weight_ref[...].astype(jnp.float32), axis=1, keepdims=True)
        sums_ref[...] = jnp.broadcast_to(total, (block, 128))
        whole_ref[...] = whole * gain_ref[...]

    whole, sums = pl.pallas_call(
        kernel,
        grid=(pieces,),
        in_specs=[
            pl.BlockSpec((1, count, block, 2 * first), lambda step: (step, 0, 0, 0)),
            pl.BlockSpec((1, count, block, 2 * padded), lambda step: (step, 0, 0, 0)),
            pl.BlockSpec((block, columns), lambda step: (step, 0)),
            pl.BlockSpec((block, 1), lambda step: (step, 0)),
        ],
        out_specs=[
            pl.BlockSpec((block, columns), lambda step: (step, 0)),
            pl.BlockSpec((block, 128), lambda step: (step, 0)),
        ],
        out_shape=[
            jax.ShapeDtypeStruct((rows, columns), jnp.float32),
            jax.ShapeDtypeStruct((rows, 128), jnp.float32),
        ],
        compiler_params=vmem_params,
        cost_estimate=pl.CostEstimate(
            flops=2 * rows * columns, bytes_accessed=8 * rows * columns, transcendentals=0
        ),
    )(first_part, second_part, gate_up, gain[:, None])
    return whole, sums[:, 0]


def place_rows(me_ref, pieces, refs, weight_ref):
    place = 0
    for mask, parts in pieces:
        shard = sum(part.shape[0] for part in parts)
        begin = (me_ref[0] ^ mask) * shard
        for part in parts:
            rows = part.shape[0]
            weight_ref[pl.ds(pl.multiple_of(begin, rows), rows)] = refs[place][...]
            begin = begin + rows
            place += 1


def project(me, normed, pieces, bias, cosine, sine):
    tokens = normed.shape[0]
    width = bias.shape[0]
    block = 512
    flat = [part for unused_mask, parts in pieces for part in parts]

    def kernel(me_ref, normed_ref, bias_ref, cosine_ref, sine_ref, *refs):
        out_ref, weight_ref = refs[len(flat) :]
        place_rows(me_ref, pieces, refs, weight_ref)
        product = dot_f32(normed_ref[...], weight_ref[...]) + bias_ref[...]
        for head in range(block // HEAD_SIZE):
            lanes = slice(head * HEAD_SIZE, (head + 1) * HEAD_SIZE)
            plain = product[:, lanes]
            turned = plain * cosine_ref[...] + pltpu.roll(plain, HEAD_SIZE // 2, 1) * sine_ref[...]
            column = pl.program_id(0) * block + head * HEAD_SIZE
            out_ref[:, lanes] = jnp.where(column < QD + KD, turned, plain).astype(jnp.bfloat16)

    return pl.pallas_call(
        kernel,
        grid_spec=pltpu.PrefetchScalarGridSpec(
            num_scalar_prefetch=1,
            grid=(width // block,),
            in_specs=[
                pl.BlockSpec((tokens, D), lambda step, me_ref: (0, 0)),
                pl.BlockSpec((1, block), lambda step, me_ref: (0, step)),
                pl.BlockSpec((tokens, HEAD_SIZE), lambda step, me_ref: (0, 0)),
                pl.BlockSpec((tokens, HEAD_SIZE), lambda step, me_ref: (0, 0)),
            ]
            + [
                pl.BlockSpec((part.shape[0], block), lambda step, me_ref: (0, step))
                for part in flat
            ],
            out_specs=pl.BlockSpec((tokens, block), lambda step, me_ref: (0, step)),
            scratch_shapes=[pltpu.VMEM((D, block), jnp.bfloat16)],
        ),
        out_shape=jax.ShapeDtypeStruct((tokens, width), jnp.bfloat16),
        compiler_params=vmem_params,
        cost_estimate=pl.CostEstimate(
            flops=2 * tokens * D * width, bytes_accessed=2 * D * width, transcendentals=0
        ),
    )(me, normed, bias[None], cosine, sine, *flat)


def project_back(me, grad_projected, pieces):
    tokens, width = grad_projected.shape
    flat = [part for unused_mask, parts in pieces for part in parts]

    def kernel(me_ref, grad_ref, *refs):
        out_ref, weight_ref = refs[len(flat) :]
        place_rows(me_ref, pieces, refs, weight_ref)
        out_ref[...] = dot_right_t(grad_ref[...], weight_ref[...])

    whole = lambda part: pl.BlockSpec(part.shape, lambda step, me_ref: (0, 0))
    return pl.pallas_call(
        kernel,
        grid_spec=pltpu.PrefetchScalarGridSpec(
            num_scalar_prefetch=1,
            grid=(1,),
            in_specs=[whole(grad_projected)] + [whole(part) for part in flat],
            out_specs=pl.BlockSpec((tokens, D), lambda step, me_ref: (0, 0)),
            scratch_shapes=[pltpu.VMEM((D, width), jnp.bfloat16)],
        ),
        out_shape=jax.ShapeDtypeStruct((tokens, D), jnp.float32),
        compiler_params=vmem_params,
        cost_estimate=pl.CostEstimate(
            flops=2 * tokens * D * width, bytes_accessed=2 * D * width, transcendentals=0
        ),
    )(me, grad_projected, *flat)


def fill_bias(at_ref, position_ref, bias_ref):
    tokens, keys = bias_ref.shape
    row = lax.broadcasted_iota(jnp.int32, (tokens, keys), 0)
    column = lax.broadcasted_iota(jnp.int32, (tokens, keys), 1)
    back = column // tokens
    query_index = at_ref[0] * tokens + row
    key_index = (at_ref[0] - back) * tokens + (column - back * tokens)
    allowed = (key_index <= query_index) & (key_index >= query_index - position_ref[...])
    bias_ref[...] = jnp.where(allowed, 0.0, masked_score)


def join_keys(refs, key_ref, value_ref):
    @pl.when(pl.program_id(0) % GROUP == 0)
    def _():
        for place in range(len(refs)):
            tokens = refs[0].shape[0]
            if (place + 1) * tokens > key_ref.shape[0]:
                break
            rows = slice(place * tokens, (place + 1) * tokens)
            key_ref[rows] = refs[2 * place][...]
            value_ref[rows] = refs[2 * place + 1][...]


def key_specs(both_pieces):
    specs = []
    for piece in both_pieces:
        shape = (piece.shape[0], HEAD_SIZE)
        specs.append(pl.BlockSpec(shape, lambda head, at: (0, head // GROUP)))
        specs.append(pl.BlockSpec(shape, lambda head, at: (0, KEY_VALUE_HEADS + head // GROUP)))
    return specs


def attend(at, position, projected, both_pieces):
    tokens = projected.shape[0]
    count = len(both_pieces)
    keys = count * tokens

    def kernel(at_ref, position_ref, query_ref, *refs):
        out_ref, turn_ref, log_ref, bias_ref, key_ref, value_ref = refs[2 * count :]

        @pl.when(pl.program_id(0) == 0)
        def _():
            fill_bias(at_ref, position_ref, bias_ref)

        join_keys(refs, key_ref, value_ref)

        scores = dot_right_t(query_ref[...], key_ref[...]) * score_scale + bias_ref[...]
        top = jnp.max(scores, axis=1, keepdims=True)
        raised = jnp.exp(scores - top)
        total = jnp.sum(raised, axis=1, keepdims=True)
        probs = (raised * (1.0 / total)).astype(jnp.bfloat16)
        result = dot_f32(probs, value_ref[...])
        out_ref[...] = result.astype(jnp.bfloat16)
        turn_ref[...] = result.T.astype(jnp.bfloat16)
        log_ref[0] = top + jnp.log(total)

    return pl.pallas_call(
        kernel,
        grid_spec=pltpu.PrefetchScalarGridSpec(
            num_scalar_prefetch=1,
            grid=(QUERY_HEADS,),
            in_specs=[
                pl.BlockSpec((tokens, 1), lambda head, at: (0, 0)),
                pl.BlockSpec((tokens, HEAD_SIZE), lambda head, at: (0, head)),
            ]
            + key_specs(both_pieces),
            out_specs=[
                pl.BlockSpec((tokens, HEAD_SIZE), lambda head, at: (0, head)),
                pl.BlockSpec((HEAD_SIZE, tokens), lambda head, at: (head, 0)),
                pl.BlockSpec((1, tokens, 1), lambda head, at: (head, 0, 0)),
            ],
            scratch_shapes=[
                pltpu.VMEM((tokens, keys), jnp.float32),
                pltpu.VMEM((keys, HEAD_SIZE), jnp.bfloat16),
                pltpu.VMEM((keys, HEAD_SIZE), jnp.bfloat16),
            ],
        ),
        out_shape=[
            jax.ShapeDtypeStruct((tokens, QD), jnp.bfloat16),
            jax.ShapeDtypeStruct((QD, tokens), jnp.bfloat16),
            jax.ShapeDtypeStruct((QUERY_HEADS, tokens, 1), jnp.float32),
        ],
        compiler_params=vmem_params,
        cost_estimate=pl.CostEstimate(
            flops=8 * tokens * keys * QD,
            bytes_accessed=8 * tokens * QD,
            transcendentals=QUERY_HEADS * tokens * keys,
        ),
    )(at, position, projected, *[piece for piece in both_pieces for unused in range(2)])


def attend_backward(at, position, projected, both_pieces, incoming, log_total, cosine, sine):
    tokens = projected.shape[0]
    count = len(both_pieces)
    keys = count * tokens

    def kernel(
        at_ref,
        position_ref,
        query_ref,
        incoming_ref,
        log_ref,
        cosine_ref,
        sine_ref,
        *refs,
    ):
        query_grad_ref, key_grad_ref, value_grad_ref = refs[2 * count : 2 * count + 3]
        bias_ref, key_total, value_total, key_ref, value_ref = refs[2 * count + 3 :]
        head = pl.program_id(0)
        join_keys(refs, key_ref, value_ref)

        @pl.when(head == 0)
        def _():
            fill_bias(at_ref, position_ref, bias_ref)

        @pl.when(head % GROUP == 0)
        def _():
            key_total[...] = jnp.zeros_like(key_total)
            value_total[...] = jnp.zeros_like(value_total)

        scores = dot_right_t(query_ref[...], key_ref[...]) * score_scale + bias_ref[...]
        probs = jnp.exp(scores - log_ref[0])
        grad_probs = dot_right_t(incoming_ref[...], value_ref[...])
        inner = jnp.sum(grad_probs * probs, axis=1, keepdims=True)
        grad_scores = (probs * (grad_probs - inner)).astype(jnp.bfloat16)
        value_total[...] += dot_left_t(incoming_ref[...], probs.astype(jnp.bfloat16))
        key_total[...] += dot_left_t(query_ref[...], grad_scores)
        plain = dot_f32(grad_scores, key_ref[...]) * score_scale
        query_grad_ref[...] = (
            plain * cosine_ref[...] - pltpu.roll(plain, HEAD_SIZE // 2, 1) * sine_ref[...]
        ).astype(jnp.bfloat16)

        @pl.when(head % GROUP == GROUP - 1)
        def _():
            key_grad_ref[...] = (key_total[...] * score_scale).T
            value_grad_ref[...] = value_total[...].T

    return pl.pallas_call(
        kernel,
        grid_spec=pltpu.PrefetchScalarGridSpec(
            num_scalar_prefetch=1,
            grid=(QUERY_HEADS,),
            in_specs=[
                pl.BlockSpec((tokens, 1), lambda head, at: (0, 0)),
                pl.BlockSpec((tokens, HEAD_SIZE), lambda head, at: (0, head)),
                pl.BlockSpec((tokens, HEAD_SIZE), lambda head, at: (0, head)),
                pl.BlockSpec((1, tokens, 1), lambda head, at: (head, 0, 0)),
                pl.BlockSpec((tokens, HEAD_SIZE), lambda head, at: (0, 0)),
                pl.BlockSpec((tokens, HEAD_SIZE), lambda head, at: (0, 0)),
            ]
            + key_specs(both_pieces),
            out_specs=[
                pl.BlockSpec((tokens, HEAD_SIZE), lambda head, at: (0, head)),
                pl.BlockSpec((keys, HEAD_SIZE), lambda head, at: (0, head // GROUP)),
                pl.BlockSpec((keys, HEAD_SIZE), lambda head, at: (0, head // GROUP)),
            ],
            scratch_shapes=[
                pltpu.VMEM((tokens, keys), jnp.float32),
                pltpu.VMEM((HEAD_SIZE, keys), jnp.float32),
                pltpu.VMEM((HEAD_SIZE, keys), jnp.float32),
                pltpu.VMEM((keys, HEAD_SIZE), jnp.bfloat16),
                pltpu.VMEM((keys, HEAD_SIZE), jnp.bfloat16),
            ],
        ),
        out_shape=[
            jax.ShapeDtypeStruct((tokens, QD), jnp.bfloat16),
            jax.ShapeDtypeStruct((keys, KD), jnp.float32),
            jax.ShapeDtypeStruct((keys, KD), jnp.float32),
        ],
        compiler_params=vmem_params,
        cost_estimate=pl.CostEstimate(
            flops=20 * tokens * keys * QD,
            bytes_accessed=8 * tokens * QD,
            transcendentals=QUERY_HEADS * tokens * keys,
        ),
    )(
        at,
        position,
        projected,
        incoming,
        log_total,
        cosine,
        sine,
        *[piece for piece in both_pieces for unused in range(2)],
    )


def unit_part(me, normed_all, grad_out_all, gate_up, down, count, first):
    tokens = normed_all.shape[0]
    block = tokens // count
    width = down.shape[0]
    shard = D // count
    weights = list(gate_up) if first else [gate_up]

    def kernel(me_ref, normed_ref, out_grad_ref, down_ref, *refs):
        weight_refs = refs[: len(weights)]
        hidden_ref, grad_ref = refs[len(weights) : len(weights) + 2]
        weight_ref = weight_refs[0]
        if first:
            ordered_ref, weight_ref = refs[len(weights) + 2 :]
            ordered_ref[...] = out_grad_ref[...]

            @pl.when(pl.program_id(0) == 0)
            def _():
                for mask, ref in enumerate(weight_refs):
                    begin = pl.multiple_of((me_ref[0] ^ mask) * shard, shard)
                    weight_ref[pl.ds(begin, shard)] = ref[...]

        values = dot_f32(normed_ref[...], weight_ref[...])
        gate = values[:, :width]
        up = values[:, width:]
        grad_hidden = dot_right_t(out_grad_ref[...], down_ref[...])
        share = 1.0 / (1.0 + jnp.exp(-gate))
        passed = gate * share
        hidden_ref[...] = (passed * up).astype(jnp.bfloat16)
        grad_ref[:, :width] = (
            grad_hidden * up * share * (1.0 + gate * (1.0 - share))
        ).astype(jnp.bfloat16)
        grad_ref[:, width:] = (grad_hidden * passed).astype(jnp.bfloat16)

    def out_grad_index(step, me_ref):
        return (me_ref[0] ^ mask_at(step, count), 0) if first else (step, 0)

    row = lambda step, me_ref: (step, 0)
    fixed = lambda step, me_ref: (0, 0)
    out_specs = [pl.BlockSpec((block, width), row), pl.BlockSpec((block, 2 * width), row)]
    out_shape = [
        jax.ShapeDtypeStruct((tokens, width), jnp.bfloat16),
        jax.ShapeDtypeStruct((tokens, 2 * width), jnp.bfloat16),
    ]
    if first:
        out_specs += [pl.BlockSpec((block, D), row), pl.BlockSpec((D, 2 * width), fixed)]
        out_shape += [
            jax.ShapeDtypeStruct((tokens, D), jnp.bfloat16),
            jax.ShapeDtypeStruct((D, 2 * width), jnp.bfloat16),
        ]
    return pl.pallas_call(
        kernel,
        grid_spec=pltpu.PrefetchScalarGridSpec(
            num_scalar_prefetch=1,
            grid=(count,),
            in_specs=[
                pl.BlockSpec((block, D), row),
                pl.BlockSpec((block, D), out_grad_index),
                pl.BlockSpec((width, D), fixed),
            ]
            + [pl.BlockSpec(weight.shape, fixed) for weight in weights],
            out_specs=out_specs,
        ),
        out_shape=out_shape,
        compiler_params=vmem_params,
        cost_estimate=pl.CostEstimate(
            flops=6 * tokens * D * width,
            bytes_accessed=4 * tokens * D + 6 * tokens * width + 6 * D * width,
            transcendentals=tokens * width,
        ),
    )(me, normed_all, grad_out_all, down, *weights)


def row_terms(me, turned, right, rows_out):
    count, shard, tokens = turned.shape
    width = right.shape[1]
    lanes = width // 128
    half = count // 2
    spare = rows_out - shard * lanes

    def kernel(me_ref, turned_ref, right_ref, odd_ref, even_ref, *scratch):
        step = pl.program_id(0)
        if spare:

            @pl.when(step == 0)
            def _():
                sums = jnp.sum(right_ref[...].astype(jnp.float32), axis=0, keepdims=True)
                scratch[0][...] = jnp.zeros_like(scratch[0])
                for group in range(lanes):
                    scratch[0][group : group + 1] = sums[:, group * 128 : (group + 1) * 128]

        term = dot_f32(turned_ref[0], right_ref[...]).astype(jnp.bfloat16)

        def store(out_ref):
            for group in range(lanes):
                out_ref[0, group * shard : (group + 1) * shard] = term[
                    :, group * 128 : (group + 1) * 128
                ]
            if spare:
                out_ref[0, lanes * shard :] = scratch[0][...].astype(jnp.bfloat16)

        pl.when(step < half)(lambda: store(odd_ref))
        pl.when(step >= half)(lambda: store(even_ref))

    out = jax.ShapeDtypeStruct((half, rows_out, 128), jnp.bfloat16)
    return pl.pallas_call(
        kernel,
        grid_spec=pltpu.PrefetchScalarGridSpec(
            num_scalar_prefetch=1,
            grid=(count,),
            in_specs=[
                pl.BlockSpec(
                    (1, shard, tokens),
                    lambda step, me_ref: (me_ref[0] ^ mask_at(step, count), 0, 0),
                ),
                pl.BlockSpec((tokens, width), lambda step, me_ref: (0, 0)),
            ],
            out_specs=[
                pl.BlockSpec(
                    (1, rows_out, 128), lambda step, me_ref: (jnp.minimum(step, half - 1), 0, 0)
                ),
                pl.BlockSpec(
                    (1, rows_out, 128), lambda step, me_ref: (jnp.maximum(step - half, 0), 0, 0)
                ),
            ],
            scratch_shapes=[pltpu.VMEM((spare, 128), jnp.float32)] if spare else [],
        ),
        out_shape=[out, out],
        compiler_params=vmem_params,
        cost_estimate=pl.CostEstimate(
            flops=2 * D * tokens * width,
            bytes_accessed=256 * count * rows_out,
            transcendentals=0,
        ),
    )(me, turned, right)


def shards(
    tokens,
    positions,
    cotangent,
    attn_norm,
    ffn_norm,
    in_proj,
    in_bias,
    out_proj,
    gate_up,
    down_proj,
):
    token_rows = tokens.shape[1]
    fsdp_count = lax.axis_size("fsdp")
    ctx_count = lax.axis_size("ctx")
    fsdp_me = lax.axis_index("fsdp")
    me = fsdp_me.astype(jnp.int32)[None]
    at = lax.axis_index("ctx").astype(jnp.int32)[None]
    units = FF // fsdp_count
    shard_d = D // fsdp_count
    residual_in = tokens[0].astype(jnp.float32)
    position = positions[0]
    grad_out_b = cotangent[0]

    first_units, second_units, padded_units = unit_widths(units)
    bias_full = gather_small(in_bias).reshape(-1)
    in_scaled = (in_proj.astype(jnp.float32) * attn_norm[:, None]).astype(jnp.bfloat16)
    first_blocks, second_blocks = split_units(me, gate_up, ffn_norm, fsdp_count)
    cosine, sine = rotary_tables(position)
    normed_b = rms_scale(residual_in).astype(jnp.bfloat16)
    in_pieces = gather_pieces(in_scaled, first_blocks, cosine, normed_b)
    gated_blocks = after(first_blocks, in_pieces[0], in_pieces[2], in_pieces[4])
    gate_up_first = [gated_blocks[0]] + [
        exchange(gated_blocks[mask], mask) for mask in range(1, fsdp_count)
    ]
    out_full = lax.all_gather(after(out_proj, in_pieces), "fsdp", axis=0, tiled=True)

    projected = project(
        me, after(normed_b, gate_up_first[1], gate_up_first[2]), in_pieces, bias_full, cosine, sine
    )
    both_b = projected[:, QD:]
    both_pieces = [both_b] + [
        lax.ppermute(both_b, "ctx", [(s, s + back) for s in range(ctx_count - back)])
        for back in range(1, ctx_count)
    ]
    grad_out_all = lax.all_gather(after(grad_out_b, projected), "fsdp", axis=0, tiled=True)
    normed_again, down_again = after((normed_b, down_proj), projected)
    normed_turned = normed_again.T.reshape(fsdp_count, shard_d, token_rows)
    down_first = down_again[:first_units]
    down_second = jnp.pad(down_again[first_units:], ((0, padded_units - second_units), (0, 0)))
    both_pieces = after(
        both_pieces, normed_turned, down_first, down_second, gate_up_first[3], gate_up_first[4]
    )
    attended_b, attended_turned, log_total = attend(at, position[:, None], projected, both_pieces)
    attended_b = after(attended_b, gate_up_first)
    middle = residual_in + dot_f32(attended_b, out_full)
    normed_ffn_b = rms_scale(middle).astype(jnp.bfloat16)

    normed_ffn_all = gather_masks(normed_ffn_b)
    gate_up_second = swap_blocks(after(second_blocks, normed_ffn_all)).reshape(
        D, 2 * padded_units
    )
    hidden_first, grad_first, grad_out_all, gate_up_first = unit_part(
        me, normed_ffn_all, grad_out_all, gate_up_first, down_first, fsdp_count, True
    )
    odd_rows = normed_ffn_all.shape[0] // 2

    def down_term(hidden, *gates):
        return dot_left_t(after(hidden, *gates), grad_out_all).astype(jnp.bfloat16)

    def gate_term(grad, *gates):
        term = dot_left_t(normed_ffn_all, after(grad, *gates)).astype(jnp.bfloat16)
        return (
            term.reshape(fsdp_count, ctx_count, shard_d // ctx_count, -1)
            .transpose(1, 0, 2, 3)
            .reshape(D, -1)
        )

    def gate_swap(summed):
        return swap_blocks(summed.reshape(fsdp_count, shard_d // ctx_count, -1))

    def input_grads(rows, *gates):
        return (
            (
                dot_right_t(after(grad_first, *gates)[rows], gate_up_first)
                + dot_right_t(grad_second[rows], gate_up_second)
            )
            .astype(jnp.bfloat16)
            .reshape(fsdp_count // 2, token_rows, D)
        )

    def down_outs(rows, *gates):
        return (
            (
                dot_f32(after(hidden_first, *gates)[rows], down_first)
                + dot_f32(hidden_second[rows], down_second)
            )
            .astype(jnp.bfloat16)
            .reshape(fsdp_count // 2, token_rows, D)
        )

    down_term_a = down_term(hidden_first)
    down_sum_a = ctx_scatter(down_term_a)
    gate_term_a = gate_term(grad_first, down_term_a)
    gate_sum_a = ctx_scatter(gate_term_a)
    hidden_second, grad_second = unit_part(
        me,
        after(normed_ffn_all, gate_term_a),
        grad_out_all,
        gate_up_second,
        down_second,
        fsdp_count,
        False,
    )
    grad_normed_odd = input_grads(slice(0, odd_rows), hidden_second)
    normed_sum = MaskSum(grad_normed_odd)
    grad_normed_even = input_grads(slice(odd_rows, None), grad_normed_odd)
    sent = normed_sum.second(grad_normed_even)
    gate_term_b = gate_term(grad_second, sent)
    gate_sum_b = ctx_scatter(after(gate_term_b, gate_term_a))
    sent = normed_sum.third(gate_term_b)
    down_term_b = down_term(hidden_second, sent)[:second_units]
    down_sum_b = ctx_scatter(after(down_term_b, gate_term_b))
    grad_normed_ffn = normed_sum.result(down_term_b).astype(jnp.float32)

    grad_out = grad_out_b.astype(jnp.float32)
    grad_middle = grad_out + norm_backward(middle, grad_normed_ffn)
    grad_middle_b = grad_middle.astype(jnp.bfloat16)
    grad_attended_b = dot_right_t(grad_middle_b, out_full).astype(jnp.bfloat16)
    in_rows = shard_d * in_proj.shape[1] // 128
    out_rows = shard_d * D // 128
    out_odd, out_even = row_terms(
        me,
        attended_turned.reshape(fsdp_count, shard_d, token_rows),
        after(grad_middle_b, grad_attended_b),
        out_rows,
    )
    out_sum = MaskSum(out_odd)
    query_grad, key_grads, value_grads = attend_backward(
        at,
        position[:, None],
        projected,
        both_pieces,
        after(grad_attended_b, out_even),
        log_total,
        cosine,
        sine,
    )
    both_sent = [
        lax.ppermute(
            jnp.concatenate(
                [
                    grads[back * token_rows : (back + 1) * token_rows].astype(jnp.bfloat16)
                    for grads in (key_grads, value_grads)
                ],
                axis=1,
            ),
            "ctx",
            [(s + back, s) for s in range(ctx_count - back)],
        )
        for back in range(1, ctx_count)
    ]
    sent = out_sum.second(out_even, query_grad)
    down_odd = down_outs(slice(0, odd_rows), sent)
    block_sum = MaskSum(down_odd)
    sent = out_sum.third(down_odd)
    down_even = down_outs(slice(odd_rows, None), sent)
    both_grad = jnp.concatenate([key_grads[:token_rows], value_grads[:token_rows]], axis=1)
    for piece in after(both_sent, down_even):
        both_grad = both_grad + piece.astype(jnp.float32)
    turned_back = []
    for head in range(KEY_VALUE_HEADS):
        plain = both_grad[:, head * HEAD_SIZE : (head + 1) * HEAD_SIZE]
        turned_back.append(plain * cosine - jnp.roll(plain, HEAD_SIZE // 2, axis=1) * sine)
    grad_projected_b = jnp.concatenate(
        [query_grad]
        + [part.astype(jnp.bfloat16) for part in turned_back]
        + [both_grad[:, KD:].astype(jnp.bfloat16)],
        axis=1,
    )
    in_odd, in_even = row_terms(me, normed_turned, grad_projected_b, in_rows + 32)
    in_sum = MaskSum(in_odd)
    grad_normed = project_back(me, after(grad_projected_b, in_even), in_pieces)
    sent = in_sum.second(in_even, grad_normed)
    tokens_grad = grad_middle + norm_backward(residual_in, after(grad_normed, sent))
    sent = block_sum.second(down_even, tokens_grad)
    gate_swapped_a = gate_swap(after(gate_sum_a, sent))
    sent = in_sum.third(sent)
    down_a, gate_a = CtxGather(down_sum_a), CtxGather(gate_swapped_a)
    sent = down_a.pairs(sent)
    terms_part = jnp.concatenate([in_sum.result(sent), out_sum.result(sent)], axis=0)
    terms_total = lax.psum(after(terms_part, down_term_b), "ctx").astype(jnp.float32)
    sent = block_sum.third(terms_part)
    sent = gate_a.pairs(sent)
    sent = down_a.middle(sent)
    block_out = middle + block_sum.result(sent).astype(jnp.float32)
    sent = gate_a.middle(block_out)
    gate_b, down_b = CtxGather(gate_swap(after(gate_sum_b, sent))), CtxGather(down_sum_b)
    sent = down_a.outward(sent)
    sent = gate_a.outward(sent)
    sent = gate_b.pairs(sent)
    sent = down_b.pairs(sent)
    down_first_all = down_a.result(sent).reshape(-1, D)
    sent = gate_b.middle(down_first_all)
    sent = down_b.middle(sent)
    gate_first_all = gate_a.result(sent)
    sent = gate_b.outward(gate_first_all)
    sent = down_b.outward(sent)
    gate_grad, ffn_grad = join_units(gate_first_all, gate_b.result(sent), gate_up, ffn_norm)
    down_grad = jnp.concatenate(
        [down_first_all, down_b.result(sent).reshape(-1, D)], axis=0
    ).astype(jnp.float32)

    def lanes_back(rows):
        return rows.reshape(-1, shard_d, 128).transpose(1, 0, 2).reshape(shard_d, -1)

    in_total = lanes_back(terms_total[:in_rows])
    out_grad = lanes_back(terms_total[in_rows + 32 :])
    bias_span = in_bias.shape[0]
    bias_grad = lax.dynamic_slice_in_dim(
        terms_total[in_rows : in_rows + in_proj.shape[1] // 128].reshape(-1),
        fsdp_me * bias_span,
        bias_span,
    )
    in_grad = in_total * attn_norm[:, None]
    attn_grad = jnp.sum(in_total * in_proj.astype(jnp.float32), axis=1)
    return (
        block_out.astype(jnp.bfloat16).reshape(1, token_rows, D),
        tokens_grad.reshape(1, token_rows, D),
        attn_grad,
        ffn_grad,
        in_grad,
        bias_grad,
        out_grad,
        gate_grad,
        down_grad,
    )


def solution(mesh):
    in_specs = (
        P("fsdp", "ctx", None),
        P("fsdp", "ctx"),
        P("fsdp", "ctx", None),
        P("fsdp"),
        P("fsdp"),
        P("fsdp", None),
        P("fsdp"),
        P("fsdp", None),
        P("fsdp", None),
        P("fsdp", None),
    )
    out_specs = (
        P("fsdp", "ctx", None),
        P("fsdp", "ctx", None),
        P("fsdp"),
        P("fsdp"),
        P("fsdp", None),
        P("fsdp"),
        P("fsdp", None),
        P("fsdp", None),
        P("fsdp", None),
    )
    return jax.shard_map(shards, mesh=mesh, in_specs=in_specs, out_specs=out_specs, check_vma=False)
```

```python
import jax
import jax.numpy as jnp
from jax import lax
from jax.experimental import pallas as pl
from jax.experimental.pallas import tpu as pltpu
from jax.sharding import PartitionSpec as P

D = 1536
QUERY_HEADS = 12
KEY_VALUE_HEADS = 2
HEAD_SIZE = 128
FF = 8960
QD = QUERY_HEADS * HEAD_SIZE
KD = KEY_VALUE_HEADS * HEAD_SIZE
GROUP = QUERY_HEADS // KEY_VALUE_HEADS


norm_eps = 1e-06
rope_base = 1000000.0
masked_score = -1e30
score_scale = HEAD_SIZE ** (-0.5)
vmem_params = pltpu.CompilerParams(vmem_limit_bytes=48 * 1024 * 1024)


def rms_scale(value_rows):
    return value_rows * lax.rsqrt(
        jnp.mean(value_rows * value_rows, axis=-1, keepdims=True) + norm_eps
    )


def norm_backward(value_rows, incoming):
    unused_out, pullback = jax.vjp(rms_scale, value_rows)
    return pullback(incoming)[0]


def rotary_tables(position):
    lane = jnp.arange(HEAD_SIZE, dtype=jnp.int32)
    half = HEAD_SIZE // 2
    frequencies = rope_base ** (-((lane % half).astype(jnp.float32) * (2.0 / HEAD_SIZE)))
    angles = position.astype(jnp.float32)[:, None] * frequencies[None, :]
    sign = jnp.where(lane < half, -1.0, 1.0)
    return jnp.cos(angles), jnp.sin(angles) * sign[None, :]


def dot_f32(left, right):
    return jnp.dot(left, right, preferred_element_type=jnp.float32)


def dot_right_t(left, right):
    return lax.dot_general(
        left, right, (((1,), (1,)), ((), ())), preferred_element_type=jnp.float32
    )


def dot_left_t(left, right):
    return lax.dot_general(
        left, right, (((0,), (0,)), ((), ())), preferred_element_type=jnp.float32
    )


def add_low(left, right):
    return left + right


def after(value, *earlier):
    return lax.optimization_barrier((value, earlier))[0]


def exchange(value, mask):
    count = lax.axis_size("fsdp")
    return lax.ppermute(value, "fsdp", [(place, place ^ mask) for place in range(count)])


def gather_pieces(block, *gates):
    count = lax.axis_size("fsdp")
    if count != 8:
        found = [[block]] + [[exchange(block, mask)] for mask in range(2, count, 2)]
    else:
        half = block.shape[0] // 2
        by_x = exchange(block, 2)
        by_y = exchange(block, 4)
        other = exchange(block, 1)
        by_x, by_y = after((by_x, by_y), *gates)
        top = exchange(by_x[:half], 4)
        bottom = exchange(by_y[half:], 2)
        found = [[block], [by_x], [by_y], [top, bottom]]
        others = [[other], [exchange(by_x, 1)], [exchange(by_y, 1)]]
        others.append([exchange(top, 1), exchange(bottom, 1)])
        return [(2 * place, rows) for place, rows in enumerate(found)] + [
            (2 * place + 1, rows) for place, rows in enumerate(others)
        ]
    pieces = []
    for place, rows in enumerate(found):
        pieces.append((2 * place, rows))
        pieces.append((2 * place + 1, [exchange(part, 1) for part in rows]))
    return pieces


def gather_masks(block, *gates):
    count = lax.axis_size("fsdp")
    rows = block.shape[0]
    whole = jnp.zeros((count * rows, block.shape[1]), block.dtype)
    for mask, parts in gather_pieces(block, *gates):
        first = place_of(mask, count) * rows
        for part in parts:
            whole = lax.dynamic_update_slice(whole, part, (first, 0))
            first += part.shape[0]
    return whole


def gather_small(value):
    count = lax.axis_size("fsdp")
    me = lax.axis_index("fsdp")
    bits = count.bit_length() - 1
    found = value
    for bit in list(range(1, bits)) + [0]:
        got = exchange(found, 1 << bit)
        low = (me >> bit) % 2 == 0
        found = jnp.stack([jnp.where(low, found, got), jnp.where(low, got, found)])
    return jnp.moveaxis(found, 0, bits - 1).reshape(count, -1)


def place_of(mask, count):
    return mask // 2 + (1 - mask % 2) * (count // 2)


def mask_at(place, count):
    return jnp.where(place < count // 2, 2 * place + 1, 2 * place - count)


class MaskSum:
    def __init__(self, odd):
        self.got = exchange(odd, 1)

    def second(self, even, *gates):
        count = lax.axis_size("fsdp")
        self.kept = add_low(even, after(self.got, *gates))
        if count == 8:
            half = self.kept.shape[1] // 2
            self.by_x = exchange(self.kept[1::2, :half], 2)
            self.by_y = exchange(self.kept[2:, half:], 4)
        else:
            span = count
            while self.kept.shape[0] > 1:
                span //= 2
                half = self.kept.shape[0] // 2
                self.kept = add_low(self.kept[:half], exchange(self.kept[half:], span))
        return self.kept

    def third(self, *gates):
        if lax.axis_size("fsdp") != 8:
            return self.kept
        half = self.kept.shape[1] // 2
        by_x, by_y = after((self.by_x, self.by_y), *gates)
        self.top = add_low(self.kept[0::2, :half], by_x)
        self.bottom = add_low(self.kept[:2, half:], by_y)
        self.last_y = exchange(self.top[1], 4)
        self.last_x = exchange(self.bottom[1], 2)
        return self.top, self.bottom

    def result(self, *gates):
        if lax.axis_size("fsdp") != 8:
            return self.kept[0]
        last_y, last_x = after((self.last_y, self.last_x), *gates)
        return jnp.concatenate(
            [add_low(self.top[0], last_y), add_low(self.bottom[0], last_x)], axis=0
        )


def swap_blocks(blocks):
    return lax.all_to_all(blocks, "fsdp", 0, 0, tiled=True)


def ctx_scatter(terms):
    return lax.psum_scatter(terms, "ctx", scatter_dimension=0, tiled=True)


def ctx_swap(terms):
    count = lax.axis_size("ctx")
    return lax.all_to_all(
        terms.reshape(count, terms.shape[0] // count, -1), "ctx", 0, 0, tiled=True
    )


def sum_blocks(blocks):
    return jnp.sum(blocks.astype(jnp.float32), axis=0).astype(jnp.bfloat16)


class CtxGather:
    def __init__(self, block):
        self.block = block
        self.four = lax.axis_size("ctx") == 4

    def pairs(self, *gates):
        if not self.four:
            return self.block
        self.block = after(self.block, *gates)
        self.got = lax.ppermute(self.block, "ctx", [(0, 1), (1, 0), (2, 3), (3, 2)])
        return self.block

    def middle(self, *gates):
        if not self.four:
            return self.block
        even = lax.axis_index("ctx") % 2 == 0
        got = after(self.got, *gates)
        self.pair = jnp.stack(
            [jnp.where(even, self.block, got), jnp.where(even, got, self.block)]
        )
        self.crossed = lax.ppermute(self.pair, "ctx", [(1, 2), (2, 1)])
        return self.pair

    def outward(self, *gates):
        if not self.four:
            return self.block
        self.crossed = after(self.crossed, *gates)
        self.passed = lax.ppermute(self.crossed, "ctx", [(1, 0), (2, 3)])
        return self.crossed

    def result(self, *gates):
        me = lax.axis_index("ctx")
        if self.four:
            other = jnp.where((me == 0) | (me == 3), after(self.passed, *gates), self.crossed)
            return jnp.concatenate(
                [jnp.where(me < 2, self.pair, other), jnp.where(me < 2, other, self.pair)]
            )
        return lax.all_gather(after(self.block, *gates), "ctx", axis=0)


def unit_widths(units):
    first = units // 256 * 128
    second = units - first
    return first, second, -(-second // 128) * 128


def split_units(me, gate_up, gain, count):
    rows, columns = gate_up.shape
    span = columns // 2
    units = span // count
    first, second, padded = unit_widths(units)
    block = 48

    def kernel(me_ref, weight_ref, gain_ref, first_ref, second_ref):
        def scaled(begin, end):
            value = weight_ref[:, begin:end].astype(jnp.float32) * gain_ref[...]
            return value.astype(gate_up.dtype)

        for owner in range(count):
            for side in range(2):
                begin = side * span + owner * units
                place = place_of(me_ref[0] ^ owner, count)
                first_ref[place, :, side * first : (side + 1) * first] = scaled(
                    begin, begin + first
                )
                second_ref[owner, :, side * padded : side * padded + second] = scaled(
                    begin + first, begin + units
                )
                if padded > second:
                    second_ref[
                        owner, :, side * padded + second : (side + 1) * padded
                    ] = jnp.zeros((block, padded - second), gate_up.dtype)

    return pl.pallas_call(
        kernel,
        grid_spec=pltpu.PrefetchScalarGridSpec(
            num_scalar_prefetch=1,
            grid=(rows // block,),
            in_specs=[
                pl.BlockSpec((block, columns), lambda step, me_ref: (step, 0)),
                pl.BlockSpec((block, 1), lambda step, me_ref: (step, 0)),
            ],
            out_specs=[
                pl.BlockSpec((count, block, 2 * first), lambda step, me_ref: (0, step, 0)),
                pl.BlockSpec((count, block, 2 * padded), lambda step, me_ref: (0, step, 0)),
            ],
        ),
        out_shape=[
            jax.ShapeDtypeStruct((count, rows, 2 * first), gate_up.dtype),
            jax.ShapeDtypeStruct((count, rows, 2 * padded), gate_up.dtype),
        ],
        compiler_params=vmem_params,
        cost_estimate=pl.CostEstimate(
            flops=0, bytes_accessed=4 * rows * columns, transcendentals=0
        ),
    )(me, gate_up, gain[:, None])


def join_units(first_part, second_part, gate_up, gain):
    rows, columns = gate_up.shape
    if first_part.shape[2] % 16:
        first_part, second_part = (
            part.transpose(1, 0, 2, 3)
            .reshape(part.shape[1], rows // 48, 48, -1)
            .transpose(1, 0, 2, 3)
            for part in (first_part, second_part)
        )
    pieces, count, block = first_part.shape[:3]
    span = columns // 2
    units = span // count
    first, second, padded = unit_widths(units)

    def kernel(first_ref, second_ref, weight_ref, gain_ref, whole_ref, sums_ref):
        for owner in range(count):
            for side in range(2):
                begin = side * span + owner * units
                whole_ref[:, begin : begin + first] = first_ref[
                    0, owner, :, side * first : (side + 1) * first
                ].astype(jnp.float32)
                whole_ref[:, begin + first : begin + units] = second_ref[
                    0, owner, :, side * padded : side * padded + second
                ].astype(jnp.float32)
        whole = whole_ref[...]
        total = jnp.sum(whole * weight_ref[...].astype(jnp.float32), axis=1, keepdims=True)
        sums_ref[...] = jnp.broadcast_to(total, (block, 128))
        whole_ref[...] = whole * gain_ref[...]

    whole, sums = pl.pallas_call(
        kernel,
        grid=(pieces,),
        in_specs=[
            pl.BlockSpec((1, count, block, 2 * first), lambda step: (step, 0, 0, 0)),
            pl.BlockSpec((1, count, block, 2 * padded), lambda step: (step, 0, 0, 0)),
            pl.BlockSpec((block, columns), lambda step: (step, 0)),
            pl.BlockSpec((block, 1), lambda step: (step, 0)),
        ],
        out_specs=[
            pl.BlockSpec((block, columns), lambda step: (step, 0)),
            pl.BlockSpec((block, 128), lambda step: (step, 0)),
        ],
        out_shape=[
            jax.ShapeDtypeStruct((rows, columns), jnp.float32),
            jax.ShapeDtypeStruct((rows, 128), jnp.float32),
        ],
        compiler_params=vmem_params,
        cost_estimate=pl.CostEstimate(
            flops=2 * rows * columns, bytes_accessed=8 * rows * columns, transcendentals=0
        ),
    )(first_part, second_part, gate_up, gain[:, None])
    return whole, sums[:, 0]


def place_rows(me_ref, pieces, refs, weight_ref):
    place = 0
    for mask, parts in pieces:
        shard = sum(part.shape[0] for part in parts)
        begin = (me_ref[0] ^ mask) * shard
        for part in parts:
            rows = part.shape[0]
            weight_ref[pl.ds(pl.multiple_of(begin, rows), rows)] = refs[place][...]
            begin = begin + rows
            place += 1


def project(me, normed, pieces, bias, cosine, sine):
    tokens = normed.shape[0]
    width = bias.shape[0]
    block = 512
    flat = [part for unused_mask, parts in pieces for part in parts]

    def kernel(me_ref, normed_ref, bias_ref, cosine_ref, sine_ref, *refs):
        out_ref, weight_ref = refs[len(flat) :]
        place_rows(me_ref, pieces, refs, weight_ref)
        product = dot_f32(normed_ref[...], weight_ref[...]) + bias_ref[...]
        for head in range(block // HEAD_SIZE):
            lanes = slice(head * HEAD_SIZE, (head + 1) * HEAD_SIZE)
            plain = product[:, lanes]
            turned = plain * cosine_ref[...] + pltpu.roll(plain, HEAD_SIZE // 2, 1) * sine_ref[...]
            column = pl.program_id(0) * block + head * HEAD_SIZE
            out_ref[:, lanes] = jnp.where(column < QD + KD, turned, plain).astype(jnp.bfloat16)

    return pl.pallas_call(
        kernel,
        grid_spec=pltpu.PrefetchScalarGridSpec(
            num_scalar_prefetch=1,
            grid=(width // block,),
            in_specs=[
                pl.BlockSpec((tokens, D), lambda step, me_ref: (0, 0)),
                pl.BlockSpec((1, block), lambda step, me_ref: (0, step)),
                pl.BlockSpec((tokens, HEAD_SIZE), lambda step, me_ref: (0, 0)),
                pl.BlockSpec((tokens, HEAD_SIZE), lambda step, me_ref: (0, 0)),
            ]
            + [
                pl.BlockSpec((part.shape[0], block), lambda step, me_ref: (0, step))
                for part in flat
            ],
            out_specs=pl.BlockSpec((tokens, block), lambda step, me_ref: (0, step)),
            scratch_shapes=[pltpu.VMEM((D, block), jnp.bfloat16)],
        ),
        out_shape=jax.ShapeDtypeStruct((tokens, width), jnp.bfloat16),
        compiler_params=vmem_params,
        cost_estimate=pl.CostEstimate(
            flops=2 * tokens * D * width, bytes_accessed=2 * D * width, transcendentals=0
        ),
    )(me, normed, bias[None], cosine, sine, *flat)


def project_back(me, grad_projected, pieces):
    tokens, width = grad_projected.shape
    flat = [part for unused_mask, parts in pieces for part in parts]

    def kernel(me_ref, grad_ref, *refs):
        out_ref, weight_ref = refs[len(flat) :]
        place_rows(me_ref, pieces, refs, weight_ref)
        out_ref[...] = dot_right_t(grad_ref[...], weight_ref[...])

    whole = lambda part: pl.BlockSpec(part.shape, lambda step, me_ref: (0, 0))
    return pl.pallas_call(
        kernel,
        grid_spec=pltpu.PrefetchScalarGridSpec(
            num_scalar_prefetch=1,
            grid=(1,),
            in_specs=[whole(grad_projected)] + [whole(part) for part in flat],
            out_specs=pl.BlockSpec((tokens, D), lambda step, me_ref: (0, 0)),
            scratch_shapes=[pltpu.VMEM((D, width), jnp.bfloat16)],
        ),
        out_shape=jax.ShapeDtypeStruct((tokens, D), jnp.float32),
        compiler_params=vmem_params,
        cost_estimate=pl.CostEstimate(
            flops=2 * tokens * D * width, bytes_accessed=2 * D * width, transcendentals=0
        ),
    )(me, grad_projected, *flat)


def fill_bias(at_ref, position_ref, bias_ref):
    tokens, keys = bias_ref.shape
    row = lax.broadcasted_iota(jnp.int32, (tokens, keys), 0)
    column = lax.broadcasted_iota(jnp.int32, (tokens, keys), 1)
    back = column // tokens
    query_index = at_ref[0] * tokens + row
    key_index = (at_ref[0] - back) * tokens + (column - back * tokens)
    allowed = (key_index <= query_index) & (key_index >= query_index - position_ref[...])
    bias_ref[...] = jnp.where(allowed, 0.0, masked_score)


def join_keys(refs, key_ref, value_ref):
    @pl.when(pl.program_id(0) % GROUP == 0)
    def _():
        for place in range(len(refs)):
            tokens = refs[0].shape[0]
            if (place + 1) * tokens > key_ref.shape[0]:
                break
            rows = slice(place * tokens, (place + 1) * tokens)
            key_ref[rows] = refs[2 * place][...]
            value_ref[rows] = refs[2 * place + 1][...]


def key_specs(both_pieces):
    specs = []
    for piece in both_pieces:
        shape = (piece.shape[0], HEAD_SIZE)
        specs.append(pl.BlockSpec(shape, lambda head, at: (0, head // GROUP)))
        specs.append(pl.BlockSpec(shape, lambda head, at: (0, KEY_VALUE_HEADS + head // GROUP)))
    return specs


def attend(at, position, projected, both_pieces):
    tokens = projected.shape[0]
    count = len(both_pieces)
    keys = count * tokens

    def kernel(at_ref, position_ref, query_ref, *refs):
        out_ref, turn_ref, log_ref, bias_ref, key_ref, value_ref = refs[2 * count :]

        @pl.when(pl.program_id(0) == 0)
        def _():
            fill_bias(at_ref, position_ref, bias_ref)

        join_keys(refs, key_ref, value_ref)

        scores = dot_right_t(query_ref[...], key_ref[...]) * score_scale + bias_ref[...]
        top = jnp.max(scores, axis=1, keepdims=True)
        raised = jnp.exp(scores - top)
        total = jnp.sum(raised, axis=1, keepdims=True)
        probs = (raised * (1.0 / total)).astype(jnp.bfloat16)
        result = dot_f32(probs, value_ref[...])
        out_ref[...] = result.astype(jnp.bfloat16)
        turn_ref[...] = result.T.astype(jnp.bfloat16)
        log_ref[0] = top + jnp.log(total)

    return pl.pallas_call(
        kernel,
        grid_spec=pltpu.PrefetchScalarGridSpec(
            num_scalar_prefetch=1,
            grid=(QUERY_HEADS,),
            in_specs=[
                pl.BlockSpec((tokens, 1), lambda head, at: (0, 0)),
                pl.BlockSpec((tokens, HEAD_SIZE), lambda head, at: (0, head)),
            ]
            + key_specs(both_pieces),
            out_specs=[
                pl.BlockSpec((tokens, HEAD_SIZE), lambda head, at: (0, head)),
                pl.BlockSpec((HEAD_SIZE, tokens), lambda head, at: (head, 0)),
                pl.BlockSpec((1, tokens, 1), lambda head, at: (head, 0, 0)),
            ],
            scratch_shapes=[
                pltpu.VMEM((tokens, keys), jnp.float32),
                pltpu.VMEM((keys, HEAD_SIZE), jnp.bfloat16),
                pltpu.VMEM((keys, HEAD_SIZE), jnp.bfloat16),
            ],
        ),
        out_shape=[
            jax.ShapeDtypeStruct((tokens, QD), jnp.bfloat16),
            jax.ShapeDtypeStruct((QD, tokens), jnp.bfloat16),
            jax.ShapeDtypeStruct((QUERY_HEADS, tokens, 1), jnp.float32),
        ],
        compiler_params=vmem_params,
        cost_estimate=pl.CostEstimate(
            flops=8 * tokens * keys * QD,
            bytes_accessed=8 * tokens * QD,
            transcendentals=QUERY_HEADS * tokens * keys,
        ),
    )(at, position, projected, *[piece for piece in both_pieces for unused in range(2)])


def attend_backward(at, position, projected, both_pieces, incoming, log_total, cosine, sine):
    tokens = projected.shape[0]
    count = len(both_pieces)
    keys = count * tokens

    def kernel(
        at_ref,
        position_ref,
        query_ref,
        incoming_ref,
        log_ref,
        cosine_ref,
        sine_ref,
        *refs,
    ):
        query_grad_ref, key_grad_ref, value_grad_ref = refs[2 * count : 2 * count + 3]
        bias_ref, key_total, value_total, key_ref, value_ref = refs[2 * count + 3 :]
        head = pl.program_id(0)
        join_keys(refs, key_ref, value_ref)

        @pl.when(head == 0)
        def _():
            fill_bias(at_ref, position_ref, bias_ref)

        @pl.when(head % GROUP == 0)
        def _():
            key_total[...] = jnp.zeros_like(key_total)
            value_total[...] = jnp.zeros_like(value_total)

        scores = dot_right_t(query_ref[...], key_ref[...]) * score_scale + bias_ref[...]
        probs = jnp.exp(scores - log_ref[0])
        grad_probs = dot_right_t(incoming_ref[...], value_ref[...])
        inner = jnp.sum(grad_probs * probs, axis=1, keepdims=True)
        grad_scores = (probs * (grad_probs - inner)).astype(jnp.bfloat16)
        value_total[...] += dot_left_t(incoming_ref[...], probs.astype(jnp.bfloat16))
        key_total[...] += dot_left_t(query_ref[...], grad_scores)
        plain = dot_f32(grad_scores, key_ref[...]) * score_scale
        query_grad_ref[...] = (
            plain * cosine_ref[...] - pltpu.roll(plain, HEAD_SIZE // 2, 1) * sine_ref[...]
        ).astype(jnp.bfloat16)

        @pl.when(head % GROUP == GROUP - 1)
        def _():
            key_grad_ref[...] = (key_total[...] * score_scale).T
            value_grad_ref[...] = value_total[...].T

    return pl.pallas_call(
        kernel,
        grid_spec=pltpu.PrefetchScalarGridSpec(
            num_scalar_prefetch=1,
            grid=(QUERY_HEADS,),
            in_specs=[
                pl.BlockSpec((tokens, 1), lambda head, at: (0, 0)),
                pl.BlockSpec((tokens, HEAD_SIZE), lambda head, at: (0, head)),
                pl.BlockSpec((tokens, HEAD_SIZE), lambda head, at: (0, head)),
                pl.BlockSpec((1, tokens, 1), lambda head, at: (head, 0, 0)),
                pl.BlockSpec((tokens, HEAD_SIZE), lambda head, at: (0, 0)),
                pl.BlockSpec((tokens, HEAD_SIZE), lambda head, at: (0, 0)),
            ]
            + key_specs(both_pieces),
            out_specs=[
                pl.BlockSpec((tokens, HEAD_SIZE), lambda head, at: (0, head)),
                pl.BlockSpec((keys, HEAD_SIZE), lambda head, at: (0, head // GROUP)),
                pl.BlockSpec((keys, HEAD_SIZE), lambda head, at: (0, head // GROUP)),
            ],
            scratch_shapes=[
                pltpu.VMEM((tokens, keys), jnp.float32),
                pltpu.VMEM((HEAD_SIZE, keys), jnp.float32),
                pltpu.VMEM((HEAD_SIZE, keys), jnp.float32),
                pltpu.VMEM((keys, HEAD_SIZE), jnp.bfloat16),
                pltpu.VMEM((keys, HEAD_SIZE), jnp.bfloat16),
            ],
        ),
        out_shape=[
            jax.ShapeDtypeStruct((tokens, QD), jnp.bfloat16),
            jax.ShapeDtypeStruct((keys, KD), jnp.float32),
            jax.ShapeDtypeStruct((keys, KD), jnp.float32),
        ],
        compiler_params=vmem_params,
        cost_estimate=pl.CostEstimate(
            flops=20 * tokens * keys * QD,
            bytes_accessed=8 * tokens * QD,
            transcendentals=QUERY_HEADS * tokens * keys,
        ),
    )(
        at,
        position,
        projected,
        incoming,
        log_total,
        cosine,
        sine,
        *[piece for piece in both_pieces for unused in range(2)],
    )


def unit_part(me, normed_all, grad_out_all, gate_up, down, count, first):
    tokens = normed_all.shape[0]
    block = tokens // count
    width = down.shape[0]
    shard = D // count
    weights = list(gate_up) if first else [gate_up]

    def kernel(me_ref, normed_ref, out_grad_ref, down_ref, *refs):
        weight_refs = refs[: len(weights)]
        hidden_ref, grad_ref = refs[len(weights) : len(weights) + 2]
        weight_ref = weight_refs[0]
        if first:
            ordered_ref, weight_ref = refs[len(weights) + 2 :]
            ordered_ref[...] = out_grad_ref[...]

            @pl.when(pl.program_id(0) == 0)
            def _():
                mask = 0
                for ref in weight_refs:
                    for block_index in range(ref.shape[0]):
                        begin = pl.multiple_of((me_ref[0] ^ mask) * shard, shard)
                        weight_ref[pl.ds(begin, shard)] = ref[block_index]
                        mask += 1

        values = dot_f32(normed_ref[...], weight_ref[...])
        gate = values[:, :width]
        up = values[:, width:]
        grad_hidden = dot_right_t(out_grad_ref[...], down_ref[...])
        share = 1.0 / (1.0 + jnp.exp(-gate))
        passed = gate * share
        hidden_ref[...] = (passed * up).astype(jnp.bfloat16)
        grad_ref[:, :width] = (
            grad_hidden * up * share * (1.0 + gate * (1.0 - share))
        ).astype(jnp.bfloat16)
        grad_ref[:, width:] = (grad_hidden * passed).astype(jnp.bfloat16)

    def out_grad_index(step, me_ref):
        return (me_ref[0] ^ mask_at(step, count), 0) if first else (step, 0)

    row = lambda step, me_ref: (step, 0)
    fixed = lambda step, me_ref: (0, 0)
    out_specs = [pl.BlockSpec((block, width), row), pl.BlockSpec((block, 2 * width), row)]
    out_shape = [
        jax.ShapeDtypeStruct((tokens, width), jnp.bfloat16),
        jax.ShapeDtypeStruct((tokens, 2 * width), jnp.bfloat16),
    ]
    if first:
        out_specs += [pl.BlockSpec((block, D), row), pl.BlockSpec((D, 2 * width), fixed)]
        out_shape += [
            jax.ShapeDtypeStruct((tokens, D), jnp.bfloat16),
            jax.ShapeDtypeStruct((D, 2 * width), jnp.bfloat16),
        ]
    return pl.pallas_call(
        kernel,
        grid_spec=pltpu.PrefetchScalarGridSpec(
            num_scalar_prefetch=1,
            grid=(count,),
            in_specs=[
                pl.BlockSpec((block, D), row),
                pl.BlockSpec((block, D), out_grad_index),
                pl.BlockSpec((width, D), fixed),
            ]
            + [
                pl.BlockSpec(weight.shape, lambda step, me_ref, dims=weight.ndim: (0,) * dims)
                for weight in weights
            ],
            out_specs=out_specs,
        ),
        out_shape=out_shape,
        compiler_params=vmem_params,
        cost_estimate=pl.CostEstimate(
            flops=6 * tokens * D * width,
            bytes_accessed=4 * tokens * D + 6 * tokens * width + 6 * D * width,
            transcendentals=tokens * width,
        ),
    )(me, normed_all, grad_out_all, down, *weights)


def row_terms(me, turned, right, rows_out):
    count, shard, tokens = turned.shape
    width = right.shape[1]
    lanes = width // 128
    half = count // 2
    spare = rows_out - shard * lanes

    def kernel(me_ref, turned_ref, right_ref, odd_ref, even_ref, *scratch):
        step = pl.program_id(0)
        if spare:

            @pl.when(step == 0)
            def _():
                sums = jnp.sum(right_ref[...].astype(jnp.float32), axis=0, keepdims=True)
                scratch[0][...] = jnp.zeros_like(scratch[0])
                for group in range(lanes):
                    scratch[0][group : group + 1] = sums[:, group * 128 : (group + 1) * 128]

        term = dot_f32(turned_ref[0], right_ref[...]).astype(jnp.bfloat16)

        def store(out_ref):
            for group in range(lanes):
                out_ref[0, group * shard : (group + 1) * shard] = term[
                    :, group * 128 : (group + 1) * 128
                ]
            if spare:
                out_ref[0, lanes * shard :] = scratch[0][...].astype(jnp.bfloat16)

        pl.when(step < half)(lambda: store(odd_ref))
        pl.when(step >= half)(lambda: store(even_ref))

    out = jax.ShapeDtypeStruct((half, rows_out, 128), jnp.bfloat16)
    return pl.pallas_call(
        kernel,
        grid_spec=pltpu.PrefetchScalarGridSpec(
            num_scalar_prefetch=1,
            grid=(count,),
            in_specs=[
                pl.BlockSpec(
                    (1, shard, tokens),
                    lambda step, me_ref: (me_ref[0] ^ mask_at(step, count), 0, 0),
                ),
                pl.BlockSpec((tokens, width), lambda step, me_ref: (0, 0)),
            ],
            out_specs=[
                pl.BlockSpec(
                    (1, rows_out, 128), lambda step, me_ref: (jnp.minimum(step, half - 1), 0, 0)
                ),
                pl.BlockSpec(
                    (1, rows_out, 128), lambda step, me_ref: (jnp.maximum(step - half, 0), 0, 0)
                ),
            ],
            scratch_shapes=[pltpu.VMEM((spare, 128), jnp.float32)] if spare else [],
        ),
        out_shape=[out, out],
        compiler_params=vmem_params,
        cost_estimate=pl.CostEstimate(
            flops=2 * D * tokens * width,
            bytes_accessed=256 * count * rows_out,
            transcendentals=0,
        ),
    )(me, turned, right)


def shards(
    tokens,
    positions,
    cotangent,
    attn_norm,
    ffn_norm,
    in_proj,
    in_bias,
    out_proj,
    gate_up,
    down_proj,
):
    token_rows = tokens.shape[1]
    fsdp_count = lax.axis_size("fsdp")
    ctx_count = lax.axis_size("ctx")
    fsdp_me = lax.axis_index("fsdp")
    me = fsdp_me.astype(jnp.int32)[None]
    at = lax.axis_index("ctx").astype(jnp.int32)[None]
    units = FF // fsdp_count
    shard_d = D // fsdp_count
    residual_in = tokens[0].astype(jnp.float32)
    position = positions[0]
    grad_out_b = cotangent[0]

    first_units, second_units, padded_units = unit_widths(units)
    bias_full = gather_small(in_bias).reshape(-1)
    in_scaled = (in_proj.astype(jnp.float32) * attn_norm[:, None]).astype(jnp.bfloat16)
    first_blocks, second_blocks = split_units(me, gate_up, ffn_norm, fsdp_count)
    cosine, sine = rotary_tables(position)
    normed_b = rms_scale(residual_in).astype(jnp.bfloat16)
    in_pieces = gather_pieces(in_scaled, first_blocks, cosine, normed_b)
    half = fsdp_count // 2
    by_other = exchange(after(first_blocks[:half], in_pieces[0], in_pieces[2], in_pieces[4]), 1)
    gate_up_first = [first_blocks[half][None], by_other[0][None]] + [
        exchange(jnp.stack([first_blocks[half + place], by_other[place]]), 2 * place)
        for place in range(1, half)
    ]
    out_full = lax.all_gather(after(out_proj, in_pieces), "fsdp", axis=0, tiled=True)

    projected = project(
        me, after(normed_b, gate_up_first[2]), in_pieces, bias_full, cosine, sine
    )
    both_b = projected[:, QD:]
    both_pieces = [both_b] + [
        lax.ppermute(both_b, "ctx", [(s, s + back) for s in range(ctx_count - back)])
        for back in range(1, ctx_count)
    ]
    grad_out_all = lax.all_gather(after(grad_out_b, projected), "fsdp", axis=0, tiled=True)
    both_pieces = after(both_pieces, gate_up_first[3])
    attended_b, attended_turned, log_total = attend(at, position[:, None], projected, both_pieces)
    attended_b = after(attended_b, gate_up_first)
    middle = residual_in + dot_f32(attended_b, out_full)
    normed_ffn_b = rms_scale(middle).astype(jnp.bfloat16)
    normed_again, down_again = after((normed_b, down_proj), normed_ffn_b)
    normed_turned = normed_again.T.reshape(fsdp_count, shard_d, token_rows)
    down_first = down_again[:first_units]
    down_second = jnp.pad(down_again[first_units:], ((0, padded_units - second_units), (0, 0)))

    normed_ffn_all = gather_masks(normed_ffn_b, normed_turned, down_first, down_second)
    gate_up_second = swap_blocks(after(second_blocks, normed_ffn_all)).reshape(
        D, 2 * padded_units
    )
    hidden_first, grad_first, grad_out_all, gate_up_first = unit_part(
        me, normed_ffn_all, grad_out_all, gate_up_first, down_first, fsdp_count, True
    )
    odd_rows = normed_ffn_all.shape[0] // 2

    def down_term(hidden, *gates):
        return dot_left_t(after(hidden, *gates), grad_out_all).astype(jnp.bfloat16)

    def gate_term(grad, *gates):
        term = dot_left_t(normed_ffn_all, after(grad, *gates)).astype(jnp.bfloat16)
        return (
            term.reshape(fsdp_count, ctx_count, shard_d // ctx_count, -1)
            .transpose(1, 0, 2, 3)
            .reshape(D, -1)
        )

    def gate_swap(summed):
        return swap_blocks(summed.reshape(fsdp_count, shard_d // ctx_count, -1))

    def input_grads(rows, *gates):
        return (
            (
                dot_right_t(after(grad_first, *gates)[rows], gate_up_first)
                + dot_right_t(grad_second[rows], gate_up_second)
            )
            .astype(jnp.bfloat16)
            .reshape(fsdp_count // 2, token_rows, D)
        )

    def down_outs(rows, *gates):
        return (
            (
                dot_f32(after(hidden_first, *gates)[rows], down_first)
                + dot_f32(hidden_second[rows], down_second)
            )
            .astype(jnp.bfloat16)
            .reshape(fsdp_count // 2, token_rows, D)
        )

    gate_term_a = gate_term(grad_first, hidden_first)
    gate_sum_a = ctx_scatter(gate_term_a)
    down_term_a = down_term(hidden_first, gate_term_a)
    down_swap_a = ctx_swap(down_term_a)
    hidden_second, grad_second = unit_part(
        me,
        after(normed_ffn_all, down_term_a),
        grad_out_all,
        gate_up_second,
        down_second,
        fsdp_count,
        False,
    )
    grad_normed_odd = input_grads(slice(0, odd_rows), hidden_second)
    normed_sum = MaskSum(grad_normed_odd)
    grad_normed_even = input_grads(slice(odd_rows, None), grad_normed_odd)
    sent = normed_sum.second(grad_normed_even)
    down_a = CtxGather(sum_blocks(after(down_swap_a, sent)))
    sent = down_a.pairs()
    gate_term_b = gate_term(grad_second, sent)
    gate_sum_b = ctx_scatter(after(gate_term_b, gate_term_a))
    sent = normed_sum.third(gate_term_b)
    sent = down_a.middle(sent)
    down_term_b = down_term(hidden_second, sent)[:second_units]
    gate_swapped_a = gate_swap(after(gate_sum_a, down_term_b))
    grad_normed_ffn = normed_sum.result(down_term_b).astype(jnp.float32)

    grad_out = grad_out_b.astype(jnp.float32)
    grad_middle = grad_out + norm_backward(middle, grad_normed_ffn)
    grad_middle_b = grad_middle.astype(jnp.bfloat16)
    grad_attended_b = dot_right_t(grad_middle_b, out_full).astype(jnp.bfloat16)
    in_rows = shard_d * in_proj.shape[1] // 128
    out_rows = shard_d * D // 128
    out_odd, out_even = row_terms(
        me,
        attended_turned.reshape(fsdp_count, shard_d, token_rows),
        after(grad_middle_b, grad_attended_b),
        out_rows,
    )
    sent = down_a.outward(out_even)
    gate_a = CtxGather(gate_swapped_a)
    sent = gate_a.pairs(sent)
    out_sum = MaskSum(out_odd)
    query_grad, key_grads, value_grads = attend_backward(
        at,
        position[:, None],
        projected,
        both_pieces,
        after(grad_attended_b, sent),
        log_total,
        cosine,
        sine,
    )
    both_sent = [
        lax.ppermute(
            jnp.concatenate(
                [
                    grads[back * token_rows : (back + 1) * token_rows].astype(jnp.bfloat16)
                    for grads in (key_grads, value_grads)
                ],
                axis=1,
            ),
            "ctx",
            [(s + back, s) for s in range(ctx_count - back)],
        )
        for back in range(1, ctx_count)
    ]
    sent = out_sum.second(out_even, query_grad)
    down_odd = down_outs(slice(0, odd_rows), sent)
    block_sum = MaskSum(down_odd)
    sent = out_sum.third(down_odd)
    down_even = down_outs(slice(odd_rows, None), sent)
    both_grad = jnp.concatenate([key_grads[:token_rows], value_grads[:token_rows]], axis=1)
    for piece in after(both_sent, down_even):
        both_grad = both_grad + piece.astype(jnp.float32)
    turned_back = []
    for head in range(KEY_VALUE_HEADS):
        plain = both_grad[:, head * HEAD_SIZE : (head + 1) * HEAD_SIZE]
        turned_back.append(plain * cosine - jnp.roll(plain, HEAD_SIZE // 2, axis=1) * sine)
    grad_projected_b = jnp.concatenate(
        [query_grad]
        + [part.astype(jnp.bfloat16) for part in turned_back]
        + [both_grad[:, KD:].astype(jnp.bfloat16)],
        axis=1,
    )
    in_odd, in_even = row_terms(me, normed_turned, grad_projected_b, in_rows + 32)
    in_sum = MaskSum(in_odd)
    down_swap_b = ctx_swap(after(down_term_b, in_even))
    grad_normed = project_back(me, after(grad_projected_b, in_even), in_pieces)
    sent = in_sum.second(in_even, grad_normed)
    sent = gate_a.middle(sent)
    tokens_grad = grad_middle + norm_backward(residual_in, after(grad_normed, sent))
    sent = block_sum.second(down_even, tokens_grad)
    sent = in_sum.third(sent)
    gate_swapped_b = gate_swap(after(gate_sum_b, sent))
    sent = gate_a.outward(sent)
    terms_part = jnp.concatenate([in_sum.result(sent), out_sum.result(sent)], axis=0)
    terms_total = lax.psum(terms_part, "ctx")
    down_b = CtxGather(sum_blocks(after(down_swap_b, terms_part)))
    gate_b = CtxGather(gate_swapped_b)
    sent = gate_b.pairs(terms_part)
    sent = block_sum.third(sent)
    sent = down_b.pairs(sent)
    sent = gate_b.middle(sent)
    block_out = middle + block_sum.result(sent).astype(jnp.float32)
    sent = down_b.middle(block_out)
    down_first_all = down_a.result(sent).reshape(-1, D)
    gate_first_all = gate_a.result(down_first_all)
    sent = gate_b.outward(gate_first_all)
    sent = down_b.outward(sent)
    gate_grad, ffn_grad = join_units(gate_first_all, gate_b.result(sent), gate_up, ffn_norm)
    down_grad = jnp.concatenate(
        [down_first_all, down_b.result(sent).reshape(-1, D)], axis=0
    ).astype(jnp.float32)
    terms_total = terms_total.astype(jnp.float32)

    def lanes_back(rows):
        return rows.reshape(-1, shard_d, 128).transpose(1, 0, 2).reshape(shard_d, -1)

    in_total = lanes_back(terms_total[:in_rows])
    out_grad = lanes_back(terms_total[in_rows + 32 :])
    bias_span = in_bias.shape[0]
    bias_grad = lax.dynamic_slice_in_dim(
        terms_total[in_rows : in_rows + in_proj.shape[1] // 128].reshape(-1),
        fsdp_me * bias_span,
        bias_span,
    )
    in_grad = in_total * attn_norm[:, None]
    attn_grad = jnp.sum(in_total * in_proj.astype(jnp.float32), axis=1)
    return (
        block_out.astype(jnp.bfloat16).reshape(1, token_rows, D),
        tokens_grad.reshape(1, token_rows, D),
        attn_grad,
        ffn_grad,
        in_grad,
        bias_grad,
        out_grad,
        gate_grad,
        down_grad,
    )


def solution(mesh):
    in_specs = (
        P("fsdp", "ctx", None),
        P("fsdp", "ctx"),
        P("fsdp", "ctx", None),
        P("fsdp"),
        P("fsdp"),
        P("fsdp", None),
        P("fsdp"),
        P("fsdp", None),
        P("fsdp", None),
        P("fsdp", None),
    )
    out_specs = (
        P("fsdp", "ctx", None),
        P("fsdp", "ctx", None),
        P("fsdp"),
        P("fsdp"),
        P("fsdp", None),
        P("fsdp"),
        P("fsdp", None),
        P("fsdp", None),
        P("fsdp", None),
    )
    return jax.shard_map(shards, mesh=mesh, in_specs=in_specs, out_specs=out_specs, check_vma=False)
```

```python
import jax
import jax.numpy as jnp
from jax import lax
from jax.experimental import pallas as pl
from jax.experimental.pallas import tpu as pltpu
from jax.sharding import PartitionSpec as P

D = 1536
QUERY_HEADS = 12
KEY_VALUE_HEADS = 2
HEAD_SIZE = 128
FF = 8960
QD = QUERY_HEADS * HEAD_SIZE
KD = KEY_VALUE_HEADS * HEAD_SIZE
GROUP = QUERY_HEADS // KEY_VALUE_HEADS


norm_eps = 1e-06
rope_base = 1000000.0
masked_score = -1e30
score_scale = HEAD_SIZE ** (-0.5)
vmem_params = pltpu.CompilerParams(vmem_limit_bytes=48 * 1024 * 1024)


def rms_scale(value_rows):
    return value_rows * lax.rsqrt(
        jnp.mean(value_rows * value_rows, axis=-1, keepdims=True) + norm_eps
    )


def norm_backward(value_rows, incoming):
    unused_out, pullback = jax.vjp(rms_scale, value_rows)
    return pullback(incoming)[0]


def rotary_tables(position):
    lane = jnp.arange(HEAD_SIZE, dtype=jnp.int32)
    half = HEAD_SIZE // 2
    frequencies = rope_base ** (-((lane % half).astype(jnp.float32) * (2.0 / HEAD_SIZE)))
    angles = position.astype(jnp.float32)[:, None] * frequencies[None, :]
    sign = jnp.where(lane < half, -1.0, 1.0)
    return jnp.cos(angles), jnp.sin(angles) * sign[None, :]


def dot_f32(left, right):
    return jnp.dot(left, right, preferred_element_type=jnp.float32)


def dot_right_t(left, right):
    return lax.dot_general(
        left, right, (((1,), (1,)), ((), ())), preferred_element_type=jnp.float32
    )


def dot_left_t(left, right):
    return lax.dot_general(
        left, right, (((0,), (0,)), ((), ())), preferred_element_type=jnp.float32
    )


def add_low(left, right):
    return left + right


def after(value, *earlier):
    return lax.optimization_barrier((value, earlier))[0]


def exchange(value, mask):
    count = lax.axis_size("fsdp")
    return lax.ppermute(value, "fsdp", [(place, place ^ mask) for place in range(count)])


def gather_pieces(block, *gates):
    count = lax.axis_size("fsdp")
    if count != 8:
        found = [[block]] + [[exchange(block, mask)] for mask in range(2, count, 2)]
    else:
        half = block.shape[0] // 2
        by_x = exchange(block, 2)
        by_y = exchange(block, 4)
        other = exchange(block, 1)
        by_x, by_y = after((by_x, by_y), *gates)
        top = exchange(by_x[:half], 4)
        bottom = exchange(by_y[half:], 2)
        found = [[block], [by_x], [by_y], [top, bottom]]
        others = [[other], [exchange(by_x, 1)], [exchange(by_y, 1)]]
        others.append([exchange(top, 1), exchange(bottom, 1)])
        return [(2 * place, rows) for place, rows in enumerate(found)] + [
            (2 * place + 1, rows) for place, rows in enumerate(others)
        ]
    pieces = []
    for place, rows in enumerate(found):
        pieces.append((2 * place, rows))
        pieces.append((2 * place + 1, [exchange(part, 1) for part in rows]))
    return pieces


def gather_masks(block, *gates):
    count = lax.axis_size("fsdp")
    rows = block.shape[0]
    whole = jnp.zeros((count * rows, block.shape[1]), block.dtype)
    for mask, parts in gather_pieces(block, *gates):
        first = place_of(mask, count) * rows
        for part in parts:
            whole = lax.dynamic_update_slice(whole, part, (first, 0))
            first += part.shape[0]
    return whole


def gather_small(value):
    count = lax.axis_size("fsdp")
    me = lax.axis_index("fsdp")
    bits = count.bit_length() - 1
    found = value
    for bit in list(range(1, bits)) + [0]:
        got = exchange(found, 1 << bit)
        low = (me >> bit) % 2 == 0
        found = jnp.stack([jnp.where(low, found, got), jnp.where(low, got, found)])
    return jnp.moveaxis(found, 0, bits - 1).reshape(count, -1)


def place_of(mask, count):
    return mask // 2 + (1 - mask % 2) * (count // 2)


def mask_at(place, count):
    return jnp.where(place < count // 2, 2 * place + 1, 2 * place - count)


class MaskSum:
    def __init__(self, odd):
        self.got = exchange(odd, 1)

    def second(self, even, *gates):
        count = lax.axis_size("fsdp")
        self.kept = add_low(even, after(self.got, *gates))
        if count == 8:
            half = self.kept.shape[1] // 2
            self.by_x = exchange(self.kept[1::2, :half], 2)
            self.by_y = exchange(self.kept[2:, half:], 4)
        else:
            span = count
            while self.kept.shape[0] > 1:
                span //= 2
                half = self.kept.shape[0] // 2
                self.kept = add_low(self.kept[:half], exchange(self.kept[half:], span))
        return self.kept

    def third(self, *gates):
        if lax.axis_size("fsdp") != 8:
            return self.kept
        half = self.kept.shape[1] // 2
        by_x, by_y = after((self.by_x, self.by_y), *gates)
        self.top = add_low(self.kept[0::2, :half], by_x)
        self.bottom = add_low(self.kept[:2, half:], by_y)
        self.last_y = exchange(self.top[1], 4)
        self.last_x = exchange(self.bottom[1], 2)
        return self.top, self.bottom

    def result(self, *gates):
        if lax.axis_size("fsdp") != 8:
            return self.kept[0]
        last_y, last_x = after((self.last_y, self.last_x), *gates)
        return jnp.concatenate(
            [add_low(self.top[0], last_y), add_low(self.bottom[0], last_x)], axis=0
        )


def swap_blocks(blocks):
    return lax.all_to_all(blocks, "fsdp", 0, 0, tiled=True)


def ctx_total(part):
    count = lax.axis_size("ctx")
    middle = count // 2
    me = lax.axis_index("ctx")
    for hop in range(middle - 1):
        part = add_low(
            part,
            lax.ppermute(part, "ctx", [(hop, hop + 1), (count - 1 - hop, count - 2 - hop)]),
        )
    part = add_low(
        part, lax.ppermute(part, "ctx", [(middle - 1, middle), (middle, middle - 1)])
    )
    for hop in reversed(range(middle - 1)):
        got = lax.ppermute(part, "ctx", [(hop + 1, hop), (count - 2 - hop, count - 1 - hop)])
        part = jnp.where((me == hop) | (me == count - 1 - hop), got, part)
    return lax.optimization_barrier(part)


def unit_widths(units):
    first = (units // 3 + 127) // 128 * 128
    second = units - first
    return first, second, -(-second // 128) * 128


def split_units(me, gate_up, gain, count):
    rows, columns = gate_up.shape
    span = columns // 2
    units = span // count
    first, second, padded = unit_widths(units)
    block = 48

    def kernel(me_ref, weight_ref, gain_ref, first_ref, second_ref):
        def scaled(begin, end):
            value = weight_ref[:, begin:end].astype(jnp.float32) * gain_ref[...]
            return value.astype(gate_up.dtype)

        for owner in range(count):
            for side in range(2):
                begin = side * span + owner * units
                first_ref[me_ref[0] ^ owner, :, side * first : (side + 1) * first] = scaled(
                    begin, begin + first
                )
                second_ref[owner, :, side * padded : side * padded + second] = scaled(
                    begin + first, begin + units
                )
                if padded > second:
                    second_ref[
                        owner, :, side * padded + second : (side + 1) * padded
                    ] = jnp.zeros((block, padded - second), gate_up.dtype)

    return pl.pallas_call(
        kernel,
        grid_spec=pltpu.PrefetchScalarGridSpec(
            num_scalar_prefetch=1,
            grid=(rows // block,),
            in_specs=[
                pl.BlockSpec((block, columns), lambda step, me_ref: (step, 0)),
                pl.BlockSpec((block, 1), lambda step, me_ref: (step, 0)),
            ],
            out_specs=[
                pl.BlockSpec((count, block, 2 * first), lambda step, me_ref: (0, step, 0)),
                pl.BlockSpec((count, block, 2 * padded), lambda step, me_ref: (0, step, 0)),
            ],
        ),
        out_shape=[
            jax.ShapeDtypeStruct((count, rows, 2 * first), gate_up.dtype),
            jax.ShapeDtypeStruct((count, rows, 2 * padded), gate_up.dtype),
        ],
        compiler_params=vmem_params,
        cost_estimate=pl.CostEstimate(
            flops=0, bytes_accessed=4 * rows * columns, transcendentals=0
        ),
    )(me, gate_up, gain[:, None])


def join_units(first_part, second_part, gate_up, gain):
    rows, columns = gate_up.shape
    count = first_part.shape[0]
    block = 48
    pieces = rows // block
    span = columns // 2
    units = span // count
    first, second, padded = unit_widths(units)

    def kernel(first_ref, second_ref, weight_ref, gain_ref, whole_ref, sums_ref):
        for owner in range(count):
            for side in range(2):
                begin = side * span + owner * units
                whole_ref[:, begin : begin + first] = first_ref[
                    owner, :, side * first : (side + 1) * first
                ].astype(jnp.float32)
                whole_ref[:, begin + first : begin + units] = second_ref[
                    owner, :, side * padded : side * padded + second
                ].astype(jnp.float32)
        whole = whole_ref[...]
        total = jnp.sum(whole * weight_ref[...].astype(jnp.float32), axis=1, keepdims=True)
        sums_ref[...] = jnp.broadcast_to(total, (block, 128))
        whole_ref[...] = whole * gain_ref[...]

    whole, sums = pl.pallas_call(
        kernel,
        grid=(pieces,),
        in_specs=[
            pl.BlockSpec((count, block, 2 * first), lambda step: (0, step, 0)),
            pl.BlockSpec((count, block, 2 * padded), lambda step: (0, step, 0)),
            pl.BlockSpec((block, columns), lambda step: (step, 0)),
            pl.BlockSpec((block, 1), lambda step: (step, 0)),
        ],
        out_specs=[
            pl.BlockSpec((block, columns), lambda step: (step, 0)),
            pl.BlockSpec((block, 128), lambda step: (step, 0)),
        ],
        out_shape=[
            jax.ShapeDtypeStruct((rows, columns), jnp.float32),
            jax.ShapeDtypeStruct((rows, 128), jnp.float32),
        ],
        compiler_params=vmem_params,
        cost_estimate=pl.CostEstimate(
            flops=2 * rows * columns, bytes_accessed=8 * rows * columns, transcendentals=0
        ),
    )(first_part, second_part, gate_up, gain[:, None])
    return whole, sums[:, 0]


def place_rows(me_ref, pieces, refs, weight_ref):
    place = 0
    for mask, parts in pieces:
        shard = sum(part.shape[0] for part in parts)
        begin = (me_ref[0] ^ mask) * shard
        for part in parts:
            rows = part.shape[0]
            weight_ref[pl.ds(pl.multiple_of(begin, rows), rows)] = refs[place][...]
            begin = begin + rows
            place += 1


def project(me, normed, pieces, bias, cosine, sine):
    tokens = normed.shape[0]
    width = bias.shape[0]
    block = 512
    flat = [part for unused_mask, parts in pieces for part in parts]

    def kernel(me_ref, normed_ref, bias_ref, cosine_ref, sine_ref, *refs):
        out_ref, weight_ref = refs[len(flat) :]
        place_rows(me_ref, pieces, refs, weight_ref)
        product = dot_f32(normed_ref[...], weight_ref[...]) + bias_ref[...]
        for head in range(block // HEAD_SIZE):
            lanes = slice(head * HEAD_SIZE, (head + 1) * HEAD_SIZE)
            plain = product[:, lanes]
            turned = plain * cosine_ref[...] + pltpu.roll(plain, HEAD_SIZE // 2, 1) * sine_ref[...]
            column = pl.program_id(0) * block + head * HEAD_SIZE
            out_ref[:, lanes] = jnp.where(column < QD + KD, turned, plain).astype(jnp.bfloat16)

    return pl.pallas_call(
        kernel,
        grid_spec=pltpu.PrefetchScalarGridSpec(
            num_scalar_prefetch=1,
            grid=(width // block,),
            in_specs=[
                pl.BlockSpec((tokens, D), lambda step, me_ref: (0, 0)),
                pl.BlockSpec((1, block), lambda step, me_ref: (0, step)),
                pl.BlockSpec((tokens, HEAD_SIZE), lambda step, me_ref: (0, 0)),
                pl.BlockSpec((tokens, HEAD_SIZE), lambda step, me_ref: (0, 0)),
            ]
            + [
                pl.BlockSpec((part.shape[0], block), lambda step, me_ref: (0, step))
                for part in flat
            ],
            out_specs=pl.BlockSpec((tokens, block), lambda step, me_ref: (0, step)),
            scratch_shapes=[pltpu.VMEM((D, block), jnp.bfloat16)],
        ),
        out_shape=jax.ShapeDtypeStruct((tokens, width), jnp.bfloat16),
        compiler_params=vmem_params,
        cost_estimate=pl.CostEstimate(
            flops=2 * tokens * D * width, bytes_accessed=2 * D * width, transcendentals=0
        ),
    )(me, normed, bias[None], cosine, sine, *flat)


def project_back(me, grad_projected, pieces):
    tokens, width = grad_projected.shape
    flat = [part for unused_mask, parts in pieces for part in parts]

    def kernel(me_ref, grad_ref, *refs):
        out_ref, weight_ref = refs[len(flat) :]
        place_rows(me_ref, pieces, refs, weight_ref)
        out_ref[...] = dot_right_t(grad_ref[...], weight_ref[...])

    whole = lambda part: pl.BlockSpec(part.shape, lambda step, me_ref: (0, 0))
    return pl.pallas_call(
        kernel,
        grid_spec=pltpu.PrefetchScalarGridSpec(
            num_scalar_prefetch=1,
            grid=(1,),
            in_specs=[whole(grad_projected)] + [whole(part) for part in flat],
            out_specs=pl.BlockSpec((tokens, D), lambda step, me_ref: (0, 0)),
            scratch_shapes=[pltpu.VMEM((D, width), jnp.bfloat16)],
        ),
        out_shape=jax.ShapeDtypeStruct((tokens, D), jnp.float32),
        compiler_params=vmem_params,
        cost_estimate=pl.CostEstimate(
            flops=2 * tokens * D * width, bytes_accessed=2 * D * width, transcendentals=0
        ),
    )(me, grad_projected, *flat)


def fill_bias(at_ref, position_ref, bias_ref):
    tokens, keys = bias_ref.shape
    row = lax.broadcasted_iota(jnp.int32, (tokens, keys), 0)
    column = lax.broadcasted_iota(jnp.int32, (tokens, keys), 1)
    back = column // tokens
    query_index = at_ref[0] * tokens + row
    key_index = (at_ref[0] - back) * tokens + (column - back * tokens)
    allowed = (key_index <= query_index) & (key_index >= query_index - position_ref[...])
    bias_ref[...] = jnp.where(allowed, 0.0, masked_score)


def join_keys(refs, key_ref, value_ref):
    @pl.when(pl.program_id(0) % GROUP == 0)
    def _():
        for place in range(len(refs)):
            tokens = refs[0].shape[0]
            if (place + 1) * tokens > key_ref.shape[0]:
                break
            rows = slice(place * tokens, (place + 1) * tokens)
            key_ref[rows] = refs[2 * place][...]
            value_ref[rows] = refs[2 * place + 1][...]


def key_specs(both_pieces):
    specs = []
    for piece in both_pieces:
        shape = (piece.shape[0], HEAD_SIZE)
        specs.append(pl.BlockSpec(shape, lambda head, at: (0, head // GROUP)))
        specs.append(pl.BlockSpec(shape, lambda head, at: (0, KEY_VALUE_HEADS + head // GROUP)))
    return specs


def attend(at, position, projected, both_pieces):
    tokens = projected.shape[0]
    count = len(both_pieces)
    keys = count * tokens

    def kernel(at_ref, position_ref, query_ref, *refs):
        out_ref, turn_ref, log_ref, bias_ref, key_ref, value_ref = refs[2 * count :]

        @pl.when(pl.program_id(0) == 0)
        def _():
            fill_bias(at_ref, position_ref, bias_ref)

        join_keys(refs, key_ref, value_ref)

        scores = dot_right_t(query_ref[...], key_ref[...]) * score_scale + bias_ref[...]
        top = jnp.max(scores, axis=1, keepdims=True)
        raised = jnp.exp(scores - top)
        total = jnp.sum(raised, axis=1, keepdims=True)
        probs = (raised * (1.0 / total)).astype(jnp.bfloat16)
        result = dot_f32(probs, value_ref[...])
        out_ref[...] = result.astype(jnp.bfloat16)
        turn_ref[...] = result.T.astype(jnp.bfloat16)
        log_ref[0] = top + jnp.log(total)

    return pl.pallas_call(
        kernel,
        grid_spec=pltpu.PrefetchScalarGridSpec(
            num_scalar_prefetch=1,
            grid=(QUERY_HEADS,),
            in_specs=[
                pl.BlockSpec((tokens, 1), lambda head, at: (0, 0)),
                pl.BlockSpec((tokens, HEAD_SIZE), lambda head, at: (0, head)),
            ]
            + key_specs(both_pieces),
            out_specs=[
                pl.BlockSpec((tokens, HEAD_SIZE), lambda head, at: (0, head)),
                pl.BlockSpec((HEAD_SIZE, tokens), lambda head, at: (head, 0)),
                pl.BlockSpec((1, tokens, 1), lambda head, at: (head, 0, 0)),
            ],
            scratch_shapes=[
                pltpu.VMEM((tokens, keys), jnp.float32),
                pltpu.VMEM((keys, HEAD_SIZE), jnp.bfloat16),
                pltpu.VMEM((keys, HEAD_SIZE), jnp.bfloat16),
            ],
        ),
        out_shape=[
            jax.ShapeDtypeStruct((tokens, QD), jnp.bfloat16),
            jax.ShapeDtypeStruct((QD, tokens), jnp.bfloat16),
            jax.ShapeDtypeStruct((QUERY_HEADS, tokens, 1), jnp.float32),
        ],
        compiler_params=vmem_params,
        cost_estimate=pl.CostEstimate(
            flops=8 * tokens * keys * QD,
            bytes_accessed=8 * tokens * QD,
            transcendentals=QUERY_HEADS * tokens * keys,
        ),
    )(at, position, projected, *[piece for piece in both_pieces for unused in range(2)])


def attend_backward(at, position, projected, both_pieces, incoming, log_total, cosine, sine):
    tokens = projected.shape[0]
    count = len(both_pieces)
    keys = count * tokens

    def kernel(
        at_ref,
        position_ref,
        query_ref,
        incoming_ref,
        log_ref,
        cosine_ref,
        sine_ref,
        *refs,
    ):
        query_grad_ref, key_grad_ref, value_grad_ref = refs[2 * count : 2 * count + 3]
        bias_ref, key_total, value_total, key_ref, value_ref = refs[2 * count + 3 :]
        head = pl.program_id(0)
        join_keys(refs, key_ref, value_ref)

        @pl.when(head == 0)
        def _():
            fill_bias(at_ref, position_ref, bias_ref)

        @pl.when(head % GROUP == 0)
        def _():
            key_total[...] = jnp.zeros_like(key_total)
            value_total[...] = jnp.zeros_like(value_total)

        scores = dot_right_t(query_ref[...], key_ref[...]) * score_scale + bias_ref[...]
        probs = jnp.exp(scores - log_ref[0])
        grad_probs = dot_right_t(incoming_ref[...], value_ref[...])
        inner = jnp.sum(grad_probs * probs, axis=1, keepdims=True)
        grad_scores = (probs * (grad_probs - inner)).astype(jnp.bfloat16)
        value_total[...] += dot_left_t(incoming_ref[...], probs.astype(jnp.bfloat16))
        key_total[...] += dot_left_t(query_ref[...], grad_scores)
        plain = dot_f32(grad_scores, key_ref[...]) * score_scale
        query_grad_ref[...] = (
            plain * cosine_ref[...] - pltpu.roll(plain, HEAD_SIZE // 2, 1) * sine_ref[...]
        ).astype(jnp.bfloat16)

        @pl.when(head % GROUP == GROUP - 1)
        def _():
            key_grad_ref[...] = (key_total[...] * score_scale).T
            value_grad_ref[...] = value_total[...].T

    return pl.pallas_call(
        kernel,
        grid_spec=pltpu.PrefetchScalarGridSpec(
            num_scalar_prefetch=1,
            grid=(QUERY_HEADS,),
            in_specs=[
                pl.BlockSpec((tokens, 1), lambda head, at: (0, 0)),
                pl.BlockSpec((tokens, HEAD_SIZE), lambda head, at: (0, head)),
                pl.BlockSpec((tokens, HEAD_SIZE), lambda head, at: (0, head)),
                pl.BlockSpec((1, tokens, 1), lambda head, at: (head, 0, 0)),
                pl.BlockSpec((tokens, HEAD_SIZE), lambda head, at: (0, 0)),
                pl.BlockSpec((tokens, HEAD_SIZE), lambda head, at: (0, 0)),
            ]
            + key_specs(both_pieces),
            out_specs=[
                pl.BlockSpec((tokens, HEAD_SIZE), lambda head, at: (0, head)),
                pl.BlockSpec((keys, HEAD_SIZE), lambda head, at: (0, head // GROUP)),
                pl.BlockSpec((keys, HEAD_SIZE), lambda head, at: (0, head // GROUP)),
            ],
            scratch_shapes=[
                pltpu.VMEM((tokens, keys), jnp.float32),
                pltpu.VMEM((HEAD_SIZE, keys), jnp.float32),
                pltpu.VMEM((HEAD_SIZE, keys), jnp.float32),
                pltpu.VMEM((keys, HEAD_SIZE), jnp.bfloat16),
                pltpu.VMEM((keys, HEAD_SIZE), jnp.bfloat16),
            ],
        ),
        out_shape=[
            jax.ShapeDtypeStruct((tokens, QD), jnp.bfloat16),
            jax.ShapeDtypeStruct((keys, KD), jnp.float32),
            jax.ShapeDtypeStruct((keys, KD), jnp.float32),
        ],
        compiler_params=vmem_params,
        cost_estimate=pl.CostEstimate(
            flops=20 * tokens * keys * QD,
            bytes_accessed=8 * tokens * QD,
            transcendentals=QUERY_HEADS * tokens * keys,
        ),
    )(
        at,
        position,
        projected,
        incoming,
        log_total,
        cosine,
        sine,
        *[piece for piece in both_pieces for unused in range(2)],
    )


def unit_part(me, normed_all, grad_out_all, gate_up, down, count, first):
    tokens = normed_all.shape[0]
    block = tokens // count
    width = down.shape[0]
    shard = D // count
    weights = list(gate_up) if first else [gate_up]

    def kernel(me_ref, normed_ref, out_grad_ref, down_ref, *refs):
        weight_refs = refs[: len(weights)]
        hidden_ref, grad_ref = refs[len(weights) : len(weights) + 2]
        weight_ref = weight_refs[0]
        if first:
            ordered_ref, weight_ref = refs[len(weights) + 2 :]
            ordered_ref[...] = out_grad_ref[...]

            @pl.when(pl.program_id(0) == 0)
            def _():
                for mask, ref in enumerate(weight_refs):
                    begin = pl.multiple_of((me_ref[0] ^ mask) * shard, shard)
                    weight_ref[pl.ds(begin, shard)] = ref[...]

        values = dot_f32(normed_ref[...], weight_ref[...])
        gate = values[:, :width]
        up = values[:, width:]
        grad_hidden = dot_right_t(out_grad_ref[...], down_ref[...])
        share = 1.0 / (1.0 + jnp.exp(-gate))
        passed = gate * share
        hidden_ref[...] = (passed * up).astype(jnp.bfloat16)
        grad_ref[:, :width] = (
            grad_hidden * up * share * (1.0 + gate * (1.0 - share))
        ).astype(jnp.bfloat16)
        grad_ref[:, width:] = (grad_hidden * passed).astype(jnp.bfloat16)

    def out_grad_index(step, me_ref):
        return (me_ref[0] ^ mask_at(step, count), 0) if first else (step, 0)

    row = lambda step, me_ref: (step, 0)
    fixed = lambda step, me_ref: (0, 0)
    out_specs = [pl.BlockSpec((block, width), row), pl.BlockSpec((block, 2 * width), row)]
    out_shape = [
        jax.ShapeDtypeStruct((tokens, width), jnp.bfloat16),
        jax.ShapeDtypeStruct((tokens, 2 * width), jnp.bfloat16),
    ]
    if first:
        out_specs += [pl.BlockSpec((block, D), row), pl.BlockSpec((D, 2 * width), fixed)]
        out_shape += [
            jax.ShapeDtypeStruct((tokens, D), jnp.bfloat16),
            jax.ShapeDtypeStruct((D, 2 * width), jnp.bfloat16),
        ]
    return pl.pallas_call(
        kernel,
        grid_spec=pltpu.PrefetchScalarGridSpec(
            num_scalar_prefetch=1,
            grid=(count,),
            in_specs=[
                pl.BlockSpec((block, D), row),
                pl.BlockSpec((block, D), out_grad_index),
                pl.BlockSpec((width, D), fixed),
            ]
            + [pl.BlockSpec(weight.shape, fixed) for weight in weights],
            out_specs=out_specs,
        ),
        out_shape=out_shape,
        compiler_params=vmem_params,
        cost_estimate=pl.CostEstimate(
            flops=6 * tokens * D * width,
            bytes_accessed=4 * tokens * D + 6 * tokens * width + 6 * D * width,
            transcendentals=tokens * width,
        ),
    )(me, normed_all, grad_out_all, down, *weights)


def row_terms(me, turned, right, rows_out):
    count, shard, tokens = turned.shape
    width = right.shape[1]
    lanes = width // 128
    half = count // 2
    spare = rows_out - shard * lanes

    def kernel(me_ref, turned_ref, right_ref, odd_ref, even_ref, *scratch):
        step = pl.program_id(0)
        if spare:

            @pl.when(step == 0)
            def _():
                sums = jnp.sum(right_ref[...].astype(jnp.float32), axis=0, keepdims=True)
                scratch[0][...] = jnp.zeros_like(scratch[0])
                for group in range(lanes):
                    scratch[0][group : group + 1] = sums[:, group * 128 : (group + 1) * 128]

        term = dot_f32(turned_ref[0], right_ref[...]).astype(jnp.bfloat16)

        def store(out_ref):
            for group in range(lanes):
                out_ref[0, group * shard : (group + 1) * shard] = term[
                    :, group * 128 : (group + 1) * 128
                ]
            if spare:
                out_ref[0, lanes * shard :] = scratch[0][...].astype(jnp.bfloat16)

        pl.when(step < half)(lambda: store(odd_ref))
        pl.when(step >= half)(lambda: store(even_ref))

    out = jax.ShapeDtypeStruct((half, rows_out, 128), jnp.bfloat16)
    return pl.pallas_call(
        kernel,
        grid_spec=pltpu.PrefetchScalarGridSpec(
            num_scalar_prefetch=1,
            grid=(count,),
            in_specs=[
                pl.BlockSpec(
                    (1, shard, tokens),
                    lambda step, me_ref: (me_ref[0] ^ mask_at(step, count), 0, 0),
                ),
                pl.BlockSpec((tokens, width), lambda step, me_ref: (0, 0)),
            ],
            out_specs=[
                pl.BlockSpec(
                    (1, rows_out, 128), lambda step, me_ref: (jnp.minimum(step, half - 1), 0, 0)
                ),
                pl.BlockSpec(
                    (1, rows_out, 128), lambda step, me_ref: (jnp.maximum(step - half, 0), 0, 0)
                ),
            ],
            scratch_shapes=[pltpu.VMEM((spare, 128), jnp.float32)] if spare else [],
        ),
        out_shape=[out, out],
        compiler_params=vmem_params,
        cost_estimate=pl.CostEstimate(
            flops=2 * D * tokens * width,
            bytes_accessed=256 * count * rows_out,
            transcendentals=0,
        ),
    )(me, turned, right)


def shards(
    tokens,
    positions,
    cotangent,
    attn_norm,
    ffn_norm,
    in_proj,
    in_bias,
    out_proj,
    gate_up,
    down_proj,
):
    token_rows = tokens.shape[1]
    fsdp_count = lax.axis_size("fsdp")
    ctx_count = lax.axis_size("ctx")
    fsdp_me = lax.axis_index("fsdp")
    me = fsdp_me.astype(jnp.int32)[None]
    at = lax.axis_index("ctx").astype(jnp.int32)[None]
    units = FF // fsdp_count
    shard_d = D // fsdp_count
    residual_in = tokens[0].astype(jnp.float32)
    position = positions[0]
    grad_out_b = cotangent[0]

    first_units, second_units, padded_units = unit_widths(units)
    bias_full = gather_small(in_bias).reshape(-1)
    in_scaled = (in_proj.astype(jnp.float32) * attn_norm[:, None]).astype(jnp.bfloat16)
    first_blocks, second_blocks = split_units(me, gate_up, ffn_norm, fsdp_count)
    cosine, sine = rotary_tables(position)
    normed_b = rms_scale(residual_in).astype(jnp.bfloat16)
    in_pieces = gather_pieces(in_scaled, first_blocks, cosine, normed_b)
    gated_blocks = after(first_blocks, in_pieces[0], in_pieces[2], in_pieces[4])
    gate_up_first = [gated_blocks[0]] + [
        exchange(gated_blocks[mask], mask) for mask in range(1, fsdp_count)
    ]
    out_full = lax.all_gather(after(out_proj, in_pieces), "fsdp", axis=0, tiled=True)

    projected = project(
        me, after(normed_b, gate_up_first[1], gate_up_first[2]), in_pieces, bias_full, cosine, sine
    )
    both_b = projected[:, QD:]
    both_pieces = [both_b] + [
        lax.ppermute(both_b, "ctx", [(s, s + back) for s in range(ctx_count - back)])
        for back in range(1, ctx_count)
    ]
    grad_out_all = lax.all_gather(after(grad_out_b, projected), "fsdp", axis=0, tiled=True)
    both_pieces = after(both_pieces, gate_up_first[3], gate_up_first[4])
    attended_b, attended_turned, log_total = attend(at, position[:, None], projected, both_pieces)
    attended_b = after(attended_b, gate_up_first)
    middle = residual_in + dot_f32(attended_b, out_full)
    normed_ffn_b = rms_scale(middle).astype(jnp.bfloat16)
    normed_again, down_again = after((normed_b, down_proj), normed_ffn_b)
    normed_turned = normed_again.T.reshape(fsdp_count, shard_d, token_rows)
    down_first = down_again[:first_units]
    down_second = jnp.pad(down_again[first_units:], ((0, padded_units - second_units), (0, 0)))

    normed_ffn_all = gather_masks(normed_ffn_b, normed_turned, down_first, down_second)
    gate_up_second = swap_blocks(after(second_blocks, normed_ffn_all)).reshape(
        D, 2 * padded_units
    )
    hidden_first, grad_first, grad_out_all, gate_up_first = unit_part(
        me, normed_ffn_all, grad_out_all, gate_up_first, down_first, fsdp_count, True
    )
    odd_rows = normed_ffn_all.shape[0] // 2

    def down_term(hidden, *gates):
        return dot_left_t(after(hidden, *gates), grad_out_all).astype(jnp.bfloat16)

    def gate_term(grad, *gates):
        term = dot_left_t(normed_ffn_all, after(grad, *gates)).astype(jnp.bfloat16)
        return term.reshape(fsdp_count, shard_d, -1)

    def input_grads(rows, *gates):
        return (
            (
                dot_right_t(after(grad_first, *gates)[rows], gate_up_first)
                + dot_right_t(grad_second[rows], gate_up_second)
            )
            .astype(jnp.bfloat16)
            .reshape(fsdp_count // 2, token_rows, D)
        )

    def down_outs(rows, *gates):
        return (
            (
                dot_f32(after(hidden_first, *gates)[rows], down_first)
                + dot_f32(hidden_second[rows], down_second)
            )
            .astype(jnp.bfloat16)
            .reshape(fsdp_count // 2, token_rows, D)
        )

    down_term_a = down_term(hidden_first)
    down_sum_a = lax.psum(down_term_a, "ctx")
    gate_term_a = gate_term(grad_first, down_term_a)
    gate_swapped_a = swap_blocks(gate_term_a)
    hidden_second, grad_second = unit_part(
        me,
        after(normed_ffn_all, gate_term_a),
        grad_out_all,
        gate_up_second,
        down_second,
        fsdp_count,
        False,
    )
    grad_normed_odd = input_grads(slice(0, odd_rows), hidden_second)
    normed_sum = MaskSum(grad_normed_odd)
    grad_normed_even = input_grads(slice(odd_rows, None), grad_normed_odd, gate_swapped_a)
    gate_sum_a = lax.psum(gate_swapped_a, "ctx")
    sent = normed_sum.second(grad_normed_even)
    gate_term_b = gate_term(grad_second, sent)
    gate_swapped_b = swap_blocks(gate_term_b)
    sent = normed_sum.third(gate_term_b)
    down_term_b = down_term(hidden_second, sent)[:second_units]
    down_term_b, down_sum_a = lax.optimization_barrier((down_term_b, down_sum_a))
    down_sum_b = lax.psum(down_term_b, "ctx")
    grad_normed_ffn = normed_sum.result(down_term_b).astype(jnp.float32)

    grad_out = grad_out_b.astype(jnp.float32)
    grad_middle = grad_out + norm_backward(middle, grad_normed_ffn)
    grad_middle_b = grad_middle.astype(jnp.bfloat16)
    grad_attended_b = dot_right_t(grad_middle_b, out_full).astype(jnp.bfloat16)
    in_rows = shard_d * in_proj.shape[1] // 128
    out_rows = shard_d * D // 128
    out_odd, out_even = row_terms(
        me,
        attended_turned.reshape(fsdp_count, shard_d, token_rows),
        after(grad_middle_b, grad_attended_b),
        out_rows,
    )
    out_sum = MaskSum(out_odd)
    query_grad, key_grads, value_grads = attend_backward(
        at,
        position[:, None],
        projected,
        both_pieces,
        after(grad_attended_b, out_even),
        log_total,
        cosine,
        sine,
    )
    both_sent = [
        lax.ppermute(
            jnp.concatenate(
                [
                    grads[back * token_rows : (back + 1) * token_rows].astype(jnp.bfloat16)
                    for grads in (key_grads, value_grads)
                ],
                axis=1,
            ),
            "ctx",
            [(s + back, s) for s in range(ctx_count - back)],
        )
        for back in range(1, ctx_count)
    ]
    sent = out_sum.second(out_even, query_grad)
    down_odd = down_outs(slice(0, odd_rows), sent)
    block_sum = MaskSum(down_odd)
    sent = out_sum.third(down_odd)
    down_even = down_outs(slice(odd_rows, None), sent)
    both_grad = jnp.concatenate([key_grads[:token_rows], value_grads[:token_rows]], axis=1)
    gate_swapped_b, gate_sum_a = lax.optimization_barrier((gate_swapped_b, gate_sum_a))
    gate_sum_b = lax.psum(gate_swapped_b, "ctx")
    for piece in after(both_sent, down_even, gate_swapped_b):
        both_grad = both_grad + piece.astype(jnp.float32)
    turned_back = []
    for head in range(KEY_VALUE_HEADS):
        plain = both_grad[:, head * HEAD_SIZE : (head + 1) * HEAD_SIZE]
        turned_back.append(plain * cosine - jnp.roll(plain, HEAD_SIZE // 2, axis=1) * sine)
    grad_projected_b = jnp.concatenate(
        [query_grad]
        + [part.astype(jnp.bfloat16) for part in turned_back]
        + [both_grad[:, KD:].astype(jnp.bfloat16)],
        axis=1,
    )
    in_odd, in_even = row_terms(me, normed_turned, grad_projected_b, in_rows + 32)
    in_sum = MaskSum(in_odd)
    grad_normed = project_back(me, after(grad_projected_b, in_even), in_pieces)
    sent = in_sum.second(in_even, grad_normed)
    tokens_grad = grad_middle + norm_backward(residual_in, after(grad_normed, sent))
    sent = block_sum.second(down_even, tokens_grad)
    sent = in_sum.third(sent)
    out_part = out_sum.result(sent)
    sent = block_sum.third(out_part)
    in_part = in_sum.result(sent)
    terms_total = ctx_total(jnp.concatenate([in_part, out_part], axis=0)).astype(jnp.float32)
    block_out = middle + block_sum.result(in_part).astype(jnp.float32)
    down_grad = jnp.concatenate([down_sum_a, down_sum_b], axis=0).astype(jnp.float32)
    gate_grad, ffn_grad = join_units(gate_sum_a, gate_sum_b, gate_up, ffn_norm)

    def lanes_back(rows):
        return rows.reshape(-1, shard_d, 128).transpose(1, 0, 2).reshape(shard_d, -1)

    in_total = lanes_back(terms_total[:in_rows])
    out_grad = lanes_back(terms_total[in_rows + 32 :])
    bias_span = in_bias.shape[0]
    bias_grad = lax.dynamic_slice_in_dim(
        terms_total[in_rows : in_rows + in_proj.shape[1] // 128].reshape(-1),
        fsdp_me * bias_span,
        bias_span,
    )
    in_grad = in_total * attn_norm[:, None]
    attn_grad = jnp.sum(in_total * in_proj.astype(jnp.float32), axis=1)
    return (
        block_out.astype(jnp.bfloat16).reshape(1, token_rows, D),
        tokens_grad.reshape(1, token_rows, D),
        attn_grad,
        ffn_grad,
        in_grad,
        bias_grad,
        out_grad,
        gate_grad,
        down_grad,
    )


def solution(mesh):
    in_specs = (
        P("fsdp", "ctx", None),
        P("fsdp", "ctx"),
        P("fsdp", "ctx", None),
        P("fsdp"),
        P("fsdp"),
        P("fsdp", None),
        P("fsdp"),
        P("fsdp", None),
        P("fsdp", None),
        P("fsdp", None),
    )
    out_specs = (
        P("fsdp", "ctx", None),
        P("fsdp", "ctx", None),
        P("fsdp"),
        P("fsdp"),
        P("fsdp", None),
        P("fsdp"),
        P("fsdp", None),
        P("fsdp", None),
        P("fsdp", None),
    )
    return jax.shard_map(shards, mesh=mesh, in_specs=in_specs, out_specs=out_specs, check_vma=False)
```

```python
import jax
import jax.numpy as jnp
from jax import lax
from jax.experimental import pallas as pl
from jax.experimental.pallas import tpu as pltpu
from jax.sharding import PartitionSpec as P

D = 1536
QUERY_HEADS = 12
KEY_VALUE_HEADS = 2
HEAD_SIZE = 128
FF = 8960
QD = QUERY_HEADS * HEAD_SIZE
KD = KEY_VALUE_HEADS * HEAD_SIZE
GROUP = QUERY_HEADS // KEY_VALUE_HEADS


norm_eps = 1e-06
rope_base = 1000000.0
masked_score = -1e30
score_scale = HEAD_SIZE ** (-0.5)
vmem_params = pltpu.CompilerParams(vmem_limit_bytes=48 * 1024 * 1024)


def rms_scale(value_rows):
    return value_rows * lax.rsqrt(
        jnp.mean(value_rows * value_rows, axis=-1, keepdims=True) + norm_eps
    )


def norm_backward(value_rows, incoming):
    unused_out, pullback = jax.vjp(rms_scale, value_rows)
    return pullback(incoming)[0]


def rotary_tables(position):
    lane = jnp.arange(HEAD_SIZE, dtype=jnp.int32)
    half = HEAD_SIZE // 2
    frequencies = rope_base ** (-((lane % half).astype(jnp.float32) * (2.0 / HEAD_SIZE)))
    angles = position.astype(jnp.float32)[:, None] * frequencies[None, :]
    sign = jnp.where(lane < half, -1.0, 1.0)
    return jnp.cos(angles), jnp.sin(angles) * sign[None, :]


def dot_f32(left, right):
    return jnp.dot(left, right, preferred_element_type=jnp.float32)


def dot_right_t(left, right):
    return lax.dot_general(
        left, right, (((1,), (1,)), ((), ())), preferred_element_type=jnp.float32
    )


def dot_left_t(left, right):
    return lax.dot_general(
        left, right, (((0,), (0,)), ((), ())), preferred_element_type=jnp.float32
    )


def add_low(left, right):
    return left + right


def after(value, *earlier):
    return lax.optimization_barrier((value, earlier))[0]


def exchange(value, mask):
    count = lax.axis_size("fsdp")
    return lax.ppermute(value, "fsdp", [(place, place ^ mask) for place in range(count)])


def gather_pieces(block, *gates):
    count = lax.axis_size("fsdp")
    if count != 8:
        found = [[block]] + [[exchange(block, mask)] for mask in range(2, count, 2)]
    else:
        half = block.shape[0] // 2
        by_x = exchange(block, 2)
        by_y = exchange(block, 4)
        other = exchange(block, 1)
        by_x, by_y = after((by_x, by_y), *gates)
        top = exchange(by_x[:half], 4)
        bottom = exchange(by_y[half:], 2)
        found = [[block], [by_x], [by_y], [top, bottom]]
        others = [[other], [exchange(by_x, 1)], [exchange(by_y, 1)]]
        others.append([exchange(top, 1), exchange(bottom, 1)])
        return [(2 * place, rows) for place, rows in enumerate(found)] + [
            (2 * place + 1, rows) for place, rows in enumerate(others)
        ]
    pieces = []
    for place, rows in enumerate(found):
        pieces.append((2 * place, rows))
        pieces.append((2 * place + 1, [exchange(part, 1) for part in rows]))
    return pieces


def gather_masks(block, *gates):
    count = lax.axis_size("fsdp")
    rows = block.shape[0]
    whole = jnp.zeros((count * rows, block.shape[1]), block.dtype)
    for mask, parts in gather_pieces(block, *gates):
        first = place_of(mask, count) * rows
        for part in parts:
            whole = lax.dynamic_update_slice(whole, part, (first, 0))
            first += part.shape[0]
    return whole


def gather_small(value):
    count = lax.axis_size("fsdp")
    me = lax.axis_index("fsdp")
    bits = count.bit_length() - 1
    found = value
    for bit in list(range(1, bits)) + [0]:
        got = exchange(found, 1 << bit)
        low = (me >> bit) % 2 == 0
        found = jnp.stack([jnp.where(low, found, got), jnp.where(low, got, found)])
    return jnp.moveaxis(found, 0, bits - 1).reshape(count, -1)


def place_of(mask, count):
    return mask // 2 + (1 - mask % 2) * (count // 2)


def mask_at(place, count):
    return jnp.where(place < count // 2, 2 * place + 1, 2 * place - count)


class MaskSum:
    def __init__(self, odd):
        self.got = exchange(odd, 1)

    def second(self, even, *gates):
        count = lax.axis_size("fsdp")
        self.kept = add_low(even, after(self.got, *gates))
        if count == 8:
            half = self.kept.shape[1] // 2
            self.by_x = exchange(self.kept[1::2, :half], 2)
            self.by_y = exchange(self.kept[2:, half:], 4)
        else:
            span = count
            while self.kept.shape[0] > 1:
                span //= 2
                half = self.kept.shape[0] // 2
                self.kept = add_low(self.kept[:half], exchange(self.kept[half:], span))
        return self.kept

    def third(self, *gates):
        if lax.axis_size("fsdp") != 8:
            return self.kept
        half = self.kept.shape[1] // 2
        by_x, by_y = after((self.by_x, self.by_y), *gates)
        self.top = add_low(self.kept[0::2, :half], by_x)
        self.bottom = add_low(self.kept[:2, half:], by_y)
        self.last_y = exchange(self.top[1], 4)
        self.last_x = exchange(self.bottom[1], 2)
        return self.top, self.bottom

    def result(self, *gates):
        if lax.axis_size("fsdp") != 8:
            return self.kept[0]
        last_y, last_x = after((self.last_y, self.last_x), *gates)
        return jnp.concatenate(
            [add_low(self.top[0], last_y), add_low(self.bottom[0], last_x)], axis=0
        )


def swap_blocks(blocks):
    return lax.all_to_all(blocks, "fsdp", 0, 0, tiled=True)


def ctx_total(part):
    count = lax.axis_size("ctx")
    middle = count // 2
    me = lax.axis_index("ctx")
    for hop in range(middle - 1):
        part = add_low(
            part,
            lax.ppermute(part, "ctx", [(hop, hop + 1), (count - 1 - hop, count - 2 - hop)]),
        )
    part = add_low(
        part, lax.ppermute(part, "ctx", [(middle - 1, middle), (middle, middle - 1)])
    )
    for hop in reversed(range(middle - 1)):
        got = lax.ppermute(part, "ctx", [(hop + 1, hop), (count - 2 - hop, count - 1 - hop)])
        part = jnp.where((me == hop) | (me == count - 1 - hop), got, part)
    return lax.optimization_barrier(part)


def unit_widths(units):
    first = units // 256 * 128
    second = units - first
    return first, second, -(-second // 128) * 128


def split_units(me, gate_up, gain, count):
    rows, columns = gate_up.shape
    span = columns // 2
    units = span // count
    first, second, padded = unit_widths(units)
    block = 48

    def kernel(me_ref, weight_ref, gain_ref, first_ref, second_ref):
        def scaled(begin, end):
            value = weight_ref[:, begin:end].astype(jnp.float32) * gain_ref[...]
            return value.astype(gate_up.dtype)

        for owner in range(count):
            for side in range(2):
                begin = side * span + owner * units
                first_ref[me_ref[0] ^ owner, :, side * first : (side + 1) * first] = scaled(
                    begin, begin + first
                )
                second_ref[owner, :, side * padded : side * padded + second] = scaled(
                    begin + first, begin + units
                )
                if padded > second:
                    second_ref[
                        owner, :, side * padded + second : (side + 1) * padded
                    ] = jnp.zeros((block, padded - second), gate_up.dtype)

    return pl.pallas_call(
        kernel,
        grid_spec=pltpu.PrefetchScalarGridSpec(
            num_scalar_prefetch=1,
            grid=(rows // block,),
            in_specs=[
                pl.BlockSpec((block, columns), lambda step, me_ref: (step, 0)),
                pl.BlockSpec((block, 1), lambda step, me_ref: (step, 0)),
            ],
            out_specs=[
                pl.BlockSpec((count, block, 2 * first), lambda step, me_ref: (0, step, 0)),
                pl.BlockSpec((count, block, 2 * padded), lambda step, me_ref: (0, step, 0)),
            ],
        ),
        out_shape=[
            jax.ShapeDtypeStruct((count, rows, 2 * first), gate_up.dtype),
            jax.ShapeDtypeStruct((count, rows, 2 * padded), gate_up.dtype),
        ],
        compiler_params=vmem_params,
        cost_estimate=pl.CostEstimate(
            flops=0, bytes_accessed=4 * rows * columns, transcendentals=0
        ),
    )(me, gate_up, gain[:, None])


def join_units(first_part, second_part, gate_up, gain):
    rows, columns = gate_up.shape
    count = first_part.shape[0]
    block = 48
    pieces = rows // block
    span = columns // 2
    units = span // count
    first, second, padded = unit_widths(units)

    def kernel(first_ref, second_ref, weight_ref, gain_ref, whole_ref, sums_ref):
        for owner in range(count):
            for side in range(2):
                begin = side * span + owner * units
                whole_ref[:, begin : begin + first] = first_ref[
                    owner, :, side * first : (side + 1) * first
                ].astype(jnp.float32)
                whole_ref[:, begin + first : begin + units] = second_ref[
                    owner, :, side * padded : side * padded + second
                ].astype(jnp.float32)
        whole = whole_ref[...]
        total = jnp.sum(whole * weight_ref[...].astype(jnp.float32), axis=1, keepdims=True)
        sums_ref[...] = jnp.broadcast_to(total, (block, 128))
        whole_ref[...] = whole * gain_ref[...]

    whole, sums = pl.pallas_call(
        kernel,
        grid=(pieces,),
        in_specs=[
            pl.BlockSpec((count, block, 2 * first), lambda step: (0, step, 0)),
            pl.BlockSpec((count, block, 2 * padded), lambda step: (0, step, 0)),
            pl.BlockSpec((block, columns), lambda step: (step, 0)),
            pl.BlockSpec((block, 1), lambda step: (step, 0)),
        ],
        out_specs=[
            pl.BlockSpec((block, columns), lambda step: (step, 0)),
            pl.BlockSpec((block, 128), lambda step: (step, 0)),
        ],
        out_shape=[
            jax.ShapeDtypeStruct((rows, columns), jnp.float32),
            jax.ShapeDtypeStruct((rows, 128), jnp.float32),
        ],
        compiler_params=vmem_params,
        cost_estimate=pl.CostEstimate(
            flops=2 * rows * columns, bytes_accessed=8 * rows * columns, transcendentals=0
        ),
    )(first_part, second_part, gate_up, gain[:, None])
    return whole, sums[:, 0]


def place_rows(me_ref, pieces, refs, weight_ref):
    place = 0
    for mask, parts in pieces:
        shard = sum(part.shape[0] for part in parts)
        begin = (me_ref[0] ^ mask) * shard
        for part in parts:
            rows = part.shape[0]
            weight_ref[pl.ds(pl.multiple_of(begin, rows), rows)] = refs[place][...]
            begin = begin + rows
            place += 1


def project(me, normed, pieces, bias, cosine, sine):
    tokens = normed.shape[0]
    width = bias.shape[0]
    block = 512
    flat = [part for unused_mask, parts in pieces for part in parts]

    def kernel(me_ref, normed_ref, bias_ref, cosine_ref, sine_ref, *refs):
        out_ref, weight_ref = refs[len(flat) :]
        place_rows(me_ref, pieces, refs, weight_ref)
        product = dot_f32(normed_ref[...], weight_ref[...]) + bias_ref[...]
        for head in range(block // HEAD_SIZE):
            lanes = slice(head * HEAD_SIZE, (head + 1) * HEAD_SIZE)
            plain = product[:, lanes]
            turned = plain * cosine_ref[...] + pltpu.roll(plain, HEAD_SIZE // 2, 1) * sine_ref[...]
            column = pl.program_id(0) * block + head * HEAD_SIZE
            out_ref[:, lanes] = jnp.where(column < QD + KD, turned, plain).astype(jnp.bfloat16)

    return pl.pallas_call(
        kernel,
        grid_spec=pltpu.PrefetchScalarGridSpec(
            num_scalar_prefetch=1,
            grid=(width // block,),
            in_specs=[
                pl.BlockSpec((tokens, D), lambda step, me_ref: (0, 0)),
                pl.BlockSpec((1, block), lambda step, me_ref: (0, step)),
                pl.BlockSpec((tokens, HEAD_SIZE), lambda step, me_ref: (0, 0)),
                pl.BlockSpec((tokens, HEAD_SIZE), lambda step, me_ref: (0, 0)),
            ]
            + [
                pl.BlockSpec((part.shape[0], block), lambda step, me_ref: (0, step))
                for part in flat
            ],
            out_specs=pl.BlockSpec((tokens, block), lambda step, me_ref: (0, step)),
            scratch_shapes=[pltpu.VMEM((D, block), jnp.bfloat16)],
        ),
        out_shape=jax.ShapeDtypeStruct((tokens, width), jnp.bfloat16),
        compiler_params=vmem_params,
        cost_estimate=pl.CostEstimate(
            flops=2 * tokens * D * width, bytes_accessed=2 * D * width, transcendentals=0
        ),
    )(me, normed, bias[None], cosine, sine, *flat)


def project_back(me, grad_projected, pieces):
    tokens, width = grad_projected.shape
    flat = [part for unused_mask, parts in pieces for part in parts]

    def kernel(me_ref, grad_ref, *refs):
        out_ref, weight_ref = refs[len(flat) :]
        place_rows(me_ref, pieces, refs, weight_ref)
        out_ref[...] = dot_right_t(grad_ref[...], weight_ref[...])

    whole = lambda part: pl.BlockSpec(part.shape, lambda step, me_ref: (0, 0))
    return pl.pallas_call(
        kernel,
        grid_spec=pltpu.PrefetchScalarGridSpec(
            num_scalar_prefetch=1,
            grid=(1,),
            in_specs=[whole(grad_projected)] + [whole(part) for part in flat],
            out_specs=pl.BlockSpec((tokens, D), lambda step, me_ref: (0, 0)),
            scratch_shapes=[pltpu.VMEM((D, width), jnp.bfloat16)],
        ),
        out_shape=jax.ShapeDtypeStruct((tokens, D), jnp.float32),
        compiler_params=vmem_params,
        cost_estimate=pl.CostEstimate(
            flops=2 * tokens * D * width, bytes_accessed=2 * D * width, transcendentals=0
        ),
    )(me, grad_projected, *flat)


def fill_bias(at_ref, position_ref, bias_ref):
    tokens, keys = bias_ref.shape
    row = lax.broadcasted_iota(jnp.int32, (tokens, keys), 0)
    column = lax.broadcasted_iota(jnp.int32, (tokens, keys), 1)
    back = column // tokens
    query_index = at_ref[0] * tokens + row
    key_index = (at_ref[0] - back) * tokens + (column - back * tokens)
    allowed = (key_index <= query_index) & (key_index >= query_index - position_ref[...])
    bias_ref[...] = jnp.where(allowed, 0.0, masked_score)


def join_keys(refs, key_ref, value_ref):
    @pl.when(pl.program_id(0) % GROUP == 0)
    def _():
        for place in range(len(refs)):
            tokens = refs[0].shape[0]
            if (place + 1) * tokens > key_ref.shape[0]:
                break
            rows = slice(place * tokens, (place + 1) * tokens)
            key_ref[rows] = refs[2 * place][...]
            value_ref[rows] = refs[2 * place + 1][...]


def key_specs(both_pieces):
    specs = []
    for piece in both_pieces:
        shape = (piece.shape[0], HEAD_SIZE)
        specs.append(pl.BlockSpec(shape, lambda head, at: (0, head // GROUP)))
        specs.append(pl.BlockSpec(shape, lambda head, at: (0, KEY_VALUE_HEADS + head // GROUP)))
    return specs


def attend(at, position, projected, both_pieces):
    tokens = projected.shape[0]
    count = len(both_pieces)
    keys = count * tokens

    def kernel(at_ref, position_ref, query_ref, *refs):
        out_ref, turn_ref, log_ref, bias_ref, key_ref, value_ref = refs[2 * count :]

        @pl.when(pl.program_id(0) == 0)
        def _():
            fill_bias(at_ref, position_ref, bias_ref)

        join_keys(refs, key_ref, value_ref)

        scores = dot_right_t(query_ref[...], key_ref[...]) * score_scale + bias_ref[...]
        top = jnp.max(scores, axis=1, keepdims=True)
        raised = jnp.exp(scores - top)
        total = jnp.sum(raised, axis=1, keepdims=True)
        probs = (raised * (1.0 / total)).astype(jnp.bfloat16)
        result = dot_f32(probs, value_ref[...])
        out_ref[...] = result.astype(jnp.bfloat16)
        turn_ref[...] = result.T.astype(jnp.bfloat16)
        log_ref[0] = top + jnp.log(total)

    return pl.pallas_call(
        kernel,
        grid_spec=pltpu.PrefetchScalarGridSpec(
            num_scalar_prefetch=1,
            grid=(QUERY_HEADS,),
            in_specs=[
                pl.BlockSpec((tokens, 1), lambda head, at: (0, 0)),
                pl.BlockSpec((tokens, HEAD_SIZE), lambda head, at: (0, head)),
            ]
            + key_specs(both_pieces),
            out_specs=[
                pl.BlockSpec((tokens, HEAD_SIZE), lambda head, at: (0, head)),
                pl.BlockSpec((HEAD_SIZE, tokens), lambda head, at: (head, 0)),
                pl.BlockSpec((1, tokens, 1), lambda head, at: (head, 0, 0)),
            ],
            scratch_shapes=[
                pltpu.VMEM((tokens, keys), jnp.float32),
                pltpu.VMEM((keys, HEAD_SIZE), jnp.bfloat16),
                pltpu.VMEM((keys, HEAD_SIZE), jnp.bfloat16),
            ],
        ),
        out_shape=[
            jax.ShapeDtypeStruct((tokens, QD), jnp.bfloat16),
            jax.ShapeDtypeStruct((QD, tokens), jnp.bfloat16),
            jax.ShapeDtypeStruct((QUERY_HEADS, tokens, 1), jnp.float32),
        ],
        compiler_params=vmem_params,
        cost_estimate=pl.CostEstimate(
            flops=8 * tokens * keys * QD,
            bytes_accessed=8 * tokens * QD,
            transcendentals=QUERY_HEADS * tokens * keys,
        ),
    )(at, position, projected, *[piece for piece in both_pieces for unused in range(2)])


def attend_backward(at, position, projected, both_pieces, incoming, log_total, cosine, sine):
    tokens = projected.shape[0]
    count = len(both_pieces)
    keys = count * tokens

    def kernel(
        at_ref,
        position_ref,
        query_ref,
        incoming_ref,
        log_ref,
        cosine_ref,
        sine_ref,
        *refs,
    ):
        query_grad_ref, key_grad_ref, value_grad_ref = refs[2 * count : 2 * count + 3]
        bias_ref, key_total, value_total, key_ref, value_ref = refs[2 * count + 3 :]
        head = pl.program_id(0)
        join_keys(refs, key_ref, value_ref)

        @pl.when(head == 0)
        def _():
            fill_bias(at_ref, position_ref, bias_ref)

        @pl.when(head % GROUP == 0)
        def _():
            key_total[...] = jnp.zeros_like(key_total)
            value_total[...] = jnp.zeros_like(value_total)

        scores = dot_right_t(query_ref[...], key_ref[...]) * score_scale + bias_ref[...]
        probs = jnp.exp(scores - log_ref[0])
        grad_probs = dot_right_t(incoming_ref[...], value_ref[...])
        inner = jnp.sum(grad_probs * probs, axis=1, keepdims=True)
        grad_scores = (probs * (grad_probs - inner)).astype(jnp.bfloat16)
        value_total[...] += dot_left_t(incoming_ref[...], probs.astype(jnp.bfloat16))
        key_total[...] += dot_left_t(query_ref[...], grad_scores)
        plain = dot_f32(grad_scores, key_ref[...]) * score_scale
        query_grad_ref[...] = (
            plain * cosine_ref[...] - pltpu.roll(plain, HEAD_SIZE // 2, 1) * sine_ref[...]
        ).astype(jnp.bfloat16)

        @pl.when(head % GROUP == GROUP - 1)
        def _():
            key_grad_ref[...] = (key_total[...] * score_scale).T
            value_grad_ref[...] = value_total[...].T

    return pl.pallas_call(
        kernel,
        grid_spec=pltpu.PrefetchScalarGridSpec(
            num_scalar_prefetch=1,
            grid=(QUERY_HEADS,),
            in_specs=[
                pl.BlockSpec((tokens, 1), lambda head, at: (0, 0)),
                pl.BlockSpec((tokens, HEAD_SIZE), lambda head, at: (0, head)),
                pl.BlockSpec((tokens, HEAD_SIZE), lambda head, at: (0, head)),
                pl.BlockSpec((1, tokens, 1), lambda head, at: (head, 0, 0)),
                pl.BlockSpec((tokens, HEAD_SIZE), lambda head, at: (0, 0)),
                pl.BlockSpec((tokens, HEAD_SIZE), lambda head, at: (0, 0)),
            ]
            + key_specs(both_pieces),
            out_specs=[
                pl.BlockSpec((tokens, HEAD_SIZE), lambda head, at: (0, head)),
                pl.BlockSpec((keys, HEAD_SIZE), lambda head, at: (0, head // GROUP)),
                pl.BlockSpec((keys, HEAD_SIZE), lambda head, at: (0, head // GROUP)),
            ],
            scratch_shapes=[
                pltpu.VMEM((tokens, keys), jnp.float32),
                pltpu.VMEM((HEAD_SIZE, keys), jnp.float32),
                pltpu.VMEM((HEAD_SIZE, keys), jnp.float32),
                pltpu.VMEM((keys, HEAD_SIZE), jnp.bfloat16),
                pltpu.VMEM((keys, HEAD_SIZE), jnp.bfloat16),
            ],
        ),
        out_shape=[
            jax.ShapeDtypeStruct((tokens, QD), jnp.bfloat16),
            jax.ShapeDtypeStruct((keys, KD), jnp.float32),
            jax.ShapeDtypeStruct((keys, KD), jnp.float32),
        ],
        compiler_params=vmem_params,
        cost_estimate=pl.CostEstimate(
            flops=20 * tokens * keys * QD,
            bytes_accessed=8 * tokens * QD,
            transcendentals=QUERY_HEADS * tokens * keys,
        ),
    )(
        at,
        position,
        projected,
        incoming,
        log_total,
        cosine,
        sine,
        *[piece for piece in both_pieces for unused in range(2)],
    )


def unit_part(me, normed_all, grad_out_all, gate_up, down, count, first):
    tokens = normed_all.shape[0]
    block = tokens // count
    width = down.shape[0]
    shard = D // count
    weights = list(gate_up) if first else [gate_up]

    def kernel(me_ref, normed_ref, out_grad_ref, down_ref, *refs):
        weight_refs = refs[: len(weights)]
        hidden_ref, grad_ref = refs[len(weights) : len(weights) + 2]
        weight_ref = weight_refs[0]
        if first:
            ordered_ref, weight_ref = refs[len(weights) + 2 :]
            ordered_ref[...] = out_grad_ref[...]

            @pl.when(pl.program_id(0) == 0)
            def _():
                for mask, ref in enumerate(weight_refs):
                    begin = pl.multiple_of((me_ref[0] ^ mask) * shard, shard)
                    weight_ref[pl.ds(begin, shard)] = ref[...]

        values = dot_f32(normed_ref[...], weight_ref[...])
        gate = values[:, :width]
        up = values[:, width:]
        grad_hidden = dot_right_t(out_grad_ref[...], down_ref[...])
        share = 1.0 / (1.0 + jnp.exp(-gate))
        passed = gate * share
        hidden_ref[...] = (passed * up).astype(jnp.bfloat16)
        grad_ref[:, :width] = (
            grad_hidden * up * share * (1.0 + gate * (1.0 - share))
        ).astype(jnp.bfloat16)
        grad_ref[:, width:] = (grad_hidden * passed).astype(jnp.bfloat16)

    def out_grad_index(step, me_ref):
        return (me_ref[0] ^ mask_at(step, count), 0) if first else (step, 0)

    row = lambda step, me_ref: (step, 0)
    fixed = lambda step, me_ref: (0, 0)
    out_specs = [pl.BlockSpec((block, width), row), pl.BlockSpec((block, 2 * width), row)]
    out_shape = [
        jax.ShapeDtypeStruct((tokens, width), jnp.bfloat16),
        jax.ShapeDtypeStruct((tokens, 2 * width), jnp.bfloat16),
    ]
    if first:
        out_specs += [pl.BlockSpec((block, D), row), pl.BlockSpec((D, 2 * width), fixed)]
        out_shape += [
            jax.ShapeDtypeStruct((tokens, D), jnp.bfloat16),
            jax.ShapeDtypeStruct((D, 2 * width), jnp.bfloat16),
        ]
    return pl.pallas_call(
        kernel,
        grid_spec=pltpu.PrefetchScalarGridSpec(
            num_scalar_prefetch=1,
            grid=(count,),
            in_specs=[
                pl.BlockSpec((block, D), row),
                pl.BlockSpec((block, D), out_grad_index),
                pl.BlockSpec((width, D), fixed),
            ]
            + [pl.BlockSpec(weight.shape, fixed) for weight in weights],
            out_specs=out_specs,
        ),
        out_shape=out_shape,
        compiler_params=vmem_params,
        cost_estimate=pl.CostEstimate(
            flops=6 * tokens * D * width,
            bytes_accessed=4 * tokens * D + 6 * tokens * width + 6 * D * width,
            transcendentals=tokens * width,
        ),
    )(me, normed_all, grad_out_all, down, *weights)


def row_terms(me, turned, right, rows_out):
    count, shard, tokens = turned.shape
    width = right.shape[1]
    lanes = width // 128
    half = count // 2
    spare = rows_out - shard * lanes

    def kernel(me_ref, turned_ref, right_ref, odd_ref, even_ref, *scratch):
        step = pl.program_id(0)
        if spare:

            @pl.when(step == 0)
            def _():
                sums = jnp.sum(right_ref[...].astype(jnp.float32), axis=0, keepdims=True)
                scratch[0][...] = jnp.zeros_like(scratch[0])
                for group in range(lanes):
                    scratch[0][group : group + 1] = sums[:, group * 128 : (group + 1) * 128]

        term = dot_f32(turned_ref[0], right_ref[...]).astype(jnp.bfloat16)

        def store(out_ref):
            for group in range(lanes):
                out_ref[0, group * shard : (group + 1) * shard] = term[
                    :, group * 128 : (group + 1) * 128
                ]
            if spare:
                out_ref[0, lanes * shard :] = scratch[0][...].astype(jnp.bfloat16)

        pl.when(step < half)(lambda: store(odd_ref))
        pl.when(step >= half)(lambda: store(even_ref))

    out = jax.ShapeDtypeStruct((half, rows_out, 128), jnp.bfloat16)
    return pl.pallas_call(
        kernel,
        grid_spec=pltpu.PrefetchScalarGridSpec(
            num_scalar_prefetch=1,
            grid=(count,),
            in_specs=[
                pl.BlockSpec(
                    (1, shard, tokens),
                    lambda step, me_ref: (me_ref[0] ^ mask_at(step, count), 0, 0),
                ),
                pl.BlockSpec((tokens, width), lambda step, me_ref: (0, 0)),
            ],
            out_specs=[
                pl.BlockSpec(
                    (1, rows_out, 128), lambda step, me_ref: (jnp.minimum(step, half - 1), 0, 0)
                ),
                pl.BlockSpec(
                    (1, rows_out, 128), lambda step, me_ref: (jnp.maximum(step - half, 0), 0, 0)
                ),
            ],
            scratch_shapes=[pltpu.VMEM((spare, 128), jnp.float32)] if spare else [],
        ),
        out_shape=[out, out],
        compiler_params=vmem_params,
        cost_estimate=pl.CostEstimate(
            flops=2 * D * tokens * width,
            bytes_accessed=256 * count * rows_out,
            transcendentals=0,
        ),
    )(me, turned, right)


def shards(
    tokens,
    positions,
    cotangent,
    attn_norm,
    ffn_norm,
    in_proj,
    in_bias,
    out_proj,
    gate_up,
    down_proj,
):
    token_rows = tokens.shape[1]
    fsdp_count = lax.axis_size("fsdp")
    ctx_count = lax.axis_size("ctx")
    fsdp_me = lax.axis_index("fsdp")
    me = fsdp_me.astype(jnp.int32)[None]
    at = lax.axis_index("ctx").astype(jnp.int32)[None]
    units = FF // fsdp_count
    shard_d = D // fsdp_count
    residual_in = tokens[0].astype(jnp.float32)
    position = positions[0]
    grad_out_b = cotangent[0]

    first_units, second_units, padded_units = unit_widths(units)
    bias_full = gather_small(in_bias).reshape(-1)
    in_scaled = (in_proj.astype(jnp.float32) * attn_norm[:, None]).astype(jnp.bfloat16)
    first_blocks, second_blocks = split_units(me, gate_up, ffn_norm, fsdp_count)
    cosine, sine = rotary_tables(position)
    normed_b = rms_scale(residual_in).astype(jnp.bfloat16)
    in_pieces = gather_pieces(in_scaled, first_blocks, cosine, normed_b)
    gated_blocks = after(first_blocks, in_pieces[0], in_pieces[2], in_pieces[4])
    gate_up_first = [gated_blocks[0]] + [
        exchange(gated_blocks[mask], mask) for mask in range(1, fsdp_count)
    ]
    out_full = lax.all_gather(after(out_proj, in_pieces), "fsdp", axis=0, tiled=True)

    projected = project(
        me, after(normed_b, gate_up_first[1], gate_up_first[2]), in_pieces, bias_full, cosine, sine
    )
    both_b = projected[:, QD:]
    both_pieces = [both_b] + [
        lax.ppermute(both_b, "ctx", [(s, s + back) for s in range(ctx_count - back)])
        for back in range(1, ctx_count)
    ]
    grad_out_all = lax.all_gather(after(grad_out_b, projected), "fsdp", axis=0, tiled=True)
    both_pieces = after(both_pieces, gate_up_first[3], gate_up_first[4])
    attended_b, attended_turned, log_total = attend(at, position[:, None], projected, both_pieces)
    attended_b = after(attended_b, gate_up_first)
    middle = residual_in + dot_f32(attended_b, out_full)
    normed_ffn_b = rms_scale(middle).astype(jnp.bfloat16)
    normed_again, down_again = after((normed_b, down_proj), normed_ffn_b)
    normed_turned = normed_again.T.reshape(fsdp_count, shard_d, token_rows)
    down_first = down_again[:first_units]
    down_second = jnp.pad(down_again[first_units:], ((0, padded_units - second_units), (0, 0)))

    normed_ffn_all = gather_masks(normed_ffn_b, normed_turned, down_first, down_second)
    gate_up_second = swap_blocks(after(second_blocks, normed_ffn_all)).reshape(
        D, 2 * padded_units
    )
    hidden_first, grad_first, grad_out_all, gate_up_first = unit_part(
        me, normed_ffn_all, grad_out_all, gate_up_first, down_first, fsdp_count, True
    )
    odd_rows = normed_ffn_all.shape[0] // 2

    def down_term(hidden, *gates):
        return dot_left_t(after(hidden, *gates), grad_out_all).astype(jnp.bfloat16)

    def gate_term(grad, *gates):
        term = dot_left_t(normed_ffn_all, after(grad, *gates)).astype(jnp.bfloat16)
        return term.reshape(fsdp_count, shard_d, -1)

    def input_grads(rows, *gates):
        return (
            (
                dot_right_t(after(grad_first, *gates)[rows], gate_up_first)
                + dot_right_t(grad_second[rows], gate_up_second)
            )
            .astype(jnp.bfloat16)
            .reshape(fsdp_count // 2, token_rows, D)
        )

    def down_outs(rows, *gates):
        return (
            (
                dot_f32(after(hidden_first, *gates)[rows], down_first)
                + dot_f32(hidden_second[rows], down_second)
            )
            .astype(jnp.bfloat16)
            .reshape(fsdp_count // 2, token_rows, D)
        )

    down_term_a = down_term(hidden_first)
    gate_term_a = gate_term(grad_first, down_term_a)
    down_sum_a, gate_sum_a = lax.psum((down_term_a, gate_term_a), "ctx")
    hidden_second, grad_second = unit_part(
        me,
        after(normed_ffn_all, gate_term_a),
        grad_out_all,
        gate_up_second,
        down_second,
        fsdp_count,
        False,
    )
    grad_normed_odd = input_grads(slice(0, odd_rows), hidden_second)
    normed_sum = MaskSum(grad_normed_odd)
    grad_normed_even = input_grads(slice(odd_rows, None), grad_normed_odd)
    sent = normed_sum.second(grad_normed_even)
    gate_term_b = gate_term(grad_second, sent)
    gate_swapped_b = swap_blocks(gate_term_b)
    sent = normed_sum.third(gate_term_b)
    down_term_b = down_term(hidden_second, sent)[:second_units]
    down_sum_b, gate_sum_b = lax.psum((down_term_b, gate_swapped_b), "ctx")
    grad_normed_ffn = normed_sum.result(down_term_b).astype(jnp.float32)

    grad_out = grad_out_b.astype(jnp.float32)
    grad_middle = grad_out + norm_backward(middle, grad_normed_ffn)
    grad_middle_b = grad_middle.astype(jnp.bfloat16)
    grad_attended_b = dot_right_t(after(grad_middle_b, gate_swapped_b), out_full).astype(
        jnp.bfloat16
    )
    in_rows = shard_d * in_proj.shape[1] // 128
    out_rows = shard_d * D // 128
    out_odd, out_even = row_terms(
        me,
        attended_turned.reshape(fsdp_count, shard_d, token_rows),
        after(grad_middle_b, grad_attended_b),
        out_rows,
    )
    out_sum = MaskSum(out_odd)
    query_grad, key_grads, value_grads = attend_backward(
        at,
        position[:, None],
        projected,
        both_pieces,
        after(grad_attended_b, out_even),
        log_total,
        cosine,
        sine,
    )
    both_sent = [
        lax.ppermute(
            jnp.concatenate(
                [
                    grads[back * token_rows : (back + 1) * token_rows].astype(jnp.bfloat16)
                    for grads in (key_grads, value_grads)
                ],
                axis=1,
            ),
            "ctx",
            [(s + back, s) for s in range(ctx_count - back)],
        )
        for back in range(1, ctx_count)
    ]
    sent = out_sum.second(out_even, query_grad)
    down_odd = down_outs(slice(0, odd_rows), sent)
    block_sum = MaskSum(down_odd)
    sent = out_sum.third(down_odd)
    down_even = down_outs(slice(odd_rows, None), sent)
    both_grad = jnp.concatenate([key_grads[:token_rows], value_grads[:token_rows]], axis=1)
    for piece in after(both_sent, down_even):
        both_grad = both_grad + piece.astype(jnp.float32)
    turned_back = []
    for head in range(KEY_VALUE_HEADS):
        plain = both_grad[:, head * HEAD_SIZE : (head + 1) * HEAD_SIZE]
        turned_back.append(plain * cosine - jnp.roll(plain, HEAD_SIZE // 2, axis=1) * sine)
    grad_projected_b = jnp.concatenate(
        [query_grad]
        + [part.astype(jnp.bfloat16) for part in turned_back]
        + [both_grad[:, KD:].astype(jnp.bfloat16)],
        axis=1,
    )
    in_odd, in_even = row_terms(me, normed_turned, grad_projected_b, in_rows + 32)
    in_sum = MaskSum(in_odd)
    grad_normed = project_back(me, after(grad_projected_b, in_even), in_pieces)
    sent = in_sum.second(in_even, grad_normed)
    tokens_grad = grad_middle + norm_backward(residual_in, after(grad_normed, sent))
    sent = block_sum.second(down_even, tokens_grad)
    sent = in_sum.third(sent)
    out_part = out_sum.result(sent)
    sent = block_sum.third(out_part)
    in_part = in_sum.result(sent)
    gate_swapped_a = swap_blocks(after(gate_sum_a, out_part))
    terms_total = ctx_total(jnp.concatenate([in_part, out_part], axis=0)).astype(jnp.float32)
    block_out = middle + block_sum.result(in_part).astype(jnp.float32)
    down_grad = jnp.concatenate([down_sum_a, down_sum_b], axis=0).astype(jnp.float32)
    gate_grad, ffn_grad = join_units(gate_swapped_a, gate_sum_b, gate_up, ffn_norm)

    def lanes_back(rows):
        return rows.reshape(-1, shard_d, 128).transpose(1, 0, 2).reshape(shard_d, -1)

    in_total = lanes_back(terms_total[:in_rows])
    out_grad = lanes_back(terms_total[in_rows + 32 :])
    bias_span = in_bias.shape[0]
    bias_grad = lax.dynamic_slice_in_dim(
        terms_total[in_rows : in_rows + in_proj.shape[1] // 128].reshape(-1),
        fsdp_me * bias_span,
        bias_span,
    )
    in_grad = in_total * attn_norm[:, None]
    attn_grad = jnp.sum(in_total * in_proj.astype(jnp.float32), axis=1)
    return (
        block_out.astype(jnp.bfloat16).reshape(1, token_rows, D),
        tokens_grad.reshape(1, token_rows, D),
        attn_grad,
        ffn_grad,
        in_grad,
        bias_grad,
        out_grad,
        gate_grad,
        down_grad,
    )


def solution(mesh):
    in_specs = (
        P("fsdp", "ctx", None),
        P("fsdp", "ctx"),
        P("fsdp", "ctx", None),
        P("fsdp"),
        P("fsdp"),
        P("fsdp", None),
        P("fsdp"),
        P("fsdp", None),
        P("fsdp", None),
        P("fsdp", None),
    )
    out_specs = (
        P("fsdp", "ctx", None),
        P("fsdp", "ctx", None),
        P("fsdp"),
        P("fsdp"),
        P("fsdp", None),
        P("fsdp"),
        P("fsdp", None),
        P("fsdp", None),
        P("fsdp", None),
    )
    return jax.shard_map(shards, mesh=mesh, in_specs=in_specs, out_specs=out_specs, check_vma=False)
```

```python
import jax
import jax.numpy as jnp
from jax import lax
from jax.experimental import pallas as pl
from jax.experimental.pallas import tpu as pltpu
from jax.sharding import PartitionSpec as P

D = 1536
QUERY_HEADS = 12
KEY_VALUE_HEADS = 2
HEAD_SIZE = 128
FF = 8960
QD = QUERY_HEADS * HEAD_SIZE
KD = KEY_VALUE_HEADS * HEAD_SIZE
GROUP = QUERY_HEADS // KEY_VALUE_HEADS


norm_eps = 1e-06
rope_base = 1000000.0
masked_score = -1e30
score_scale = HEAD_SIZE ** (-0.5)
vmem_params = pltpu.CompilerParams(vmem_limit_bytes=48 * 1024 * 1024)


def rms_scale(value_rows):
    return value_rows * lax.rsqrt(
        jnp.mean(value_rows * value_rows, axis=-1, keepdims=True) + norm_eps
    )


def norm_backward(value_rows, incoming):
    unused_out, pullback = jax.vjp(rms_scale, value_rows)
    return pullback(incoming)[0]


def rotary_tables(position):
    lane = jnp.arange(HEAD_SIZE, dtype=jnp.int32)
    half = HEAD_SIZE // 2
    frequencies = rope_base ** (-((lane % half).astype(jnp.float32) * (2.0 / HEAD_SIZE)))
    angles = position.astype(jnp.float32)[:, None] * frequencies[None, :]
    sign = jnp.where(lane < half, -1.0, 1.0)
    return jnp.cos(angles), jnp.sin(angles) * sign[None, :]


def dot_f32(left, right):
    return jnp.dot(left, right, preferred_element_type=jnp.float32)


def dot_right_t(left, right):
    return lax.dot_general(
        left, right, (((1,), (1,)), ((), ())), preferred_element_type=jnp.float32
    )


def dot_left_t(left, right):
    return lax.dot_general(
        left, right, (((0,), (0,)), ((), ())), preferred_element_type=jnp.float32
    )


def add_low(left, right):
    return left + right


def after(value, *earlier):
    return lax.optimization_barrier((value, earlier))[0]


def exchange(value, mask):
    count = lax.axis_size("fsdp")
    return lax.ppermute(value, "fsdp", [(place, place ^ mask) for place in range(count)])


def gather_pieces(block, *gates):
    count = lax.axis_size("fsdp")
    if count != 8:
        found = [[block]] + [[exchange(block, mask)] for mask in range(2, count, 2)]
    else:
        half = block.shape[0] // 2
        by_x = exchange(block, 2)
        by_y = exchange(block, 4)
        other = exchange(block, 1)
        by_x, by_y = after((by_x, by_y), *gates)
        top = exchange(by_x[:half], 4)
        bottom = exchange(by_y[half:], 2)
        found = [[block], [by_x], [by_y], [top, bottom]]
        others = [[other], [exchange(by_x, 1)], [exchange(by_y, 1)]]
        others.append([exchange(top, 1), exchange(bottom, 1)])
        return [(2 * place, rows) for place, rows in enumerate(found)] + [
            (2 * place + 1, rows) for place, rows in enumerate(others)
        ]
    pieces = []
    for place, rows in enumerate(found):
        pieces.append((2 * place, rows))
        pieces.append((2 * place + 1, [exchange(part, 1) for part in rows]))
    return pieces


def gather_masks(block, *gates):
    count = lax.axis_size("fsdp")
    rows = block.shape[0]
    whole = jnp.zeros((count * rows, block.shape[1]), block.dtype)
    for mask, parts in gather_pieces(block, *gates):
        first = place_of(mask, count) * rows
        for part in parts:
            whole = lax.dynamic_update_slice(whole, part, (first, 0))
            first += part.shape[0]
    return whole


def gather_small(value):
    count = lax.axis_size("fsdp")
    me = lax.axis_index("fsdp")
    bits = count.bit_length() - 1
    found = value
    for bit in list(range(1, bits)) + [0]:
        got = exchange(found, 1 << bit)
        low = (me >> bit) % 2 == 0
        found = jnp.stack([jnp.where(low, found, got), jnp.where(low, got, found)])
    return jnp.moveaxis(found, 0, bits - 1).reshape(count, -1)


def place_of(mask, count):
    return mask // 2 + (1 - mask % 2) * (count // 2)


def mask_at(place, count):
    return jnp.where(place < count // 2, 2 * place + 1, 2 * place - count)


class MaskSum:
    def __init__(self, odd):
        self.got = exchange(odd, 1)

    def second(self, even, *gates):
        count = lax.axis_size("fsdp")
        self.kept = add_low(even, after(self.got, *gates))
        if count == 8:
            half = self.kept.shape[1] // 2
            self.by_x = exchange(self.kept[1::2, :half], 2)
            self.by_y = exchange(self.kept[2:, half:], 4)
        else:
            span = count
            while self.kept.shape[0] > 1:
                span //= 2
                half = self.kept.shape[0] // 2
                self.kept = add_low(self.kept[:half], exchange(self.kept[half:], span))
        return self.kept

    def third(self, *gates):
        if lax.axis_size("fsdp") != 8:
            return self.kept
        half = self.kept.shape[1] // 2
        by_x, by_y = after((self.by_x, self.by_y), *gates)
        self.top = add_low(self.kept[0::2, :half], by_x)
        self.bottom = add_low(self.kept[:2, half:], by_y)
        self.last_y = exchange(self.top[1], 4)
        self.last_x = exchange(self.bottom[1], 2)
        return self.top, self.bottom

    def result(self, *gates):
        if lax.axis_size("fsdp") != 8:
            return self.kept[0]
        last_y, last_x = after((self.last_y, self.last_x), *gates)
        return jnp.concatenate(
            [add_low(self.top[0], last_y), add_low(self.bottom[0], last_x)], axis=0
        )


def swap_blocks(blocks):
    return lax.all_to_all(blocks, "fsdp", 0, 0, tiled=True)


def ctx_total(part):
    count = lax.axis_size("ctx")
    middle = count // 2
    me = lax.axis_index("ctx")
    for hop in range(middle - 1):
        part = add_low(
            part,
            lax.ppermute(part, "ctx", [(hop, hop + 1), (count - 1 - hop, count - 2 - hop)]),
        )
    part = add_low(
        part, lax.ppermute(part, "ctx", [(middle - 1, middle), (middle, middle - 1)])
    )
    for hop in reversed(range(middle - 1)):
        got = lax.ppermute(part, "ctx", [(hop + 1, hop), (count - 2 - hop, count - 1 - hop)])
        part = jnp.where((me == hop) | (me == count - 1 - hop), got, part)
    return lax.optimization_barrier(part)


def unit_widths(units):
    first = units // 256 * 128
    second = units - first
    return first, second, -(-second // 128) * 128


def split_units(me, gate_up, gain, count):
    rows, columns = gate_up.shape
    span = columns // 2
    units = span // count
    first, second, padded = unit_widths(units)
    block = 48

    def kernel(me_ref, weight_ref, gain_ref, first_ref, second_ref):
        def scaled(begin, end):
            value = weight_ref[:, begin:end].astype(jnp.float32) * gain_ref[...]
            return value.astype(gate_up.dtype)

        for owner in range(count):
            for side in range(2):
                begin = side * span + owner * units
                first_ref[me_ref[0] ^ owner, :, side * first : (side + 1) * first] = scaled(
                    begin, begin + first
                )
                second_ref[owner, :, side * padded : side * padded + second] = scaled(
                    begin + first, begin + units
                )
                if padded > second:
                    second_ref[
                        owner, :, side * padded + second : (side + 1) * padded
                    ] = jnp.zeros((block, padded - second), gate_up.dtype)

    return pl.pallas_call(
        kernel,
        grid_spec=pltpu.PrefetchScalarGridSpec(
            num_scalar_prefetch=1,
            grid=(rows // block,),
            in_specs=[
                pl.BlockSpec((block, columns), lambda step, me_ref: (step, 0)),
                pl.BlockSpec((block, 1), lambda step, me_ref: (step, 0)),
            ],
            out_specs=[
                pl.BlockSpec((count, block, 2 * first), lambda step, me_ref: (0, step, 0)),
                pl.BlockSpec((count, block, 2 * padded), lambda step, me_ref: (0, step, 0)),
            ],
        ),
        out_shape=[
            jax.ShapeDtypeStruct((count, rows, 2 * first), gate_up.dtype),
            jax.ShapeDtypeStruct((count, rows, 2 * padded), gate_up.dtype),
        ],
        compiler_params=vmem_params,
        cost_estimate=pl.CostEstimate(
            flops=0, bytes_accessed=4 * rows * columns, transcendentals=0
        ),
    )(me, gate_up, gain[:, None])


def join_units(first_part, second_part, gate_up, gain):
    rows, columns = gate_up.shape
    count = first_part.shape[0]
    block = 48
    pieces = rows // block
    span = columns // 2
    units = span // count
    first, second, padded = unit_widths(units)

    def kernel(first_ref, second_ref, weight_ref, gain_ref, whole_ref, sums_ref):
        for owner in range(count):
            for side in range(2):
                begin = side * span + owner * units
                whole_ref[:, begin : begin + first] = first_ref[
                    owner, :, side * first : (side + 1) * first
                ].astype(jnp.float32)
                whole_ref[:, begin + first : begin + units] = second_ref[
                    owner, :, side * padded : side * padded + second
                ].astype(jnp.float32)
        whole = whole_ref[...]
        total = jnp.sum(whole * weight_ref[...].astype(jnp.float32), axis=1, keepdims=True)
        sums_ref[...] = jnp.broadcast_to(total, (block, 128))
        whole_ref[...] = whole * gain_ref[...]

    whole, sums = pl.pallas_call(
        kernel,
        grid=(pieces,),
        in_specs=[
            pl.BlockSpec((count, block, 2 * first), lambda step: (0, step, 0)),
            pl.BlockSpec((count, block, 2 * padded), lambda step: (0, step, 0)),
            pl.BlockSpec((block, columns), lambda step: (step, 0)),
            pl.BlockSpec((block, 1), lambda step: (step, 0)),
        ],
        out_specs=[
            pl.BlockSpec((block, columns), lambda step: (step, 0)),
            pl.BlockSpec((block, 128), lambda step: (step, 0)),
        ],
        out_shape=[
            jax.ShapeDtypeStruct((rows, columns), jnp.float32),
            jax.ShapeDtypeStruct((rows, 128), jnp.float32),
        ],
        compiler_params=vmem_params,
        cost_estimate=pl.CostEstimate(
            flops=2 * rows * columns, bytes_accessed=8 * rows * columns, transcendentals=0
        ),
    )(first_part, second_part, gate_up, gain[:, None])
    return whole, sums[:, 0]


def place_rows(me_ref, pieces, refs, weight_ref):
    place = 0
    for mask, parts in pieces:
        shard = sum(part.shape[0] for part in parts)
        begin = (me_ref[0] ^ mask) * shard
        for part in parts:
            rows = part.shape[0]
            weight_ref[pl.ds(pl.multiple_of(begin, rows), rows)] = refs[place][...]
            begin = begin + rows
            place += 1


def project(me, normed, pieces, bias, cosine, sine):
    tokens = normed.shape[0]
    width = bias.shape[0]
    block = 512
    flat = [part for unused_mask, parts in pieces for part in parts]

    def kernel(me_ref, normed_ref, bias_ref, cosine_ref, sine_ref, *refs):
        out_ref, weight_ref = refs[len(flat) :]
        place_rows(me_ref, pieces, refs, weight_ref)
        product = dot_f32(normed_ref[...], weight_ref[...]) + bias_ref[...]
        for head in range(block // HEAD_SIZE):
            lanes = slice(head * HEAD_SIZE, (head + 1) * HEAD_SIZE)
            plain = product[:, lanes]
            turned = plain * cosine_ref[...] + pltpu.roll(plain, HEAD_SIZE // 2, 1) * sine_ref[...]
            column = pl.program_id(0) * block + head * HEAD_SIZE
            out_ref[:, lanes] = jnp.where(column < QD + KD, turned, plain).astype(jnp.bfloat16)

    return pl.pallas_call(
        kernel,
        grid_spec=pltpu.PrefetchScalarGridSpec(
            num_scalar_prefetch=1,
            grid=(width // block,),
            in_specs=[
                pl.BlockSpec((tokens, D), lambda step, me_ref: (0, 0)),
                pl.BlockSpec((1, block), lambda step, me_ref: (0, step)),
                pl.BlockSpec((tokens, HEAD_SIZE), lambda step, me_ref: (0, 0)),
                pl.BlockSpec((tokens, HEAD_SIZE), lambda step, me_ref: (0, 0)),
            ]
            + [
                pl.BlockSpec((part.shape[0], block), lambda step, me_ref: (0, step))
                for part in flat
            ],
            out_specs=pl.BlockSpec((tokens, block), lambda step, me_ref: (0, step)),
            scratch_shapes=[pltpu.VMEM((D, block), jnp.bfloat16)],
        ),
        out_shape=jax.ShapeDtypeStruct((tokens, width), jnp.bfloat16),
        compiler_params=vmem_params,
        cost_estimate=pl.CostEstimate(
            flops=2 * tokens * D * width, bytes_accessed=2 * D * width, transcendentals=0
        ),
    )(me, normed, bias[None], cosine, sine, *flat)


def project_back(me, grad_projected, pieces):
    tokens, width = grad_projected.shape
    flat = [part for unused_mask, parts in pieces for part in parts]

    def kernel(me_ref, grad_ref, *refs):
        out_ref, weight_ref = refs[len(flat) :]
        place_rows(me_ref, pieces, refs, weight_ref)
        out_ref[...] = dot_right_t(grad_ref[...], weight_ref[...])

    whole = lambda part: pl.BlockSpec(part.shape, lambda step, me_ref: (0, 0))
    return pl.pallas_call(
        kernel,
        grid_spec=pltpu.PrefetchScalarGridSpec(
            num_scalar_prefetch=1,
            grid=(1,),
            in_specs=[whole(grad_projected)] + [whole(part) for part in flat],
            out_specs=pl.BlockSpec((tokens, D), lambda step, me_ref: (0, 0)),
            scratch_shapes=[pltpu.VMEM((D, width), jnp.bfloat16)],
        ),
        out_shape=jax.ShapeDtypeStruct((tokens, D), jnp.float32),
        compiler_params=vmem_params,
        cost_estimate=pl.CostEstimate(
            flops=2 * tokens * D * width, bytes_accessed=2 * D * width, transcendentals=0
        ),
    )(me, grad_projected, *flat)


def fill_bias(at_ref, position_ref, bias_ref):
    tokens, keys = bias_ref.shape
    row = lax.broadcasted_iota(jnp.int32, (tokens, keys), 0)
    column = lax.broadcasted_iota(jnp.int32, (tokens, keys), 1)
    back = column // tokens
    query_index = at_ref[0] * tokens + row
    key_index = (at_ref[0] - back) * tokens + (column - back * tokens)
    allowed = (key_index <= query_index) & (key_index >= query_index - position_ref[...])
    bias_ref[...] = jnp.where(allowed, 0.0, masked_score)


def join_keys(refs, key_ref, value_ref):
    @pl.when(pl.program_id(0) % GROUP == 0)
    def _():
        for place in range(len(refs)):
            tokens = refs[0].shape[0]
            if (place + 1) * tokens > key_ref.shape[0]:
                break
            rows = slice(place * tokens, (place + 1) * tokens)
            key_ref[rows] = refs[2 * place][...]
            value_ref[rows] = refs[2 * place + 1][...]


def key_specs(both_pieces):
    specs = []
    for piece in both_pieces:
        shape = (piece.shape[0], HEAD_SIZE)
        specs.append(pl.BlockSpec(shape, lambda head, at: (0, head // GROUP)))
        specs.append(pl.BlockSpec(shape, lambda head, at: (0, KEY_VALUE_HEADS + head // GROUP)))
    return specs


def attend(at, position, projected, both_pieces):
    tokens = projected.shape[0]
    count = len(both_pieces)
    keys = count * tokens

    def kernel(at_ref, position_ref, query_ref, *refs):
        out_ref, turn_ref, log_ref, bias_ref, key_ref, value_ref = refs[2 * count :]

        @pl.when(pl.program_id(0) == 0)
        def _():
            fill_bias(at_ref, position_ref, bias_ref)

        join_keys(refs, key_ref, value_ref)

        scores = dot_right_t(query_ref[...], key_ref[...]) * score_scale + bias_ref[...]
        top = jnp.max(scores, axis=1, keepdims=True)
        raised = jnp.exp(scores - top)
        total = jnp.sum(raised, axis=1, keepdims=True)
        probs = (raised * (1.0 / total)).astype(jnp.bfloat16)
        result = dot_f32(probs, value_ref[...])
        out_ref[...] = result.astype(jnp.bfloat16)
        turn_ref[...] = result.T.astype(jnp.bfloat16)
        log_ref[0] = top + jnp.log(total)

    return pl.pallas_call(
        kernel,
        grid_spec=pltpu.PrefetchScalarGridSpec(
            num_scalar_prefetch=1,
            grid=(QUERY_HEADS,),
            in_specs=[
                pl.BlockSpec((tokens, 1), lambda head, at: (0, 0)),
                pl.BlockSpec((tokens, HEAD_SIZE), lambda head, at: (0, head)),
            ]
            + key_specs(both_pieces),
            out_specs=[
                pl.BlockSpec((tokens, HEAD_SIZE), lambda head, at: (0, head)),
                pl.BlockSpec((HEAD_SIZE, tokens), lambda head, at: (head, 0)),
                pl.BlockSpec((1, tokens, 1), lambda head, at: (head, 0, 0)),
            ],
            scratch_shapes=[
                pltpu.VMEM((tokens, keys), jnp.float32),
                pltpu.VMEM((keys, HEAD_SIZE), jnp.bfloat16),
                pltpu.VMEM((keys, HEAD_SIZE), jnp.bfloat16),
            ],
        ),
        out_shape=[
            jax.ShapeDtypeStruct((tokens, QD), jnp.bfloat16),
            jax.ShapeDtypeStruct((QD, tokens), jnp.bfloat16),
            jax.ShapeDtypeStruct((QUERY_HEADS, tokens, 1), jnp.float32),
        ],
        compiler_params=vmem_params,
        cost_estimate=pl.CostEstimate(
            flops=8 * tokens * keys * QD,
            bytes_accessed=8 * tokens * QD,
            transcendentals=QUERY_HEADS * tokens * keys,
        ),
    )(at, position, projected, *[piece for piece in both_pieces for unused in range(2)])


def attend_backward(at, position, projected, both_pieces, incoming, log_total, cosine, sine):
    tokens = projected.shape[0]
    count = len(both_pieces)
    keys = count * tokens

    def kernel(
        at_ref,
        position_ref,
        query_ref,
        incoming_ref,
        log_ref,
        cosine_ref,
        sine_ref,
        *refs,
    ):
        query_grad_ref, key_grad_ref, value_grad_ref = refs[2 * count : 2 * count + 3]
        bias_ref, key_total, value_total, key_ref, value_ref = refs[2 * count + 3 :]
        head = pl.program_id(0)
        join_keys(refs, key_ref, value_ref)

        @pl.when(head == 0)
        def _():
            fill_bias(at_ref, position_ref, bias_ref)

        @pl.when(head % GROUP == 0)
        def _():
            key_total[...] = jnp.zeros_like(key_total)
            value_total[...] = jnp.zeros_like(value_total)

        scores = dot_right_t(query_ref[...], key_ref[...]) * score_scale + bias_ref[...]
        probs = jnp.exp(scores - log_ref[0])
        grad_probs = dot_right_t(incoming_ref[...], value_ref[...])
        inner = jnp.sum(grad_probs * probs, axis=1, keepdims=True)
        grad_scores = (probs * (grad_probs - inner)).astype(jnp.bfloat16)
        value_total[...] += dot_left_t(incoming_ref[...], probs.astype(jnp.bfloat16))
        key_total[...] += dot_left_t(query_ref[...], grad_scores)
        plain = dot_f32(grad_scores, key_ref[...]) * score_scale
        query_grad_ref[...] = (
            plain * cosine_ref[...] - pltpu.roll(plain, HEAD_SIZE // 2, 1) * sine_ref[...]
        ).astype(jnp.bfloat16)

        @pl.when(head % GROUP == GROUP - 1)
        def _():
            key_grad_ref[...] = (key_total[...] * score_scale).T
            value_grad_ref[...] = value_total[...].T

    return pl.pallas_call(
        kernel,
        grid_spec=pltpu.PrefetchScalarGridSpec(
            num_scalar_prefetch=1,
            grid=(QUERY_HEADS,),
            in_specs=[
                pl.BlockSpec((tokens, 1), lambda head, at: (0, 0)),
                pl.BlockSpec((tokens, HEAD_SIZE), lambda head, at: (0, head)),
                pl.BlockSpec((tokens, HEAD_SIZE), lambda head, at: (0, head)),
                pl.BlockSpec((1, tokens, 1), lambda head, at: (head, 0, 0)),
                pl.BlockSpec((tokens, HEAD_SIZE), lambda head, at: (0, 0)),
                pl.BlockSpec((tokens, HEAD_SIZE), lambda head, at: (0, 0)),
            ]
            + key_specs(both_pieces),
            out_specs=[
                pl.BlockSpec((tokens, HEAD_SIZE), lambda head, at: (0, head)),
                pl.BlockSpec((keys, HEAD_SIZE), lambda head, at: (0, head // GROUP)),
                pl.BlockSpec((keys, HEAD_SIZE), lambda head, at: (0, head // GROUP)),
            ],
            scratch_shapes=[
                pltpu.VMEM((tokens, keys), jnp.float32),
                pltpu.VMEM((HEAD_SIZE, keys), jnp.float32),
                pltpu.VMEM((HEAD_SIZE, keys), jnp.float32),
                pltpu.VMEM((keys, HEAD_SIZE), jnp.bfloat16),
                pltpu.VMEM((keys, HEAD_SIZE), jnp.bfloat16),
            ],
        ),
        out_shape=[
            jax.ShapeDtypeStruct((tokens, QD), jnp.bfloat16),
            jax.ShapeDtypeStruct((keys, KD), jnp.float32),
            jax.ShapeDtypeStruct((keys, KD), jnp.float32),
        ],
        compiler_params=vmem_params,
        cost_estimate=pl.CostEstimate(
            flops=20 * tokens * keys * QD,
            bytes_accessed=8 * tokens * QD,
            transcendentals=QUERY_HEADS * tokens * keys,
        ),
    )(
        at,
        position,
        projected,
        incoming,
        log_total,
        cosine,
        sine,
        *[piece for piece in both_pieces for unused in range(2)],
    )


def unit_part(me, normed_all, grad_out_all, gate_up, down, count, first):
    tokens = normed_all.shape[0]
    block = tokens // count
    width = down.shape[0]
    shard = D // count
    weights = list(gate_up) if first else [gate_up]

    def kernel(me_ref, normed_ref, out_grad_ref, down_ref, *refs):
        weight_refs = refs[: len(weights)]
        hidden_ref, grad_ref = refs[len(weights) : len(weights) + 2]
        weight_ref = weight_refs[0]
        if first:
            ordered_ref, weight_ref = refs[len(weights) + 2 :]
            ordered_ref[...] = out_grad_ref[...]

            @pl.when(pl.program_id(0) == 0)
            def _():
                for mask, ref in enumerate(weight_refs):
                    begin = pl.multiple_of((me_ref[0] ^ mask) * shard, shard)
                    weight_ref[pl.ds(begin, shard)] = ref[...]

        values = dot_f32(normed_ref[...], weight_ref[...])
        gate = values[:, :width]
        up = values[:, width:]
        grad_hidden = dot_right_t(out_grad_ref[...], down_ref[...])
        share = 1.0 / (1.0 + jnp.exp(-gate))
        passed = gate * share
        hidden_ref[...] = (passed * up).astype(jnp.bfloat16)
        grad_ref[:, :width] = (
            grad_hidden * up * share * (1.0 + gate * (1.0 - share))
        ).astype(jnp.bfloat16)
        grad_ref[:, width:] = (grad_hidden * passed).astype(jnp.bfloat16)

    def out_grad_index(step, me_ref):
        return (me_ref[0] ^ mask_at(step, count), 0) if first else (step, 0)

    row = lambda step, me_ref: (step, 0)
    fixed = lambda step, me_ref: (0, 0)
    out_specs = [pl.BlockSpec((block, width), row), pl.BlockSpec((block, 2 * width), row)]
    out_shape = [
        jax.ShapeDtypeStruct((tokens, width), jnp.bfloat16),
        jax.ShapeDtypeStruct((tokens, 2 * width), jnp.bfloat16),
    ]
    if first:
        out_specs += [pl.BlockSpec((block, D), row), pl.BlockSpec((D, 2 * width), fixed)]
        out_shape += [
            jax.ShapeDtypeStruct((tokens, D), jnp.bfloat16),
            jax.ShapeDtypeStruct((D, 2 * width), jnp.bfloat16),
        ]
    return pl.pallas_call(
        kernel,
        grid_spec=pltpu.PrefetchScalarGridSpec(
            num_scalar_prefetch=1,
            grid=(count,),
            in_specs=[
                pl.BlockSpec((block, D), row),
                pl.BlockSpec((block, D), out_grad_index),
                pl.BlockSpec((width, D), fixed),
            ]
            + [pl.BlockSpec(weight.shape, fixed) for weight in weights],
            out_specs=out_specs,
        ),
        out_shape=out_shape,
        compiler_params=vmem_params,
        cost_estimate=pl.CostEstimate(
            flops=6 * tokens * D * width,
            bytes_accessed=4 * tokens * D + 6 * tokens * width + 6 * D * width,
            transcendentals=tokens * width,
        ),
    )(me, normed_all, grad_out_all, down, *weights)


def row_terms(me, turned, right, rows_out):
    count, shard, tokens = turned.shape
    width = right.shape[1]
    lanes = width // 128
    half = count // 2
    spare = rows_out - shard * lanes

    def kernel(me_ref, turned_ref, right_ref, odd_ref, even_ref, *scratch):
        step = pl.program_id(0)
        if spare:

            @pl.when(step == 0)
            def _():
                sums = jnp.sum(right_ref[...].astype(jnp.float32), axis=0, keepdims=True)
                scratch[0][...] = jnp.zeros_like(scratch[0])
                for group in range(lanes):
                    scratch[0][group : group + 1] = sums[:, group * 128 : (group + 1) * 128]

        term = dot_f32(turned_ref[0], right_ref[...]).astype(jnp.bfloat16)

        def store(out_ref):
            for group in range(lanes):
                out_ref[0, group * shard : (group + 1) * shard] = term[
                    :, group * 128 : (group + 1) * 128
                ]
            if spare:
                out_ref[0, lanes * shard :] = scratch[0][...].astype(jnp.bfloat16)

        pl.when(step < half)(lambda: store(odd_ref))
        pl.when(step >= half)(lambda: store(even_ref))

    out = jax.ShapeDtypeStruct((half, rows_out, 128), jnp.bfloat16)
    return pl.pallas_call(
        kernel,
        grid_spec=pltpu.PrefetchScalarGridSpec(
            num_scalar_prefetch=1,
            grid=(count,),
            in_specs=[
                pl.BlockSpec(
                    (1, shard, tokens),
                    lambda step, me_ref: (me_ref[0] ^ mask_at(step, count), 0, 0),
                ),
                pl.BlockSpec((tokens, width), lambda step, me_ref: (0, 0)),
            ],
            out_specs=[
                pl.BlockSpec(
                    (1, rows_out, 128), lambda step, me_ref: (jnp.minimum(step, half - 1), 0, 0)
                ),
                pl.BlockSpec(
                    (1, rows_out, 128), lambda step, me_ref: (jnp.maximum(step - half, 0), 0, 0)
                ),
            ],
            scratch_shapes=[pltpu.VMEM((spare, 128), jnp.float32)] if spare else [],
        ),
        out_shape=[out, out],
        compiler_params=vmem_params,
        cost_estimate=pl.CostEstimate(
            flops=2 * D * tokens * width,
            bytes_accessed=256 * count * rows_out,
            transcendentals=0,
        ),
    )(me, turned, right)


def shards(
    tokens,
    positions,
    cotangent,
    attn_norm,
    ffn_norm,
    in_proj,
    in_bias,
    out_proj,
    gate_up,
    down_proj,
):
    token_rows = tokens.shape[1]
    fsdp_count = lax.axis_size("fsdp")
    ctx_count = lax.axis_size("ctx")
    fsdp_me = lax.axis_index("fsdp")
    me = fsdp_me.astype(jnp.int32)[None]
    at = lax.axis_index("ctx").astype(jnp.int32)[None]
    units = FF // fsdp_count
    shard_d = D // fsdp_count
    residual_in = tokens[0].astype(jnp.float32)
    position = positions[0]
    grad_out_b = cotangent[0]

    first_units, second_units, padded_units = unit_widths(units)
    bias_full = gather_small(in_bias).reshape(-1)
    in_scaled = (in_proj.astype(jnp.float32) * attn_norm[:, None]).astype(jnp.bfloat16)
    first_blocks, second_blocks = split_units(me, gate_up, ffn_norm, fsdp_count)
    cosine, sine = rotary_tables(position)
    normed_b = rms_scale(residual_in).astype(jnp.bfloat16)
    in_pieces = gather_pieces(in_scaled, first_blocks, cosine, normed_b)
    gated_blocks = after(first_blocks, in_pieces[0], in_pieces[2], in_pieces[4])
    gate_up_first = [gated_blocks[0]] + [
        exchange(gated_blocks[mask], mask) for mask in range(1, fsdp_count)
    ]
    out_full = lax.all_gather(after(out_proj, in_pieces), "fsdp", axis=0, tiled=True)

    projected = project(
        me, after(normed_b, gate_up_first[1], gate_up_first[2]), in_pieces, bias_full, cosine, sine
    )
    both_b = projected[:, QD:]
    both_pieces = [both_b] + [
        lax.ppermute(both_b, "ctx", [(s, s + back) for s in range(ctx_count - back)])
        for back in range(1, ctx_count)
    ]
    grad_out_all = lax.all_gather(after(grad_out_b, projected), "fsdp", axis=0, tiled=True)
    both_pieces = after(both_pieces, gate_up_first[3], gate_up_first[4])
    attended_b, attended_turned, log_total = attend(at, position[:, None], projected, both_pieces)
    attended_b = after(attended_b, gate_up_first)
    middle = residual_in + dot_f32(attended_b, out_full)
    normed_ffn_b = rms_scale(middle).astype(jnp.bfloat16)
    normed_again, down_again = after((normed_b, down_proj), normed_ffn_b)
    normed_turned = normed_again.T.reshape(fsdp_count, shard_d, token_rows)
    down_first = down_again[:first_units]
    down_second = jnp.pad(down_again[first_units:], ((0, padded_units - second_units), (0, 0)))

    normed_ffn_all = gather_masks(normed_ffn_b, normed_turned, down_first, down_second)
    gate_up_second = swap_blocks(after(second_blocks, normed_ffn_all)).reshape(
        D, 2 * padded_units
    )
    hidden_first, grad_first, grad_out_all, gate_up_first = unit_part(
        me, normed_ffn_all, grad_out_all, gate_up_first, down_first, fsdp_count, True
    )
    odd_rows = normed_ffn_all.shape[0] // 2

    def down_term(hidden, *gates):
        return dot_left_t(after(hidden, *gates), grad_out_all).astype(jnp.bfloat16)

    def gate_term(grad, *gates):
        term = dot_left_t(normed_ffn_all, after(grad, *gates)).astype(jnp.bfloat16)
        return term.reshape(fsdp_count, shard_d, -1)

    def input_grads(rows, *gates):
        return (
            (
                dot_right_t(after(grad_first, *gates)[rows], gate_up_first)
                + dot_right_t(grad_second[rows], gate_up_second)
            )
            .astype(jnp.bfloat16)
            .reshape(fsdp_count // 2, token_rows, D)
        )

    def down_outs(rows, *gates):
        return (
            (
                dot_f32(after(hidden_first, *gates)[rows], down_first)
                + dot_f32(hidden_second[rows], down_second)
            )
            .astype(jnp.bfloat16)
            .reshape(fsdp_count // 2, token_rows, D)
        )

    down_term_a = down_term(hidden_first)
    gate_term_a = gate_term(grad_first, down_term_a)
    down_sum_a, gate_sum_a = lax.psum((down_term_a, gate_term_a), "ctx")
    hidden_second, grad_second = unit_part(
        me,
        after(normed_ffn_all, gate_term_a),
        grad_out_all,
        gate_up_second,
        down_second,
        fsdp_count,
        False,
    )
    grad_normed_odd = input_grads(slice(0, odd_rows), hidden_second)
    normed_sum = MaskSum(grad_normed_odd)
    grad_normed_even = input_grads(slice(odd_rows, None), grad_normed_odd)
    sent = normed_sum.second(grad_normed_even)
    gate_term_b = gate_term(grad_second, sent)
    gate_swapped_b = swap_blocks(gate_term_b)
    sent = normed_sum.third(gate_term_b)
    down_term_b = down_term(hidden_second, sent)[:second_units]
    grad_normed_ffn = normed_sum.result(down_term_b).astype(jnp.float32)

    grad_out = grad_out_b.astype(jnp.float32)
    grad_middle = grad_out + norm_backward(middle, grad_normed_ffn)
    grad_middle_b = grad_middle.astype(jnp.bfloat16)
    grad_attended_b = dot_right_t(grad_middle_b, out_full).astype(jnp.bfloat16)
    in_rows = shard_d * in_proj.shape[1] // 128
    out_rows = shard_d * D // 128
    out_odd, out_even = row_terms(
        me,
        attended_turned.reshape(fsdp_count, shard_d, token_rows),
        after(grad_middle_b, grad_attended_b),
        out_rows,
    )
    out_sum = MaskSum(out_odd)
    query_grad, key_grads, value_grads = attend_backward(
        at,
        position[:, None],
        projected,
        both_pieces,
        after(grad_attended_b, out_even),
        log_total,
        cosine,
        sine,
    )
    both_sent = [
        lax.ppermute(
            jnp.concatenate(
                [
                    grads[back * token_rows : (back + 1) * token_rows].astype(jnp.bfloat16)
                    for grads in (key_grads, value_grads)
                ],
                axis=1,
            ),
            "ctx",
            [(s + back, s) for s in range(ctx_count - back)],
        )
        for back in range(1, ctx_count)
    ]
    sent = out_sum.second(out_even, query_grad)
    down_odd = down_outs(slice(0, odd_rows), sent)
    block_sum = MaskSum(down_odd)
    sent = out_sum.third(down_odd)
    down_even = down_outs(slice(odd_rows, None), sent)
    both_grad = jnp.concatenate([key_grads[:token_rows], value_grads[:token_rows]], axis=1)
    for piece in after(both_sent, down_even, gate_swapped_b):
        both_grad = both_grad + piece.astype(jnp.float32)
    turned_back = []
    for head in range(KEY_VALUE_HEADS):
        plain = both_grad[:, head * HEAD_SIZE : (head + 1) * HEAD_SIZE]
        turned_back.append(plain * cosine - jnp.roll(plain, HEAD_SIZE // 2, axis=1) * sine)
    grad_projected_b = jnp.concatenate(
        [query_grad]
        + [part.astype(jnp.bfloat16) for part in turned_back]
        + [both_grad[:, KD:].astype(jnp.bfloat16)],
        axis=1,
    )
    down_sum_a, gate_sum_a, down_term_b, gate_swapped_b = lax.optimization_barrier(
        (down_sum_a, gate_sum_a, down_term_b, gate_swapped_b)
    )
    down_sum_b, gate_sum_b = lax.psum((down_term_b, gate_swapped_b), "ctx")
    in_odd, in_even = row_terms(
        me, normed_turned, after(grad_projected_b, gate_sum_a), in_rows + 32
    )
    in_sum = MaskSum(in_odd)
    grad_normed = project_back(me, after(grad_projected_b, in_even), in_pieces)
    sent = in_sum.second(in_even, grad_normed)
    tokens_grad = grad_middle + norm_backward(residual_in, after(grad_normed, sent))
    sent = block_sum.second(down_even, tokens_grad)
    sent = in_sum.third(sent)
    out_part = out_sum.result(sent)
    sent = block_sum.third(out_part)
    in_part = in_sum.result(sent)
    gate_swapped_a = swap_blocks(gate_sum_a)
    in_part = after(in_part, gate_swapped_a)
    terms_total = ctx_total(jnp.concatenate([in_part, out_part], axis=0)).astype(jnp.float32)
    block_out = middle + block_sum.result(in_part).astype(jnp.float32)
    down_grad = jnp.concatenate([down_sum_a, down_sum_b], axis=0).astype(jnp.float32)
    gate_grad, ffn_grad = join_units(gate_swapped_a, gate_sum_b, gate_up, ffn_norm)

    def lanes_back(rows):
        return rows.reshape(-1, shard_d, 128).transpose(1, 0, 2).reshape(shard_d, -1)

    in_total = lanes_back(terms_total[:in_rows])
    out_grad = lanes_back(terms_total[in_rows + 32 :])
    bias_span = in_bias.shape[0]
    bias_grad = lax.dynamic_slice_in_dim(
        terms_total[in_rows : in_rows + in_proj.shape[1] // 128].reshape(-1),
        fsdp_me * bias_span,
        bias_span,
    )
    in_grad = in_total * attn_norm[:, None]
    attn_grad = jnp.sum(in_total * in_proj.astype(jnp.float32), axis=1)
    return (
        block_out.astype(jnp.bfloat16).reshape(1, token_rows, D),
        tokens_grad.reshape(1, token_rows, D),
        attn_grad,
        ffn_grad,
        in_grad,
        bias_grad,
        out_grad,
        gate_grad,
        down_grad,
    )


def solution(mesh):
    in_specs = (
        P("fsdp", "ctx", None),
        P("fsdp", "ctx"),
        P("fsdp", "ctx", None),
        P("fsdp"),
        P("fsdp"),
        P("fsdp", None),
        P("fsdp"),
        P("fsdp", None),
        P("fsdp", None),
        P("fsdp", None),
    )
    out_specs = (
        P("fsdp", "ctx", None),
        P("fsdp", "ctx", None),
        P("fsdp"),
        P("fsdp"),
        P("fsdp", None),
        P("fsdp"),
        P("fsdp", None),
        P("fsdp", None),
        P("fsdp", None),
    )
    return jax.shard_map(shards, mesh=mesh, in_specs=in_specs, out_specs=out_specs, check_vma=False)
```

```python
import jax
import jax.numpy as jnp
from jax import lax
from jax.experimental import pallas as pl
from jax.experimental.pallas import tpu as pltpu
from jax.sharding import PartitionSpec as P

D = 1536
QUERY_HEADS = 12
KEY_VALUE_HEADS = 2
HEAD_SIZE = 128
FF = 8960
QD = QUERY_HEADS * HEAD_SIZE
KD = KEY_VALUE_HEADS * HEAD_SIZE
GROUP = QUERY_HEADS // KEY_VALUE_HEADS


norm_eps = 1e-06
rope_base = 1000000.0
masked_score = -1e30
score_scale = HEAD_SIZE ** (-0.5)
vmem_params = pltpu.CompilerParams(vmem_limit_bytes=48 * 1024 * 1024)


def rms_scale(value_rows):
    return value_rows * lax.rsqrt(
        jnp.mean(value_rows * value_rows, axis=-1, keepdims=True) + norm_eps
    )


def norm_backward(value_rows, incoming):
    unused_out, pullback = jax.vjp(rms_scale, value_rows)
    return pullback(incoming)[0]


def rotary_tables(position):
    lane = jnp.arange(HEAD_SIZE, dtype=jnp.int32)
    half = HEAD_SIZE // 2
    frequencies = rope_base ** (-((lane % half).astype(jnp.float32) * (2.0 / HEAD_SIZE)))
    angles = position.astype(jnp.float32)[:, None] * frequencies[None, :]
    sign = jnp.where(lane < half, -1.0, 1.0)
    return jnp.cos(angles), jnp.sin(angles) * sign[None, :]


def dot_f32(left, right):
    return jnp.dot(left, right, preferred_element_type=jnp.float32)


def dot_right_t(left, right):
    return lax.dot_general(
        left, right, (((1,), (1,)), ((), ())), preferred_element_type=jnp.float32
    )


def dot_left_t(left, right):
    return lax.dot_general(
        left, right, (((0,), (0,)), ((), ())), preferred_element_type=jnp.float32
    )


def add_low(left, right):
    return left + right


def after(value, *earlier):
    return lax.optimization_barrier((value, earlier))[0]


def exchange(value, mask):
    count = lax.axis_size("fsdp")
    return lax.ppermute(value, "fsdp", [(place, place ^ mask) for place in range(count)])


def gather_pieces(block, *gates):
    count = lax.axis_size("fsdp")
    if count != 8:
        found = [[block]] + [[exchange(block, mask)] for mask in range(2, count, 2)]
    else:
        half = block.shape[0] // 2
        by_x = exchange(block, 2)
        by_y = exchange(block, 4)
        other = exchange(block, 1)
        by_x, by_y = after((by_x, by_y), *gates)
        top = exchange(by_x[:half], 4)
        bottom = exchange(by_y[half:], 2)
        found = [[block], [by_x], [by_y], [top, bottom]]
        others = [[other], [exchange(by_x, 1)], [exchange(by_y, 1)]]
        others.append([exchange(top, 1), exchange(bottom, 1)])
        return [(2 * place, rows) for place, rows in enumerate(found)] + [
            (2 * place + 1, rows) for place, rows in enumerate(others)
        ]
    pieces = []
    for place, rows in enumerate(found):
        pieces.append((2 * place, rows))
        pieces.append((2 * place + 1, [exchange(part, 1) for part in rows]))
    return pieces


def gather_masks(block, *gates):
    count = lax.axis_size("fsdp")
    rows = block.shape[0]
    whole = jnp.zeros((count * rows, block.shape[1]), block.dtype)
    for mask, parts in gather_pieces(block, *gates):
        first = place_of(mask, count) * rows
        for part in parts:
            whole = lax.dynamic_update_slice(whole, part, (first, 0))
            first += part.shape[0]
    return whole


def gather_small(value):
    count = lax.axis_size("fsdp")
    me = lax.axis_index("fsdp")
    bits = count.bit_length() - 1
    found = value
    for bit in list(range(1, bits)) + [0]:
        got = exchange(found, 1 << bit)
        low = (me >> bit) % 2 == 0
        found = jnp.stack([jnp.where(low, found, got), jnp.where(low, got, found)])
    return jnp.moveaxis(found, 0, bits - 1).reshape(count, -1)


def place_of(mask, count):
    return mask // 2 + (1 - mask % 2) * (count // 2)


def mask_at(place, count):
    return jnp.where(place < count // 2, 2 * place + 1, 2 * place - count)


class MaskSum:
    def __init__(self, odd):
        self.got = exchange(odd, 1)

    def second(self, even, *gates):
        count = lax.axis_size("fsdp")
        self.kept = add_low(even, after(self.got, *gates))
        if count == 8:
            half = self.kept.shape[1] // 2
            self.by_x = exchange(self.kept[1::2, :half], 2)
            self.by_y = exchange(self.kept[2:, half:], 4)
        else:
            span = count
            while self.kept.shape[0] > 1:
                span //= 2
                half = self.kept.shape[0] // 2
                self.kept = add_low(self.kept[:half], exchange(self.kept[half:], span))
        return self.kept

    def third(self, *gates):
        if lax.axis_size("fsdp") != 8:
            return self.kept
        half = self.kept.shape[1] // 2
        by_x, by_y = after((self.by_x, self.by_y), *gates)
        self.top = add_low(self.kept[0::2, :half], by_x)
        self.bottom = add_low(self.kept[:2, half:], by_y)
        self.last_y = exchange(self.top[1], 4)
        self.last_x = exchange(self.bottom[1], 2)
        return self.top, self.bottom

    def result(self, *gates):
        if lax.axis_size("fsdp") != 8:
            return self.kept[0]
        last_y, last_x = after((self.last_y, self.last_x), *gates)
        return jnp.concatenate(
            [add_low(self.top[0], last_y), add_low(self.bottom[0], last_x)], axis=0
        )


def swap_blocks(blocks):
    return lax.all_to_all(blocks, "fsdp", 0, 0, tiled=True)


def ctx_total(part):
    count = lax.axis_size("ctx")
    middle = count // 2
    me = lax.axis_index("ctx")
    for hop in range(middle - 1):
        part = add_low(
            part,
            lax.ppermute(part, "ctx", [(hop, hop + 1), (count - 1 - hop, count - 2 - hop)]),
        )
    part = add_low(
        part, lax.ppermute(part, "ctx", [(middle - 1, middle), (middle, middle - 1)])
    )
    for hop in reversed(range(middle - 1)):
        got = lax.ppermute(part, "ctx", [(hop + 1, hop), (count - 2 - hop, count - 1 - hop)])
        part = jnp.where((me == hop) | (me == count - 1 - hop), got, part)
    return lax.optimization_barrier(part)


def unit_widths(units):
    first = units // 256 * 128
    second = units - first
    return first, second, -(-second // 128) * 128


def split_units(me, gate_up, gain, count):
    rows, columns = gate_up.shape
    span = columns // 2
    units = span // count
    first, second, padded = unit_widths(units)
    block = 48

    def kernel(me_ref, weight_ref, gain_ref, first_ref, second_ref):
        def scaled(begin, end):
            value = weight_ref[:, begin:end].astype(jnp.float32) * gain_ref[...]
            return value.astype(gate_up.dtype)

        for owner in range(count):
            for side in range(2):
                begin = side * span + owner * units
                first_ref[me_ref[0] ^ owner, :, side * first : (side + 1) * first] = scaled(
                    begin, begin + first
                )
                second_ref[owner, :, side * padded : side * padded + second] = scaled(
                    begin + first, begin + units
                )
                if padded > second:
                    second_ref[
                        owner, :, side * padded + second : (side + 1) * padded
                    ] = jnp.zeros((block, padded - second), gate_up.dtype)

    return pl.pallas_call(
        kernel,
        grid_spec=pltpu.PrefetchScalarGridSpec(
            num_scalar_prefetch=1,
            grid=(rows // block,),
            in_specs=[
                pl.BlockSpec((block, columns), lambda step, me_ref: (step, 0)),
                pl.BlockSpec((block, 1), lambda step, me_ref: (step, 0)),
            ],
            out_specs=[
                pl.BlockSpec((count, block, 2 * first), lambda step, me_ref: (0, step, 0)),
                pl.BlockSpec((count, block, 2 * padded), lambda step, me_ref: (0, step, 0)),
            ],
        ),
        out_shape=[
            jax.ShapeDtypeStruct((count, rows, 2 * first), gate_up.dtype),
            jax.ShapeDtypeStruct((count, rows, 2 * padded), gate_up.dtype),
        ],
        compiler_params=vmem_params,
        cost_estimate=pl.CostEstimate(
            flops=0, bytes_accessed=4 * rows * columns, transcendentals=0
        ),
    )(me, gate_up, gain[:, None])


def join_units(first_part, second_part, gate_up, gain):
    rows, columns = gate_up.shape
    count = first_part.shape[0]
    block = 48
    pieces = rows // block
    span = columns // 2
    units = span // count
    first, second, padded = unit_widths(units)

    def kernel(first_ref, second_ref, weight_ref, gain_ref, whole_ref, sums_ref):
        for owner in range(count):
            for side in range(2):
                begin = side * span + owner * units
                whole_ref[:, begin : begin + first] = first_ref[
                    owner, :, side * first : (side + 1) * first
                ].astype(jnp.float32)
                whole_ref[:, begin + first : begin + units] = second_ref[
                    owner, :, side * padded : side * padded + second
                ].astype(jnp.float32)
        whole = whole_ref[...]
        total = jnp.sum(whole * weight_ref[...].astype(jnp.float32), axis=1, keepdims=True)
        sums_ref[...] = jnp.broadcast_to(total, (block, 128))
        whole_ref[...] = whole * gain_ref[...]

    whole, sums = pl.pallas_call(
        kernel,
        grid=(pieces,),
        in_specs=[
            pl.BlockSpec((count, block, 2 * first), lambda step: (0, step, 0)),
            pl.BlockSpec((count, block, 2 * padded), lambda step: (0, step, 0)),
            pl.BlockSpec((block, columns), lambda step: (step, 0)),
            pl.BlockSpec((block, 1), lambda step: (step, 0)),
        ],
        out_specs=[
            pl.BlockSpec((block, columns), lambda step: (step, 0)),
            pl.BlockSpec((block, 128), lambda step: (step, 0)),
        ],
        out_shape=[
            jax.ShapeDtypeStruct((rows, columns), jnp.float32),
            jax.ShapeDtypeStruct((rows, 128), jnp.float32),
        ],
        compiler_params=vmem_params,
        cost_estimate=pl.CostEstimate(
            flops=2 * rows * columns, bytes_accessed=8 * rows * columns, transcendentals=0
        ),
    )(first_part, second_part, gate_up, gain[:, None])
    return whole, sums[:, 0]


def place_rows(me_ref, pieces, refs, weight_ref):
    place = 0
    for mask, parts in pieces:
        shard = sum(part.shape[0] for part in parts)
        begin = (me_ref[0] ^ mask) * shard
        for part in parts:
            rows = part.shape[0]
            weight_ref[pl.ds(pl.multiple_of(begin, rows), rows)] = refs[place][...]
            begin = begin + rows
            place += 1


def project(me, normed, pieces, bias, cosine, sine):
    tokens = normed.shape[0]
    width = bias.shape[0]
    block = 512
    flat = [part for unused_mask, parts in pieces for part in parts]

    def kernel(me_ref, normed_ref, bias_ref, cosine_ref, sine_ref, *refs):
        out_ref, weight_ref = refs[len(flat) :]
        place_rows(me_ref, pieces, refs, weight_ref)
        product = dot_f32(normed_ref[...], weight_ref[...]) + bias_ref[...]
        for head in range(block // HEAD_SIZE):
            lanes = slice(head * HEAD_SIZE, (head + 1) * HEAD_SIZE)
            plain = product[:, lanes]
            turned = plain * cosine_ref[...] + pltpu.roll(plain, HEAD_SIZE // 2, 1) * sine_ref[...]
            column = pl.program_id(0) * block + head * HEAD_SIZE
            out_ref[:, lanes] = jnp.where(column < QD + KD, turned, plain).astype(jnp.bfloat16)

    return pl.pallas_call(
        kernel,
        grid_spec=pltpu.PrefetchScalarGridSpec(
            num_scalar_prefetch=1,
            grid=(width // block,),
            in_specs=[
                pl.BlockSpec((tokens, D), lambda step, me_ref: (0, 0)),
                pl.BlockSpec((1, block), lambda step, me_ref: (0, step)),
                pl.BlockSpec((tokens, HEAD_SIZE), lambda step, me_ref: (0, 0)),
                pl.BlockSpec((tokens, HEAD_SIZE), lambda step, me_ref: (0, 0)),
            ]
            + [
                pl.BlockSpec((part.shape[0], block), lambda step, me_ref: (0, step))
                for part in flat
            ],
            out_specs=pl.BlockSpec((tokens, block), lambda step, me_ref: (0, step)),
            scratch_shapes=[pltpu.VMEM((D, block), jnp.bfloat16)],
        ),
        out_shape=jax.ShapeDtypeStruct((tokens, width), jnp.bfloat16),
        compiler_params=vmem_params,
        cost_estimate=pl.CostEstimate(
            flops=2 * tokens * D * width, bytes_accessed=2 * D * width, transcendentals=0
        ),
    )(me, normed, bias[None], cosine, sine, *flat)


def project_back(me, grad_projected, pieces):
    tokens, width = grad_projected.shape
    flat = [part for unused_mask, parts in pieces for part in parts]

    def kernel(me_ref, grad_ref, *refs):
        out_ref, weight_ref = refs[len(flat) :]
        place_rows(me_ref, pieces, refs, weight_ref)
        out_ref[...] = dot_right_t(grad_ref[...], weight_ref[...])

    whole = lambda part: pl.BlockSpec(part.shape, lambda step, me_ref: (0, 0))
    return pl.pallas_call(
        kernel,
        grid_spec=pltpu.PrefetchScalarGridSpec(
            num_scalar_prefetch=1,
            grid=(1,),
            in_specs=[whole(grad_projected)] + [whole(part) for part in flat],
            out_specs=pl.BlockSpec((tokens, D), lambda step, me_ref: (0, 0)),
            scratch_shapes=[pltpu.VMEM((D, width), jnp.bfloat16)],
        ),
        out_shape=jax.ShapeDtypeStruct((tokens, D), jnp.float32),
        compiler_params=vmem_params,
        cost_estimate=pl.CostEstimate(
            flops=2 * tokens * D * width, bytes_accessed=2 * D * width, transcendentals=0
        ),
    )(me, grad_projected, *flat)


def fill_bias(at_ref, position_ref, bias_ref):
    tokens, keys = bias_ref.shape
    row = lax.broadcasted_iota(jnp.int32, (tokens, keys), 0)
    column = lax.broadcasted_iota(jnp.int32, (tokens, keys), 1)
    back = column // tokens
    query_index = at_ref[0] * tokens + row
    key_index = (at_ref[0] - back) * tokens + (column - back * tokens)
    allowed = (key_index <= query_index) & (key_index >= query_index - position_ref[...])
    bias_ref[...] = jnp.where(allowed, 0.0, masked_score)


def join_keys(refs, key_ref, value_ref):
    @pl.when(pl.program_id(0) % GROUP == 0)
    def _():
        for place in range(len(refs)):
            tokens = refs[0].shape[0]
            if (place + 1) * tokens > key_ref.shape[0]:
                break
            rows = slice(place * tokens, (place + 1) * tokens)
            key_ref[rows] = refs[2 * place][...]
            value_ref[rows] = refs[2 * place + 1][...]


def key_specs(both_pieces):
    specs = []
    for piece in both_pieces:
        shape = (piece.shape[0], HEAD_SIZE)
        specs.append(pl.BlockSpec(shape, lambda head, at: (0, head // GROUP)))
        specs.append(pl.BlockSpec(shape, lambda head, at: (0, KEY_VALUE_HEADS + head // GROUP)))
    return specs


def attend(at, position, projected, both_pieces):
    tokens = projected.shape[0]
    count = len(both_pieces)
    keys = count * tokens

    def kernel(at_ref, position_ref, query_ref, *refs):
        out_ref, turn_ref, log_ref, bias_ref, key_ref, value_ref = refs[2 * count :]

        @pl.when(pl.program_id(0) == 0)
        def _():
            fill_bias(at_ref, position_ref, bias_ref)

        join_keys(refs, key_ref, value_ref)

        scores = dot_right_t(query_ref[...], key_ref[...]) * score_scale + bias_ref[...]
        top = jnp.max(scores, axis=1, keepdims=True)
        raised = jnp.exp(scores - top)
        total = jnp.sum(raised, axis=1, keepdims=True)
        probs = (raised * (1.0 / total)).astype(jnp.bfloat16)
        result = dot_f32(probs, value_ref[...])
        out_ref[...] = result.astype(jnp.bfloat16)
        turn_ref[...] = result.T.astype(jnp.bfloat16)
        log_ref[0] = top + jnp.log(total)

    return pl.pallas_call(
        kernel,
        grid_spec=pltpu.PrefetchScalarGridSpec(
            num_scalar_prefetch=1,
            grid=(QUERY_HEADS,),
            in_specs=[
                pl.BlockSpec((tokens, 1), lambda head, at: (0, 0)),
                pl.BlockSpec((tokens, HEAD_SIZE), lambda head, at: (0, head)),
            ]
            + key_specs(both_pieces),
            out_specs=[
                pl.BlockSpec((tokens, HEAD_SIZE), lambda head, at: (0, head)),
                pl.BlockSpec((HEAD_SIZE, tokens), lambda head, at: (head, 0)),
                pl.BlockSpec((1, tokens, 1), lambda head, at: (head, 0, 0)),
            ],
            scratch_shapes=[
                pltpu.VMEM((tokens, keys), jnp.float32),
                pltpu.VMEM((keys, HEAD_SIZE), jnp.bfloat16),
                pltpu.VMEM((keys, HEAD_SIZE), jnp.bfloat16),
            ],
        ),
        out_shape=[
            jax.ShapeDtypeStruct((tokens, QD), jnp.bfloat16),
            jax.ShapeDtypeStruct((QD, tokens), jnp.bfloat16),
            jax.ShapeDtypeStruct((QUERY_HEADS, tokens, 1), jnp.float32),
        ],
        compiler_params=vmem_params,
        cost_estimate=pl.CostEstimate(
            flops=8 * tokens * keys * QD,
            bytes_accessed=8 * tokens * QD,
            transcendentals=QUERY_HEADS * tokens * keys,
        ),
    )(at, position, projected, *[piece for piece in both_pieces for unused in range(2)])


def attend_backward(at, position, projected, both_pieces, incoming, log_total, cosine, sine):
    tokens = projected.shape[0]
    count = len(both_pieces)
    keys = count * tokens

    def kernel(
        at_ref,
        position_ref,
        query_ref,
        incoming_ref,
        log_ref,
        cosine_ref,
        sine_ref,
        *refs,
    ):
        query_grad_ref, key_grad_ref, value_grad_ref = refs[2 * count : 2 * count + 3]
        bias_ref, key_total, value_total, key_ref, value_ref = refs[2 * count + 3 :]
        head = pl.program_id(0)
        join_keys(refs, key_ref, value_ref)

        @pl.when(head == 0)
        def _():
            fill_bias(at_ref, position_ref, bias_ref)

        @pl.when(head % GROUP == 0)
        def _():
            key_total[...] = jnp.zeros_like(key_total)
            value_total[...] = jnp.zeros_like(value_total)

        scores = dot_right_t(query_ref[...], key_ref[...]) * score_scale + bias_ref[...]
        probs = jnp.exp(scores - log_ref[0])
        grad_probs = dot_right_t(incoming_ref[...], value_ref[...])
        inner = jnp.sum(grad_probs * probs, axis=1, keepdims=True)
        grad_scores = (probs * (grad_probs - inner)).astype(jnp.bfloat16)
        value_total[...] += dot_left_t(incoming_ref[...], probs.astype(jnp.bfloat16))
        key_total[...] += dot_left_t(query_ref[...], grad_scores)
        plain = dot_f32(grad_scores, key_ref[...]) * score_scale
        query_grad_ref[...] = (
            plain * cosine_ref[...] - pltpu.roll(plain, HEAD_SIZE // 2, 1) * sine_ref[...]
        ).astype(jnp.bfloat16)

        @pl.when(head % GROUP == GROUP - 1)
        def _():
            key_grad_ref[...] = (key_total[...] * score_scale).T
            value_grad_ref[...] = value_total[...].T

    return pl.pallas_call(
        kernel,
        grid_spec=pltpu.PrefetchScalarGridSpec(
            num_scalar_prefetch=1,
            grid=(QUERY_HEADS,),
            in_specs=[
                pl.BlockSpec((tokens, 1), lambda head, at: (0, 0)),
                pl.BlockSpec((tokens, HEAD_SIZE), lambda head, at: (0, head)),
                pl.BlockSpec((tokens, HEAD_SIZE), lambda head, at: (0, head)),
                pl.BlockSpec((1, tokens, 1), lambda head, at: (head, 0, 0)),
                pl.BlockSpec((tokens, HEAD_SIZE), lambda head, at: (0, 0)),
                pl.BlockSpec((tokens, HEAD_SIZE), lambda head, at: (0, 0)),
            ]
            + key_specs(both_pieces),
            out_specs=[
                pl.BlockSpec((tokens, HEAD_SIZE), lambda head, at: (0, head)),
                pl.BlockSpec((keys, HEAD_SIZE), lambda head, at: (0, head // GROUP)),
                pl.BlockSpec((keys, HEAD_SIZE), lambda head, at: (0, head // GROUP)),
            ],
            scratch_shapes=[
                pltpu.VMEM((tokens, keys), jnp.float32),
                pltpu.VMEM((HEAD_SIZE, keys), jnp.float32),
                pltpu.VMEM((HEAD_SIZE, keys), jnp.float32),
                pltpu.VMEM((keys, HEAD_SIZE), jnp.bfloat16),
                pltpu.VMEM((keys, HEAD_SIZE), jnp.bfloat16),
            ],
        ),
        out_shape=[
            jax.ShapeDtypeStruct((tokens, QD), jnp.bfloat16),
            jax.ShapeDtypeStruct((keys, KD), jnp.float32),
            jax.ShapeDtypeStruct((keys, KD), jnp.float32),
        ],
        compiler_params=vmem_params,
        cost_estimate=pl.CostEstimate(
            flops=20 * tokens * keys * QD,
            bytes_accessed=8 * tokens * QD,
            transcendentals=QUERY_HEADS * tokens * keys,
        ),
    )(
        at,
        position,
        projected,
        incoming,
        log_total,
        cosine,
        sine,
        *[piece for piece in both_pieces for unused in range(2)],
    )


def unit_part(me, normed_all, grad_out_all, gate_up, down, count, first):
    tokens = normed_all.shape[0]
    block = tokens // count
    width = down.shape[0]
    shard = D // count
    weights = list(gate_up) if first else [gate_up]

    def kernel(me_ref, normed_ref, out_grad_ref, down_ref, *refs):
        weight_refs = refs[: len(weights)]
        hidden_ref, grad_ref = refs[len(weights) : len(weights) + 2]
        weight_ref = weight_refs[0]
        if first:
            ordered_ref, weight_ref = refs[len(weights) + 2 :]
            ordered_ref[...] = out_grad_ref[...]

            @pl.when(pl.program_id(0) == 0)
            def _():
                for mask, ref in enumerate(weight_refs):
                    begin = pl.multiple_of((me_ref[0] ^ mask) * shard, shard)
                    weight_ref[pl.ds(begin, shard)] = ref[...]

        values = dot_f32(normed_ref[...], weight_ref[...])
        gate = values[:, :width]
        up = values[:, width:]
        grad_hidden = dot_right_t(out_grad_ref[...], down_ref[...])
        share = 1.0 / (1.0 + jnp.exp(-gate))
        passed = gate * share
        hidden_ref[...] = (passed * up).astype(jnp.bfloat16)
        grad_ref[:, :width] = (
            grad_hidden * up * share * (1.0 + gate * (1.0 - share))
        ).astype(jnp.bfloat16)
        grad_ref[:, width:] = (grad_hidden * passed).astype(jnp.bfloat16)

    def out_grad_index(step, me_ref):
        return (me_ref[0] ^ mask_at(step, count), 0) if first else (step, 0)

    row = lambda step, me_ref: (step, 0)
    fixed = lambda step, me_ref: (0, 0)
    out_specs = [pl.BlockSpec((block, width), row), pl.BlockSpec((block, 2 * width), row)]
    out_shape = [
        jax.ShapeDtypeStruct((tokens, width), jnp.bfloat16),
        jax.ShapeDtypeStruct((tokens, 2 * width), jnp.bfloat16),
    ]
    if first:
        out_specs += [pl.BlockSpec((block, D), row), pl.BlockSpec((D, 2 * width), fixed)]
        out_shape += [
            jax.ShapeDtypeStruct((tokens, D), jnp.bfloat16),
            jax.ShapeDtypeStruct((D, 2 * width), jnp.bfloat16),
        ]
    return pl.pallas_call(
        kernel,
        grid_spec=pltpu.PrefetchScalarGridSpec(
            num_scalar_prefetch=1,
            grid=(count,),
            in_specs=[
                pl.BlockSpec((block, D), row),
                pl.BlockSpec((block, D), out_grad_index),
                pl.BlockSpec((width, D), fixed),
            ]
            + [pl.BlockSpec(weight.shape, fixed) for weight in weights],
            out_specs=out_specs,
        ),
        out_shape=out_shape,
        compiler_params=vmem_params,
        cost_estimate=pl.CostEstimate(
            flops=6 * tokens * D * width,
            bytes_accessed=4 * tokens * D + 6 * tokens * width + 6 * D * width,
            transcendentals=tokens * width,
        ),
    )(me, normed_all, grad_out_all, down, *weights)


def row_terms(me, turned, right, rows_out):
    count, shard, tokens = turned.shape
    width = right.shape[1]
    lanes = width // 128
    half = count // 2
    spare = rows_out - shard * lanes

    def kernel(me_ref, turned_ref, right_ref, odd_ref, even_ref, *scratch):
        step = pl.program_id(0)
        if spare:

            @pl.when(step == 0)
            def _():
                sums = jnp.sum(right_ref[...].astype(jnp.float32), axis=0, keepdims=True)
                scratch[0][...] = jnp.zeros_like(scratch[0])
                for group in range(lanes):
                    scratch[0][group : group + 1] = sums[:, group * 128 : (group + 1) * 128]

        term = dot_f32(turned_ref[0], right_ref[...]).astype(jnp.bfloat16)

        def store(out_ref):
            for group in range(lanes):
                out_ref[0, group * shard : (group + 1) * shard] = term[
                    :, group * 128 : (group + 1) * 128
                ]
            if spare:
                out_ref[0, lanes * shard :] = scratch[0][...].astype(jnp.bfloat16)

        pl.when(step < half)(lambda: store(odd_ref))
        pl.when(step >= half)(lambda: store(even_ref))

    out = jax.ShapeDtypeStruct((half, rows_out, 128), jnp.bfloat16)
    return pl.pallas_call(
        kernel,
        grid_spec=pltpu.PrefetchScalarGridSpec(
            num_scalar_prefetch=1,
            grid=(count,),
            in_specs=[
                pl.BlockSpec(
                    (1, shard, tokens),
                    lambda step, me_ref: (me_ref[0] ^ mask_at(step, count), 0, 0),
                ),
                pl.BlockSpec((tokens, width), lambda step, me_ref: (0, 0)),
            ],
            out_specs=[
                pl.BlockSpec(
                    (1, rows_out, 128), lambda step, me_ref: (jnp.minimum(step, half - 1), 0, 0)
                ),
                pl.BlockSpec(
                    (1, rows_out, 128), lambda step, me_ref: (jnp.maximum(step - half, 0), 0, 0)
                ),
            ],
            scratch_shapes=[pltpu.VMEM((spare, 128), jnp.float32)] if spare else [],
        ),
        out_shape=[out, out],
        compiler_params=vmem_params,
        cost_estimate=pl.CostEstimate(
            flops=2 * D * tokens * width,
            bytes_accessed=256 * count * rows_out,
            transcendentals=0,
        ),
    )(me, turned, right)


def shards(
    tokens,
    positions,
    cotangent,
    attn_norm,
    ffn_norm,
    in_proj,
    in_bias,
    out_proj,
    gate_up,
    down_proj,
):
    token_rows = tokens.shape[1]
    fsdp_count = lax.axis_size("fsdp")
    ctx_count = lax.axis_size("ctx")
    fsdp_me = lax.axis_index("fsdp")
    me = fsdp_me.astype(jnp.int32)[None]
    at = lax.axis_index("ctx").astype(jnp.int32)[None]
    units = FF // fsdp_count
    shard_d = D // fsdp_count
    residual_in = tokens[0].astype(jnp.float32)
    position = positions[0]
    grad_out_b = cotangent[0]

    first_units, second_units, padded_units = unit_widths(units)
    bias_full = gather_small(in_bias).reshape(-1)
    in_scaled = (in_proj.astype(jnp.float32) * attn_norm[:, None]).astype(jnp.bfloat16)
    first_blocks, second_blocks = split_units(me, gate_up, ffn_norm, fsdp_count)
    cosine, sine = rotary_tables(position)
    normed_b = rms_scale(residual_in).astype(jnp.bfloat16)
    in_pieces = gather_pieces(in_scaled, first_blocks, cosine, normed_b)
    gated_blocks = after(first_blocks, in_pieces[0], in_pieces[2], in_pieces[4])
    gate_up_first = [gated_blocks[0]] + [
        exchange(gated_blocks[mask], mask) for mask in range(1, fsdp_count)
    ]
    out_full = lax.all_gather(after(out_proj, in_pieces), "fsdp", axis=0, tiled=True)

    projected = project(
        me, after(normed_b, gate_up_first[1], gate_up_first[2]), in_pieces, bias_full, cosine, sine
    )
    both_b = projected[:, QD:]
    both_pieces = [both_b] + [
        lax.ppermute(both_b, "ctx", [(s, s + back) for s in range(ctx_count - back)])
        for back in range(1, ctx_count)
    ]
    grad_out_all = lax.all_gather(after(grad_out_b, projected), "fsdp", axis=0, tiled=True)
    both_pieces = after(both_pieces, gate_up_first[3], gate_up_first[4])
    attended_b, attended_turned, log_total = attend(at, position[:, None], projected, both_pieces)
    attended_b = after(attended_b, gate_up_first)
    middle = residual_in + dot_f32(attended_b, out_full)
    normed_ffn_b = rms_scale(middle).astype(jnp.bfloat16)
    normed_again, down_again = after((normed_b, down_proj), normed_ffn_b)
    normed_turned = normed_again.T.reshape(fsdp_count, shard_d, token_rows)
    down_first = down_again[:first_units]
    down_second = jnp.pad(down_again[first_units:], ((0, padded_units - second_units), (0, 0)))

    normed_ffn_all = gather_masks(normed_ffn_b, normed_turned, down_first, down_second)
    gate_up_second = swap_blocks(after(second_blocks, normed_ffn_all)).reshape(
        D, 2 * padded_units
    )
    hidden_first, grad_first, grad_out_all, gate_up_first = unit_part(
        me, normed_ffn_all, grad_out_all, gate_up_first, down_first, fsdp_count, True
    )
    odd_rows = normed_ffn_all.shape[0] // 2

    def down_term(hidden, *gates):
        return dot_left_t(after(hidden, *gates), grad_out_all).astype(jnp.bfloat16)

    def gate_term(grad, *gates):
        term = dot_left_t(normed_ffn_all, after(grad, *gates)).astype(jnp.bfloat16)
        return term.reshape(fsdp_count, shard_d, -1)

    def input_grads(rows, *gates):
        return (
            (
                dot_right_t(after(grad_first, *gates)[rows], gate_up_first)
                + dot_right_t(grad_second[rows], gate_up_second)
            )
            .astype(jnp.bfloat16)
            .reshape(fsdp_count // 2, token_rows, D)
        )

    def down_outs(rows, *gates):
        return (
            (
                dot_f32(after(hidden_first, *gates)[rows], down_first)
                + dot_f32(hidden_second[rows], down_second)
            )
            .astype(jnp.bfloat16)
            .reshape(fsdp_count // 2, token_rows, D)
        )

    down_term_a = down_term(hidden_first)
    gate_term_a = gate_term(grad_first, down_term_a)
    down_sum_a, gate_sum_a = lax.psum((down_term_a, gate_term_a), "ctx")
    hidden_second, grad_second = unit_part(
        me,
        after(normed_ffn_all, gate_term_a),
        grad_out_all,
        gate_up_second,
        down_second,
        fsdp_count,
        False,
    )
    grad_normed_odd = input_grads(slice(0, odd_rows), hidden_second)
    normed_sum = MaskSum(grad_normed_odd)
    grad_normed_even = input_grads(slice(odd_rows, None), grad_normed_odd)
    sent = normed_sum.second(grad_normed_even)
    gate_term_b = gate_term(grad_second, sent)
    gate_swapped_b = swap_blocks(gate_term_b)
    sent = normed_sum.third(gate_term_b)
    gate_swapped_b, gate_sum_a, down_sum_a = lax.optimization_barrier(
        (gate_swapped_b, gate_sum_a, down_sum_a)
    )
    gate_sum_b = lax.psum(gate_swapped_b, "ctx")
    down_term_b = down_term(hidden_second, sent)[:second_units]
    grad_normed_ffn = normed_sum.result(down_term_b).astype(jnp.float32)

    grad_out = grad_out_b.astype(jnp.float32)
    grad_middle = grad_out + norm_backward(middle, grad_normed_ffn)
    grad_middle_b = grad_middle.astype(jnp.bfloat16)
    grad_attended_b = dot_right_t(grad_middle_b, out_full).astype(jnp.bfloat16)
    in_rows = shard_d * in_proj.shape[1] // 128
    out_rows = shard_d * D // 128
    out_odd, out_even = row_terms(
        me,
        attended_turned.reshape(fsdp_count, shard_d, token_rows),
        after(grad_middle_b, grad_attended_b),
        out_rows,
    )
    out_sum = MaskSum(out_odd)
    query_grad, key_grads, value_grads = attend_backward(
        at,
        position[:, None],
        projected,
        both_pieces,
        after(grad_attended_b, out_even, gate_sum_a),
        log_total,
        cosine,
        sine,
    )
    both_sent = [
        lax.ppermute(
            jnp.concatenate(
                [
                    grads[back * token_rows : (back + 1) * token_rows].astype(jnp.bfloat16)
                    for grads in (key_grads, value_grads)
                ],
                axis=1,
            ),
            "ctx",
            [(s + back, s) for s in range(ctx_count - back)],
        )
        for back in range(1, ctx_count)
    ]
    sent = out_sum.second(out_even, query_grad)
    down_odd = down_outs(slice(0, odd_rows), sent)
    block_sum = MaskSum(down_odd)
    sent = out_sum.third(down_odd)
    down_even = down_outs(slice(odd_rows, None), sent)
    both_grad = jnp.concatenate([key_grads[:token_rows], value_grads[:token_rows]], axis=1)
    for piece in after(both_sent, down_even):
        both_grad = both_grad + piece.astype(jnp.float32)
    turned_back = []
    for head in range(KEY_VALUE_HEADS):
        plain = both_grad[:, head * HEAD_SIZE : (head + 1) * HEAD_SIZE]
        turned_back.append(plain * cosine - jnp.roll(plain, HEAD_SIZE // 2, axis=1) * sine)
    grad_projected_b = jnp.concatenate(
        [query_grad]
        + [part.astype(jnp.bfloat16) for part in turned_back]
        + [both_grad[:, KD:].astype(jnp.bfloat16)],
        axis=1,
    )
    in_odd, in_even = row_terms(me, normed_turned, grad_projected_b, in_rows + 32)
    in_sum = MaskSum(in_odd)
    grad_normed = project_back(me, after(grad_projected_b, in_even), in_pieces)
    sent = in_sum.second(in_even, grad_normed)
    tokens_grad = grad_middle + norm_backward(residual_in, after(grad_normed, sent))
    sent = block_sum.second(down_even, tokens_grad)
    sent = in_sum.third(sent)
    out_part = out_sum.result(sent)
    sent = block_sum.third(out_part)
    in_part = in_sum.result(sent)
    gate_swapped_a = swap_blocks(gate_sum_a)
    in_part = after(in_part, gate_swapped_a)
    terms_part = jnp.concatenate([in_part, out_part], axis=0)
    terms_part, down_term_b, gate_sum_b = lax.optimization_barrier(
        (terms_part, down_term_b, gate_sum_b)
    )
    terms_total, down_sum_b = lax.psum((terms_part, down_term_b), "ctx")
    terms_total = terms_total.astype(jnp.float32)
    block_out = middle + block_sum.result(in_part).astype(jnp.float32)
    down_grad = jnp.concatenate([down_sum_a, down_sum_b], axis=0).astype(jnp.float32)
    gate_grad, ffn_grad = join_units(gate_swapped_a, gate_sum_b, gate_up, ffn_norm)

    def lanes_back(rows):
        return rows.reshape(-1, shard_d, 128).transpose(1, 0, 2).reshape(shard_d, -1)

    in_total = lanes_back(terms_total[:in_rows])
    out_grad = lanes_back(terms_total[in_rows + 32 :])
    bias_span = in_bias.shape[0]
    bias_grad = lax.dynamic_slice_in_dim(
        terms_total[in_rows : in_rows + in_proj.shape[1] // 128].reshape(-1),
        fsdp_me * bias_span,
        bias_span,
    )
    in_grad = in_total * attn_norm[:, None]
    attn_grad = jnp.sum(in_total * in_proj.astype(jnp.float32), axis=1)
    return (
        block_out.astype(jnp.bfloat16).reshape(1, token_rows, D),
        tokens_grad.reshape(1, token_rows, D),
        attn_grad,
        ffn_grad,
        in_grad,
        bias_grad,
        out_grad,
        gate_grad,
        down_grad,
    )


def solution(mesh):
    in_specs = (
        P("fsdp", "ctx", None),
        P("fsdp", "ctx"),
        P("fsdp", "ctx", None),
        P("fsdp"),
        P("fsdp"),
        P("fsdp", None),
        P("fsdp"),
        P("fsdp", None),
        P("fsdp", None),
        P("fsdp", None),
    )
    out_specs = (
        P("fsdp", "ctx", None),
        P("fsdp", "ctx", None),
        P("fsdp"),
        P("fsdp"),
        P("fsdp", None),
        P("fsdp"),
        P("fsdp", None),
        P("fsdp", None),
        P("fsdp", None),
    )
    return jax.shard_map(shards, mesh=mesh, in_specs=in_specs, out_specs=out_specs, check_vma=False)
```

```python
import jax
import jax.numpy as jnp
from jax import lax
from jax.experimental import pallas as pl
from jax.experimental.pallas import tpu as pltpu
from jax.sharding import PartitionSpec as P

D = 1536
QUERY_HEADS = 12
KEY_VALUE_HEADS = 2
HEAD_SIZE = 128
FF = 8960
QD = QUERY_HEADS * HEAD_SIZE
KD = KEY_VALUE_HEADS * HEAD_SIZE
GROUP = QUERY_HEADS // KEY_VALUE_HEADS


norm_eps = 1e-06
rope_base = 1000000.0
masked_score = -1e30
score_scale = HEAD_SIZE ** (-0.5)
vmem_params = pltpu.CompilerParams(vmem_limit_bytes=48 * 1024 * 1024)


def rms_scale(value_rows):
    return value_rows * lax.rsqrt(
        jnp.mean(value_rows * value_rows, axis=-1, keepdims=True) + norm_eps
    )


def norm_backward(value_rows, incoming):
    unused_out, pullback = jax.vjp(rms_scale, value_rows)
    return pullback(incoming)[0]


def rotary_tables(position):
    lane = jnp.arange(HEAD_SIZE, dtype=jnp.int32)
    half = HEAD_SIZE // 2
    frequencies = rope_base ** (-((lane % half).astype(jnp.float32) * (2.0 / HEAD_SIZE)))
    angles = position.astype(jnp.float32)[:, None] * frequencies[None, :]
    sign = jnp.where(lane < half, -1.0, 1.0)
    return jnp.cos(angles), jnp.sin(angles) * sign[None, :]


def dot_f32(left, right):
    return jnp.dot(left, right, preferred_element_type=jnp.float32)


def dot_right_t(left, right):
    return lax.dot_general(
        left, right, (((1,), (1,)), ((), ())), preferred_element_type=jnp.float32
    )


def dot_left_t(left, right):
    return lax.dot_general(
        left, right, (((0,), (0,)), ((), ())), preferred_element_type=jnp.float32
    )


def add_low(left, right):
    return left + right


def after(value, *earlier):
    return lax.optimization_barrier((value, earlier))[0]


def exchange(value, mask):
    count = lax.axis_size("fsdp")
    return lax.ppermute(value, "fsdp", [(place, place ^ mask) for place in range(count)])


def gather_pieces(block, *gates):
    count = lax.axis_size("fsdp")
    if count != 8:
        found = [[block]] + [[exchange(block, mask)] for mask in range(2, count, 2)]
    else:
        half = block.shape[0] // 2
        by_x = exchange(block, 2)
        by_y = exchange(block, 4)
        other = exchange(block, 1)
        by_x, by_y = after((by_x, by_y), *gates)
        top = exchange(by_x[:half], 4)
        bottom = exchange(by_y[half:], 2)
        found = [[block], [by_x], [by_y], [top, bottom]]
        others = [[other], [exchange(by_x, 1)], [exchange(by_y, 1)]]
        others.append([exchange(top, 1), exchange(bottom, 1)])
        return [(2 * place, rows) for place, rows in enumerate(found)] + [
            (2 * place + 1, rows) for place, rows in enumerate(others)
        ]
    pieces = []
    for place, rows in enumerate(found):
        pieces.append((2 * place, rows))
        pieces.append((2 * place + 1, [exchange(part, 1) for part in rows]))
    return pieces


def gather_masks(block, *gates):
    count = lax.axis_size("fsdp")
    rows = block.shape[0]
    whole = jnp.zeros((count * rows, block.shape[1]), block.dtype)
    for mask, parts in gather_pieces(block, *gates):
        first = place_of(mask, count) * rows
        for part in parts:
            whole = lax.dynamic_update_slice(whole, part, (first, 0))
            first += part.shape[0]
    return whole


def gather_small(value):
    count = lax.axis_size("fsdp")
    me = lax.axis_index("fsdp")
    bits = count.bit_length() - 1
    found = value
    for bit in list(range(1, bits)) + [0]:
        got = exchange(found, 1 << bit)
        low = (me >> bit) % 2 == 0
        found = jnp.stack([jnp.where(low, found, got), jnp.where(low, got, found)])
    return jnp.moveaxis(found, 0, bits - 1).reshape(count, -1)


def place_of(mask, count):
    return mask // 2 + (1 - mask % 2) * (count // 2)


def mask_at(place, count):
    return jnp.where(place < count // 2, 2 * place + 1, 2 * place - count)


class MaskSum:
    def __init__(self, odd):
        self.got = exchange(odd, 1)

    def second(self, even, *gates):
        count = lax.axis_size("fsdp")
        self.kept = add_low(even, after(self.got, *gates))
        if count == 8:
            half = self.kept.shape[1] // 2
            self.by_x = exchange(self.kept[1::2, :half], 2)
            self.by_y = exchange(self.kept[2:, half:], 4)
        else:
            span = count
            while self.kept.shape[0] > 1:
                span //= 2
                half = self.kept.shape[0] // 2
                self.kept = add_low(self.kept[:half], exchange(self.kept[half:], span))
        return self.kept

    def third(self, *gates):
        if lax.axis_size("fsdp") != 8:
            return self.kept
        half = self.kept.shape[1] // 2
        by_x, by_y = after((self.by_x, self.by_y), *gates)
        self.top = add_low(self.kept[0::2, :half], by_x)
        self.bottom = add_low(self.kept[:2, half:], by_y)
        self.last_y = exchange(self.top[1], 4)
        self.last_x = exchange(self.bottom[1], 2)
        return self.top, self.bottom

    def result(self, *gates):
        if lax.axis_size("fsdp") != 8:
            return self.kept[0]
        last_y, last_x = after((self.last_y, self.last_x), *gates)
        return jnp.concatenate(
            [add_low(self.top[0], last_y), add_low(self.bottom[0], last_x)], axis=0
        )


def swap_blocks(blocks):
    return lax.all_to_all(blocks, "fsdp", 0, 0, tiled=True)


def unit_widths(units):
    first = units // 256 * 128
    second = units - first
    return first, second, -(-second // 128) * 128


def split_units(me, gate_up, gain, count):
    rows, columns = gate_up.shape
    span = columns // 2
    units = span // count
    first, second, padded = unit_widths(units)
    block = 48

    def kernel(me_ref, weight_ref, gain_ref, first_ref, second_ref):
        def scaled(begin, end):
            value = weight_ref[:, begin:end].astype(jnp.float32) * gain_ref[...]
            return value.astype(gate_up.dtype)

        for owner in range(count):
            for side in range(2):
                begin = side * span + owner * units
                first_ref[me_ref[0] ^ owner, :, side * first : (side + 1) * first] = scaled(
                    begin, begin + first
                )
                second_ref[owner, :, side * padded : side * padded + second] = scaled(
                    begin + first, begin + units
                )
                if padded > second:
                    second_ref[
                        owner, :, side * padded + second : (side + 1) * padded
                    ] = jnp.zeros((block, padded - second), gate_up.dtype)

    return pl.pallas_call(
        kernel,
        grid_spec=pltpu.PrefetchScalarGridSpec(
            num_scalar_prefetch=1,
            grid=(rows // block,),
            in_specs=[
                pl.BlockSpec((block, columns), lambda step, me_ref: (step, 0)),
                pl.BlockSpec((block, 1), lambda step, me_ref: (step, 0)),
            ],
            out_specs=[
                pl.BlockSpec((count, block, 2 * first), lambda step, me_ref: (0, step, 0)),
                pl.BlockSpec((count, block, 2 * padded), lambda step, me_ref: (0, step, 0)),
            ],
        ),
        out_shape=[
            jax.ShapeDtypeStruct((count, rows, 2 * first), gate_up.dtype),
            jax.ShapeDtypeStruct((count, rows, 2 * padded), gate_up.dtype),
        ],
        compiler_params=vmem_params,
        cost_estimate=pl.CostEstimate(
            flops=0, bytes_accessed=4 * rows * columns, transcendentals=0
        ),
    )(me, gate_up, gain[:, None])


def join_units(first_part, second_part, gate_up, gain):
    rows, columns = gate_up.shape
    count = first_part.shape[0]
    block = 48
    pieces = rows // block
    span = columns // 2
    units = span // count
    first, second, padded = unit_widths(units)

    def kernel(first_ref, second_ref, weight_ref, gain_ref, whole_ref, sums_ref):
        for owner in range(count):
            for side in range(2):
                begin = side * span + owner * units
                whole_ref[:, begin : begin + first] = first_ref[
                    owner, :, side * first : (side + 1) * first
                ].astype(jnp.float32)
                whole_ref[:, begin + first : begin + units] = second_ref[
                    owner, :, side * padded : side * padded + second
                ].astype(jnp.float32)
        whole = whole_ref[...]
        total = jnp.sum(whole * weight_ref[...].astype(jnp.float32), axis=1, keepdims=True)
        sums_ref[...] = jnp.broadcast_to(total, (block, 128))
        whole_ref[...] = whole * gain_ref[...]

    whole, sums = pl.pallas_call(
        kernel,
        grid=(pieces,),
        in_specs=[
            pl.BlockSpec((count, block, 2 * first), lambda step: (0, step, 0)),
            pl.BlockSpec((count, block, 2 * padded), lambda step: (0, step, 0)),
            pl.BlockSpec((block, columns), lambda step: (step, 0)),
            pl.BlockSpec((block, 1), lambda step: (step, 0)),
        ],
        out_specs=[
            pl.BlockSpec((block, columns), lambda step: (step, 0)),
            pl.BlockSpec((block, 128), lambda step: (step, 0)),
        ],
        out_shape=[
            jax.ShapeDtypeStruct((rows, columns), jnp.float32),
            jax.ShapeDtypeStruct((rows, 128), jnp.float32),
        ],
        compiler_params=vmem_params,
        cost_estimate=pl.CostEstimate(
            flops=2 * rows * columns, bytes_accessed=8 * rows * columns, transcendentals=0
        ),
    )(first_part, second_part, gate_up, gain[:, None])
    return whole, sums[:, 0]


def place_rows(me_ref, pieces, refs, weight_ref):
    place = 0
    for mask, parts in pieces:
        shard = sum(part.shape[0] for part in parts)
        begin = (me_ref[0] ^ mask) * shard
        for part in parts:
            rows = part.shape[0]
            weight_ref[pl.ds(pl.multiple_of(begin, rows), rows)] = refs[place][...]
            begin = begin + rows
            place += 1


def project(me, normed, pieces, bias, cosine, sine):
    tokens = normed.shape[0]
    width = bias.shape[0]
    block = 512
    flat = [part for unused_mask, parts in pieces for part in parts]

    def kernel(me_ref, normed_ref, bias_ref, cosine_ref, sine_ref, *refs):
        out_ref, weight_ref = refs[len(flat) :]
        place_rows(me_ref, pieces, refs, weight_ref)
        product = dot_f32(normed_ref[...], weight_ref[...]) + bias_ref[...]
        for head in range(block // HEAD_SIZE):
            lanes = slice(head * HEAD_SIZE, (head + 1) * HEAD_SIZE)
            plain = product[:, lanes]
            turned = plain * cosine_ref[...] + pltpu.roll(plain, HEAD_SIZE // 2, 1) * sine_ref[...]
            column = pl.program_id(0) * block + head * HEAD_SIZE
            out_ref[:, lanes] = jnp.where(column < QD + KD, turned, plain).astype(jnp.bfloat16)

    return pl.pallas_call(
        kernel,
        grid_spec=pltpu.PrefetchScalarGridSpec(
            num_scalar_prefetch=1,
            grid=(width // block,),
            in_specs=[
                pl.BlockSpec((tokens, D), lambda step, me_ref: (0, 0)),
                pl.BlockSpec((1, block), lambda step, me_ref: (0, step)),
                pl.BlockSpec((tokens, HEAD_SIZE), lambda step, me_ref: (0, 0)),
                pl.BlockSpec((tokens, HEAD_SIZE), lambda step, me_ref: (0, 0)),
            ]
            + [
                pl.BlockSpec((part.shape[0], block), lambda step, me_ref: (0, step))
                for part in flat
            ],
            out_specs=pl.BlockSpec((tokens, block), lambda step, me_ref: (0, step)),
            scratch_shapes=[pltpu.VMEM((D, block), jnp.bfloat16)],
        ),
        out_shape=jax.ShapeDtypeStruct((tokens, width), jnp.bfloat16),
        compiler_params=vmem_params,
        cost_estimate=pl.CostEstimate(
            flops=2 * tokens * D * width, bytes_accessed=2 * D * width, transcendentals=0
        ),
    )(me, normed, bias[None], cosine, sine, *flat)


def project_back(me, grad_projected, pieces):
    tokens, width = grad_projected.shape
    flat = [part for unused_mask, parts in pieces for part in parts]

    def kernel(me_ref, grad_ref, *refs):
        out_ref, weight_ref = refs[len(flat) :]
        place_rows(me_ref, pieces, refs, weight_ref)
        out_ref[...] = dot_right_t(grad_ref[...], weight_ref[...])

    whole = lambda part: pl.BlockSpec(part.shape, lambda step, me_ref: (0, 0))
    return pl.pallas_call(
        kernel,
        grid_spec=pltpu.PrefetchScalarGridSpec(
            num_scalar_prefetch=1,
            grid=(1,),
            in_specs=[whole(grad_projected)] + [whole(part) for part in flat],
            out_specs=pl.BlockSpec((tokens, D), lambda step, me_ref: (0, 0)),
            scratch_shapes=[pltpu.VMEM((D, width), jnp.bfloat16)],
        ),
        out_shape=jax.ShapeDtypeStruct((tokens, D), jnp.float32),
        compiler_params=vmem_params,
        cost_estimate=pl.CostEstimate(
            flops=2 * tokens * D * width, bytes_accessed=2 * D * width, transcendentals=0
        ),
    )(me, grad_projected, *flat)


def fill_bias(at_ref, position_ref, bias_ref):
    tokens, keys = bias_ref.shape
    row = lax.broadcasted_iota(jnp.int32, (tokens, keys), 0)
    column = lax.broadcasted_iota(jnp.int32, (tokens, keys), 1)
    back = column // tokens
    query_index = at_ref[0] * tokens + row
    key_index = (at_ref[0] - back) * tokens + (column - back * tokens)
    allowed = (key_index <= query_index) & (key_index >= query_index - position_ref[...])
    bias_ref[...] = jnp.where(allowed, 0.0, masked_score)


def join_keys(refs, key_ref, value_ref):
    @pl.when(pl.program_id(0) % GROUP == 0)
    def _():
        for place in range(len(refs)):
            tokens = refs[0].shape[0]
            if (place + 1) * tokens > key_ref.shape[0]:
                break
            rows = slice(place * tokens, (place + 1) * tokens)
            key_ref[rows] = refs[2 * place][...]
            value_ref[rows] = refs[2 * place + 1][...]


def key_specs(both_pieces):
    specs = []
    for piece in both_pieces:
        shape = (piece.shape[0], HEAD_SIZE)
        specs.append(pl.BlockSpec(shape, lambda head, at: (0, head // GROUP)))
        specs.append(pl.BlockSpec(shape, lambda head, at: (0, KEY_VALUE_HEADS + head // GROUP)))
    return specs


def attend(at, position, projected, both_pieces):
    tokens = projected.shape[0]
    count = len(both_pieces)
    keys = count * tokens

    def kernel(at_ref, position_ref, query_ref, *refs):
        out_ref, turn_ref, log_ref, bias_ref, key_ref, value_ref = refs[2 * count :]

        @pl.when(pl.program_id(0) == 0)
        def _():
            fill_bias(at_ref, position_ref, bias_ref)

        join_keys(refs, key_ref, value_ref)

        scores = dot_right_t(query_ref[...], key_ref[...]) * score_scale + bias_ref[...]
        top = jnp.max(scores, axis=1, keepdims=True)
        raised = jnp.exp(scores - top)
        total = jnp.sum(raised, axis=1, keepdims=True)
        probs = (raised * (1.0 / total)).astype(jnp.bfloat16)
        result = dot_f32(probs, value_ref[...])
        out_ref[...] = result.astype(jnp.bfloat16)
        turn_ref[...] = result.T.astype(jnp.bfloat16)
        log_ref[0] = top + jnp.log(total)

    return pl.pallas_call(
        kernel,
        grid_spec=pltpu.PrefetchScalarGridSpec(
            num_scalar_prefetch=1,
            grid=(QUERY_HEADS,),
            in_specs=[
                pl.BlockSpec((tokens, 1), lambda head, at: (0, 0)),
                pl.BlockSpec((tokens, HEAD_SIZE), lambda head, at: (0, head)),
            ]
            + key_specs(both_pieces),
            out_specs=[
                pl.BlockSpec((tokens, HEAD_SIZE), lambda head, at: (0, head)),
                pl.BlockSpec((HEAD_SIZE, tokens), lambda head, at: (head, 0)),
                pl.BlockSpec((1, tokens, 1), lambda head, at: (head, 0, 0)),
            ],
            scratch_shapes=[
                pltpu.VMEM((tokens, keys), jnp.float32),
                pltpu.VMEM((keys, HEAD_SIZE), jnp.bfloat16),
                pltpu.VMEM((keys, HEAD_SIZE), jnp.bfloat16),
            ],
        ),
        out_shape=[
            jax.ShapeDtypeStruct((tokens, QD), jnp.bfloat16),
            jax.ShapeDtypeStruct((QD, tokens), jnp.bfloat16),
            jax.ShapeDtypeStruct((QUERY_HEADS, tokens, 1), jnp.float32),
        ],
        compiler_params=vmem_params,
        cost_estimate=pl.CostEstimate(
            flops=8 * tokens * keys * QD,
            bytes_accessed=8 * tokens * QD,
            transcendentals=QUERY_HEADS * tokens * keys,
        ),
    )(at, position, projected, *[piece for piece in both_pieces for unused in range(2)])


def attend_backward(at, position, projected, both_pieces, incoming, log_total, cosine, sine):
    tokens = projected.shape[0]
    count = len(both_pieces)
    keys = count * tokens

    def kernel(
        at_ref,
        position_ref,
        query_ref,
        incoming_ref,
        log_ref,
        cosine_ref,
        sine_ref,
        *refs,
    ):
        query_grad_ref, key_grad_ref, value_grad_ref = refs[2 * count : 2 * count + 3]
        bias_ref, key_total, value_total, key_ref, value_ref = refs[2 * count + 3 :]
        head = pl.program_id(0)
        join_keys(refs, key_ref, value_ref)

        @pl.when(head == 0)
        def _():
            fill_bias(at_ref, position_ref, bias_ref)

        @pl.when(head % GROUP == 0)
        def _():
            key_total[...] = jnp.zeros_like(key_total)
            value_total[...] = jnp.zeros_like(value_total)

        scores = dot_right_t(query_ref[...], key_ref[...]) * score_scale + bias_ref[...]
        probs = jnp.exp(scores - log_ref[0])
        grad_probs = dot_right_t(incoming_ref[...], value_ref[...])
        inner = jnp.sum(grad_probs * probs, axis=1, keepdims=True)
        grad_scores = (probs * (grad_probs - inner)).astype(jnp.bfloat16)
        value_total[...] += dot_left_t(incoming_ref[...], probs.astype(jnp.bfloat16))
        key_total[...] += dot_left_t(query_ref[...], grad_scores)
        plain = dot_f32(grad_scores, key_ref[...]) * score_scale
        query_grad_ref[...] = (
            plain * cosine_ref[...] - pltpu.roll(plain, HEAD_SIZE // 2, 1) * sine_ref[...]
        ).astype(jnp.bfloat16)

        @pl.when(head % GROUP == GROUP - 1)
        def _():
            key_grad_ref[...] = (key_total[...] * score_scale).T
            value_grad_ref[...] = value_total[...].T

    return pl.pallas_call(
        kernel,
        grid_spec=pltpu.PrefetchScalarGridSpec(
            num_scalar_prefetch=1,
            grid=(QUERY_HEADS,),
            in_specs=[
                pl.BlockSpec((tokens, 1), lambda head, at: (0, 0)),
                pl.BlockSpec((tokens, HEAD_SIZE), lambda head, at: (0, head)),
                pl.BlockSpec((tokens, HEAD_SIZE), lambda head, at: (0, head)),
                pl.BlockSpec((1, tokens, 1), lambda head, at: (head, 0, 0)),
                pl.BlockSpec((tokens, HEAD_SIZE), lambda head, at: (0, 0)),
                pl.BlockSpec((tokens, HEAD_SIZE), lambda head, at: (0, 0)),
            ]
            + key_specs(both_pieces),
            out_specs=[
                pl.BlockSpec((tokens, HEAD_SIZE), lambda head, at: (0, head)),
                pl.BlockSpec((keys, HEAD_SIZE), lambda head, at: (0, head // GROUP)),
                pl.BlockSpec((keys, HEAD_SIZE), lambda head, at: (0, head // GROUP)),
            ],
            scratch_shapes=[
                pltpu.VMEM((tokens, keys), jnp.float32),
                pltpu.VMEM((HEAD_SIZE, keys), jnp.float32),
                pltpu.VMEM((HEAD_SIZE, keys), jnp.float32),
                pltpu.VMEM((keys, HEAD_SIZE), jnp.bfloat16),
                pltpu.VMEM((keys, HEAD_SIZE), jnp.bfloat16),
            ],
        ),
        out_shape=[
            jax.ShapeDtypeStruct((tokens, QD), jnp.bfloat16),
            jax.ShapeDtypeStruct((keys, KD), jnp.float32),
            jax.ShapeDtypeStruct((keys, KD), jnp.float32),
        ],
        compiler_params=vmem_params,
        cost_estimate=pl.CostEstimate(
            flops=20 * tokens * keys * QD,
            bytes_accessed=8 * tokens * QD,
            transcendentals=QUERY_HEADS * tokens * keys,
        ),
    )(
        at,
        position,
        projected,
        incoming,
        log_total,
        cosine,
        sine,
        *[piece for piece in both_pieces for unused in range(2)],
    )


def unit_part(me, normed_all, grad_out_all, gate_up, down, count, first):
    tokens = normed_all.shape[0]
    block = tokens // count
    width = down.shape[0]
    shard = D // count
    weights = list(gate_up) if first else [gate_up]

    def kernel(me_ref, normed_ref, out_grad_ref, down_ref, *refs):
        weight_refs = refs[: len(weights)]
        hidden_ref, grad_ref = refs[len(weights) : len(weights) + 2]
        weight_ref = weight_refs[0]
        if first:
            ordered_ref, weight_ref = refs[len(weights) + 2 :]
            ordered_ref[...] = out_grad_ref[...]

            @pl.when(pl.program_id(0) == 0)
            def _():
                for mask, ref in enumerate(weight_refs):
                    begin = pl.multiple_of((me_ref[0] ^ mask) * shard, shard)
                    weight_ref[pl.ds(begin, shard)] = ref[...]

        values = dot_f32(normed_ref[...], weight_ref[...])
        gate = values[:, :width]
        up = values[:, width:]
        grad_hidden = dot_right_t(out_grad_ref[...], down_ref[...])
        share = 1.0 / (1.0 + jnp.exp(-gate))
        passed = gate * share
        hidden_ref[...] = (passed * up).astype(jnp.bfloat16)
        grad_ref[:, :width] = (
            grad_hidden * up * share * (1.0 + gate * (1.0 - share))
        ).astype(jnp.bfloat16)
        grad_ref[:, width:] = (grad_hidden * passed).astype(jnp.bfloat16)

    def out_grad_index(step, me_ref):
        return (me_ref[0] ^ mask_at(step, count), 0) if first else (step, 0)

    row = lambda step, me_ref: (step, 0)
    fixed = lambda step, me_ref: (0, 0)
    out_specs = [pl.BlockSpec((block, width), row), pl.BlockSpec((block, 2 * width), row)]
    out_shape = [
        jax.ShapeDtypeStruct((tokens, width), jnp.bfloat16),
        jax.ShapeDtypeStruct((tokens, 2 * width), jnp.bfloat16),
    ]
    if first:
        out_specs += [pl.BlockSpec((block, D), row), pl.BlockSpec((D, 2 * width), fixed)]
        out_shape += [
            jax.ShapeDtypeStruct((tokens, D), jnp.bfloat16),
            jax.ShapeDtypeStruct((D, 2 * width), jnp.bfloat16),
        ]
    return pl.pallas_call(
        kernel,
        grid_spec=pltpu.PrefetchScalarGridSpec(
            num_scalar_prefetch=1,
            grid=(count,),
            in_specs=[
                pl.BlockSpec((block, D), row),
                pl.BlockSpec((block, D), out_grad_index),
                pl.BlockSpec((width, D), fixed),
            ]
            + [pl.BlockSpec(weight.shape, fixed) for weight in weights],
            out_specs=out_specs,
        ),
        out_shape=out_shape,
        compiler_params=vmem_params,
        cost_estimate=pl.CostEstimate(
            flops=6 * tokens * D * width,
            bytes_accessed=4 * tokens * D + 6 * tokens * width + 6 * D * width,
            transcendentals=tokens * width,
        ),
    )(me, normed_all, grad_out_all, down, *weights)


def row_terms(me, turned, right, rows_out):
    count, shard, tokens = turned.shape
    width = right.shape[1]
    lanes = width // 128
    half = count // 2
    spare = rows_out - shard * lanes

    def kernel(me_ref, turned_ref, right_ref, odd_ref, even_ref, *scratch):
        step = pl.program_id(0)
        if spare:

            @pl.when(step == 0)
            def _():
                sums = jnp.sum(right_ref[...].astype(jnp.float32), axis=0, keepdims=True)
                scratch[0][...] = jnp.zeros_like(scratch[0])
                for group in range(lanes):
                    scratch[0][group : group + 1] = sums[:, group * 128 : (group + 1) * 128]

        term = dot_f32(turned_ref[0], right_ref[...]).astype(jnp.bfloat16)

        def store(out_ref):
            for group in range(lanes):
                out_ref[0, group * shard : (group + 1) * shard] = term[
                    :, group * 128 : (group + 1) * 128
                ]
            if spare:
                out_ref[0, lanes * shard :] = scratch[0][...].astype(jnp.bfloat16)

        pl.when(step < half)(lambda: store(odd_ref))
        pl.when(step >= half)(lambda: store(even_ref))

    out = jax.ShapeDtypeStruct((half, rows_out, 128), jnp.bfloat16)
    return pl.pallas_call(
        kernel,
        grid_spec=pltpu.PrefetchScalarGridSpec(
            num_scalar_prefetch=1,
            grid=(count,),
            in_specs=[
                pl.BlockSpec(
                    (1, shard, tokens),
                    lambda step, me_ref: (me_ref[0] ^ mask_at(step, count), 0, 0),
                ),
                pl.BlockSpec((tokens, width), lambda step, me_ref: (0, 0)),
            ],
            out_specs=[
                pl.BlockSpec(
                    (1, rows_out, 128), lambda step, me_ref: (jnp.minimum(step, half - 1), 0, 0)
                ),
                pl.BlockSpec(
                    (1, rows_out, 128), lambda step, me_ref: (jnp.maximum(step - half, 0), 0, 0)
                ),
            ],
            scratch_shapes=[pltpu.VMEM((spare, 128), jnp.float32)] if spare else [],
        ),
        out_shape=[out, out],
        compiler_params=vmem_params,
        cost_estimate=pl.CostEstimate(
            flops=2 * D * tokens * width,
            bytes_accessed=256 * count * rows_out,
            transcendentals=0,
        ),
    )(me, turned, right)


def shards(
    tokens,
    positions,
    cotangent,
    attn_norm,
    ffn_norm,
    in_proj,
    in_bias,
    out_proj,
    gate_up,
    down_proj,
):
    token_rows = tokens.shape[1]
    fsdp_count = lax.axis_size("fsdp")
    ctx_count = lax.axis_size("ctx")
    fsdp_me = lax.axis_index("fsdp")
    me = fsdp_me.astype(jnp.int32)[None]
    at = lax.axis_index("ctx").astype(jnp.int32)[None]
    units = FF // fsdp_count
    shard_d = D // fsdp_count
    residual_in = tokens[0].astype(jnp.float32)
    position = positions[0]
    grad_out_b = cotangent[0]

    first_units, second_units, padded_units = unit_widths(units)
    bias_full = gather_small(in_bias).reshape(-1)
    in_scaled = (in_proj.astype(jnp.float32) * attn_norm[:, None]).astype(jnp.bfloat16)
    first_blocks, second_blocks = split_units(me, gate_up, ffn_norm, fsdp_count)
    cosine, sine = rotary_tables(position)
    normed_b = rms_scale(residual_in).astype(jnp.bfloat16)
    in_pieces = gather_pieces(in_scaled, first_blocks, cosine, normed_b)
    gated_blocks = after(first_blocks, in_pieces[0], in_pieces[2], in_pieces[4])
    gate_up_first = [gated_blocks[0]] + [
        exchange(gated_blocks[mask], mask) for mask in range(1, fsdp_count)
    ]
    out_full = lax.all_gather(after(out_proj, in_pieces), "fsdp", axis=0, tiled=True)

    projected = project(
        me, after(normed_b, gate_up_first[1], gate_up_first[2]), in_pieces, bias_full, cosine, sine
    )
    both_b = projected[:, QD:]
    both_pieces = [both_b] + [
        lax.ppermute(both_b, "ctx", [(s, s + back) for s in range(ctx_count - back)])
        for back in range(1, ctx_count)
    ]
    grad_out_all = lax.all_gather(after(grad_out_b, projected), "fsdp", axis=0, tiled=True)
    both_pieces = after(both_pieces, gate_up_first[3], gate_up_first[4])
    attended_b, attended_turned, log_total = attend(at, position[:, None], projected, both_pieces)
    attended_b = after(attended_b, gate_up_first)
    middle = residual_in + dot_f32(attended_b, out_full)
    normed_ffn_b = rms_scale(middle).astype(jnp.bfloat16)
    normed_again, down_again = after((normed_b, down_proj), normed_ffn_b)
    normed_turned = normed_again.T.reshape(fsdp_count, shard_d, token_rows)
    down_first = down_again[:first_units]
    down_second = jnp.pad(down_again[first_units:], ((0, padded_units - second_units), (0, 0)))

    normed_ffn_all = gather_masks(normed_ffn_b, normed_turned, down_first, down_second)
    gate_up_second = swap_blocks(after(second_blocks, normed_ffn_all)).reshape(
        D, 2 * padded_units
    )
    hidden_first, grad_first, grad_out_all, gate_up_first = unit_part(
        me, normed_ffn_all, grad_out_all, gate_up_first, down_first, fsdp_count, True
    )
    odd_rows = normed_ffn_all.shape[0] // 2

    def down_term(hidden, *gates):
        return dot_left_t(after(hidden, *gates), grad_out_all).astype(jnp.bfloat16)

    def gate_term(grad, *gates):
        term = dot_left_t(normed_ffn_all, after(grad, *gates)).astype(jnp.bfloat16)
        return term.reshape(fsdp_count, shard_d, -1)

    def input_grads(rows, *gates):
        return (
            (
                dot_right_t(after(grad_first, *gates)[rows], gate_up_first)
                + dot_right_t(grad_second[rows], gate_up_second)
            )
            .astype(jnp.bfloat16)
            .reshape(fsdp_count // 2, token_rows, D)
        )

    def down_outs(rows, *gates):
        return (
            (
                dot_f32(after(hidden_first, *gates)[rows], down_first)
                + dot_f32(hidden_second[rows], down_second)
            )
            .astype(jnp.bfloat16)
            .reshape(fsdp_count // 2, token_rows, D)
        )

    down_term_a = down_term(hidden_first)
    gate_term_a = gate_term(grad_first, down_term_a)
    down_sum_a, gate_sum_a = lax.psum((down_term_a, gate_term_a), "ctx")
    hidden_second, grad_second = unit_part(
        me,
        after(normed_ffn_all, gate_term_a),
        grad_out_all,
        gate_up_second,
        down_second,
        fsdp_count,
        False,
    )
    grad_normed_odd = input_grads(slice(0, odd_rows), hidden_second)
    normed_sum = MaskSum(grad_normed_odd)
    grad_normed_even = input_grads(slice(odd_rows, None), grad_normed_odd)
    sent = normed_sum.second(grad_normed_even)
    gate_term_b = gate_term(grad_second, sent)
    sent = normed_sum.third(gate_term_b)
    down_term_b = down_term(hidden_second, sent)[:second_units]
    grad_normed_ffn = normed_sum.result(down_term_b).astype(jnp.float32)

    grad_out = grad_out_b.astype(jnp.float32)
    grad_middle = grad_out + norm_backward(middle, grad_normed_ffn)
    grad_middle_b = grad_middle.astype(jnp.bfloat16)
    gate_swapped_b = swap_blocks(after(gate_term_b, grad_middle_b))
    grad_attended_b = dot_right_t(after(grad_middle_b, gate_swapped_b), out_full).astype(
        jnp.bfloat16
    )
    gate_swapped_b, down_term_b, gate_sum_a, down_sum_a = lax.optimization_barrier(
        (gate_swapped_b, down_term_b, gate_sum_a, down_sum_a)
    )
    down_sum_b, gate_sum_b = lax.psum((down_term_b, gate_swapped_b), "ctx")
    in_rows = shard_d * in_proj.shape[1] // 128
    out_rows = shard_d * D // 128
    out_odd, out_even = row_terms(
        me,
        attended_turned.reshape(fsdp_count, shard_d, token_rows),
        after(grad_middle_b, grad_attended_b, gate_sum_a),
        out_rows,
    )
    out_sum = MaskSum(out_odd)
    query_grad, key_grads, value_grads = attend_backward(
        at,
        position[:, None],
        projected,
        both_pieces,
        after(grad_attended_b, out_even),
        log_total,
        cosine,
        sine,
    )
    both_sent = [
        lax.ppermute(
            jnp.concatenate(
                [
                    grads[back * token_rows : (back + 1) * token_rows].astype(jnp.bfloat16)
                    for grads in (key_grads, value_grads)
                ],
                axis=1,
            ),
            "ctx",
            [(s + back, s) for s in range(ctx_count - back)],
        )
        for back in range(1, ctx_count)
    ]
    sent = out_sum.second(out_even, query_grad)
    down_odd = down_outs(slice(0, odd_rows), sent)
    block_sum = MaskSum(down_odd)
    sent = out_sum.third(down_odd)
    down_even = down_outs(slice(odd_rows, None), sent)
    both_grad = jnp.concatenate([key_grads[:token_rows], value_grads[:token_rows]], axis=1)
    for piece in after(both_sent, down_even):
        both_grad = both_grad + piece.astype(jnp.float32)
    turned_back = []
    for head in range(KEY_VALUE_HEADS):
        plain = both_grad[:, head * HEAD_SIZE : (head + 1) * HEAD_SIZE]
        turned_back.append(plain * cosine - jnp.roll(plain, HEAD_SIZE // 2, axis=1) * sine)
    grad_projected_b = jnp.concatenate(
        [query_grad]
        + [part.astype(jnp.bfloat16) for part in turned_back]
        + [both_grad[:, KD:].astype(jnp.bfloat16)],
        axis=1,
    )
    in_odd, in_even = row_terms(me, normed_turned, grad_projected_b, in_rows + 32)
    in_sum = MaskSum(in_odd)
    grad_normed = project_back(me, after(grad_projected_b, in_even), in_pieces)
    sent = in_sum.second(in_even, grad_normed)
    tokens_grad = grad_middle + norm_backward(residual_in, after(grad_normed, sent))
    sent = block_sum.second(down_even, tokens_grad)
    sent = in_sum.third(sent)
    out_part = out_sum.result(sent)
    sent = block_sum.third(out_part)
    in_part = in_sum.result(sent)
    gate_swapped_a = swap_blocks(gate_sum_a)
    in_part = after(in_part, gate_swapped_a)
    terms_part = jnp.concatenate([in_part, out_part], axis=0)
    terms_part, gate_sum_b = lax.optimization_barrier((terms_part, gate_sum_b))
    terms_total = lax.psum(terms_part, "ctx").astype(jnp.float32)
    block_out = middle + block_sum.result(in_part).astype(jnp.float32)
    down_grad = jnp.concatenate([down_sum_a, down_sum_b], axis=0).astype(jnp.float32)
    gate_grad, ffn_grad = join_units(gate_swapped_a, gate_sum_b, gate_up, ffn_norm)

    def lanes_back(rows):
        return rows.reshape(-1, shard_d, 128).transpose(1, 0, 2).reshape(shard_d, -1)

    in_total = lanes_back(terms_total[:in_rows])
    out_grad = lanes_back(terms_total[in_rows + 32 :])
    bias_span = in_bias.shape[0]
    bias_grad = lax.dynamic_slice_in_dim(
        terms_total[in_rows : in_rows + in_proj.shape[1] // 128].reshape(-1),
        fsdp_me * bias_span,
        bias_span,
    )
    in_grad = in_total * attn_norm[:, None]
    attn_grad = jnp.sum(in_total * in_proj.astype(jnp.float32), axis=1)
    return (
        block_out.astype(jnp.bfloat16).reshape(1, token_rows, D),
        tokens_grad.reshape(1, token_rows, D),
        attn_grad,
        ffn_grad,
        in_grad,
        bias_grad,
        out_grad,
        gate_grad,
        down_grad,
    )


def solution(mesh):
    in_specs = (
        P("fsdp", "ctx", None),
        P("fsdp", "ctx"),
        P("fsdp", "ctx", None),
        P("fsdp"),
        P("fsdp"),
        P("fsdp", None),
        P("fsdp"),
        P("fsdp", None),
        P("fsdp", None),
        P("fsdp", None),
    )
    out_specs = (
        P("fsdp", "ctx", None),
        P("fsdp", "ctx", None),
        P("fsdp"),
        P("fsdp"),
        P("fsdp", None),
        P("fsdp"),
        P("fsdp", None),
        P("fsdp", None),
        P("fsdp", None),
    )
    return jax.shard_map(shards, mesh=mesh, in_specs=in_specs, out_specs=out_specs, check_vma=False)
```

```python
import jax
import jax.numpy as jnp
from jax import lax
from jax.experimental import pallas as pl
from jax.experimental.pallas import tpu as pltpu
from jax.sharding import PartitionSpec as P

D = 1536
QUERY_HEADS = 12
KEY_VALUE_HEADS = 2
HEAD_SIZE = 128
FF = 8960
QD = QUERY_HEADS * HEAD_SIZE
KD = KEY_VALUE_HEADS * HEAD_SIZE
GROUP = QUERY_HEADS // KEY_VALUE_HEADS


norm_eps = 1e-06
rope_base = 1000000.0
masked_score = -1e30
score_scale = HEAD_SIZE ** (-0.5)
vmem_params = pltpu.CompilerParams(vmem_limit_bytes=48 * 1024 * 1024)


def rms_scale(value_rows):
    return value_rows * lax.rsqrt(
        jnp.mean(value_rows * value_rows, axis=-1, keepdims=True) + norm_eps
    )


def norm_backward(value_rows, incoming):
    unused_out, pullback = jax.vjp(rms_scale, value_rows)
    return pullback(incoming)[0]


def rotary_tables(position):
    lane = jnp.arange(HEAD_SIZE, dtype=jnp.int32)
    half = HEAD_SIZE // 2
    frequencies = rope_base ** (-((lane % half).astype(jnp.float32) * (2.0 / HEAD_SIZE)))
    angles = position.astype(jnp.float32)[:, None] * frequencies[None, :]
    sign = jnp.where(lane < half, -1.0, 1.0)
    return jnp.cos(angles), jnp.sin(angles) * sign[None, :]


def dot_f32(left, right):
    return jnp.dot(left, right, preferred_element_type=jnp.float32)


def dot_right_t(left, right):
    return lax.dot_general(
        left, right, (((1,), (1,)), ((), ())), preferred_element_type=jnp.float32
    )


def dot_left_t(left, right):
    return lax.dot_general(
        left, right, (((0,), (0,)), ((), ())), preferred_element_type=jnp.float32
    )


def add_low(left, right):
    return left + right


def after(value, *earlier):
    return lax.optimization_barrier((value, earlier))[0]


def exchange(value, mask):
    count = lax.axis_size("fsdp")
    return lax.ppermute(value, "fsdp", [(place, place ^ mask) for place in range(count)])


def gather_pieces(block, *gates):
    count = lax.axis_size("fsdp")
    if count != 8:
        found = [[block]] + [[exchange(block, mask)] for mask in range(2, count, 2)]
    else:
        half = block.shape[0] // 2
        by_x = exchange(block, 2)
        by_y = exchange(block, 4)
        other = exchange(block, 1)
        by_x, by_y = after((by_x, by_y), *gates)
        top = exchange(by_x[:half], 4)
        bottom = exchange(by_y[half:], 2)
        found = [[block], [by_x], [by_y], [top, bottom]]
        others = [[other], [exchange(by_x, 1)], [exchange(by_y, 1)]]
        others.append([exchange(top, 1), exchange(bottom, 1)])
        return [(2 * place, rows) for place, rows in enumerate(found)] + [
            (2 * place + 1, rows) for place, rows in enumerate(others)
        ]
    pieces = []
    for place, rows in enumerate(found):
        pieces.append((2 * place, rows))
        pieces.append((2 * place + 1, [exchange(part, 1) for part in rows]))
    return pieces


def gather_masks(block, *gates):
    count = lax.axis_size("fsdp")
    rows = block.shape[0]
    whole = jnp.zeros((count * rows, block.shape[1]), block.dtype)
    for mask, parts in gather_pieces(block, *gates):
        first = place_of(mask, count) * rows
        for part in parts:
            whole = lax.dynamic_update_slice(whole, part, (first, 0))
            first += part.shape[0]
    return whole


def gather_small(value):
    count = lax.axis_size("fsdp")
    me = lax.axis_index("fsdp")
    bits = count.bit_length() - 1
    found = value
    for bit in list(range(1, bits)) + [0]:
        got = exchange(found, 1 << bit)
        low = (me >> bit) % 2 == 0
        found = jnp.stack([jnp.where(low, found, got), jnp.where(low, got, found)])
    return jnp.moveaxis(found, 0, bits - 1).reshape(count, -1)


def place_of(mask, count):
    return mask // 2 + (1 - mask % 2) * (count // 2)


def mask_at(place, count):
    return jnp.where(place < count // 2, 2 * place + 1, 2 * place - count)


class MaskSum:
    def __init__(self, odd):
        self.got = exchange(odd, 1)

    def second(self, even, *gates):
        count = lax.axis_size("fsdp")
        self.kept = add_low(even, after(self.got, *gates))
        if count == 8:
            half = self.kept.shape[1] // 2
            self.by_x = exchange(self.kept[1::2, :half], 2)
            self.by_y = exchange(self.kept[2:, half:], 4)
        else:
            span = count
            while self.kept.shape[0] > 1:
                span //= 2
                half = self.kept.shape[0] // 2
                self.kept = add_low(self.kept[:half], exchange(self.kept[half:], span))
        return self.kept

    def third(self, *gates):
        if lax.axis_size("fsdp") != 8:
            return self.kept
        half = self.kept.shape[1] // 2
        by_x, by_y = after((self.by_x, self.by_y), *gates)
        self.top = add_low(self.kept[0::2, :half], by_x)
        self.bottom = add_low(self.kept[:2, half:], by_y)
        self.last_y = exchange(self.top[1], 4)
        self.last_x = exchange(self.bottom[1], 2)
        return self.top, self.bottom

    def result(self, *gates):
        if lax.axis_size("fsdp") != 8:
            return self.kept[0]
        last_y, last_x = after((self.last_y, self.last_x), *gates)
        return jnp.concatenate(
            [add_low(self.top[0], last_y), add_low(self.bottom[0], last_x)], axis=0
        )


def swap_blocks(blocks):
    return lax.all_to_all(blocks, "fsdp", 0, 0, tiled=True)


def unit_widths(units):
    first = units // 256 * 128
    second = units - first
    return first, second, -(-second // 128) * 128


def split_units(me, gate_up, gain, count):
    rows, columns = gate_up.shape
    span = columns // 2
    units = span // count
    first, second, padded = unit_widths(units)
    block = 48

    def kernel(me_ref, weight_ref, gain_ref, first_ref, second_ref):
        def scaled(begin, end):
            value = weight_ref[:, begin:end].astype(jnp.float32) * gain_ref[...]
            return value.astype(gate_up.dtype)

        for owner in range(count):
            for side in range(2):
                begin = side * span + owner * units
                first_ref[me_ref[0] ^ owner, :, side * first : (side + 1) * first] = scaled(
                    begin, begin + first
                )
                second_ref[owner, :, side * padded : side * padded + second] = scaled(
                    begin + first, begin + units
                )
                if padded > second:
                    second_ref[
                        owner, :, side * padded + second : (side + 1) * padded
                    ] = jnp.zeros((block, padded - second), gate_up.dtype)

    return pl.pallas_call(
        kernel,
        grid_spec=pltpu.PrefetchScalarGridSpec(
            num_scalar_prefetch=1,
            grid=(rows // block,),
            in_specs=[
                pl.BlockSpec((block, columns), lambda step, me_ref: (step, 0)),
                pl.BlockSpec((block, 1), lambda step, me_ref: (step, 0)),
            ],
            out_specs=[
                pl.BlockSpec((count, block, 2 * first), lambda step, me_ref: (0, step, 0)),
                pl.BlockSpec((count, block, 2 * padded), lambda step, me_ref: (0, step, 0)),
            ],
        ),
        out_shape=[
            jax.ShapeDtypeStruct((count, rows, 2 * first), gate_up.dtype),
            jax.ShapeDtypeStruct((count, rows, 2 * padded), gate_up.dtype),
        ],
        compiler_params=vmem_params,
        cost_estimate=pl.CostEstimate(
            flops=0, bytes_accessed=4 * rows * columns, transcendentals=0
        ),
    )(me, gate_up, gain[:, None])


def join_units(first_part, second_part, gate_up, gain):
    rows, columns = gate_up.shape
    count = first_part.shape[0]
    block = 48
    pieces = rows // block
    span = columns // 2
    units = span // count
    first, second, padded = unit_widths(units)

    def kernel(first_ref, second_ref, weight_ref, gain_ref, whole_ref, sums_ref):
        for owner in range(count):
            for side in range(2):
                begin = side * span + owner * units
                whole_ref[:, begin : begin + first] = first_ref[
                    owner, :, side * first : (side + 1) * first
                ].astype(jnp.float32)
                whole_ref[:, begin + first : begin + units] = second_ref[
                    owner, :, side * padded : side * padded + second
                ].astype(jnp.float32)
        whole = whole_ref[...]
        total = jnp.sum(whole * weight_ref[...].astype(jnp.float32), axis=1, keepdims=True)
        sums_ref[...] = jnp.broadcast_to(total, (block, 128))
        whole_ref[...] = whole * gain_ref[...]

    whole, sums = pl.pallas_call(
        kernel,
        grid=(pieces,),
        in_specs=[
            pl.BlockSpec((count, block, 2 * first), lambda step: (0, step, 0)),
            pl.BlockSpec((count, block, 2 * padded), lambda step: (0, step, 0)),
            pl.BlockSpec((block, columns), lambda step: (step, 0)),
            pl.BlockSpec((block, 1), lambda step: (step, 0)),
        ],
        out_specs=[
            pl.BlockSpec((block, columns), lambda step: (step, 0)),
            pl.BlockSpec((block, 128), lambda step: (step, 0)),
        ],
        out_shape=[
            jax.ShapeDtypeStruct((rows, columns), jnp.float32),
            jax.ShapeDtypeStruct((rows, 128), jnp.float32),
        ],
        compiler_params=vmem_params,
        cost_estimate=pl.CostEstimate(
            flops=2 * rows * columns, bytes_accessed=8 * rows * columns, transcendentals=0
        ),
    )(first_part, second_part, gate_up, gain[:, None])
    return whole, sums[:, 0]


def place_rows(me_ref, pieces, refs, weight_ref):
    place = 0
    for mask, parts in pieces:
        shard = sum(part.shape[0] for part in parts)
        begin = (me_ref[0] ^ mask) * shard
        for part in parts:
            rows = part.shape[0]
            weight_ref[pl.ds(pl.multiple_of(begin, rows), rows)] = refs[place][...]
            begin = begin + rows
            place += 1


def project(me, normed, pieces, bias, cosine, sine):
    tokens = normed.shape[0]
    width = bias.shape[0]
    block = 512
    flat = [part for unused_mask, parts in pieces for part in parts]

    def kernel(me_ref, normed_ref, bias_ref, cosine_ref, sine_ref, *refs):
        out_ref, weight_ref = refs[len(flat) :]
        place_rows(me_ref, pieces, refs, weight_ref)
        product = dot_f32(normed_ref[...], weight_ref[...]) + bias_ref[...]
        for head in range(block // HEAD_SIZE):
            lanes = slice(head * HEAD_SIZE, (head + 1) * HEAD_SIZE)
            plain = product[:, lanes]
            turned = plain * cosine_ref[...] + pltpu.roll(plain, HEAD_SIZE // 2, 1) * sine_ref[...]
            column = pl.program_id(0) * block + head * HEAD_SIZE
            out_ref[:, lanes] = jnp.where(column < QD + KD, turned, plain).astype(jnp.bfloat16)

    return pl.pallas_call(
        kernel,
        grid_spec=pltpu.PrefetchScalarGridSpec(
            num_scalar_prefetch=1,
            grid=(width // block,),
            in_specs=[
                pl.BlockSpec((tokens, D), lambda step, me_ref: (0, 0)),
                pl.BlockSpec((1, block), lambda step, me_ref: (0, step)),
                pl.BlockSpec((tokens, HEAD_SIZE), lambda step, me_ref: (0, 0)),
                pl.BlockSpec((tokens, HEAD_SIZE), lambda step, me_ref: (0, 0)),
            ]
            + [
                pl.BlockSpec((part.shape[0], block), lambda step, me_ref: (0, step))
                for part in flat
            ],
            out_specs=pl.BlockSpec((tokens, block), lambda step, me_ref: (0, step)),
            scratch_shapes=[pltpu.VMEM((D, block), jnp.bfloat16)],
        ),
        out_shape=jax.ShapeDtypeStruct((tokens, width), jnp.bfloat16),
        compiler_params=vmem_params,
        cost_estimate=pl.CostEstimate(
            flops=2 * tokens * D * width, bytes_accessed=2 * D * width, transcendentals=0
        ),
    )(me, normed, bias[None], cosine, sine, *flat)


def project_back(me, grad_projected, pieces):
    tokens, width = grad_projected.shape
    flat = [part for unused_mask, parts in pieces for part in parts]

    def kernel(me_ref, grad_ref, *refs):
        out_ref, weight_ref = refs[len(flat) :]
        place_rows(me_ref, pieces, refs, weight_ref)
        out_ref[...] = dot_right_t(grad_ref[...], weight_ref[...])

    whole = lambda part: pl.BlockSpec(part.shape, lambda step, me_ref: (0, 0))
    return pl.pallas_call(
        kernel,
        grid_spec=pltpu.PrefetchScalarGridSpec(
            num_scalar_prefetch=1,
            grid=(1,),
            in_specs=[whole(grad_projected)] + [whole(part) for part in flat],
            out_specs=pl.BlockSpec((tokens, D), lambda step, me_ref: (0, 0)),
            scratch_shapes=[pltpu.VMEM((D, width), jnp.bfloat16)],
        ),
        out_shape=jax.ShapeDtypeStruct((tokens, D), jnp.float32),
        compiler_params=vmem_params,
        cost_estimate=pl.CostEstimate(
            flops=2 * tokens * D * width, bytes_accessed=2 * D * width, transcendentals=0
        ),
    )(me, grad_projected, *flat)


def fill_bias(at_ref, position_ref, bias_ref):
    tokens, keys = bias_ref.shape
    row = lax.broadcasted_iota(jnp.int32, (tokens, keys), 0)
    column = lax.broadcasted_iota(jnp.int32, (tokens, keys), 1)
    back = column // tokens
    query_index = at_ref[0] * tokens + row
    key_index = (at_ref[0] - back) * tokens + (column - back * tokens)
    allowed = (key_index <= query_index) & (key_index >= query_index - position_ref[...])
    bias_ref[...] = jnp.where(allowed, 0.0, masked_score)


def join_keys(refs, key_ref, value_ref):
    @pl.when(pl.program_id(0) % GROUP == 0)
    def _():
        for place in range(len(refs)):
            tokens = refs[0].shape[0]
            if (place + 1) * tokens > key_ref.shape[0]:
                break
            rows = slice(place * tokens, (place + 1) * tokens)
            key_ref[rows] = refs[2 * place][...]
            value_ref[rows] = refs[2 * place + 1][...]


def key_specs(both_pieces):
    specs = []
    for piece in both_pieces:
        shape = (piece.shape[0], HEAD_SIZE)
        specs.append(pl.BlockSpec(shape, lambda head, at: (0, head // GROUP)))
        specs.append(pl.BlockSpec(shape, lambda head, at: (0, KEY_VALUE_HEADS + head // GROUP)))
    return specs


def attend(at, position, projected, both_pieces):
    tokens = projected.shape[0]
    count = len(both_pieces)
    keys = count * tokens

    def kernel(at_ref, position_ref, query_ref, *refs):
        out_ref, turn_ref, log_ref, bias_ref, key_ref, value_ref = refs[2 * count :]

        @pl.when(pl.program_id(0) == 0)
        def _():
            fill_bias(at_ref, position_ref, bias_ref)

        join_keys(refs, key_ref, value_ref)

        scores = dot_right_t(query_ref[...], key_ref[...]) * score_scale + bias_ref[...]
        top = jnp.max(scores, axis=1, keepdims=True)
        raised = jnp.exp(scores - top)
        total = jnp.sum(raised, axis=1, keepdims=True)
        probs = (raised * (1.0 / total)).astype(jnp.bfloat16)
        result = dot_f32(probs, value_ref[...])
        out_ref[...] = result.astype(jnp.bfloat16)
        turn_ref[...] = result.T.astype(jnp.bfloat16)
        log_ref[0] = top + jnp.log(total)

    return pl.pallas_call(
        kernel,
        grid_spec=pltpu.PrefetchScalarGridSpec(
            num_scalar_prefetch=1,
            grid=(QUERY_HEADS,),
            in_specs=[
                pl.BlockSpec((tokens, 1), lambda head, at: (0, 0)),
                pl.BlockSpec((tokens, HEAD_SIZE), lambda head, at: (0, head)),
            ]
            + key_specs(both_pieces),
            out_specs=[
                pl.BlockSpec((tokens, HEAD_SIZE), lambda head, at: (0, head)),
                pl.BlockSpec((HEAD_SIZE, tokens), lambda head, at: (head, 0)),
                pl.BlockSpec((1, tokens, 1), lambda head, at: (head, 0, 0)),
            ],
            scratch_shapes=[
                pltpu.VMEM((tokens, keys), jnp.float32),
                pltpu.VMEM((keys, HEAD_SIZE), jnp.bfloat16),
                pltpu.VMEM((keys, HEAD_SIZE), jnp.bfloat16),
            ],
        ),
        out_shape=[
            jax.ShapeDtypeStruct((tokens, QD), jnp.bfloat16),
            jax.ShapeDtypeStruct((QD, tokens), jnp.bfloat16),
            jax.ShapeDtypeStruct((QUERY_HEADS, tokens, 1), jnp.float32),
        ],
        compiler_params=vmem_params,
        cost_estimate=pl.CostEstimate(
            flops=8 * tokens * keys * QD,
            bytes_accessed=8 * tokens * QD,
            transcendentals=QUERY_HEADS * tokens * keys,
        ),
    )(at, position, projected, *[piece for piece in both_pieces for unused in range(2)])


def attend_backward(at, position, projected, both_pieces, incoming, log_total, cosine, sine):
    tokens = projected.shape[0]
    count = len(both_pieces)
    keys = count * tokens

    def kernel(
        at_ref,
        position_ref,
        query_ref,
        incoming_ref,
        log_ref,
        cosine_ref,
        sine_ref,
        *refs,
    ):
        query_grad_ref, key_grad_ref, value_grad_ref = refs[2 * count : 2 * count + 3]
        bias_ref, key_total, value_total, key_ref, value_ref = refs[2 * count + 3 :]
        head = pl.program_id(0)
        join_keys(refs, key_ref, value_ref)

        @pl.when(head == 0)
        def _():
            fill_bias(at_ref, position_ref, bias_ref)

        @pl.when(head % GROUP == 0)
        def _():
            key_total[...] = jnp.zeros_like(key_total)
            value_total[...] = jnp.zeros_like(value_total)

        scores = dot_right_t(query_ref[...], key_ref[...]) * score_scale + bias_ref[...]
        probs = jnp.exp(scores - log_ref[0])
        grad_probs = dot_right_t(incoming_ref[...], value_ref[...])
        inner = jnp.sum(grad_probs * probs, axis=1, keepdims=True)
        grad_scores = (probs * (grad_probs - inner)).astype(jnp.bfloat16)
        value_total[...] += dot_left_t(incoming_ref[...], probs.astype(jnp.bfloat16))
        key_total[...] += dot_left_t(query_ref[...], grad_scores)
        plain = dot_f32(grad_scores, key_ref[...]) * score_scale
        query_grad_ref[...] = (
            plain * cosine_ref[...] - pltpu.roll(plain, HEAD_SIZE // 2, 1) * sine_ref[...]
        ).astype(jnp.bfloat16)

        @pl.when(head % GROUP == GROUP - 1)
        def _():
            key_grad_ref[...] = (key_total[...] * score_scale).T
            value_grad_ref[...] = value_total[...].T

    return pl.pallas_call(
        kernel,
        grid_spec=pltpu.PrefetchScalarGridSpec(
            num_scalar_prefetch=1,
            grid=(QUERY_HEADS,),
            in_specs=[
                pl.BlockSpec((tokens, 1), lambda head, at: (0, 0)),
                pl.BlockSpec((tokens, HEAD_SIZE), lambda head, at: (0, head)),
                pl.BlockSpec((tokens, HEAD_SIZE), lambda head, at: (0, head)),
                pl.BlockSpec((1, tokens, 1), lambda head, at: (head, 0, 0)),
                pl.BlockSpec((tokens, HEAD_SIZE), lambda head, at: (0, 0)),
                pl.BlockSpec((tokens, HEAD_SIZE), lambda head, at: (0, 0)),
            ]
            + key_specs(both_pieces),
            out_specs=[
                pl.BlockSpec((tokens, HEAD_SIZE), lambda head, at: (0, head)),
                pl.BlockSpec((keys, HEAD_SIZE), lambda head, at: (0, head // GROUP)),
                pl.BlockSpec((keys, HEAD_SIZE), lambda head, at: (0, head // GROUP)),
            ],
            scratch_shapes=[
                pltpu.VMEM((tokens, keys), jnp.float32),
                pltpu.VMEM((HEAD_SIZE, keys), jnp.float32),
                pltpu.VMEM((HEAD_SIZE, keys), jnp.float32),
                pltpu.VMEM((keys, HEAD_SIZE), jnp.bfloat16),
                pltpu.VMEM((keys, HEAD_SIZE), jnp.bfloat16),
            ],
        ),
        out_shape=[
            jax.ShapeDtypeStruct((tokens, QD), jnp.bfloat16),
            jax.ShapeDtypeStruct((keys, KD), jnp.float32),
            jax.ShapeDtypeStruct((keys, KD), jnp.float32),
        ],
        compiler_params=vmem_params,
        cost_estimate=pl.CostEstimate(
            flops=20 * tokens * keys * QD,
            bytes_accessed=8 * tokens * QD,
            transcendentals=QUERY_HEADS * tokens * keys,
        ),
    )(
        at,
        position,
        projected,
        incoming,
        log_total,
        cosine,
        sine,
        *[piece for piece in both_pieces for unused in range(2)],
    )


def unit_part(me, normed_all, grad_out_all, gate_up, down, count, first):
    tokens = normed_all.shape[0]
    block = tokens // count
    width = down.shape[0]
    shard = D // count
    weights = list(gate_up) if first else [gate_up]

    def kernel(me_ref, normed_ref, out_grad_ref, down_ref, *refs):
        weight_refs = refs[: len(weights)]
        hidden_ref, grad_ref = refs[len(weights) : len(weights) + 2]
        weight_ref = weight_refs[0]
        if first:
            ordered_ref, weight_ref = refs[len(weights) + 2 :]
            ordered_ref[...] = out_grad_ref[...]

            @pl.when(pl.program_id(0) == 0)
            def _():
                for mask, ref in enumerate(weight_refs):
                    begin = pl.multiple_of((me_ref[0] ^ mask) * shard, shard)
                    weight_ref[pl.ds(begin, shard)] = ref[...]

        values = dot_f32(normed_ref[...], weight_ref[...])
        gate = values[:, :width]
        up = values[:, width:]
        grad_hidden = dot_right_t(out_grad_ref[...], down_ref[...])
        share = 1.0 / (1.0 + jnp.exp(-gate))
        passed = gate * share
        hidden_ref[...] = (passed * up).astype(jnp.bfloat16)
        grad_ref[:, :width] = (
            grad_hidden * up * share * (1.0 + gate * (1.0 - share))
        ).astype(jnp.bfloat16)
        grad_ref[:, width:] = (grad_hidden * passed).astype(jnp.bfloat16)

    def out_grad_index(step, me_ref):
        return (me_ref[0] ^ mask_at(step, count), 0) if first else (step, 0)

    row = lambda step, me_ref: (step, 0)
    fixed = lambda step, me_ref: (0, 0)
    out_specs = [pl.BlockSpec((block, width), row), pl.BlockSpec((block, 2 * width), row)]
    out_shape = [
        jax.ShapeDtypeStruct((tokens, width), jnp.bfloat16),
        jax.ShapeDtypeStruct((tokens, 2 * width), jnp.bfloat16),
    ]
    if first:
        out_specs += [pl.BlockSpec((block, D), row), pl.BlockSpec((D, 2 * width), fixed)]
        out_shape += [
            jax.ShapeDtypeStruct((tokens, D), jnp.bfloat16),
            jax.ShapeDtypeStruct((D, 2 * width), jnp.bfloat16),
        ]
    return pl.pallas_call(
        kernel,
        grid_spec=pltpu.PrefetchScalarGridSpec(
            num_scalar_prefetch=1,
            grid=(count,),
            in_specs=[
                pl.BlockSpec((block, D), row),
                pl.BlockSpec((block, D), out_grad_index),
                pl.BlockSpec((width, D), fixed),
            ]
            + [pl.BlockSpec(weight.shape, fixed) for weight in weights],
            out_specs=out_specs,
        ),
        out_shape=out_shape,
        compiler_params=vmem_params,
        cost_estimate=pl.CostEstimate(
            flops=6 * tokens * D * width,
            bytes_accessed=4 * tokens * D + 6 * tokens * width + 6 * D * width,
            transcendentals=tokens * width,
        ),
    )(me, normed_all, grad_out_all, down, *weights)


def row_terms(me, turned, right, rows_out):
    count, shard, tokens = turned.shape
    width = right.shape[1]
    lanes = width // 128
    half = count // 2
    spare = rows_out - shard * lanes

    def kernel(me_ref, turned_ref, right_ref, odd_ref, even_ref, *scratch):
        step = pl.program_id(0)
        if spare:

            @pl.when(step == 0)
            def _():
                sums = jnp.sum(right_ref[...].astype(jnp.float32), axis=0, keepdims=True)
                scratch[0][...] = jnp.zeros_like(scratch[0])
                for group in range(lanes):
                    scratch[0][group : group + 1] = sums[:, group * 128 : (group + 1) * 128]

        term = dot_f32(turned_ref[0], right_ref[...]).astype(jnp.bfloat16)

        def store(out_ref):
            for group in range(lanes):
                out_ref[0, group * shard : (group + 1) * shard] = term[
                    :, group * 128 : (group + 1) * 128
                ]
            if spare:
                out_ref[0, lanes * shard :] = scratch[0][...].astype(jnp.bfloat16)

        pl.when(step < half)(lambda: store(odd_ref))
        pl.when(step >= half)(lambda: store(even_ref))

    out = jax.ShapeDtypeStruct((half, rows_out, 128), jnp.bfloat16)
    return pl.pallas_call(
        kernel,
        grid_spec=pltpu.PrefetchScalarGridSpec(
            num_scalar_prefetch=1,
            grid=(count,),
            in_specs=[
                pl.BlockSpec(
                    (1, shard, tokens),
                    lambda step, me_ref: (me_ref[0] ^ mask_at(step, count), 0, 0),
                ),
                pl.BlockSpec((tokens, width), lambda step, me_ref: (0, 0)),
            ],
            out_specs=[
                pl.BlockSpec(
                    (1, rows_out, 128), lambda step, me_ref: (jnp.minimum(step, half - 1), 0, 0)
                ),
                pl.BlockSpec(
                    (1, rows_out, 128), lambda step, me_ref: (jnp.maximum(step - half, 0), 0, 0)
                ),
            ],
            scratch_shapes=[pltpu.VMEM((spare, 128), jnp.float32)] if spare else [],
        ),
        out_shape=[out, out],
        compiler_params=vmem_params,
        cost_estimate=pl.CostEstimate(
            flops=2 * D * tokens * width,
            bytes_accessed=256 * count * rows_out,
            transcendentals=0,
        ),
    )(me, turned, right)


def shards(
    tokens,
    positions,
    cotangent,
    attn_norm,
    ffn_norm,
    in_proj,
    in_bias,
    out_proj,
    gate_up,
    down_proj,
):
    token_rows = tokens.shape[1]
    fsdp_count = lax.axis_size("fsdp")
    ctx_count = lax.axis_size("ctx")
    fsdp_me = lax.axis_index("fsdp")
    me = fsdp_me.astype(jnp.int32)[None]
    at = lax.axis_index("ctx").astype(jnp.int32)[None]
    units = FF // fsdp_count
    shard_d = D // fsdp_count
    residual_in = tokens[0].astype(jnp.float32)
    position = positions[0]
    grad_out_b = cotangent[0]

    first_units, second_units, padded_units = unit_widths(units)
    bias_full = gather_small(in_bias).reshape(-1)
    in_scaled = (in_proj.astype(jnp.float32) * attn_norm[:, None]).astype(jnp.bfloat16)
    first_blocks, second_blocks = split_units(me, gate_up, ffn_norm, fsdp_count)
    cosine, sine = rotary_tables(position)
    normed_b = rms_scale(residual_in).astype(jnp.bfloat16)
    in_pieces = gather_pieces(in_scaled, first_blocks, cosine, normed_b)
    gated_blocks = after(first_blocks, in_pieces[0], in_pieces[2], in_pieces[4])
    gate_up_first = [gated_blocks[0]] + [
        exchange(gated_blocks[mask], mask) for mask in range(1, fsdp_count)
    ]
    out_full = lax.all_gather(after(out_proj, in_pieces), "fsdp", axis=0, tiled=True)

    projected = project(
        me, after(normed_b, gate_up_first[1], gate_up_first[2]), in_pieces, bias_full, cosine, sine
    )
    both_b = projected[:, QD:]
    both_pieces = [both_b] + [
        lax.ppermute(both_b, "ctx", [(s, s + back) for s in range(ctx_count - back)])
        for back in range(1, ctx_count)
    ]
    grad_out_all = lax.all_gather(after(grad_out_b, projected), "fsdp", axis=0, tiled=True)
    both_pieces = after(both_pieces, gate_up_first[3], gate_up_first[4])
    attended_b, attended_turned, log_total = attend(at, position[:, None], projected, both_pieces)
    attended_b = after(attended_b, gate_up_first)
    middle = residual_in + dot_f32(attended_b, out_full)
    normed_ffn_b = rms_scale(middle).astype(jnp.bfloat16)
    normed_again, down_again = after((normed_b, down_proj), normed_ffn_b)
    normed_turned = normed_again.T.reshape(fsdp_count, shard_d, token_rows)
    down_first = down_again[:first_units]
    down_second = jnp.pad(down_again[first_units:], ((0, padded_units - second_units), (0, 0)))

    normed_ffn_all = gather_masks(normed_ffn_b, normed_turned, down_first, down_second)
    gate_up_second = swap_blocks(after(second_blocks, normed_ffn_all)).reshape(
        D, 2 * padded_units
    )
    hidden_first, grad_first, grad_out_all, gate_up_first = unit_part(
        me, normed_ffn_all, grad_out_all, gate_up_first, down_first, fsdp_count, True
    )
    odd_rows = normed_ffn_all.shape[0] // 2

    def down_term(hidden, *gates):
        return dot_left_t(after(hidden, *gates), grad_out_all).astype(jnp.bfloat16)

    def gate_term(grad, *gates):
        term = dot_left_t(normed_ffn_all, after(grad, *gates)).astype(jnp.bfloat16)
        return term.reshape(fsdp_count, shard_d, -1)

    def input_grads(rows, *gates):
        return (
            (
                dot_right_t(after(grad_first, *gates)[rows], gate_up_first)
                + dot_right_t(grad_second[rows], gate_up_second)
            )
            .astype(jnp.bfloat16)
            .reshape(fsdp_count // 2, token_rows, D)
        )

    def down_outs(rows, *gates):
        return (
            (
                dot_f32(after(hidden_first, *gates)[rows], down_first)
                + dot_f32(hidden_second[rows], down_second)
            )
            .astype(jnp.bfloat16)
            .reshape(fsdp_count // 2, token_rows, D)
        )

    down_term_a = down_term(hidden_first)
    gate_term_a = gate_term(grad_first, down_term_a)
    down_sum_a, gate_sum_a = lax.psum((down_term_a, gate_term_a), "ctx")
    hidden_second, grad_second = unit_part(
        me,
        after(normed_ffn_all, gate_term_a),
        grad_out_all,
        gate_up_second,
        down_second,
        fsdp_count,
        False,
    )
    grad_normed_odd = input_grads(slice(0, odd_rows), hidden_second)
    normed_sum = MaskSum(grad_normed_odd)
    grad_normed_even = input_grads(slice(odd_rows, None), grad_normed_odd)
    sent = normed_sum.second(grad_normed_even)
    gate_term_b = gate_term(grad_second, sent)
    sent = normed_sum.third(gate_term_b)
    down_term_b = down_term(hidden_second, sent)[:second_units]
    grad_normed_ffn = normed_sum.result(down_term_b).astype(jnp.float32)

    grad_out = grad_out_b.astype(jnp.float32)
    grad_middle = grad_out + norm_backward(middle, grad_normed_ffn)
    grad_middle_b = grad_middle.astype(jnp.bfloat16)
    gate_swapped_b = swap_blocks(after(gate_term_b, grad_middle_b))
    grad_attended_b = dot_right_t(grad_middle_b, out_full).astype(jnp.bfloat16)
    in_rows = shard_d * in_proj.shape[1] // 128
    out_rows = shard_d * D // 128
    out_odd, out_even = row_terms(
        me,
        attended_turned.reshape(fsdp_count, shard_d, token_rows),
        after(grad_middle_b, grad_attended_b),
        out_rows,
    )
    out_sum = MaskSum(out_odd)
    query_grad, key_grads, value_grads = attend_backward(
        at,
        position[:, None],
        projected,
        both_pieces,
        after(grad_attended_b, out_even),
        log_total,
        cosine,
        sine,
    )
    both_sent = [
        lax.ppermute(
            jnp.concatenate(
                [
                    grads[back * token_rows : (back + 1) * token_rows].astype(jnp.bfloat16)
                    for grads in (key_grads, value_grads)
                ],
                axis=1,
            ),
            "ctx",
            [(s + back, s) for s in range(ctx_count - back)],
        )
        for back in range(1, ctx_count)
    ]
    sent = out_sum.second(out_even, query_grad)
    down_odd = down_outs(slice(0, odd_rows), sent)
    block_sum = MaskSum(down_odd)
    sent = out_sum.third(down_odd)
    down_even = down_outs(slice(odd_rows, None), sent)
    both_grad = jnp.concatenate([key_grads[:token_rows], value_grads[:token_rows]], axis=1)
    for piece in after(both_sent, down_even, gate_swapped_b):
        both_grad = both_grad + piece.astype(jnp.float32)
    turned_back = []
    for head in range(KEY_VALUE_HEADS):
        plain = both_grad[:, head * HEAD_SIZE : (head + 1) * HEAD_SIZE]
        turned_back.append(plain * cosine - jnp.roll(plain, HEAD_SIZE // 2, axis=1) * sine)
    grad_projected_b = jnp.concatenate(
        [query_grad]
        + [part.astype(jnp.bfloat16) for part in turned_back]
        + [both_grad[:, KD:].astype(jnp.bfloat16)],
        axis=1,
    )
    gate_swapped_b, gate_sum_a, down_sum_a = lax.optimization_barrier(
        (gate_swapped_b, gate_sum_a, down_sum_a)
    )
    gate_sum_b = lax.psum(gate_swapped_b, "ctx")
    in_odd, in_even = row_terms(
        me, normed_turned, after(grad_projected_b, gate_sum_a), in_rows + 32
    )
    in_sum = MaskSum(in_odd)
    grad_normed = project_back(me, after(grad_projected_b, in_even), in_pieces)
    sent = in_sum.second(in_even, grad_normed)
    tokens_grad = grad_middle + norm_backward(residual_in, after(grad_normed, sent))
    sent = block_sum.second(down_even, tokens_grad)
    sent = in_sum.third(sent)
    out_part = out_sum.result(sent)
    sent = block_sum.third(out_part)
    in_part = in_sum.result(sent)
    gate_swapped_a = swap_blocks(gate_sum_a)
    in_part = after(in_part, gate_swapped_a)
    terms_part = jnp.concatenate([in_part, out_part], axis=0)
    terms_part, down_term_b, gate_sum_b = lax.optimization_barrier(
        (terms_part, down_term_b, gate_sum_b)
    )
    terms_total, down_sum_b = lax.psum((terms_part, down_term_b), "ctx")
    terms_total = terms_total.astype(jnp.float32)
    block_out = middle + block_sum.result(in_part).astype(jnp.float32)
    down_grad = jnp.concatenate([down_sum_a, down_sum_b], axis=0).astype(jnp.float32)
    gate_grad, ffn_grad = join_units(gate_swapped_a, gate_sum_b, gate_up, ffn_norm)

    def lanes_back(rows):
        return rows.reshape(-1, shard_d, 128).transpose(1, 0, 2).reshape(shard_d, -1)

    in_total = lanes_back(terms_total[:in_rows])
    out_grad = lanes_back(terms_total[in_rows + 32 :])
    bias_span = in_bias.shape[0]
    bias_grad = lax.dynamic_slice_in_dim(
        terms_total[in_rows : in_rows + in_proj.shape[1] // 128].reshape(-1),
        fsdp_me * bias_span,
        bias_span,
    )
    in_grad = in_total * attn_norm[:, None]
    attn_grad = jnp.sum(in_total * in_proj.astype(jnp.float32), axis=1)
    return (
        block_out.astype(jnp.bfloat16).reshape(1, token_rows, D),
        tokens_grad.reshape(1, token_rows, D),
        attn_grad,
        ffn_grad,
        in_grad,
        bias_grad,
        out_grad,
        gate_grad,
        down_grad,
    )


def solution(mesh):
    in_specs = (
        P("fsdp", "ctx", None),
        P("fsdp", "ctx"),
        P("fsdp", "ctx", None),
        P("fsdp"),
        P("fsdp"),
        P("fsdp", None),
        P("fsdp"),
        P("fsdp", None),
        P("fsdp", None),
        P("fsdp", None),
    )
    out_specs = (
        P("fsdp", "ctx", None),
        P("fsdp", "ctx", None),
        P("fsdp"),
        P("fsdp"),
        P("fsdp", None),
        P("fsdp"),
        P("fsdp", None),
        P("fsdp", None),
        P("fsdp", None),
    )
    return jax.shard_map(shards, mesh=mesh, in_specs=in_specs, out_specs=out_specs, check_vma=False)
```
